32 devices in a mesh: col: 4 (over x, core), af: 8 (over z, y).
Axes of the slice: x: 2, y: 2, z: 4, core: 2. Of those that a mesh axis runs over, the one named last changes fastest.
Arguments:
- coarse_state: float32 [3, 8, 128, 1024], P(None, None, 'af', 'col'), may hold values from 0.1 to 2
- coarse_kappa: float32 [8, 128, 1024], P(None, 'af', 'col'), may hold values from 0.25 to 1
- coarse_rate: float32 [8, 128, 1024], P(None, 'af', 'col'), may hold values from 0.5 to 6
- fine_state: float32 [128, 3, 32, 1024], P(('col', 'af')), may hold values from 0.1 to 2
- fine_kappa: float32 [128, 32, 1024], P(('col', 'af')), may hold values from 0.25 to 1
- fine_rate: float32 [128, 32, 1024], P(('col', 'af')), may hold values from 0.5 to 6
- boxes: int32 [128, 2], replicated, may hold values from 0 to 127, as said below
- cover: int32 [16, 128], replicated, may hold values from -1 to 127, as said below
Outputs:
- coarse_out: float32 [3, 8, 128, 1024], P(None, None, 'af', 'col')
- fine_out: float32 [128, 3, 32, 1024], P(('col', 'af'))
The draws below stay inside these ranges and needn't reach their ends.
Inputs may be any that keep to these rules, and one draw needn't show every extreme that they name: `boxes`: A patch's block spans all 8 planes; it lies in the 32 block rows of one col index, never in the first or last of them nor in the slab's first or last block column, and no two patches share a face. The patches whose blocks lie in one col index's rows are the rows of the fine arrays held by that col index, in no particular order. The 2 block columns of one af index hold at most 10 patches, and in every col index some af index holds exactly that many. cover[bx, by] is the patch whose block is (bx, by), or -1 where none is; it agrees with boxes, and every patch appears once.
All inputs are finite; a program needn't handle non-finite values.
Results may differ from the reference program's by a relative error of at most 0.0003.
Values sent between devices are 32-bit elements; how exact they have to be, the bound alone decides.
No kernel may reach another device: no remote copies, remote signals or barrier semaphores. Data moves between devices by JAX's collectives and lax.ppermute only.
A program may use at most 192 MiB of HBM per device.

```python
import math
import jax
import jax.numpy as jnp
from jax import lax

NZC = 8
RATIO = 4
BLK = 8
CXB = 2
CYB = 32
SLOT_DEV = 4
MOST_OWN = 10
NBX = 16
NBY = 128
NXC = 128
NYC = 1024
PATCHES = 128
FZ = 32
FXY = 1024
N_COL = 4
N_AF = 8


def owner_counts(key):
    others = N_AF - 1
    share_total = N_AF * SLOT_DEV - MOST_OWN
    base_count = share_total // others
    leftover = share_total - base_count * others
    key_star, key_extra = jax.random.split(key, 2)
    busiest = jax.random.randint(key_star, (), 1, N_AF - 1)
    ranking = jax.random.permutation(key_extra, others)
    counts = base_count + (ranking < leftover).astype(jnp.int32)
    owners = jnp.arange(N_AF, dtype=jnp.int32)
    shifted = jnp.clip(owners - (owners > busiest).astype(jnp.int32), 0, others - 1)
    return jnp.where(owners == busiest, MOST_OWN, counts[shifted]).astype(jnp.int32)


def region_pick(key, col_id, owner_id, wanted):
    cell_count = CXB * CYB
    region_key = jax.random.fold_in(jax.random.fold_in(key, col_id + 1000), owner_id)
    priority = jax.random.permutation(region_key, cell_count).reshape(CXB, CYB)
    global_x = owner_id * CXB + jnp.arange(CXB, dtype=jnp.int32)[:, None]
    local_y = jnp.arange(CYB, dtype=jnp.int32)[None, :]
    global_y = col_id * CYB + local_y
    eligible = ((global_x + global_y) % 2 == 0) & (global_x >= 1) & (global_x <= NBX - 2) & (local_y >= 1) & (local_y <= CYB - 2)
    scores = jnp.where(eligible, priority, priority + cell_count).reshape(-1)
    ranks = jnp.argsort(jnp.argsort(scores, stable=True), stable=True)
    return (ranks < wanted).reshape(CXB, CYB)


def relabel(key, col_id, grid_row):
    group_size = N_AF * SLOT_DEV
    ranks = jnp.clip(jnp.cumsum(grid_row).astype(jnp.int32) - 1, 0, group_size - 1)
    shuffled = jax.random.permutation(jax.random.fold_in(key, col_id + 5000), group_size).astype(jnp.int32)
    first_owner = jnp.argmax(grid_row).astype(jnp.int32) // CYB // CXB
    target = ((first_owner + N_AF // 2) % N_AF * SLOT_DEV).astype(jnp.int32)
    first_value = shuffled[0]
    shuffled = jnp.where(shuffled == target, first_value, shuffled)
    shuffled = shuffled.at[0].set(target)
    labels = shuffled[ranks] + col_id * group_size
    return jnp.where(grid_row > 0, labels, -1).astype(jnp.int32)


def patch_layout(key):
    base_key = jax.random.fold_in(key, 77)
    col_ids = jnp.arange(N_COL, dtype=jnp.int32)
    counts = jax.vmap(lambda col_id: owner_counts(jax.random.fold_in(base_key, col_id)))(col_ids)
    owner_ids = jnp.arange(N_AF, dtype=jnp.int32)
    chosen = jax.vmap(lambda col_id, want_row: jax.vmap(lambda owner_id, wanted: region_pick(base_key, col_id, owner_id, wanted))(owner_ids, want_row))(col_ids, counts)
    flat_grid = chosen.reshape(N_COL, NBX * CYB).astype(jnp.int32)
    cover_cols = jax.vmap(lambda col_id, grid_row: relabel(base_key, col_id, grid_row))(col_ids, flat_grid).reshape(N_COL, NBX, CYB)
    cover = cover_cols.transpose(1, 0, 2).reshape(NBX, NBY).astype(jnp.int32)
    grid_x = jnp.broadcast_to(jnp.arange(NBX, dtype=jnp.int32)[:, None], (NBX, NBY))
    grid_y = jnp.broadcast_to(jnp.arange(NBY, dtype=jnp.int32)[None, :], (NBX, NBY))
    target = jnp.where(cover >= 0, cover, PATCHES).reshape(-1)
    boxes = jnp.zeros((PATCHES, 2), jnp.int32)
    boxes = boxes.at[target, 0].set(grid_x.reshape(-1), mode='drop')
    boxes = boxes.at[target, 1].set(grid_y.reshape(-1), mode='drop')
    return (boxes, cover)


def draw_boxes(key, part):
    return patch_layout(key)[0]


def draw_cover(key, part):
    return patch_layout(key)[1]


def block_levels(own_key, dims, cuts, smallest, largest):
    def one(axis_at, blocks):
        steps = jax.random.uniform(jax.random.fold_in(jax.random.fold_in(own_key, 6), axis_at), (blocks,), jnp.float32, smallest / len(cuts), largest / len(cuts))
        return jnp.repeat(jnp.exp(steps), dims[axis_at] // blocks).reshape((-1,) + (1,) * (len(dims) - axis_at - 1))

    gain = one(*cuts[0])
    for cut in cuts[1:]:
        gain = gain * one(*cut)
    return gain


def setup_inputs(seed: int = 0) -> dict:
    splits = jax.random.split(jax.random.key(seed), 9)
    coarse_state = jnp.clip(0.1 + 1.9 * jax.random.uniform(splits[0], (3, NZC, NXC, NYC), jnp.float32) ** block_levels(splits[0], (3, NZC, NXC, NYC), ((2, 8), (3, 4)), -0.2, 0.2), 0.1, 2.0)
    coarse_kappa = jnp.clip(jnp.exp(math.log(1.0) - 1.3862944 * jax.random.uniform(splits[1], (NZC, NXC, NYC), jnp.float32) ** block_levels(splits[1], (NZC, NXC, NYC), ((1, 8), (2, 4)), -0.2, 0.2)), 0.25, 1.0)
    coarse_rate = jnp.clip(jnp.exp(math.log(6.0) - 2.4849066 * jax.random.uniform(splits[2], (NZC, NXC, NYC), jnp.float32) ** block_levels(splits[2], (NZC, NXC, NYC), ((1, 8), (2, 4)), -0.2, 0.2)), 0.5, 6.0)
    fine_state = jnp.clip(0.1 + 1.9 * jax.random.uniform(splits[3], (PATCHES, 3, FZ, FXY), jnp.float32) ** block_levels(splits[3], (PATCHES, 3, FZ, FXY), ((0, 32),), -0.2, 0.2), 0.1, 2.0)
    fine_kappa = jnp.clip(jnp.exp(math.log(1.0) - 1.3862944 * jax.random.uniform(splits[4], (PATCHES, FZ, FXY), jnp.float32) ** block_levels(splits[4], (PATCHES, FZ, FXY), ((0, 32),), -0.2, 0.2)), 0.25, 1.0)
    fine_rate = jnp.clip(jnp.exp(math.log(6.0) - 2.4849066 * jax.random.uniform(splits[5], (PATCHES, FZ, FXY), jnp.float32) ** block_levels(splits[5], (PATCHES, FZ, FXY), ((0, 32),), -0.2, 0.2)), 0.5, 6.0)
    boxes = draw_boxes(jax.random.fold_in(splits[8], 71), 0)
    cover = draw_cover(jax.random.fold_in(splits[8], 71), 0)
    return {"coarse_state": coarse_state, "coarse_kappa": coarse_kappa, "coarse_rate": coarse_rate, "fine_state": fine_state, "fine_kappa": fine_kappa, "fine_rate": fine_rate, "boxes": boxes, "cover": cover}


DT_COARSE = 1.0 / 28.0
DIFFUSE = (1.0, 0.7, 0.45)
NEIGHBOURS = ((1, 0, 0), (-1, 0, 0), (0, 1, 0), (0, -1, 0), (0, 0, 1), (0, 0, -1))


def harmonic(first, second):
    summed = first + second
    positive = summed > 0.0
    return jnp.where(positive, 2.0 * first * second / jnp.where(positive, summed, 1.0), 0.0)


def combine(center, conduct, neighbour_list, reaction, inv_square, step_size):
    summed = jnp.zeros_like(center)
    for values, coeffs in neighbour_list:
        summed = summed + harmonic(conduct, coeffs) * (values - center)
    spread = jnp.stack([DIFFUSE[0] * summed[0], DIFFUSE[1] * summed[1], DIFFUSE[2] * summed[2]]) * inv_square
    forward = reaction * (center[0] * center[1] - center[2])
    change = spread + jnp.stack([-forward, -forward, forward])
    return center + step_size * change


def window(values, step_z, step_x, step_y):
    depth_len = values.shape[-3] - 2
    across = values.shape[-2] - 2
    along_len = values.shape[-1] - 2
    return values[..., 1 + step_z:1 + step_z + depth_len, 1 + step_x:1 + step_x + across, 1 + step_y:1 + step_y + along_len]


def coarse_advance(padded_xy, conduct_xy, reaction):
    padded = jnp.pad(padded_xy, ((0, 0), (1, 1), (0, 0), (0, 0)))
    conduct = jnp.pad(conduct_xy, ((1, 1), (0, 0), (0, 0)))
    neighbour_list = [(window(padded, offsets[0], offsets[1], offsets[2]), window(conduct, offsets[0], offsets[1], offsets[2])) for offsets in NEIGHBOURS]
    return combine(window(padded, 0, 0, 0), window(conduct, 0, 0, 0), neighbour_list, reaction, 1.0, DT_COARSE)


def upsample(strips):
    return jnp.repeat(jnp.repeat(strips, RATIO, axis=-2), RATIO, axis=-1)


def patch_step(fields, conduct, reaction, strips):
    ghosts = upsample(strips)
    edge_len = ghosts.shape[-1]
    position = lax.broadcasted_iota(jnp.int32, (1, edge_len * edge_len), 1)
    column = position % edge_len
    row_pos = position // edge_len
    zero_fields = jnp.zeros_like(fields[:, :1])
    zero_conduct = jnp.zeros_like(conduct[:1])
    upward = (jnp.concatenate([fields[:, 1:], zero_fields], axis=1), jnp.concatenate([conduct[1:], zero_conduct], axis=0))
    downward = (jnp.concatenate([zero_fields, fields[:, :-1]], axis=1), jnp.concatenate([zero_conduct, conduct[:-1]], axis=0))
    last_row = row_pos == edge_len - 1
    first_row = row_pos == 0
    last_col = column == edge_len - 1
    first_col = column == 0
    next_x = (jnp.where(last_row, jnp.tile(ghosts[1], (1, 1, edge_len)), jnp.roll(fields, -edge_len, axis=-1)), jnp.where(last_row, conduct, jnp.roll(conduct, -edge_len, axis=-1)))
    prev_x = (jnp.where(first_row, jnp.tile(ghosts[0], (1, 1, edge_len)), jnp.roll(fields, edge_len, axis=-1)), jnp.where(first_row, conduct, jnp.roll(conduct, edge_len, axis=-1)))
    next_y = (jnp.where(last_col, jnp.repeat(ghosts[3], edge_len, axis=-1), jnp.roll(fields, -1, axis=-1)), jnp.where(last_col, conduct, jnp.roll(conduct, -1, axis=-1)))
    prev_y = (jnp.where(first_col, jnp.repeat(ghosts[2], edge_len, axis=-1), jnp.roll(fields, 1, axis=-1)), jnp.where(first_col, conduct, jnp.roll(conduct, 1, axis=-1)))
    return combine(fields, conduct, [upward, downward, next_x, prev_x, next_y, prev_y], reaction, float(RATIO * RATIO), DT_COARSE / RATIO)


def restrict(fields):
    shaped = fields.reshape(3, NZC, RATIO, BLK, RATIO, BLK, RATIO)
    return jnp.mean(shaped, axis=(2, 4, 6)).reshape(-1)


def patch_rims(coarse, block_xy):
    anchor = jnp.zeros((), jnp.int32)
    start_x = (block_xy[0] * BLK).astype(jnp.int32)
    start_y = (block_xy[1] * BLK).astype(jnp.int32)
    lower_x = lax.dynamic_slice(coarse, (anchor, anchor, start_x - 1, start_y), (3, NZC, 1, BLK))[:, :, 0, :]
    upper_x = lax.dynamic_slice(coarse, (anchor, anchor, start_x + BLK, start_y), (3, NZC, 1, BLK))[:, :, 0, :]
    lower_y = lax.dynamic_slice(coarse, (anchor, anchor, start_x, start_y - 1), (3, NZC, BLK, 1))[:, :, :, 0]
    upper_y = lax.dynamic_slice(coarse, (anchor, anchor, start_x, start_y + BLK), (3, NZC, BLK, 1))[:, :, :, 0]
    return jnp.stack([lower_x, upper_x, lower_y, upper_y])


def reference(coarse_state, coarse_kappa, coarse_rate, fine_state, fine_kappa, fine_rate, boxes, cover):
    padded = jnp.pad(coarse_state, ((0, 0), (0, 0), (1, 1), (1, 1)))
    conduct = jnp.pad(coarse_kappa, ((0, 0), (1, 1), (1, 1)))
    coarse_new = coarse_advance(padded, conduct, coarse_rate)

    def one_patch(patch_items):
        fields, patch_kappa, patch_rate, block_xy = patch_items
        earlier = patch_rims(coarse_state, block_xy)
        updated = patch_rims(coarse_new, block_xy)
        for substep in range(RATIO):
            fraction = substep / RATIO
            strips = earlier + fraction * (updated - earlier)
            fields = patch_step(fields, patch_kappa, patch_rate, strips)
        return fields, restrict(fields)

    group_count = PATCHES // 32
    batched = jax.vmap(one_patch)
    stacked = (fine_state.reshape(group_count, 32, 3, FZ, FXY), fine_kappa.reshape(group_count, 32, FZ, FXY), fine_rate.reshape(group_count, 32, FZ, FXY), boxes.reshape(group_count, 32, 2))
    fine_out, averages = lax.map(batched, stacked)
    fine_out = fine_out.reshape(PATCHES, 3, FZ, FXY)
    averages = averages.reshape(PATCHES, -1)
    picked = averages[jnp.maximum(cover, 0)]
    picked = picked.reshape(NBX, NBY, 3, NZC, BLK, BLK).transpose(2, 3, 0, 4, 1, 5).reshape(3, NZC, NXC, NYC)
    covered = jnp.repeat(jnp.repeat(cover >= 0, BLK, axis=0), BLK, axis=1)
    coarse_out = jnp.where(covered[None, None], picked, coarse_new)
    return coarse_out, fine_out
```

```python
import functools

import jax
import jax.numpy as jnp
import ml_dtypes
import numpy as np
from jax import lax
from jax.experimental import pallas as pl
from jax.experimental.pallas import tpu as pltpu
from jax.sharding import PartitionSpec as P

NZC = 8
RATIO = 4
BLK = 8
SPECIES = 3
EDGE = BLK * RATIO
FZ = NZC * RATIO
LANES = 128
TILES = EDGE * EDGE // LANES
STRIDE = 48
PAD = 8
FACES = 4
STRIP_ROWS = 2 * SPECIES * NZC
AVG_ROWS = SPECIES * NZC * BLK

DT_COARSE = 1.0 / 28.0
DIFFUSE = (1.0, 0.7, 0.45)
SIGNS = (-1.0, -1.0, 1.0)
FINE_SCALE = RATIO * RATIO * DT_COARSE / RATIO
DT_FINE = DT_COARSE / RATIO


def lane_ids(shape):
    return lax.broadcasted_iota(jnp.int32, shape, len(shape) - 1)


def roll_lanes(values, shift):
    width = values.shape[-1]
    shift = shift % width
    return values if shift == 0 else pltpu.roll(values, shift, values.ndim - 1)


def split_pair(values):
    high = values.astype(jnp.bfloat16)
    low = (values - high.astype(jnp.float32)).astype(jnp.bfloat16)
    return high, low


def harmonic(first, second):
    summed = first + second
    positive = summed > 0.0
    return jnp.where(positive, 2.0 * first * second / jnp.where(positive, summed, 1.0), 0.0)


def block_vectors(boxes_ref, group, block_cols, block_rows):
    lanes = group * BLK
    patch = lane_ids((8, lanes)) // BLK
    base = lax.axis_index("col") * group
    first_col = lax.axis_index("af") * block_cols
    first_row = lax.axis_index("col") * block_rows
    columns = jnp.full((8, lanes), -9, jnp.int32)
    starts = jnp.full((8, lanes), -9, jnp.int32)
    for q in range(group):
        here = patch == q
        columns = jnp.where(here, boxes_ref[base + q, 0] - first_col, columns)
        starts = jnp.where(here, (boxes_ref[base + q, 1] - first_row) * BLK, starts)
    return columns, starts + lane_ids((8, lanes)) % BLK


def selector(columns, cells, column, cells_y):
    wanted = jnp.where(columns == column, cells, -1)
    lanes = wanted.shape[-1]
    row = lax.broadcasted_iota(jnp.int32, (8, lanes), 0)
    pieces = [
        jnp.where(row + 8 * piece == wanted, 1.0, 0.0).astype(jnp.float32)
        for piece in range(cells_y // 8)
    ]
    return jnp.concatenate(pieces, axis=0).astype(jnp.bfloat16)


def edges_kernel(state_ref, kappa_ref, xlo_ref, xhi_ref, ylo_ref, yhi_ref, *, cells_x, cells_y):
    planes = SPECIES * NZC
    lane = lane_ids((cells_x, LANES))
    low = jnp.zeros((cells_x, LANES), jnp.float32)
    high = jnp.zeros((cells_x, LANES), jnp.float32)
    for plane in range(planes + NZC):
        if plane < planes:
            ref, start = state_ref, plane * cells_x
        else:
            ref, start = kappa_ref, (plane - planes) * cells_x
        first = ref[start : start + cells_x, 0:LANES]
        last = ref[start : start + cells_x, cells_y - LANES : cells_y]
        xlo_ref[plane : plane + 1, :] = ref[start : start + 1, :]
        xhi_ref[plane : plane + 1, :] = ref[start + cells_x - 1 : start + cells_x, :]
        low = jnp.where(lane == plane, roll_lanes(first, plane), low)
        high = jnp.where(lane == plane, roll_lanes(last, plane + 1), high)
    ylo_ref[...] = low
    yhi_ref[...] = high


def coarse_kernel(
    boxes_ref,
    state_ref,
    kappa_ref,
    rate_ref,
    xl_ref,
    xr_ref,
    yl_ref,
    yr_ref,
    new_ref,
    send_ref,
    padded,
    fresh,
    *,
    cells_x,
    cells_y,
    group,
    slots,
):
    halves = cells_y // LANES
    span = cells_x + 2 * PAD

    def base(field, half, z):
        return ((field * halves + half) * NZC + z) * span

    for field in range(SPECIES + 1):
        for half in range(halves):
            cols = pl.ds(half * LANES, LANES)
            for z in range(NZC):
                if field < SPECIES:
                    start = (field * NZC + z) * cells_x
                    plane = state_ref[start : start + cells_x, cols]
                else:
                    plane = kappa_ref[z * cells_x : (z + 1) * cells_x, cols]
                at = base(field, half, z) + PAD
                padded[at : at + cells_x, :] = plane
            at = base(field, half, 0) + PAD
            rows = slice(field * NZC, (field + 1) * NZC)
            padded[pl.ds(at - 1, NZC, stride=span), :] = xl_ref[rows, cols]
            padded[pl.ds(at + cells_x, NZC, stride=span), :] = xr_ref[rows, cols]

    lane = lane_ids((cells_x, LANES))
    lower_edge = yl_ref[...]
    upper_edge = yr_ref[...]

    def load(field, half, z, shift):
        at = base(field, half, z) + PAD + shift
        return padded[at : at + cells_x, :]

    def along_y(field, half, z):
        plane = field * NZC + z
        here = load(field, half, z, 0)
        if half + 1 < halves:
            after = roll_lanes(load(field, half + 1, z, 0), -1)
        else:
            after = roll_lanes(upper_edge, LANES - 1 - plane)
        if half > 0:
            before = roll_lanes(load(field, half - 1, z, 0), 1)
        else:
            before = roll_lanes(lower_edge, -plane)
        return (
            jnp.where(lane == LANES - 1, after, roll_lanes(here, -1)),
            jnp.where(lane == 0, before, roll_lanes(here, 1)),
        )

    def neighbours(field, half, z):
        found = [load(field, half, z, 1), load(field, half, z, -1), *along_y(field, half, z)]
        if z + 1 < NZC:
            found.append(load(field, half, z + 1, 0))
        if z > 0:
            found.append(load(field, half, z - 1, 0))
        return found

    for z in range(NZC):
        for half in range(halves):
            cols = pl.ds(half * LANES, LANES)
            conduct = load(SPECIES, half, z, 0)
            coeffs = [harmonic(conduct, other) for other in neighbours(SPECIES, half, z)]
            centers = [load(field, half, z, 0) for field in range(SPECIES)]
            forward = (DT_COARSE * rate_ref[z * cells_x : (z + 1) * cells_x, cols]) * (
                centers[0] * centers[1] - centers[2]
            )
            for field in range(SPECIES):
                center = centers[field]
                flux = jnp.zeros_like(center)
                for coeff, other in zip(coeffs, neighbours(field, half, z)):
                    flux = flux + coeff * (other - center)
                start = (field * NZC + z) * cells_x
                result = center + (DT_COARSE * DIFFUSE[field]) * flux + SIGNS[field] * forward
                new_ref[start : start + cells_x, cols] = result
                start = ((field * halves + half) * NZC + z) * cells_x
                fresh[start : start + cells_x, :] = result

    def rows_at(row):
        columns = []
        for half in range(halves):
            pieces = []
            for field in range(SPECIES):
                pieces.append(padded[pl.ds(base(field, half, 0) + PAD + row, NZC, stride=span), :])
            for field in range(SPECIES):
                start = (field * halves + half) * NZC * cells_x
                pieces.append(fresh[pl.ds(start + row, NZC, stride=cells_x), :])
            columns.append(jnp.concatenate(pieces, axis=0))
        return jnp.concatenate(columns, axis=1)

    block_cols = cells_x // BLK
    spot = lane_ids((STRIP_ROWS, cells_y)) % BLK
    lower_y = []
    upper_y = []
    for column in range(block_cols):
        below = jnp.zeros((STRIP_ROWS, cells_y), jnp.float32)
        above = jnp.zeros((STRIP_ROWS, cells_y), jnp.float32)
        for x in range(BLK):
            strip = rows_at(column * BLK + x)
            below = jnp.where(spot == x, roll_lanes(strip, x + 1), below)
            above = jnp.where(spot == x, roll_lanes(strip, x - BLK), above)
        lower_y.append(below)
        upper_y.append(above)

    columns, cells = block_vectors(boxes_ref, group, block_cols, cells_y // BLK)
    faces = [None] * FACES

    def add(face, part):
        faces[face] = part if faces[face] is None else faces[face] + part

    for column in range(-1, block_cols + 1):
        members = []
        if column >= 1:
            members.append((0, rows_at(column * BLK - 1)))
        if column < block_cols - 1:
            members.append((1, rows_at(column * BLK + BLK)))
        if 0 <= column < block_cols:
            members.append((2, lower_y[column]))
            members.append((3, upper_y[column]))
        operands = []
        for _, rows in members:
            operands.extend(split_pair(rows))
        moved = jnp.dot(
            jnp.concatenate(operands, axis=0),
            selector(columns, cells, column, cells_y),
            preferred_element_type=jnp.float32,
        )
        for index, (face, _) in enumerate(members):
            at = 2 * index * STRIP_ROWS
            add(face, moved[at : at + STRIP_ROWS] + moved[at + STRIP_ROWS : at + 2 * STRIP_ROWS])

    width = slots * BLK
    part = lane_ids((STRIP_ROWS, LANES)) // width
    for target in range(group // slots):
        first = target * width
        tile = first // LANES * LANES
        chunk = jnp.zeros((STRIP_ROWS, LANES), jnp.float32)
        for face in range(FACES):
            piece = faces[face][:, tile : tile + LANES]
            chunk = jnp.where(part == face, roll_lanes(piece, face * width - (first - tile)), chunk)
        send_ref[target] = chunk


def ghost_table():
    table = np.zeros((LANES, EDGE * EDGE), np.float32)
    x, y = np.divmod(np.arange(EDGE * EDGE), EDGE)
    width = LANES // FACES
    for pos in range(BLK):
        table[0 * width + pos] = (x == 0) & (y // RATIO == pos)
        table[1 * width + pos] = (x == EDGE - 1) & (y // RATIO == pos)
        table[2 * width + pos] = (y == 0) & (x // RATIO == pos)
        table[3 * width + pos] = (y == EDGE - 1) & (x // RATIO == pos)
    return np.concatenate([table, table]).astype(ml_dtypes.bfloat16)


def plane_table():
    rows = np.arange(2 * SPECIES * FZ)
    return (rows[:, None] // RATIO == np.arange(STRIP_ROWS)[None, :]).astype(ml_dtypes.bfloat16)


def mean_table():
    lane = np.arange(LANES)
    table = (lane[:, None] % EDGE // RATIO == lane[None, :] % BLK) / float(RATIO**3)
    return np.concatenate([table, table]).astype(ml_dtypes.bfloat16)


def fine_kernel(
    state_ref,
    kappa_ref,
    rate_ref,
    strips_ref,
    ghost_ref,
    plane_ref,
    mean_ref,
    out_ref,
    avg_ref,
    first,
    second,
    conduct,
    upward,
    coeffs,
    still,
    drift,
    *,
    slots,
):
    slot = pl.program_id(0)
    sources = strips_ref.shape[0]
    ztiles = FZ // 8

    def at(block, tile):
        return block * STRIDE + PAD + 8 * tile

    @pl.when(slot == 0)
    def _():
        edge = jnp.zeros((PAD, LANES), jnp.float32)
        for ref in (first, second, conduct, upward):
            for block in range(ref.shape[0] // STRIDE):
                ref[block * STRIDE : block * STRIDE + PAD, :] = edge
                ref[block * STRIDE + PAD + FZ : (block + 1) * STRIDE, :] = edge

    for tile in range(TILES):
        cols = pl.ds(tile * LANES, LANES)
        for field in range(SPECIES):
            row = at(field * TILES + tile, 0)
            first[row : row + FZ, :] = state_ref[0, field, :, cols]
        row = at(tile, 0)
        conduct[row : row + FZ, :] = kappa_ref[0, :, cols]

    gathered = strips_ref[0]
    for source in range(1, sources):
        gathered = gathered + strips_ref[source]
    gathered = pltpu.roll(gathered, (LANES - slot * BLK) % LANES, 1)
    half = STRIP_ROWS // 2
    gathered = jnp.concatenate(
        [gathered[:half], (gathered[half:] - gathered[:half]) * (1.0 / RATIO)], axis=0
    )
    stretched = jnp.dot(
        plane_ref[...],
        jnp.concatenate(split_pair(gathered), axis=1),
        preferred_element_type=jnp.float32,
    ).astype(jnp.bfloat16)
    for tile in range(TILES):
        ghosts = jnp.dot(
            stretched,
            ghost_ref[:, tile * LANES : (tile + 1) * LANES],
            preferred_element_type=jnp.float32,
        )
        scale = conduct[pl.ds(at(tile, 0), FZ), :] * FINE_SCALE
        for field in range(SPECIES):
            row = (field * TILES + tile) * FZ
            still[row : row + FZ, :] = scale * ghosts[field * FZ : (field + 1) * FZ]
            drift[row : row + FZ, :] = (
                scale * ghosts[(SPECIES + field) * FZ : (SPECIES + field + 1) * FZ]
            )

    lane = lane_ids((8, LANES))
    column = lane % EDGE
    side_y = jnp.where((column == 0) | (column == EDGE - 1), 1.0, 0.0)

    def face(one, other):
        return (2.0 * FINE_SCALE) * one * other / (one + other)

    def keep(kind, tile, ztile, values):
        row = ((kind * TILES + tile) * ztiles) * 8
        coeffs[pl.ds(pl.multiple_of(row + 8 * ztile, 8), 8), :] = values

    def prepare(ztile, carry):
        def here(tile, shift):
            return conduct[pl.ds(tile * STRIDE + PAD + shift + 8 * ztile, 8), :]

        centers = [here(tile, 0) for tile in range(TILES)]
        turned = [roll_lanes(center, -EDGE) for center in centers]
        next_x = []
        for tile in range(TILES):
            other = jnp.where(lane < LANES - EDGE, turned[tile], turned[(tile + 1) % TILES])
            values = face(centers[tile], other)
            if tile == TILES - 1:
                values = jnp.where(lane < LANES - EDGE, values, 0.0)
            next_x.append(values)
        back = [roll_lanes(values, EDGE) for values in next_x]
        for tile in range(TILES):
            center = centers[tile]
            prev_x = jnp.where(lane >= EDGE, back[tile], back[tile - 1])
            next_y = jnp.where(column < EDGE - 1, face(center, roll_lanes(center, -1)), 0.0)
            prev_y = roll_lanes(next_y, 1)
            next_z = face(center, here(tile, 1))
            prev_z = face(center, here(tile, -1))
            sides = side_y
            if tile == 0:
                sides = sides + jnp.where(lane < EDGE, 1.0, 0.0)
            if tile == TILES - 1:
                sides = sides + jnp.where(lane >= LANES - EDGE, 1.0, 0.0)
            total = (next_x[tile] + prev_x) + (next_y + prev_y) + (next_z + prev_z)
            total = total + (FINE_SCALE * sides) * center
            upward[pl.ds(tile * STRIDE + PAD + 8 * ztile, 8), :] = next_z
            keep(0, tile, ztile, next_x[tile])
            keep(1, tile, ztile, prev_x)
            keep(2, tile, ztile, next_y)
            keep(3, tile, ztile, prev_y)
            keep(4, tile, ztile, total)
            keep(
                5,
                tile,
                ztile,
                DT_FINE
                * rate_ref[0, pl.ds(pl.multiple_of(8 * ztile, 8), 8), pl.ds(tile * LANES, LANES)],
            )
        return carry

    lax.fori_loop(0, ztiles, prepare, 0)

    def substep(source, target, step, ztile):
        def value(field, tile, shift):
            return source[pl.ds((field * TILES + tile) * STRIDE + PAD + shift + 8 * ztile, 8), :]

        def get(kind, tile):
            row = ((kind * TILES + tile) * ztiles) * 8
            return coeffs[pl.ds(pl.multiple_of(row + 8 * ztile, 8), 8), :]

        centers = [[value(field, tile, 0) for tile in range(TILES)] for field in range(SPECIES)]
        down = [[roll_lanes(values, -EDGE) for values in row] for row in centers]
        up = [[roll_lanes(values, EDGE) for values in row] for row in centers]
        for tile in range(TILES):
            next_x, prev_x, next_y, prev_y, total, rate = [get(kind, tile) for kind in range(6)]
            next_z = upward[pl.ds(tile * STRIDE + PAD + 8 * ztile, 8), :]
            prev_z = upward[pl.ds(tile * STRIDE + PAD - 1 + 8 * ztile, 8), :]
            forward = rate * (
                centers[0][tile] * centers[1][tile] - centers[2][tile]
            )
            for field in range(SPECIES):
                center = centers[field][tile]
                ahead = jnp.where(
                    lane < LANES - EDGE, down[field][tile], down[field][(tile + 1) % TILES]
                )
                behind = jnp.where(lane >= EDGE, up[field][tile], up[field][tile - 1])
                row = (field * TILES + tile) * FZ
                spot = pl.ds(pl.multiple_of(row + 8 * ztile, 8), 8)
                flux = (next_x * ahead + prev_x * behind) + (
                    next_y * roll_lanes(center, -1) + prev_y * roll_lanes(center, 1)
                )
                flux = flux + (
                    next_z * value(field, tile, 1) + prev_z * value(field, tile, -1)
                )
                flux = flux + (still[spot, :] + step * drift[spot, :]) - total * center
                result = center + DIFFUSE[field] * flux + SIGNS[field] * forward
                target[
                    pl.ds(
                        pl.multiple_of((field * TILES + tile) * STRIDE + PAD + 8 * ztile, 8), 8
                    ),
                    :,
                ] = result

    def pair(index, carry):
        def go(source, target, step):
            def body(ztile, inner):
                substep(source, target, step, ztile)
                return inner

            lax.fori_loop(0, ztiles, body, 0)

        start = (2 * index).astype(jnp.float32)
        go(first, second, start)
        go(second, first, start + 1.0)
        return carry

    lax.fori_loop(0, RATIO // 2, pair, 0)

    for tile in range(TILES):
        for field in range(SPECIES):
            row = at(field * TILES + tile, 0)
            out_ref[0, field, :, pl.ds(tile * LANES, LANES)] = first[row : row + FZ, :]

    sums = []
    for field in range(SPECIES):
        for plane in range(NZC):
            start = field * TILES * STRIDE + PAD + RATIO * plane
            part = first[pl.ds(start, TILES, stride=STRIDE), :]
            for z in range(1, RATIO):
                part = part + first[pl.ds(start + z, TILES, stride=STRIDE), :]
            sums.append(part)
    means = jnp.dot(
        jnp.concatenate(split_pair(jnp.concatenate(sums, axis=0)), axis=1),
        mean_ref[...],
        preferred_element_type=jnp.float32,
    )
    quarter = AVG_ROWS // FACES
    spot = lane_ids((quarter, LANES)) // BLK
    chunk = avg_ref[0]
    for part in range(FACES):
        chunk = jnp.where(
            spot == part * slots + slot, means[part * quarter : (part + 1) * quarter], chunk
        )
    avg_ref[0] = chunk

    @pl.when(slot == slots - 1)
    def _():
        for target in range(1, avg_ref.shape[0]):
            avg_ref[target] = chunk


def place_kernel(boxes_ref, avg_ref, new_ref, out_ref, *, cells_x, cells_y, group, slots):
    width = slots * BLK
    quarter = AVG_ROWS // FACES
    per_tile = LANES // width
    part = lane_ids((quarter, LANES)) // width
    columns = []
    for tile in range(group * BLK // LANES):
        rows = []
        for index in range(FACES):
            merged = jnp.zeros((quarter, LANES), jnp.float32)
            for place in range(per_tile):
                piece = roll_lanes(avg_ref[tile * per_tile + place], (place - index) * width)
                merged = jnp.where(part == place, piece, merged)
            rows.append(merged)
        columns.append(jnp.concatenate(rows, axis=0))
    averages = jnp.concatenate(columns, axis=1)
    high, low = split_pair(averages)
    ones = jnp.ones((16, averages.shape[1]), jnp.bfloat16)
    stacked = jnp.concatenate([high, low, ones], axis=0)

    block_cols = cells_x // BLK
    block_of, cells = block_vectors(boxes_ref, group, block_cols, cells_y // BLK)
    for column in range(block_cols):
        placed = lax.dot_general(
            stacked,
            selector(block_of, cells, column, cells_y),
            (((1,), (1,)), ((), ())),
            preferred_element_type=jnp.float32,
        )
        covered = placed[2 * AVG_ROWS : 2 * AVG_ROWS + 8] > 0.5
        for plane in range(SPECIES * NZC):
            values = (
                placed[plane * BLK : (plane + 1) * BLK]
                + placed[AVG_ROWS + plane * BLK : AVG_ROWS + (plane + 1) * BLK]
            )
            row = plane * cells_x + column * BLK
            out_ref[row : row + BLK, :] = jnp.where(covered, values, new_ref[row : row + BLK, :])


def vmem():
    return pl.BlockSpec(memory_space=pltpu.VMEM)


def smem():
    return pl.BlockSpec(memory_space=pltpu.SMEM)


def f32(*shape):
    return jax.ShapeDtypeStruct(shape, jnp.float32)


PARAMS = pltpu.CompilerParams(vmem_limit_bytes=40 * 1024 * 1024)


def shifted(values, axis, step):
    count = lax.axis_size(axis)
    pairs = [(i, i + step) for i in range(count) if 0 <= i + step < count]
    return lax.ppermute(values, axis, pairs)


def exchange(chunks):
    return lax.all_to_all(chunks, "af", split_axis=0, concat_axis=0, tiled=True)


def per_device(
    coarse_state, coarse_kappa, coarse_rate, fine_state, fine_kappa, fine_rate, boxes, cover
):
    af_count = lax.axis_size("af")
    slots = fine_state.shape[0]
    cells_x, cells_y = coarse_state.shape[2:]
    group = af_count * slots
    planes = SPECIES * NZC
    state = coarse_state.reshape(planes * cells_x, cells_y)
    kappa = coarse_kappa.reshape(NZC * cells_x, cells_y)
    rate = coarse_rate.reshape(NZC * cells_x, cells_y)
    sizes = dict(cells_x=cells_x, cells_y=cells_y)

    xlo, xhi, ylo, yhi = pl.pallas_call(
        functools.partial(edges_kernel, **sizes),
        out_shape=[f32(planes + NZC, cells_y)] * 2 + [f32(cells_x, LANES)] * 2,
        in_specs=[vmem()] * 2,
        out_specs=[vmem()] * 4,
        compiler_params=PARAMS,
        name="edges",
    )(state, kappa)
    xl = shifted(xhi, "af", 1)
    xr = shifted(xlo, "af", -1)
    yl = shifted(yhi, "col", 1)
    yr = shifted(ylo, "col", -1)

    span = cells_x + 2 * PAD
    new, send = pl.pallas_call(
        functools.partial(coarse_kernel, group=group, slots=slots, **sizes),
        out_shape=[f32(planes * cells_x, cells_y), f32(af_count, STRIP_ROWS, LANES)],
        in_specs=[smem()] + [vmem()] * 7,
        out_specs=[vmem()] * 2,
        scratch_shapes=[
            pltpu.VMEM(((SPECIES + 1) * (cells_y // LANES) * NZC * span, LANES), jnp.float32),
            pltpu.VMEM((planes * cells_x * (cells_y // LANES), LANES), jnp.float32),
        ],
        compiler_params=PARAMS,
        name="coarse",
    )(boxes, state, kappa, rate, xl, xr, yl, yr)

    strips = exchange(send)

    blocks = SPECIES * TILES
    fine_out, averages = pl.pallas_call(
        functools.partial(fine_kernel, slots=slots),
        grid=(slots,),
        out_shape=[f32(*fine_state.shape), f32(af_count, AVG_ROWS // FACES, LANES)],
        in_specs=[
            pl.BlockSpec((1, SPECIES, FZ, EDGE * EDGE), lambda s: (s, 0, 0, 0)),
            pl.BlockSpec((1, FZ, EDGE * EDGE), lambda s: (s, 0, 0)),
            pl.BlockSpec((1, FZ, EDGE * EDGE), lambda s: (s, 0, 0)),
        ]
        + [vmem()] * 4,
        out_specs=[
            pl.BlockSpec((1, SPECIES, FZ, EDGE * EDGE), lambda s: (s, 0, 0, 0)),
            pl.BlockSpec((af_count, AVG_ROWS // FACES, LANES), lambda s: (0, 0, 0)),
        ],
        scratch_shapes=[
            pltpu.VMEM((blocks * STRIDE, LANES), jnp.float32),
            pltpu.VMEM((blocks * STRIDE, LANES), jnp.float32),
            pltpu.VMEM((TILES * STRIDE, LANES), jnp.float32),
            pltpu.VMEM((TILES * STRIDE, LANES), jnp.float32),
            pltpu.VMEM((6 * TILES * FZ, LANES), jnp.float32),
            pltpu.VMEM((blocks * FZ, LANES), jnp.float32),
            pltpu.VMEM((blocks * FZ, LANES), jnp.float32),
        ],
        compiler_params=PARAMS,
        name="fine",
    )(
        fine_state,
        fine_kappa,
        fine_rate,
        strips,
        jnp.asarray(ghost_table()),
        jnp.asarray(plane_table()),
        jnp.asarray(mean_table()),
    )

    arrived = exchange(averages)

    placed = pl.pallas_call(
        functools.partial(place_kernel, group=group, slots=slots, **sizes),
        out_shape=f32(planes * cells_x, cells_y),
        in_specs=[smem()] + [vmem()] * 2,
        out_specs=vmem(),
        compiler_params=PARAMS,
        name="place",
    )(boxes, arrived, new)
    return (placed.reshape(coarse_state.shape), fine_out)


def solution(mesh):
    return jax.shard_map(
        per_device,
        mesh=mesh,
        in_specs=(
            P(None, None, "af", "col"),
            P(None, "af", "col"),
            P(None, "af", "col"),
            P(("col", "af"), None, None, None),
            P(("col", "af"), None, None),
            P(("col", "af"), None, None),
            P(),
            P(),
        ),
        out_specs=(P(None, None, "af", "col"), P(("col", "af"), None, None, None)),
        check_vma=False,
    )
```

```python
import functools

import jax
import jax.numpy as jnp
import ml_dtypes
import numpy as np
from jax import lax
from jax.experimental import pallas as pl
from jax.experimental.pallas import tpu as pltpu
from jax.sharding import PartitionSpec as P

NZC = 8
RATIO = 4
BLK = 8
SPECIES = 3
EDGE = BLK * RATIO
FZ = NZC * RATIO
LANES = 128
TILES = EDGE * EDGE // LANES
ZTILES = FZ // 8
STRIDE = 48
PAD = 8
FACES = 4
PLANES = SPECIES * NZC
STRIP_ROWS = 2 * PLANES
AVG_ROWS = PLANES * BLK
KINDS = 9

DT_COARSE = 1.0 / 28.0
DIFFUSE = (1.0, 0.7, 0.45)
SIGNS = (-1.0, -1.0, 1.0)
FINE_SCALE = RATIO * RATIO * DT_COARSE / RATIO
DT_FINE = DT_COARSE / RATIO


def lane_ids(shape):
    return lax.broadcasted_iota(jnp.int32, shape, len(shape) - 1)


def roll_lanes(values, shift):
    width = values.shape[-1]
    shift = shift % width
    return values if shift == 0 else pltpu.roll(values, shift, values.ndim - 1)


def split_pair(values):
    high = values.astype(jnp.bfloat16)
    low = (values - high.astype(jnp.float32)).astype(jnp.bfloat16)
    return high, low


def face(scale, one, other):
    summed = one + other
    inverse = pl.reciprocal(summed, approx=True)
    inverse = inverse * (2.0 - summed * inverse)
    return (2.0 * scale) * (one * other) * inverse


def start_all(copies):
    for copy in copies:
        copy.start()


def load_kernel(
    boxes_hbm,
    state_hbm,
    kappa_hbm,
    rate_hbm,
    state_ref,
    kappa_ref,
    rate_ref,
    place_ref,
    xlo_ref,
    xhi_ref,
    ylo_ref,
    yhi_ref,
    boxes_ref,
    sems,
    *,
    cells_x,
    cells_y,
    group,
):
    pairs = (
        (boxes_hbm, boxes_ref),
        (state_hbm, state_ref),
        (kappa_hbm, kappa_ref),
        (rate_hbm, rate_ref),
    )
    copies = [
        pltpu.make_async_copy(source, target, sems.at[index])
        for index, (source, target) in enumerate(pairs)
    ]
    start_all(copies)

    patches = boxes_ref.shape[1]
    lanes = group * BLK
    base = lax.axis_index("col") * group
    member = lax.broadcasted_iota(jnp.int32, (patches, lanes), 0) - base
    spread = jnp.where(member == lane_ids((patches, lanes)) // BLK, 1.0, 0.0).astype(jnp.bfloat16)
    first_col = lax.axis_index("af") * (cells_x // BLK)
    first_cell = lax.axis_index("col") * cells_y
    copies[0].wait()
    boxes = boxes_ref[...].astype(jnp.float32)
    stacked = jnp.concatenate(
        [jnp.broadcast_to(boxes[row : row + 1], (8, patches)) for row in range(2)], axis=0
    )
    found = jnp.dot(
        stacked.astype(jnp.bfloat16), spread, preferred_element_type=jnp.float32
    ).astype(jnp.int32)
    place_ref[0:8, :] = found[0:8] - first_col
    place_ref[8:16, :] = found[8:16] * BLK - first_cell + lane_ids((8, lanes)) % BLK

    copies[1].wait()
    copies[2].wait()
    lane = lane_ids((cells_x, LANES))
    low = jnp.zeros((cells_x, LANES), jnp.float32)
    high = jnp.zeros((cells_x, LANES), jnp.float32)
    for plane in range(PLANES + NZC):
        if plane < PLANES:
            ref, start = state_ref, plane * cells_x
        else:
            ref, start = kappa_ref, (plane - PLANES) * cells_x
        first = ref[start : start + cells_x, 0:LANES]
        last = ref[start : start + cells_x, cells_y - LANES : cells_y]
        xlo_ref[plane : plane + 1, :] = ref[start : start + 1, :]
        xhi_ref[plane : plane + 1, :] = ref[start + cells_x - 1 : start + cells_x, :]
        low = jnp.where(lane == plane, roll_lanes(first, plane), low)
        high = jnp.where(lane == plane, roll_lanes(last, plane + 1), high)
    ylo_ref[...] = low
    yhi_ref[...] = high
    copies[3].wait()


def coarse_kernel(
    place_ref,
    state_ref,
    kappa_ref,
    rate_ref,
    xl_ref,
    xr_ref,
    new_ref,
    send_ref,
    pick_ref,
    padded,
    fresh,
    *,
    cells_x,
    cells_y,
    group,
    slots,
):
    halves = cells_y // LANES
    span = cells_x + 2 * PAD

    def base(field, half, z):
        return ((field * halves + half) * NZC + z) * span

    for field in range(SPECIES + 1):
        for half in range(halves):
            cols = pl.ds(half * LANES, LANES)
            for z in range(NZC):
                if field < SPECIES:
                    start = (field * NZC + z) * cells_x
                    plane = state_ref[start : start + cells_x, cols]
                else:
                    plane = kappa_ref[z * cells_x : (z + 1) * cells_x, cols]
                at = base(field, half, z) + PAD
                padded[at : at + cells_x, :] = plane
            at = base(field, half, 0) + PAD
            rows = slice(field * NZC, (field + 1) * NZC)
            padded[pl.ds(at - 1, NZC, stride=span), :] = xl_ref[rows, cols]
            padded[pl.ds(at + cells_x, NZC, stride=span), :] = xr_ref[rows, cols]

    lane = lane_ids((cells_x, LANES))

    def load(field, half, z, shift):
        at = base(field, half, z) + PAD + shift
        return padded[at : at + cells_x, :]

    def neighbours(field, half, z):
        here = load(field, half, z, 0)
        after = roll_lanes(here, -1)
        if half + 1 < halves:
            after = jnp.where(
                lane == LANES - 1, roll_lanes(load(field, half + 1, z, 0), -1), after
            )
        before = roll_lanes(here, 1)
        if half > 0:
            before = jnp.where(lane == 0, roll_lanes(load(field, half - 1, z, 0), 1), before)
        found = [after, before, load(field, half, z, 1), load(field, half, z, -1)]
        if z + 1 < NZC:
            found.append(load(field, half, z + 1, 0))
        if z > 0:
            found.append(load(field, half, z - 1, 0))
        return found

    for z in range(NZC):
        for half in range(halves):
            cols = pl.ds(half * LANES, LANES)
            conduct = load(SPECIES, half, z, 0)
            coeffs = [face(DT_COARSE, conduct, other) for other in neighbours(SPECIES, half, z)]
            if half == halves - 1:
                coeffs[0] = jnp.where(lane == LANES - 1, 0.0, coeffs[0])
            if half == 0:
                coeffs[1] = jnp.where(lane == 0, 0.0, coeffs[1])
            centers = [load(field, half, z, 0) for field in range(SPECIES)]
            forward = (DT_COARSE * rate_ref[z * cells_x : (z + 1) * cells_x, cols]) * (
                centers[0] * centers[1] - centers[2]
            )
            for field in range(SPECIES):
                center = centers[field]
                flux = None
                for coeff, other in zip(coeffs, neighbours(field, half, z)):
                    term = coeff * (other - center)
                    flux = term if flux is None else flux + term
                start = (field * NZC + z) * cells_x
                result = center + DIFFUSE[field] * flux + SIGNS[field] * forward
                new_ref[start : start + cells_x, cols] = result
                start = ((field * halves + half) * NZC + z) * cells_x
                fresh[start : start + cells_x, :] = result

    def rows_at(row):
        columns = []
        for half in range(halves):
            pieces = []
            for field in range(SPECIES):
                pieces.append(padded[pl.ds(base(field, half, 0) + PAD + row, NZC, stride=span), :])
            for field in range(SPECIES):
                start = (field * halves + half) * NZC * cells_x
                pieces.append(fresh[pl.ds(start + row, NZC, stride=cells_x), :])
            columns.append(jnp.concatenate(pieces, axis=0))
        return jnp.concatenate(columns, axis=1)

    block_cols = cells_x // BLK
    spot = lane_ids((STRIP_ROWS, cells_y)) % BLK
    lower_y = []
    upper_y = []
    for column in range(block_cols):
        below = jnp.zeros((STRIP_ROWS, cells_y), jnp.float32)
        above = jnp.zeros((STRIP_ROWS, cells_y), jnp.float32)
        for x in range(BLK):
            strip = rows_at(column * BLK + x)
            below = jnp.where(spot == x, roll_lanes(strip, x + 1), below)
            above = jnp.where(spot == x, roll_lanes(strip, x - BLK), above)
        lower_y.append(below)
        upper_y.append(above)

    columns = place_ref[0:8, :]
    cells = place_ref[8:16, :]
    lanes = group * BLK
    row = lax.broadcasted_iota(jnp.int32, (8, lanes), 0)
    faces = [None] * FACES

    def add(index, part):
        faces[index] = part if faces[index] is None else faces[index] + part

    for column in range(-1, block_cols + 1):
        wanted = jnp.where(columns == column, cells, -1)
        pick = jnp.concatenate(
            [jnp.where(row + 8 * at == wanted, 1.0, 0.0) for at in range(cells_y // 8)], axis=0
        ).astype(jnp.bfloat16)
        if 0 <= column < block_cols:
            pick_ref[column] = pick
        members = []
        if column >= 1:
            members.append((0, rows_at(column * BLK - 1)))
        if column < block_cols - 1:
            members.append((1, rows_at(column * BLK + BLK)))
        if 0 <= column < block_cols:
            members.append((2, lower_y[column]))
            members.append((3, upper_y[column]))
        operands = []
        for _, rows in members:
            operands.extend(split_pair(rows))
        moved = jnp.dot(
            jnp.concatenate(operands, axis=0), pick, preferred_element_type=jnp.float32
        )
        for order, (index, _) in enumerate(members):
            at = 2 * order * STRIP_ROWS
            add(index, moved[at : at + STRIP_ROWS] + moved[at + STRIP_ROWS : at + 2 * STRIP_ROWS])

    width = slots * BLK
    part = lane_ids((STRIP_ROWS, LANES)) // width
    for target in range(group // slots):
        first = target * width
        tile = first // LANES * LANES
        chunk = jnp.zeros((STRIP_ROWS, LANES), jnp.float32)
        for index in range(FACES):
            piece = faces[index][:, tile : tile + LANES]
            chunk = jnp.where(
                part == index, roll_lanes(piece, index * width - (first - tile)), chunk
            )
        send_ref[target] = chunk


def ghost_table():
    table = np.zeros((LANES, EDGE * EDGE), np.float32)
    x, y = np.divmod(np.arange(EDGE * EDGE), EDGE)
    width = LANES // FACES
    for pos in range(BLK):
        table[0 * width + pos] = (x == 0) & (y // RATIO == pos)
        table[1 * width + pos] = (x == EDGE - 1) & (y // RATIO == pos)
        table[2 * width + pos] = (y == 0) & (x // RATIO == pos)
        table[3 * width + pos] = (y == EDGE - 1) & (x // RATIO == pos)
    return np.concatenate([table, table]).astype(ml_dtypes.bfloat16)


def plane_table():
    rows = np.arange(2 * SPECIES * FZ)
    return (rows[:, None] // RATIO == np.arange(STRIP_ROWS)[None, :]).astype(ml_dtypes.bfloat16)


def mean_table():
    lane = np.arange(LANES)
    table = (lane[:, None] % EDGE // RATIO == lane[None, :] % BLK) / float(RATIO**3)
    return np.concatenate([table, table]).astype(ml_dtypes.bfloat16)


def aligned(start, size):
    return pl.ds(pl.multiple_of(start, 8), size)


def padded_at(block, ztile):
    return block * STRIDE + PAD + 8 * ztile


def advance(source, target, coeffs, upward, slot, from_rows, to_rows, ztile, ghosts):
    lane = lane_ids((8, LANES))

    def value(field, tile, shift):
        return source[pl.ds(from_rows + padded_at(field * TILES + tile, ztile) + shift, 8), :]

    def get(kind, tile):
        return coeffs[
            aligned(slot * (KINDS * TILES * FZ) + (kind * TILES + tile) * FZ + 8 * ztile, 8), :
        ]

    centers = [value(field, 0, 0) for field in range(SPECIES)]
    down = [roll_lanes(center, -EDGE) for center in centers]
    up = [roll_lanes(center, EDGE) for center in centers]
    up_before = list(up)
    for tile in range(TILES):
        if tile + 1 < TILES:
            centers_after = [value(field, tile + 1, 0) for field in range(SPECIES)]
            down_after = [roll_lanes(center, -EDGE) for center in centers_after]
        next_x, prev_x, next_y, prev_y, rate = [get(kind, tile) for kind in range(5)]
        base = slot * (TILES * STRIDE) + padded_at(tile, ztile)
        next_z = upward[pl.ds(base, 8), :]
        prev_z = upward[pl.ds(base - 1, 8), :]
        forward = rate * (centers[0] * centers[1] - centers[2])
        for field in range(SPECIES):
            center = centers[field]
            ahead, behind = down[field], up[field]
            if tile + 1 < TILES:
                ahead = jnp.where(lane < LANES - EDGE, ahead, down_after[field])
            if tile > 0:
                behind = jnp.where(lane >= EDGE, behind, up_before[field])
            flux = (next_x * ahead + prev_x * behind) + (
                next_y * roll_lanes(center, -1) + prev_y * roll_lanes(center, 1)
            )
            flux = flux + (next_z * value(field, tile, 1) + prev_z * value(field, tile, -1))
            share = ghosts(field, tile)
            if share is not None:
                flux = flux + share
            if DIFFUSE[field] != 1.0:
                flux = DIFFUSE[field] * flux
            result = get(5 + field, tile) * center + flux
            result = result - forward if SIGNS[field] < 0 else result + forward
            target[aligned(to_rows + padded_at(field * TILES + tile, ztile), 8), :] = result
        if tile + 1 < TILES:
            up_before = up
            centers, down = centers_after, down_after
            up = [roll_lanes(center, EDGE) for center in centers]


def clear_pads(ref):
    edge = jnp.zeros((PAD, LANES), jnp.float32)

    def body(block, carry):
        ref[aligned(block * STRIDE, PAD), :] = edge
        ref[aligned(block * STRIDE + PAD + FZ, PAD), :] = edge
        return carry

    lax.fori_loop(0, ref.shape[0] // STRIDE, body, 0)


def prepare_kernel(
    after_ref,
    state_hbm,
    kappa_hbm,
    rate_hbm,
    ghost_hbm,
    plane_hbm,
    mean_hbm,
    fields_ref,
    coeffs,
    upward,
    ghost_ref,
    plane_ref,
    mean_ref,
    state_ref,
    kappa_ref,
    rate_ref,
    first,
    conduct,
    sems,
    table_sems,
    *,
    slots,
):
    def loads(slot):
        return [
            pltpu.make_async_copy(source.at[slot], target.at[slot], sems.at[order, slot])
            for order, (source, target) in enumerate(
                ((kappa_hbm, kappa_ref), (rate_hbm, rate_ref), (state_hbm, state_ref))
            )
        ]

    for slot in range(slots):
        start_all(loads(slot))
    tables = [
        pltpu.make_async_copy(source, target, table_sems.at[order])
        for order, (source, target) in enumerate(
            ((ghost_hbm, ghost_ref), (plane_hbm, plane_ref), (mean_hbm, mean_ref))
        )
    ]
    start_all(tables)
    for ref in (fields_ref, upward, first, conduct):
        clear_pads(ref)

    lane = lane_ids((8, LANES))
    column = lane % EDGE
    side_y = jnp.where((column == 0) | (column == EDGE - 1), 1.0, 0.0)

    def one_patch(slot, carry):
        for copy in loads(slot):
            copy.wait()

        for tile in range(TILES):
            cols = pl.ds(tile * LANES, LANES)
            for field in range(SPECIES):
                row = padded_at(field * TILES + tile, 0)
                first[row : row + FZ, :] = state_ref[slot, field, :, cols]
            row = padded_at(tile, 0)
            conduct[row : row + FZ, :] = kappa_ref[slot, :, cols]

        def keep(kind, tile, ztile, values):
            coeffs[
                aligned(slot * (KINDS * TILES * FZ) + (kind * TILES + tile) * FZ + 8 * ztile, 8), :
            ] = values

        for ztile in range(ZTILES):

            def here(tile, shift):
                return conduct[pl.ds(padded_at(tile, ztile) + shift, 8), :]

            center = here(0, 0)
            turned = roll_lanes(center, -EDGE)
            back_before = None
            for tile in range(TILES):
                other = turned
                if tile + 1 < TILES:
                    center_after = here(tile + 1, 0)
                    turned_after = roll_lanes(center_after, -EDGE)
                    other = jnp.where(lane < LANES - EDGE, turned, turned_after)
                next_x = face(FINE_SCALE, center, other)
                if tile == TILES - 1:
                    next_x = jnp.where(lane < LANES - EDGE, next_x, 0.0)
                back = roll_lanes(next_x, EDGE)
                prev_x = jnp.where(lane >= EDGE, back, 0.0 if tile == 0 else back_before)
                next_y = jnp.where(
                    column < EDGE - 1, face(FINE_SCALE, center, roll_lanes(center, -1)), 0.0
                )
                prev_y = roll_lanes(next_y, 1)
                next_z = face(FINE_SCALE, center, here(tile, 1))
                prev_z = face(FINE_SCALE, center, here(tile, -1))
                sides = side_y
                if tile == 0:
                    sides = sides + jnp.where(lane < EDGE, 1.0, 0.0)
                if tile == TILES - 1:
                    sides = sides + jnp.where(lane >= LANES - EDGE, 1.0, 0.0)
                scale = FINE_SCALE * center
                total = (next_x + prev_x) + (next_y + prev_y) + (next_z + prev_z) + sides * scale
                upward[aligned(slot * (TILES * STRIDE) + padded_at(tile, ztile), 8), :] = next_z
                keep(0, tile, ztile, next_x)
                keep(1, tile, ztile, prev_x)
                keep(2, tile, ztile, next_y)
                keep(3, tile, ztile, prev_y)
                rate = rate_ref[slot, pl.ds(8 * ztile, 8), pl.ds(tile * LANES, LANES)]
                keep(4, tile, ztile, DT_FINE * rate)
                for field in range(SPECIES):
                    keep(5 + field, tile, ztile, 1.0 - DIFFUSE[field] * total)
                keep(8, tile, ztile, scale)
                back_before = back
                if tile + 1 < TILES:
                    center, turned = center_after, turned_after

        for ztile in range(ZTILES):
            advance(
                first,
                fields_ref,
                coeffs,
                upward,
                slot,
                0,
                slot * (SPECIES * TILES * STRIDE),
                ztile,
                lambda field, tile: None,
            )
        return carry

    lax.fori_loop(0, slots, one_patch, 0)
    for copy in tables:
        copy.wait()


def finish_kernel(
    strips_ref,
    fields_ref,
    coeffs,
    upward,
    ghost_ref,
    plane_ref,
    mean_ref,
    out_hbm,
    avg_ref,
    first,
    second,
    share,
    drift,
    staged,
    sems,
    *,
    slots,
):
    sources = strips_ref.shape[0]
    clear_pads(first)
    clear_pads(second)

    gathered = strips_ref[0]
    for source in range(1, sources):
        gathered = gathered + strips_ref[source]
    half = STRIP_ROWS // 2
    gathered = jnp.concatenate(
        [gathered[:half], (gathered[half:] - gathered[:half]) * (1.0 / RATIO)], axis=0
    )
    quarter = AVG_ROWS // FACES
    group_of = lane_ids((quarter, LANES)) // BLK

    def send_out(slot):
        return pltpu.make_async_copy(staged.at[slot], out_hbm.at[slot], sems.at[slot])

    def one_patch(slot, carry):
        turned = pltpu.roll(gathered, (LANES - slot * BLK) % LANES, 1)
        stretched = jnp.dot(
            plane_ref[...],
            jnp.concatenate(split_pair(turned), axis=1),
            preferred_element_type=jnp.float32,
        ).astype(jnp.bfloat16)
        base = slot * (SPECIES * TILES * STRIDE)
        scales = slot * (KINDS * TILES * FZ)
        for tile in range(TILES):
            ghosts = jnp.dot(
                stretched,
                ghost_ref[:, tile * LANES : (tile + 1) * LANES],
                preferred_element_type=jnp.float32,
            )
            scale = coeffs[aligned(scales + (8 * TILES + tile) * FZ, FZ), :]
            for field in range(SPECIES):
                row = (field * TILES + tile) * FZ
                old = scale * ghosts[field * FZ : (field + 1) * FZ]
                step = scale * ghosts[(SPECIES + field) * FZ : (SPECIES + field + 1) * FZ]
                drift[row : row + FZ, :] = step
                share[row : row + FZ, :] = old + step
                row = padded_at(field * TILES + tile, 0)
                second[row : row + FZ, :] = (
                    fields_ref[aligned(base + row, FZ), :] + DIFFUSE[field] * old
                )

        for step in range(1, RATIO):
            source, target = (second, first) if step % 2 else (first, second)
            for ztile in range(ZTILES):

                def ghosts(field, tile):
                    spot = pl.ds((field * TILES + tile) * FZ + 8 * ztile, 8)
                    value = share[spot, :]
                    if step + 1 < RATIO:
                        share[spot, :] = value + drift[spot, :]
                    return value

                advance(source, target, coeffs, upward, slot, 0, 0, ztile, ghosts)

        for tile in range(TILES):
            for field in range(SPECIES):
                row = padded_at(field * TILES + tile, 0)
                staged[slot, field, :, pl.ds(tile * LANES, LANES)] = first[row : row + FZ, :]
        send_out(slot).start()

        sums = []
        for field in range(SPECIES):
            for plane in range(NZC):
                start = field * TILES * STRIDE + PAD + RATIO * plane
                part = first[pl.ds(start, TILES, stride=STRIDE), :]
                for z in range(1, RATIO):
                    part = part + first[pl.ds(start + z, TILES, stride=STRIDE), :]
                sums.append(part)
        means = jnp.dot(
            jnp.concatenate(split_pair(jnp.concatenate(sums, axis=0)), axis=1),
            mean_ref[...],
            preferred_element_type=jnp.float32,
        )
        chunk = avg_ref[0]
        for part in range(FACES):
            chunk = jnp.where(
                group_of == part * slots + slot,
                means[part * quarter : (part + 1) * quarter],
                chunk,
            )
        avg_ref[0] = chunk
        return carry

    avg_ref[0] = jnp.zeros((quarter, LANES), jnp.float32)
    lax.fori_loop(0, slots, one_patch, 0)
    chunk = avg_ref[0]
    for target in range(1, avg_ref.shape[0]):
        avg_ref[target] = chunk
    for slot in range(slots):
        send_out(slot).wait()


def place_kernel(
    pick_ref,
    avg_ref,
    new_ref,
    ylo_ref,
    yhi_ref,
    yl_ref,
    yr_ref,
    out_ref,
    *,
    cells_x,
    cells_y,
    group,
    slots,
):
    def edge_share(own_ref, other_ref):
        own = own_ref[...]
        other = other_ref[...]
        coeff = face(DT_COARSE, jnp.maximum(own, 0.125), other)
        lane = lane_ids(own.shape)
        spread = jnp.zeros_like(own)
        for field in range(SPECIES):
            moved = roll_lanes(coeff, (field - SPECIES) * NZC)
            spread = jnp.where(lane // NZC == field, DIFFUSE[field] * moved, spread)
        return spread * (other - own)

    lower = edge_share(ylo_ref, yl_ref)
    upper = edge_share(yhi_ref, yr_ref)

    width = slots * BLK
    quarter = AVG_ROWS // FACES
    per_tile = LANES // width
    part = lane_ids((quarter, LANES)) // width
    columns = []
    for tile in range(group * BLK // LANES):
        rows = []
        for index in range(FACES):
            merged = jnp.zeros((quarter, LANES), jnp.float32)
            for place in range(per_tile):
                piece = roll_lanes(avg_ref[tile * per_tile + place], (place - index) * width)
                merged = jnp.where(part == place, piece, merged)
            rows.append(merged)
        columns.append(jnp.concatenate(rows, axis=0))
    high, low = split_pair(jnp.concatenate(columns, axis=1))
    ones = jnp.ones((16, high.shape[1]), jnp.bfloat16)
    stacked = jnp.concatenate([high, low, ones], axis=0)

    lane = lane_ids((BLK, LANES))
    halves = cells_y // LANES
    for column in range(cells_x // BLK):
        placed = lax.dot_general(
            stacked,
            pick_ref[column],
            (((1,), (1,)), ((), ())),
            preferred_element_type=jnp.float32,
        )
        covered = placed[2 * AVG_ROWS : 2 * AVG_ROWS + 8] > 0.5
        for plane in range(PLANES):
            values = (
                placed[plane * BLK : (plane + 1) * BLK]
                + placed[AVG_ROWS + plane * BLK : AVG_ROWS + (plane + 1) * BLK]
            )
            row = plane * cells_x + column * BLK
            edge_rows = slice(column * BLK, (column + 1) * BLK)
            for half in range(halves):
                cols = slice(half * LANES, (half + 1) * LANES)
                coarse = new_ref[row : row + BLK, cols]
                if half == 0:
                    share = roll_lanes(lower[edge_rows], -plane)
                    coarse = coarse + jnp.where(lane == 0, share, 0.0)
                if half == halves - 1:
                    share = roll_lanes(upper[edge_rows], LANES - 1 - plane)
                    coarse = coarse + jnp.where(lane == LANES - 1, share, 0.0)
                out_ref[row : row + BLK, cols] = jnp.where(
                    covered[:, cols], values[:, cols], coarse
                )


VMEM = pl.BlockSpec(memory_space=pltpu.VMEM)
HBM = pl.BlockSpec(memory_space=pl.ANY)
PARAMS = pltpu.CompilerParams(vmem_limit_bytes=40 * 1024 * 1024)


def f32(*shape):
    return jax.ShapeDtypeStruct(shape, jnp.float32)


def b16(*shape):
    return jax.ShapeDtypeStruct(shape, jnp.bfloat16)


def shifted(values, axis, step):
    count = lax.axis_size(axis)
    pairs = [(i, i + step) for i in range(count) if 0 <= i + step < count]
    return lax.ppermute(values, axis, pairs)


def exchange(chunks):
    return lax.all_to_all(chunks, "af", split_axis=0, concat_axis=0, tiled=True)


def per_device(
    coarse_state, coarse_kappa, coarse_rate, fine_state, fine_kappa, fine_rate, boxes, cover
):
    af_count = lax.axis_size("af")
    slots = fine_state.shape[0]
    cells_x, cells_y = coarse_state.shape[2:]
    group = af_count * slots
    lanes = group * BLK
    halves = cells_y // LANES
    block_cols = cells_x // BLK
    rows = PLANES * cells_x
    plain = NZC * cells_x
    sizes = dict(cells_x=cells_x, cells_y=cells_y, group=group)

    state, kappa, rate, place, xlo, xhi, ylo, yhi = pl.pallas_call(
        functools.partial(load_kernel, **sizes),
        out_shape=[f32(rows, cells_y), f32(plain, cells_y), f32(plain, cells_y)]
        + [jax.ShapeDtypeStruct((16, lanes), jnp.int32)]
        + [f32(PLANES + NZC, cells_y)] * 2
        + [f32(cells_x, LANES)] * 2,
        in_specs=[HBM] * 4,
        out_specs=[VMEM] * 8,
        scratch_shapes=[
            pltpu.VMEM((2, boxes.shape[0]), jnp.int32),
            pltpu.SemaphoreType.DMA((4,)),
        ],
        compiler_params=PARAMS,
        name="load",
    )(
        boxes.T,
        coarse_state.reshape(rows, cells_y),
        coarse_kappa.reshape(plain, cells_y),
        coarse_rate.reshape(plain, cells_y),
    )
    xl = shifted(xhi, "af", 1)
    xr = shifted(xlo, "af", -1)

    span = cells_x + 2 * PAD
    new, send, pick = pl.pallas_call(
        functools.partial(coarse_kernel, slots=slots, **sizes),
        out_shape=[
            f32(rows, cells_y),
            f32(af_count, STRIP_ROWS, LANES),
            b16(block_cols, cells_y, lanes),
        ],
        in_specs=[VMEM] * 6,
        out_specs=[VMEM] * 3,
        scratch_shapes=[
            pltpu.VMEM(((SPECIES + 1) * halves * NZC * span, LANES), jnp.float32),
            pltpu.VMEM((rows * halves, LANES), jnp.float32),
        ],
        compiler_params=PARAMS,
        name="coarse",
    )(place, state, kappa, rate, xl, xr)

    strips = exchange(send)

    blocks = SPECIES * TILES
    tables = [jnp.asarray(table) for table in (ghost_table(), plane_table(), mean_table())]
    fields, coeffs, upward, *tables = pl.pallas_call(
        functools.partial(prepare_kernel, slots=slots),
        out_shape=[
            f32(slots * blocks * STRIDE, LANES),
            f32(slots * KINDS * TILES * FZ, LANES),
            f32(slots * TILES * STRIDE, LANES),
        ]
        + [b16(*table.shape) for table in tables],
        in_specs=[HBM] * 7,
        out_specs=[VMEM] * 6,
        scratch_shapes=[
            pltpu.VMEM(fine_state.shape, jnp.float32),
            pltpu.VMEM(fine_kappa.shape, jnp.float32),
            pltpu.VMEM(fine_rate.shape, jnp.float32),
            pltpu.VMEM((blocks * STRIDE, LANES), jnp.float32),
            pltpu.VMEM((TILES * STRIDE, LANES), jnp.float32),
            pltpu.SemaphoreType.DMA((3, slots)),
            pltpu.SemaphoreType.DMA((3,)),
        ],
        compiler_params=PARAMS,
        name="prepare",
    )(new, fine_state, fine_kappa, fine_rate, *tables)

    fine_out, averages = pl.pallas_call(
        functools.partial(finish_kernel, slots=slots),
        out_shape=[f32(*fine_state.shape), f32(af_count, AVG_ROWS // FACES, LANES)],
        in_specs=[VMEM] * 7,
        out_specs=[HBM, VMEM],
        scratch_shapes=[
            pltpu.VMEM((blocks * STRIDE, LANES), jnp.float32),
            pltpu.VMEM((blocks * STRIDE, LANES), jnp.float32),
            pltpu.VMEM((blocks * FZ, LANES), jnp.float32),
            pltpu.VMEM((blocks * FZ, LANES), jnp.float32),
            pltpu.VMEM(fine_state.shape, jnp.float32),
            pltpu.SemaphoreType.DMA((slots,)),
        ],
        compiler_params=PARAMS,
        name="finish",
    )(strips, fields, coeffs, upward, *tables)

    arrived = exchange(averages)
    ylo_after, yhi_after, _ = lax.optimization_barrier((ylo, yhi, averages))
    yl = shifted(yhi_after, "col", 1)
    yr = shifted(ylo_after, "col", -1)

    placed = pl.pallas_call(
        functools.partial(place_kernel, slots=slots, **sizes),
        out_shape=f32(rows, cells_y),
        in_specs=[VMEM] * 7,
        out_specs=VMEM,
        compiler_params=PARAMS,
        name="place",
    )(pick, arrived, new, ylo, yhi, yl, yr)
    return (placed.reshape(coarse_state.shape), fine_out)


def solution(mesh):
    return jax.shard_map(
        per_device,
        mesh=mesh,
        in_specs=(
            P(None, None, "af", "col"),
            P(None, "af", "col"),
            P(None, "af", "col"),
            P(("col", "af"), None, None, None),
            P(("col", "af"), None, None),
            P(("col", "af"), None, None),
            P(),
            P(),
        ),
        out_specs=(P(None, None, "af", "col"), P(("col", "af"), None, None, None)),
        check_vma=False,
    )
```

```python
import functools

import jax
import jax.numpy as jnp
import ml_dtypes
import numpy as np
from jax import lax
from jax.experimental import pallas as pl
from jax.experimental.pallas import tpu as pltpu
from jax.sharding import PartitionSpec as P

NZC = 8
RATIO = 4
BLK = 8
SPECIES = 3
EDGE = BLK * RATIO
FZ = NZC * RATIO
LANES = 128
TILES = EDGE * EDGE // LANES
ZTILES = FZ // 8
STRIDE = 48
PAD = 8
FACES = 4
PLANES = SPECIES * NZC
STRIP_ROWS = 2 * PLANES
AVG_ROWS = PLANES * BLK
KINDS = 9
FIELD_ROWS = SPECIES * TILES * STRIDE
COEFF_ROWS = KINDS * TILES * FZ
UPWARD_ROWS = TILES * STRIDE

DT_COARSE = 1.0 / 28.0
DIFFUSE = (1.0, 0.7, 0.45)
SIGNS = (-1.0, -1.0, 1.0)
FINE_SCALE = RATIO * RATIO * DT_COARSE / RATIO
DT_FINE = DT_COARSE / RATIO


def lane_ids(shape):
    return lax.broadcasted_iota(jnp.int32, shape, len(shape) - 1)


def roll_lanes(values, shift):
    width = values.shape[-1]
    shift = shift % width
    return values if shift == 0 else pltpu.roll(values, shift, values.ndim - 1)


def split_pair(values):
    high = values.astype(jnp.bfloat16)
    low = (values - high.astype(jnp.float32)).astype(jnp.bfloat16)
    return high, low


def face(scale, one, other):
    summed = one + other
    inverse = pl.reciprocal(summed, approx=True)
    inverse = inverse * (2.0 - summed * inverse)
    return (2.0 * scale) * (one * other) * inverse


def start_all(copies):
    for copy in copies:
        copy.start()


def selector(place_ref, column, cells_y):
    wanted = jnp.where(place_ref[0:8, :] == column, place_ref[8:16, :], -1)
    row = lax.broadcasted_iota(jnp.int32, wanted.shape, 0)
    return jnp.concatenate(
        [jnp.where(row + 8 * at == wanted, 1.0, 0.0) for at in range(cells_y // 8)], axis=0
    ).astype(jnp.bfloat16)


def load_kernel(
    boxes_hbm,
    state_hbm,
    kappa_hbm,
    rate_hbm,
    state_ref,
    kappa_ref,
    rate_ref,
    place_ref,
    xlo_ref,
    xhi_ref,
    ylo_ref,
    yhi_ref,
    boxes_ref,
    sems,
    *,
    cells_x,
    cells_y,
    group,
):
    pairs = (
        (boxes_hbm, boxes_ref),
        (state_hbm, state_ref),
        (kappa_hbm, kappa_ref),
        (rate_hbm, rate_ref),
    )
    copies = [
        pltpu.make_async_copy(source, target, sems.at[index])
        for index, (source, target) in enumerate(pairs)
    ]
    start_all(copies)

    patches = boxes_ref.shape[1]
    lanes = group * BLK
    base = lax.axis_index("col") * group
    member = lax.broadcasted_iota(jnp.int32, (patches, lanes), 0) - base
    spread = jnp.where(member == lane_ids((patches, lanes)) // BLK, 1.0, 0.0).astype(jnp.bfloat16)
    first_col = lax.axis_index("af") * (cells_x // BLK)
    first_cell = lax.axis_index("col") * cells_y
    copies[0].wait()
    boxes = boxes_ref[...].astype(jnp.float32)
    stacked = jnp.concatenate(
        [jnp.broadcast_to(boxes[row : row + 1], (8, patches)) for row in range(2)], axis=0
    )
    found = jnp.dot(
        stacked.astype(jnp.bfloat16), spread, preferred_element_type=jnp.float32
    ).astype(jnp.int32)
    place_ref[0:8, :] = found[0:8] - first_col
    place_ref[8:16, :] = found[8:16] * BLK - first_cell + lane_ids((8, lanes)) % BLK

    copies[1].wait()
    copies[2].wait()
    lane = lane_ids((cells_x, LANES))
    low = jnp.zeros((cells_x, LANES), jnp.float32)
    high = jnp.zeros((cells_x, LANES), jnp.float32)
    for plane in range(PLANES + NZC):
        if plane < PLANES:
            ref, start = state_ref, plane * cells_x
        else:
            ref, start = kappa_ref, (plane - PLANES) * cells_x
        first = ref[start : start + cells_x, 0:LANES]
        last = ref[start : start + cells_x, cells_y - LANES : cells_y]
        xlo_ref[plane : plane + 1, :] = ref[start : start + 1, :]
        xhi_ref[plane : plane + 1, :] = ref[start + cells_x - 1 : start + cells_x, :]
        low = jnp.where(lane == plane, roll_lanes(first, plane), low)
        high = jnp.where(lane == plane, roll_lanes(last, plane + 1), high)
    ylo_ref[...] = low
    yhi_ref[...] = high
    copies[3].wait()


def coarse_kernel(
    place_ref,
    state_ref,
    kappa_ref,
    rate_ref,
    xl_ref,
    xr_ref,
    new_ref,
    send_ref,
    padded,
    fresh,
    *,
    cells_x,
    cells_y,
    group,
    slots,
):
    halves = cells_y // LANES
    span = cells_x + 2 * PAD

    def base(field, half, z):
        return ((field * halves + half) * NZC + z) * span

    for field in range(SPECIES + 1):
        for half in range(halves):
            cols = pl.ds(half * LANES, LANES)
            for z in range(NZC):
                if field < SPECIES:
                    start = (field * NZC + z) * cells_x
                    plane = state_ref[start : start + cells_x, cols]
                else:
                    plane = kappa_ref[z * cells_x : (z + 1) * cells_x, cols]
                at = base(field, half, z) + PAD
                padded[at : at + cells_x, :] = plane
            at = base(field, half, 0) + PAD
            rows = slice(field * NZC, (field + 1) * NZC)
            padded[pl.ds(at - 1, NZC, stride=span), :] = xl_ref[rows, cols]
            padded[pl.ds(at + cells_x, NZC, stride=span), :] = xr_ref[rows, cols]

    lane = lane_ids((cells_x, LANES))

    def load(field, half, z, shift):
        at = base(field, half, z) + PAD + shift
        return padded[at : at + cells_x, :]

    def neighbours(field, half, z):
        here = load(field, half, z, 0)
        after = roll_lanes(here, -1)
        if half + 1 < halves:
            after = jnp.where(
                lane == LANES - 1, roll_lanes(load(field, half + 1, z, 0), -1), after
            )
        before = roll_lanes(here, 1)
        if half > 0:
            before = jnp.where(lane == 0, roll_lanes(load(field, half - 1, z, 0), 1), before)
        found = [after, before, load(field, half, z, 1), load(field, half, z, -1)]
        if z + 1 < NZC:
            found.append(load(field, half, z + 1, 0))
        if z > 0:
            found.append(load(field, half, z - 1, 0))
        return found

    for z in range(NZC):
        for half in range(halves):
            cols = pl.ds(half * LANES, LANES)
            conduct = load(SPECIES, half, z, 0)
            coeffs = [face(DT_COARSE, conduct, other) for other in neighbours(SPECIES, half, z)]
            if half == halves - 1:
                coeffs[0] = jnp.where(lane == LANES - 1, 0.0, coeffs[0])
            if half == 0:
                coeffs[1] = jnp.where(lane == 0, 0.0, coeffs[1])
            centers = [load(field, half, z, 0) for field in range(SPECIES)]
            forward = (DT_COARSE * rate_ref[z * cells_x : (z + 1) * cells_x, cols]) * (
                centers[0] * centers[1] - centers[2]
            )
            for field in range(SPECIES):
                center = centers[field]
                flux = None
                for coeff, other in zip(coeffs, neighbours(field, half, z)):
                    term = coeff * (other - center)
                    flux = term if flux is None else flux + term
                start = (field * NZC + z) * cells_x
                result = center + DIFFUSE[field] * flux + SIGNS[field] * forward
                new_ref[start : start + cells_x, cols] = result
                start = ((field * halves + half) * NZC + z) * cells_x
                fresh[start : start + cells_x, :] = result

    def rows_at(row):
        columns = []
        for half in range(halves):
            pieces = []
            for field in range(SPECIES):
                pieces.append(padded[pl.ds(base(field, half, 0) + PAD + row, NZC, stride=span), :])
            for field in range(SPECIES):
                start = (field * halves + half) * NZC * cells_x
                pieces.append(fresh[pl.ds(start + row, NZC, stride=cells_x), :])
            columns.append(jnp.concatenate(pieces, axis=0))
        return jnp.concatenate(columns, axis=1)

    block_cols = cells_x // BLK
    spot = lane_ids((STRIP_ROWS, cells_y)) % BLK
    lower_y = []
    upper_y = []
    for column in range(block_cols):
        below = jnp.zeros((STRIP_ROWS, cells_y), jnp.float32)
        above = jnp.zeros((STRIP_ROWS, cells_y), jnp.float32)
        for x in range(BLK):
            strip = rows_at(column * BLK + x)
            below = jnp.where(spot == x, roll_lanes(strip, x + 1), below)
            above = jnp.where(spot == x, roll_lanes(strip, x - BLK), above)
        lower_y.append(below)
        upper_y.append(above)

    faces = [None] * FACES

    def add(index, part):
        faces[index] = part if faces[index] is None else faces[index] + part

    for column in range(-1, block_cols + 1):
        pick = selector(place_ref, column, cells_y)
        members = []
        if column >= 1:
            members.append((0, rows_at(column * BLK - 1)))
        if column < block_cols - 1:
            members.append((1, rows_at(column * BLK + BLK)))
        if 0 <= column < block_cols:
            members.append((2, lower_y[column]))
            members.append((3, upper_y[column]))
        operands = []
        for _, rows in members:
            operands.extend(split_pair(rows))
        moved = jnp.dot(
            jnp.concatenate(operands, axis=0), pick, preferred_element_type=jnp.float32
        )
        for order, (index, _) in enumerate(members):
            at = 2 * order * STRIP_ROWS
            add(index, moved[at : at + STRIP_ROWS] + moved[at + STRIP_ROWS : at + 2 * STRIP_ROWS])

    width = slots * BLK
    part = lane_ids((STRIP_ROWS, LANES)) // width
    for target in range(group // slots):
        first = target * width
        tile = first // LANES * LANES
        chunk = jnp.zeros((STRIP_ROWS, LANES), jnp.float32)
        for index in range(FACES):
            piece = faces[index][:, tile : tile + LANES]
            chunk = jnp.where(
                part == index, roll_lanes(piece, index * width - (first - tile)), chunk
            )
        send_ref[target] = chunk


def ghost_table():
    table = np.zeros((LANES, EDGE * EDGE), np.float32)
    x, y = np.divmod(np.arange(EDGE * EDGE), EDGE)
    width = LANES // FACES
    for pos in range(BLK):
        table[0 * width + pos] = (x == 0) & (y // RATIO == pos)
        table[1 * width + pos] = (x == EDGE - 1) & (y // RATIO == pos)
        table[2 * width + pos] = (y == 0) & (x // RATIO == pos)
        table[3 * width + pos] = (y == EDGE - 1) & (x // RATIO == pos)
    return np.concatenate([table, table]).astype(ml_dtypes.bfloat16)


def plane_table():
    rows = np.arange(2 * SPECIES * FZ)
    return (rows[:, None] // RATIO == np.arange(STRIP_ROWS)[None, :]).astype(ml_dtypes.bfloat16)


def mean_table():
    lane = np.arange(LANES)
    table = (lane[:, None] % EDGE // RATIO == lane[None, :] % BLK) / float(RATIO**3)
    return np.concatenate([table, table]).astype(ml_dtypes.bfloat16)


def aligned(start, size):
    return pl.ds(pl.multiple_of(start, 8), size)


def padded_at(block, ztile):
    return block * STRIDE + PAD + 8 * ztile


def advance(source, target, coeffs, upward, slot, from_rows, to_rows, ztile, ghosts):
    lane = lane_ids((8, LANES))

    def value(field, tile, shift):
        return source[pl.ds(from_rows + padded_at(field * TILES + tile, ztile) + shift, 8), :]

    def get(kind, tile):
        return coeffs[
            aligned(slot * COEFF_ROWS + (kind * TILES + tile) * FZ + 8 * ztile, 8), :
        ]

    centers = [value(field, 0, 0) for field in range(SPECIES)]
    down = [roll_lanes(center, -EDGE) for center in centers]
    up = [roll_lanes(center, EDGE) for center in centers]
    up_before = list(up)
    for tile in range(TILES):
        if tile + 1 < TILES:
            centers_after = [value(field, tile + 1, 0) for field in range(SPECIES)]
            down_after = [roll_lanes(center, -EDGE) for center in centers_after]
        next_x, prev_x, next_y, prev_y, rate = [get(kind, tile) for kind in range(5)]
        base = slot * UPWARD_ROWS + padded_at(tile, ztile)
        next_z = upward[pl.ds(base, 8), :]
        prev_z = upward[pl.ds(base - 1, 8), :]
        forward = rate * (centers[0] * centers[1] - centers[2])
        for field in range(SPECIES):
            center = centers[field]
            ahead, behind = down[field], up[field]
            if tile + 1 < TILES:
                ahead = jnp.where(lane < LANES - EDGE, ahead, down_after[field])
            if tile > 0:
                behind = jnp.where(lane >= EDGE, behind, up_before[field])
            flux = (next_x * ahead + prev_x * behind) + (
                next_y * roll_lanes(center, -1) + prev_y * roll_lanes(center, 1)
            )
            flux = flux + (next_z * value(field, tile, 1) + prev_z * value(field, tile, -1))
            share = ghosts(field, tile)
            if share is not None:
                flux = flux + share
            if DIFFUSE[field] != 1.0:
                flux = DIFFUSE[field] * flux
            result = get(5 + field, tile) * center + flux
            result = result - forward if SIGNS[field] < 0 else result + forward
            target[aligned(to_rows + padded_at(field * TILES + tile, ztile), 8), :] = result
        if tile + 1 < TILES:
            up_before = up
            centers, down = centers_after, down_after
            up = [roll_lanes(center, EDGE) for center in centers]


def clear_pads(ref):
    edge = jnp.zeros((PAD, LANES), jnp.float32)

    def body(block, carry):
        ref[aligned(block * STRIDE, PAD), :] = edge
        ref[aligned(block * STRIDE + PAD + FZ, PAD), :] = edge
        return carry

    lax.fori_loop(0, ref.shape[0] // STRIDE, body, 0)


def prepare_kernel(
    after_ref,
    state_hbm,
    kappa_hbm,
    rate_hbm,
    fields_hbm,
    coeffs_hbm,
    upward_hbm,
    fields_ref,
    coeffs,
    upward,
    state_ref,
    kappa_ref,
    rate_ref,
    first,
    conduct,
    sems,
    out_sems,
    *,
    slots,
):
    def loads(slot):
        return [
            pltpu.make_async_copy(source.at[slot], target.at[slot], sems.at[order, slot])
            for order, (source, target) in enumerate(
                ((kappa_hbm, kappa_ref), (rate_hbm, rate_ref), (state_hbm, state_ref))
            )
        ]

    for slot in range(slots):
        start_all(loads(slot))
    def stores(slot):
        return [
            pltpu.make_async_copy(
                source.at[aligned(slot * size, size)],
                target.at[aligned(slot * size, size)],
                out_sems.at[order, slot],
            )
            for order, (source, target, size) in enumerate(
                (
                    (fields_ref, fields_hbm, FIELD_ROWS),
                    (coeffs, coeffs_hbm, COEFF_ROWS),
                    (upward, upward_hbm, UPWARD_ROWS),
                )
            )
        ]

    for ref in (fields_ref, upward, first, conduct):
        clear_pads(ref)

    lane = lane_ids((8, LANES))
    column = lane % EDGE
    side_y = jnp.where((column == 0) | (column == EDGE - 1), 1.0, 0.0)

    def one_patch(slot, carry):
        for copy in loads(slot):
            copy.wait()

        for tile in range(TILES):
            cols = pl.ds(tile * LANES, LANES)
            for field in range(SPECIES):
                row = padded_at(field * TILES + tile, 0)
                first[row : row + FZ, :] = state_ref[slot, field, :, cols]
            row = padded_at(tile, 0)
            conduct[row : row + FZ, :] = kappa_ref[slot, :, cols]

        def keep(kind, tile, ztile, values):
            coeffs[
                aligned(slot * COEFF_ROWS + (kind * TILES + tile) * FZ + 8 * ztile, 8), :
            ] = values

        for ztile in range(ZTILES):

            def here(tile, shift):
                return conduct[pl.ds(padded_at(tile, ztile) + shift, 8), :]

            center = here(0, 0)
            turned = roll_lanes(center, -EDGE)
            back_before = None
            for tile in range(TILES):
                other = turned
                if tile + 1 < TILES:
                    center_after = here(tile + 1, 0)
                    turned_after = roll_lanes(center_after, -EDGE)
                    other = jnp.where(lane < LANES - EDGE, turned, turned_after)
                next_x = face(FINE_SCALE, center, other)
                if tile == TILES - 1:
                    next_x = jnp.where(lane < LANES - EDGE, next_x, 0.0)
                back = roll_lanes(next_x, EDGE)
                prev_x = jnp.where(lane >= EDGE, back, 0.0 if tile == 0 else back_before)
                next_y = jnp.where(
                    column < EDGE - 1, face(FINE_SCALE, center, roll_lanes(center, -1)), 0.0
                )
                prev_y = roll_lanes(next_y, 1)
                next_z = face(FINE_SCALE, center, here(tile, 1))
                prev_z = face(FINE_SCALE, center, here(tile, -1))
                sides = side_y
                if tile == 0:
                    sides = sides + jnp.where(lane < EDGE, 1.0, 0.0)
                if tile == TILES - 1:
                    sides = sides + jnp.where(lane >= LANES - EDGE, 1.0, 0.0)
                scale = FINE_SCALE * center
                total = (next_x + prev_x) + (next_y + prev_y) + (next_z + prev_z) + sides * scale
                upward[aligned(slot * UPWARD_ROWS + padded_at(tile, ztile), 8), :] = next_z
                keep(0, tile, ztile, next_x)
                keep(1, tile, ztile, prev_x)
                keep(2, tile, ztile, next_y)
                keep(3, tile, ztile, prev_y)
                rate = rate_ref[slot, pl.ds(8 * ztile, 8), pl.ds(tile * LANES, LANES)]
                keep(4, tile, ztile, DT_FINE * rate)
                for field in range(SPECIES):
                    keep(5 + field, tile, ztile, 1.0 - DIFFUSE[field] * total)
                keep(8, tile, ztile, scale)
                back_before = back
                if tile + 1 < TILES:
                    center, turned = center_after, turned_after

        for ztile in range(ZTILES):
            advance(
                first,
                fields_ref,
                coeffs,
                upward,
                slot,
                0,
                slot * FIELD_ROWS,
                ztile,
                lambda field, tile: None,
            )
        start_all(stores(slot))
        return carry

    lax.fori_loop(0, slots, one_patch, 0)
    for slot in range(slots):
        for copy in stores(slot):
            copy.wait()


def finish_kernel(
    strips_hbm,
    fields_hbm,
    coeffs_hbm,
    upward_hbm,
    ghost_hbm,
    plane_hbm,
    mean_hbm,
    out_hbm,
    avg_hbm,
    strips_ref,
    fields_ref,
    coeffs,
    upward,
    ghost_ref,
    plane_ref,
    mean_ref,
    avg_ref,
    first,
    second,
    share,
    drift,
    staged,
    sems,
    in_sems,
    table_sems,
    avg_sems,
    *,
    slots,
):
    tables = [
        pltpu.make_async_copy(source, target, table_sems.at[order])
        for order, (source, target) in enumerate(
            (
                (strips_hbm, strips_ref),
                (plane_hbm, plane_ref),
                (ghost_hbm, ghost_ref),
                (mean_hbm, mean_ref),
            )
        )
    ]
    start_all(tables)

    def loads(slot):
        return [
            pltpu.make_async_copy(
                source.at[aligned(slot * size, size)],
                target.at[aligned(slot * size, size)],
                in_sems.at[order, slot],
            )
            for order, (source, target, size) in enumerate(
                (
                    (fields_hbm, fields_ref, FIELD_ROWS),
                    (coeffs_hbm, coeffs, COEFF_ROWS),
                    (upward_hbm, upward, UPWARD_ROWS),
                )
            )
        ]

    for slot in range(slots):
        start_all(loads(slot))
    sources = strips_ref.shape[0]
    clear_pads(first)
    clear_pads(second)
    for copy in tables:
        copy.wait()

    gathered = strips_ref[0]
    for source in range(1, sources):
        gathered = gathered + strips_ref[source]
    half = STRIP_ROWS // 2
    gathered = jnp.concatenate(
        [gathered[:half], (gathered[half:] - gathered[:half]) * (1.0 / RATIO)], axis=0
    )
    quarter = AVG_ROWS // FACES
    group_of = lane_ids((quarter, LANES)) // BLK

    def send_out(slot):
        return pltpu.make_async_copy(staged.at[slot], out_hbm.at[slot], sems.at[slot])

    def one_patch(slot, carry):
        for copy in loads(slot):
            copy.wait()
        turned = pltpu.roll(gathered, (LANES - slot * BLK) % LANES, 1)
        stretched = jnp.dot(
            plane_ref[...],
            jnp.concatenate(split_pair(turned), axis=1),
            preferred_element_type=jnp.float32,
        ).astype(jnp.bfloat16)
        base = slot * FIELD_ROWS
        scales = slot * COEFF_ROWS
        for tile in range(TILES):
            ghosts = jnp.dot(
                stretched,
                ghost_ref[:, tile * LANES : (tile + 1) * LANES],
                preferred_element_type=jnp.float32,
            )
            scale = coeffs[aligned(scales + (8 * TILES + tile) * FZ, FZ), :]
            for field in range(SPECIES):
                row = (field * TILES + tile) * FZ
                old = scale * ghosts[field * FZ : (field + 1) * FZ]
                step = scale * ghosts[(SPECIES + field) * FZ : (SPECIES + field + 1) * FZ]
                drift[row : row + FZ, :] = step
                share[row : row + FZ, :] = old + step
                row = padded_at(field * TILES + tile, 0)
                second[row : row + FZ, :] = (
                    fields_ref[aligned(base + row, FZ), :] + DIFFUSE[field] * old
                )

        for step in range(1, RATIO):
            source, target = (second, first) if step % 2 else (first, second)
            for ztile in range(ZTILES):

                def ghosts(field, tile):
                    spot = pl.ds((field * TILES + tile) * FZ + 8 * ztile, 8)
                    value = share[spot, :]
                    if step + 1 < RATIO:
                        share[spot, :] = value + drift[spot, :]
                    return value

                advance(source, target, coeffs, upward, slot, 0, 0, ztile, ghosts)

        for tile in range(TILES):
            for field in range(SPECIES):
                row = padded_at(field * TILES + tile, 0)
                staged[slot, field, :, pl.ds(tile * LANES, LANES)] = first[row : row + FZ, :]
        send_out(slot).start()

        sums = []
        for field in range(SPECIES):
            for plane in range(NZC):
                start = field * TILES * STRIDE + PAD + RATIO * plane
                part = first[pl.ds(start, TILES, stride=STRIDE), :]
                for z in range(1, RATIO):
                    part = part + first[pl.ds(start + z, TILES, stride=STRIDE), :]
                sums.append(part)
        means = jnp.dot(
            jnp.concatenate(split_pair(jnp.concatenate(sums, axis=0)), axis=1),
            mean_ref[...],
            preferred_element_type=jnp.float32,
        )
        chunk = avg_ref[...]
        for part in range(FACES):
            chunk = jnp.where(
                group_of == part * slots + slot,
                means[part * quarter : (part + 1) * quarter],
                chunk,
            )
        avg_ref[...] = chunk
        return carry

    avg_ref[...] = jnp.zeros((quarter, LANES), jnp.float32)
    lax.fori_loop(0, slots, one_patch, 0)
    copies = [
        pltpu.make_async_copy(avg_ref, avg_hbm.at[target], avg_sems.at[target])
        for target in range(sources)
    ]
    start_all(copies)
    for copy in copies:
        copy.wait()
    for slot in range(slots):
        send_out(slot).wait()


def place_kernel(
    place_ref,
    avg_ref,
    new_ref,
    ylo_ref,
    yhi_ref,
    yl_ref,
    yr_ref,
    out_ref,
    *,
    cells_x,
    cells_y,
    group,
    slots,
):
    def edge_share(own_ref, other_ref):
        own = own_ref[...]
        other = other_ref[...]
        coeff = face(DT_COARSE, jnp.maximum(own, 0.125), other)
        lane = lane_ids(own.shape)
        spread = jnp.zeros_like(own)
        for field in range(SPECIES):
            moved = roll_lanes(coeff, (field - SPECIES) * NZC)
            spread = jnp.where(lane // NZC == field, DIFFUSE[field] * moved, spread)
        return spread * (other - own)

    lower = edge_share(ylo_ref, yl_ref)
    upper = edge_share(yhi_ref, yr_ref)

    width = slots * BLK
    quarter = AVG_ROWS // FACES
    per_tile = LANES // width
    part = lane_ids((quarter, LANES)) // width
    columns = []
    for tile in range(group * BLK // LANES):
        rows = []
        for index in range(FACES):
            merged = jnp.zeros((quarter, LANES), jnp.float32)
            for place in range(per_tile):
                piece = roll_lanes(avg_ref[tile * per_tile + place], (place - index) * width)
                merged = jnp.where(part == place, piece, merged)
            rows.append(merged)
        columns.append(jnp.concatenate(rows, axis=0))
    high, low = split_pair(jnp.concatenate(columns, axis=1))
    ones = jnp.ones((16, high.shape[1]), jnp.bfloat16)
    stacked = jnp.concatenate([high, low, ones], axis=0)

    lane = lane_ids((BLK, LANES))
    halves = cells_y // LANES
    for column in range(cells_x // BLK):
        placed = lax.dot_general(
            stacked,
            selector(place_ref, column, cells_y),
            (((1,), (1,)), ((), ())),
            preferred_element_type=jnp.float32,
        )
        covered = placed[2 * AVG_ROWS : 2 * AVG_ROWS + 8] > 0.5
        for plane in range(PLANES):
            values = (
                placed[plane * BLK : (plane + 1) * BLK]
                + placed[AVG_ROWS + plane * BLK : AVG_ROWS + (plane + 1) * BLK]
            )
            row = plane * cells_x + column * BLK
            edge_rows = slice(column * BLK, (column + 1) * BLK)
            for half in range(halves):
                cols = slice(half * LANES, (half + 1) * LANES)
                coarse = new_ref[row : row + BLK, cols]
                if half == 0:
                    share = roll_lanes(lower[edge_rows], -plane)
                    coarse = coarse + jnp.where(lane == 0, share, 0.0)
                if half == halves - 1:
                    share = roll_lanes(upper[edge_rows], LANES - 1 - plane)
                    coarse = coarse + jnp.where(lane == LANES - 1, share, 0.0)
                out_ref[row : row + BLK, cols] = jnp.where(
                    covered[:, cols], values[:, cols], coarse
                )


VMEM = pl.BlockSpec(memory_space=pltpu.VMEM)
HBM = pl.BlockSpec(memory_space=pltpu.HBM)
PARAMS = pltpu.CompilerParams(vmem_limit_bytes=40 * 1024 * 1024)


def f32(*shape):
    return jax.ShapeDtypeStruct(shape, jnp.float32)


def shifted(values, axis, step):
    count = lax.axis_size(axis)
    pairs = [(i, i + step) for i in range(count) if 0 <= i + step < count]
    return lax.ppermute(values, axis, pairs)


def exchange(chunks):
    return lax.all_to_all(chunks, "af", split_axis=0, concat_axis=0, tiled=True)


def per_device(
    coarse_state, coarse_kappa, coarse_rate, fine_state, fine_kappa, fine_rate, boxes, cover
):
    af_count = lax.axis_size("af")
    slots = fine_state.shape[0]
    cells_x, cells_y = coarse_state.shape[2:]
    group = af_count * slots
    lanes = group * BLK
    halves = cells_y // LANES
    rows = PLANES * cells_x
    plain = NZC * cells_x
    sizes = dict(cells_x=cells_x, cells_y=cells_y, group=group)

    state, kappa, rate, place, xlo, xhi, ylo, yhi = pl.pallas_call(
        functools.partial(load_kernel, **sizes),
        out_shape=[f32(rows, cells_y), f32(plain, cells_y), f32(plain, cells_y)]
        + [jax.ShapeDtypeStruct((16, lanes), jnp.int32)]
        + [f32(PLANES + NZC, cells_y)] * 2
        + [f32(cells_x, LANES)] * 2,
        in_specs=[HBM] * 4,
        out_specs=[VMEM] * 8,
        scratch_shapes=[
            pltpu.VMEM((2, boxes.shape[0]), jnp.int32),
            pltpu.SemaphoreType.DMA((4,)),
        ],
        compiler_params=PARAMS,
        name="load",
    )(
        boxes.T,
        coarse_state.reshape(rows, cells_y),
        coarse_kappa.reshape(plain, cells_y),
        coarse_rate.reshape(plain, cells_y),
    )
    xl = shifted(xhi, "af", 1)
    xr = shifted(xlo, "af", -1)
    yl = shifted(yhi, "col", 1)
    yr = shifted(ylo, "col", -1)

    span = cells_x + 2 * PAD
    new, send = pl.pallas_call(
        functools.partial(coarse_kernel, slots=slots, **sizes),
        out_shape=[
            f32(rows, cells_y),
            f32(af_count, STRIP_ROWS, LANES),
        ],
        in_specs=[VMEM] * 6,
        out_specs=[VMEM] * 2,
        scratch_shapes=[
            pltpu.VMEM(((SPECIES + 1) * halves * NZC * span, LANES), jnp.float32),
            pltpu.VMEM((rows * halves, LANES), jnp.float32),
        ],
        compiler_params=PARAMS,
        name="coarse",
    )(place, state, kappa, rate, xl, xr)

    strips = exchange(send)

    kept = [f32(slots * size, LANES) for size in (FIELD_ROWS, COEFF_ROWS, UPWARD_ROWS)]
    kept_scratch = [pltpu.VMEM(shape.shape, jnp.float32) for shape in kept]
    fields, coeffs, upward = pl.pallas_call(
        functools.partial(prepare_kernel, slots=slots),
        out_shape=kept,
        in_specs=[HBM] * 4,
        out_specs=[HBM] * 3,
        scratch_shapes=kept_scratch
        + [
            pltpu.VMEM(fine_state.shape, jnp.float32),
            pltpu.VMEM(fine_kappa.shape, jnp.float32),
            pltpu.VMEM(fine_rate.shape, jnp.float32),
            pltpu.VMEM((FIELD_ROWS, LANES), jnp.float32),
            pltpu.VMEM((UPWARD_ROWS, LANES), jnp.float32),
            pltpu.SemaphoreType.DMA((3, slots)),
            pltpu.SemaphoreType.DMA((3, slots)),
        ],
        compiler_params=PARAMS,
        name="prepare",
    )(send, fine_state, fine_kappa, fine_rate)

    tables = [jnp.asarray(table) for table in (ghost_table(), plane_table(), mean_table())]
    chunk = (AVG_ROWS // FACES, LANES)
    fine_out, averages = pl.pallas_call(
        functools.partial(finish_kernel, slots=slots),
        out_shape=[f32(*fine_state.shape), f32(af_count, *chunk)],
        in_specs=[HBM] * 7,
        out_specs=[HBM, HBM],
        scratch_shapes=[pltpu.VMEM(strips.shape, jnp.float32)]
        + kept_scratch
        + [pltpu.VMEM(table.shape, jnp.bfloat16) for table in tables]
        + [
            pltpu.VMEM(chunk, jnp.float32),
            pltpu.VMEM((FIELD_ROWS, LANES), jnp.float32),
            pltpu.VMEM((FIELD_ROWS, LANES), jnp.float32),
            pltpu.VMEM((SPECIES * TILES * FZ, LANES), jnp.float32),
            pltpu.VMEM((SPECIES * TILES * FZ, LANES), jnp.float32),
            pltpu.VMEM(fine_state.shape, jnp.float32),
            pltpu.SemaphoreType.DMA((slots,)),
            pltpu.SemaphoreType.DMA((3, slots)),
            pltpu.SemaphoreType.DMA((4,)),
            pltpu.SemaphoreType.DMA((af_count,)),
        ],
        compiler_params=PARAMS,
        name="finish",
    )(strips, fields, coeffs, upward, *tables)

    arrived = exchange(averages)

    placed = pl.pallas_call(
        functools.partial(place_kernel, slots=slots, **sizes),
        out_shape=f32(rows, cells_y),
        in_specs=[VMEM] * 7,
        out_specs=VMEM,
        compiler_params=PARAMS,
        name="place",
    )(place, arrived, new, ylo, yhi, yl, yr)
    return (placed.reshape(coarse_state.shape), fine_out)


def solution(mesh):
    return jax.shard_map(
        per_device,
        mesh=mesh,
        in_specs=(
            P(None, None, "af", "col"),
            P(None, "af", "col"),
            P(None, "af", "col"),
            P(("col", "af"), None, None, None),
            P(("col", "af"), None, None),
            P(("col", "af"), None, None),
            P(),
            P(),
        ),
        out_specs=(P(None, None, "af", "col"), P(("col", "af"), None, None, None)),
        check_vma=False,
    )
```

```python
import functools

import jax
import jax.numpy as jnp
import ml_dtypes
import numpy as np
from jax import lax
from jax.experimental import pallas as pl
from jax.experimental.pallas import tpu as pltpu
from jax.sharding import PartitionSpec as P

NZC = 8
RATIO = 4
BLK = 8
SPECIES = 3
EDGE = BLK * RATIO
FZ = NZC * RATIO
LANES = 128
TILES = EDGE * EDGE // LANES
ZTILES = FZ // 8
STRIDE = 48
PAD = 8
FACES = 4
PLANES = SPECIES * NZC
STRIP_ROWS = 2 * PLANES
AVG_ROWS = PLANES * BLK
KINDS = 9
FIELD_ROWS = SPECIES * TILES * STRIDE
COEFF_ROWS = KINDS * TILES * FZ
UPWARD_ROWS = TILES * STRIDE

DT_COARSE = 1.0 / 28.0
DIFFUSE = (1.0, 0.7, 0.45)
SIGNS = (-1.0, -1.0, 1.0)
FINE_SCALE = RATIO * RATIO * DT_COARSE / RATIO
DT_FINE = DT_COARSE / RATIO


def lane_ids(shape):
    return lax.broadcasted_iota(jnp.int32, shape, len(shape) - 1)


def roll_lanes(values, shift):
    width = values.shape[-1]
    shift = shift % width
    return values if shift == 0 else pltpu.roll(values, shift, values.ndim - 1)


def split_pair(values):
    high = values.astype(jnp.bfloat16)
    low = (values - high.astype(jnp.float32)).astype(jnp.bfloat16)
    return high, low


def face(scale, one, other):
    summed = one + other
    inverse = pl.reciprocal(summed, approx=True)
    inverse = inverse * (2.0 - summed * inverse)
    return (2.0 * scale) * (one * other) * inverse


def start_all(copies):
    for copy in copies:
        copy.start()


def selector(place_ref, column, cells_y):
    wanted = jnp.where(place_ref[0:8, :] == column, place_ref[8:16, :], -1)
    row = lax.broadcasted_iota(jnp.int32, wanted.shape, 0)
    return jnp.concatenate(
        [jnp.where(row + 8 * at == wanted, 1.0, 0.0) for at in range(cells_y // 8)], axis=0
    ).astype(jnp.bfloat16)


def load_kernel(
    boxes_hbm,
    state_hbm,
    kappa_hbm,
    rate_hbm,
    state_ref,
    kappa_ref,
    rate_ref,
    place_ref,
    xlo_ref,
    xhi_ref,
    ylo_ref,
    yhi_ref,
    boxes_ref,
    sems,
    *,
    cells_x,
    cells_y,
    group,
):
    pairs = (
        (boxes_hbm, boxes_ref),
        (state_hbm, state_ref),
        (kappa_hbm, kappa_ref),
        (rate_hbm, rate_ref),
    )
    copies = [
        pltpu.make_async_copy(source, target, sems.at[index])
        for index, (source, target) in enumerate(pairs)
    ]
    start_all(copies)

    patches = boxes_ref.shape[1]
    lanes = group * BLK
    base = lax.axis_index("col") * group
    member = lax.broadcasted_iota(jnp.int32, (patches, lanes), 0) - base
    spread = jnp.where(member == lane_ids((patches, lanes)) // BLK, 1.0, 0.0).astype(jnp.bfloat16)
    first_col = lax.axis_index("af") * (cells_x // BLK)
    first_cell = lax.axis_index("col") * cells_y
    copies[0].wait()
    boxes = boxes_ref[...].astype(jnp.float32)
    stacked = jnp.concatenate(
        [jnp.broadcast_to(boxes[row : row + 1], (8, patches)) for row in range(2)], axis=0
    )
    found = jnp.dot(
        stacked.astype(jnp.bfloat16), spread, preferred_element_type=jnp.float32
    ).astype(jnp.int32)
    place_ref[0:8, :] = found[0:8] - first_col
    place_ref[8:16, :] = found[8:16] * BLK - first_cell + lane_ids((8, lanes)) % BLK

    copies[1].wait()
    copies[2].wait()
    lane = lane_ids((cells_x, LANES))
    low = jnp.zeros((cells_x, LANES), jnp.float32)
    high = jnp.zeros((cells_x, LANES), jnp.float32)
    for plane in range(PLANES + NZC):
        if plane < PLANES:
            ref, start = state_ref, plane * cells_x
        else:
            ref, start = kappa_ref, (plane - PLANES) * cells_x
        first = ref[start : start + cells_x, 0:LANES]
        last = ref[start : start + cells_x, cells_y - LANES : cells_y]
        xlo_ref[plane : plane + 1, :] = ref[start : start + 1, :]
        xhi_ref[plane : plane + 1, :] = ref[start + cells_x - 1 : start + cells_x, :]
        low = jnp.where(lane == plane, roll_lanes(first, plane), low)
        high = jnp.where(lane == plane, roll_lanes(last, plane + 1), high)
    ylo_ref[...] = low
    yhi_ref[...] = high
    copies[3].wait()


def coarse_kernel(
    place_ref,
    state_ref,
    kappa_ref,
    rate_ref,
    xl_ref,
    xr_ref,
    yl_ref,
    yr_ref,
    new_hbm,
    send_ref,
    new_ref,
    padded,
    fresh,
    sem,
    *,
    cells_x,
    cells_y,
    group,
    slots,
):
    halves = cells_y // LANES
    span = cells_x + 2 * PAD

    def base(field, half, z):
        return ((field * halves + half) * NZC + z) * span

    for field in range(SPECIES + 1):
        for half in range(halves):
            cols = pl.ds(half * LANES, LANES)
            for z in range(NZC):
                if field < SPECIES:
                    start = (field * NZC + z) * cells_x
                    plane = state_ref[start : start + cells_x, cols]
                else:
                    plane = kappa_ref[z * cells_x : (z + 1) * cells_x, cols]
                at = base(field, half, z) + PAD
                padded[at : at + cells_x, :] = plane
            at = base(field, half, 0) + PAD
            rows = slice(field * NZC, (field + 1) * NZC)
            padded[pl.ds(at - 1, NZC, stride=span), :] = xl_ref[rows, cols]
            padded[pl.ds(at + cells_x, NZC, stride=span), :] = xr_ref[rows, cols]

    lane = lane_ids((cells_x, LANES))

    def load(field, half, z, shift):
        at = base(field, half, z) + PAD + shift
        return padded[at : at + cells_x, :]

    def neighbours(field, half, z):
        here = load(field, half, z, 0)
        after = roll_lanes(here, -1)
        if half + 1 < halves:
            after = jnp.where(
                lane == LANES - 1, roll_lanes(load(field, half + 1, z, 0), -1), after
            )
        before = roll_lanes(here, 1)
        if half > 0:
            before = jnp.where(lane == 0, roll_lanes(load(field, half - 1, z, 0), 1), before)
        found = [after, before, load(field, half, z, 1), load(field, half, z, -1)]
        if z + 1 < NZC:
            found.append(load(field, half, z + 1, 0))
        if z > 0:
            found.append(load(field, half, z - 1, 0))
        return found

    for z in range(NZC):
        for half in range(halves):
            cols = pl.ds(half * LANES, LANES)
            conduct = load(SPECIES, half, z, 0)
            coeffs = [face(DT_COARSE, conduct, other) for other in neighbours(SPECIES, half, z)]
            if half == halves - 1:
                coeffs[0] = jnp.where(lane == LANES - 1, 0.0, coeffs[0])
            if half == 0:
                coeffs[1] = jnp.where(lane == 0, 0.0, coeffs[1])
            centers = [load(field, half, z, 0) for field in range(SPECIES)]
            forward = (DT_COARSE * rate_ref[z * cells_x : (z + 1) * cells_x, cols]) * (
                centers[0] * centers[1] - centers[2]
            )
            for field in range(SPECIES):
                center = centers[field]
                flux = None
                for coeff, other in zip(coeffs, neighbours(field, half, z)):
                    term = coeff * (other - center)
                    flux = term if flux is None else flux + term
                start = (field * NZC + z) * cells_x
                result = center + DIFFUSE[field] * flux + SIGNS[field] * forward
                new_ref[start : start + cells_x, cols] = result
                start = ((field * halves + half) * NZC + z) * cells_x
                fresh[start : start + cells_x, :] = result

    keep_new = pltpu.make_async_copy(new_ref, new_hbm, sem)
    keep_new.start()

    def rows_at(row):
        columns = []
        for half in range(halves):
            pieces = []
            for field in range(SPECIES):
                pieces.append(padded[pl.ds(base(field, half, 0) + PAD + row, NZC, stride=span), :])
            for field in range(SPECIES):
                start = (field * halves + half) * NZC * cells_x
                pieces.append(fresh[pl.ds(start + row, NZC, stride=cells_x), :])
            columns.append(jnp.concatenate(pieces, axis=0))
        return jnp.concatenate(columns, axis=1)

    block_cols = cells_x // BLK
    spot = lane_ids((STRIP_ROWS, cells_y)) % BLK
    lower_y = []
    upper_y = []
    for column in range(block_cols):
        below = jnp.zeros((STRIP_ROWS, cells_y), jnp.float32)
        above = jnp.zeros((STRIP_ROWS, cells_y), jnp.float32)
        for x in range(BLK):
            strip = rows_at(column * BLK + x)
            below = jnp.where(spot == x, roll_lanes(strip, x + 1), below)
            above = jnp.where(spot == x, roll_lanes(strip, x - BLK), above)
        lower_y.append(below)
        upper_y.append(above)

    faces = [None] * FACES

    def add(index, part):
        faces[index] = part if faces[index] is None else faces[index] + part

    for column in range(-1, block_cols + 1):
        pick = selector(place_ref, column, cells_y)
        members = []
        if column >= 1:
            members.append((0, rows_at(column * BLK - 1)))
        if column < block_cols - 1:
            members.append((1, rows_at(column * BLK + BLK)))
        if 0 <= column < block_cols:
            members.append((2, lower_y[column]))
            members.append((3, upper_y[column]))
        operands = []
        for _, rows in members:
            operands.extend(split_pair(rows))
        moved = jnp.dot(
            jnp.concatenate(operands, axis=0), pick, preferred_element_type=jnp.float32
        )
        for order, (index, _) in enumerate(members):
            at = 2 * order * STRIP_ROWS
            add(index, moved[at : at + STRIP_ROWS] + moved[at + STRIP_ROWS : at + 2 * STRIP_ROWS])

    width = slots * BLK
    part = lane_ids((STRIP_ROWS, LANES)) // width
    for target in range(group // slots):
        first = target * width
        tile = first // LANES * LANES
        chunk = jnp.zeros((STRIP_ROWS, LANES), jnp.float32)
        for index in range(FACES):
            piece = faces[index][:, tile : tile + LANES]
            chunk = jnp.where(
                part == index, roll_lanes(piece, index * width - (first - tile)), chunk
            )
        send_ref[target] = chunk
    keep_new.wait()


def ghost_table():
    table = np.zeros((LANES, EDGE * EDGE), np.float32)
    x, y = np.divmod(np.arange(EDGE * EDGE), EDGE)
    width = LANES // FACES
    for pos in range(BLK):
        table[0 * width + pos] = (x == 0) & (y // RATIO == pos)
        table[1 * width + pos] = (x == EDGE - 1) & (y // RATIO == pos)
        table[2 * width + pos] = (y == 0) & (x // RATIO == pos)
        table[3 * width + pos] = (y == EDGE - 1) & (x // RATIO == pos)
    return np.concatenate([table, table]).astype(ml_dtypes.bfloat16)


def plane_table():
    rows = np.arange(2 * SPECIES * FZ)
    return (rows[:, None] // RATIO == np.arange(STRIP_ROWS)[None, :]).astype(ml_dtypes.bfloat16)


def mean_table():
    lane = np.arange(LANES)
    table = (lane[:, None] % EDGE // RATIO == lane[None, :] % BLK) / float(RATIO**3)
    return np.concatenate([table, table]).astype(ml_dtypes.bfloat16)


def aligned(start, size):
    return pl.ds(pl.multiple_of(start, 8), size)


def padded_at(block, ztile):
    return block * STRIDE + PAD + 8 * ztile


def advance(source, target, coeffs, upward, slot, from_rows, to_rows, ztile, ghosts):
    lane = lane_ids((8, LANES))

    def value(field, tile, shift):
        return source[pl.ds(from_rows + padded_at(field * TILES + tile, ztile) + shift, 8), :]

    def get(kind, tile):
        return coeffs[
            aligned(slot * COEFF_ROWS + (kind * TILES + tile) * FZ + 8 * ztile, 8), :
        ]

    centers = [value(field, 0, 0) for field in range(SPECIES)]
    down = [roll_lanes(center, -EDGE) for center in centers]
    up = [roll_lanes(center, EDGE) for center in centers]
    up_before = list(up)
    for tile in range(TILES):
        if tile + 1 < TILES:
            centers_after = [value(field, tile + 1, 0) for field in range(SPECIES)]
            down_after = [roll_lanes(center, -EDGE) for center in centers_after]
        next_x, prev_x, next_y, prev_y, rate = [get(kind, tile) for kind in range(5)]
        base = slot * UPWARD_ROWS + padded_at(tile, ztile)
        next_z = upward[pl.ds(base, 8), :]
        prev_z = upward[pl.ds(base - 1, 8), :]
        forward = rate * (centers[0] * centers[1] - centers[2])
        for field in range(SPECIES):
            center = centers[field]
            ahead, behind = down[field], up[field]
            if tile + 1 < TILES:
                ahead = jnp.where(lane < LANES - EDGE, ahead, down_after[field])
            if tile > 0:
                behind = jnp.where(lane >= EDGE, behind, up_before[field])
            flux = (next_x * ahead + prev_x * behind) + (
                next_y * roll_lanes(center, -1) + prev_y * roll_lanes(center, 1)
            )
            flux = flux + (next_z * value(field, tile, 1) + prev_z * value(field, tile, -1))
            share = ghosts(field, tile)
            if share is not None:
                flux = flux + share
            if DIFFUSE[field] != 1.0:
                flux = DIFFUSE[field] * flux
            result = get(5 + field, tile) * center + flux
            result = result - forward if SIGNS[field] < 0 else result + forward
            target[aligned(to_rows + padded_at(field * TILES + tile, ztile), 8), :] = result
        if tile + 1 < TILES:
            up_before = up
            centers, down = centers_after, down_after
            up = [roll_lanes(center, EDGE) for center in centers]


def clear_pads(ref):
    edge = jnp.zeros((PAD, LANES), jnp.float32)

    def body(block, carry):
        ref[aligned(block * STRIDE, PAD), :] = edge
        ref[aligned(block * STRIDE + PAD + FZ, PAD), :] = edge
        return carry

    lax.fori_loop(0, ref.shape[0] // STRIDE, body, 0)


def prepare_kernel(
    after_ref,
    state_hbm,
    kappa_hbm,
    rate_hbm,
    fields_hbm,
    coeffs_hbm,
    upward_hbm,
    fields_ref,
    coeffs,
    upward,
    state_ref,
    kappa_ref,
    rate_ref,
    first,
    conduct,
    sems,
    out_sems,
    *,
    slots,
):
    def loads(slot):
        return [
            pltpu.make_async_copy(source.at[slot], target.at[slot], sems.at[order, slot])
            for order, (source, target) in enumerate(
                ((kappa_hbm, kappa_ref), (rate_hbm, rate_ref), (state_hbm, state_ref))
            )
        ]

    for slot in range(slots):
        start_all(loads(slot))
    def stores(slot):
        return [
            pltpu.make_async_copy(
                source.at[aligned(slot * size, size)],
                target.at[aligned(slot * size, size)],
                out_sems.at[order, slot],
            )
            for order, (source, target, size) in enumerate(
                (
                    (fields_ref, fields_hbm, FIELD_ROWS),
                    (coeffs, coeffs_hbm, COEFF_ROWS),
                    (upward, upward_hbm, UPWARD_ROWS),
                )
            )
        ]

    for ref in (fields_ref, upward, first, conduct):
        clear_pads(ref)

    lane = lane_ids((8, LANES))
    column = lane % EDGE
    side_y = jnp.where((column == 0) | (column == EDGE - 1), 1.0, 0.0)

    def one_patch(slot, carry):
        for copy in loads(slot):
            copy.wait()

        for tile in range(TILES):
            cols = pl.ds(tile * LANES, LANES)
            for field in range(SPECIES):
                row = padded_at(field * TILES + tile, 0)
                first[row : row + FZ, :] = state_ref[slot, field, :, cols]
            row = padded_at(tile, 0)
            conduct[row : row + FZ, :] = kappa_ref[slot, :, cols]

        def keep(kind, tile, ztile, values):
            coeffs[
                aligned(slot * COEFF_ROWS + (kind * TILES + tile) * FZ + 8 * ztile, 8), :
            ] = values

        for ztile in range(ZTILES):

            def here(tile, shift):
                return conduct[pl.ds(padded_at(tile, ztile) + shift, 8), :]

            center = here(0, 0)
            turned = roll_lanes(center, -EDGE)
            back_before = None
            for tile in range(TILES):
                other = turned
                if tile + 1 < TILES:
                    center_after = here(tile + 1, 0)
                    turned_after = roll_lanes(center_after, -EDGE)
                    other = jnp.where(lane < LANES - EDGE, turned, turned_after)
                next_x = face(FINE_SCALE, center, other)
                if tile == TILES - 1:
                    next_x = jnp.where(lane < LANES - EDGE, next_x, 0.0)
                back = roll_lanes(next_x, EDGE)
                prev_x = jnp.where(lane >= EDGE, back, 0.0 if tile == 0 else back_before)
                next_y = jnp.where(
                    column < EDGE - 1, face(FINE_SCALE, center, roll_lanes(center, -1)), 0.0
                )
                prev_y = roll_lanes(next_y, 1)
                next_z = face(FINE_SCALE, center, here(tile, 1))
                prev_z = face(FINE_SCALE, center, here(tile, -1))
                sides = side_y
                if tile == 0:
                    sides = sides + jnp.where(lane < EDGE, 1.0, 0.0)
                if tile == TILES - 1:
                    sides = sides + jnp.where(lane >= LANES - EDGE, 1.0, 0.0)
                scale = FINE_SCALE * center
                total = (next_x + prev_x) + (next_y + prev_y) + (next_z + prev_z) + sides * scale
                upward[aligned(slot * UPWARD_ROWS + padded_at(tile, ztile), 8), :] = next_z
                keep(0, tile, ztile, next_x)
                keep(1, tile, ztile, prev_x)
                keep(2, tile, ztile, next_y)
                keep(3, tile, ztile, prev_y)
                rate = rate_ref[slot, pl.ds(8 * ztile, 8), pl.ds(tile * LANES, LANES)]
                keep(4, tile, ztile, DT_FINE * rate)
                for field in range(SPECIES):
                    keep(5 + field, tile, ztile, 1.0 - DIFFUSE[field] * total)
                keep(8, tile, ztile, scale)
                back_before = back
                if tile + 1 < TILES:
                    center, turned = center_after, turned_after

        for ztile in range(ZTILES):
            advance(
                first,
                fields_ref,
                coeffs,
                upward,
                slot,
                0,
                slot * FIELD_ROWS,
                ztile,
                lambda field, tile: None,
            )
        start_all(stores(slot))
        return carry

    lax.fori_loop(0, slots, one_patch, 0)
    for slot in range(slots):
        for copy in stores(slot):
            copy.wait()


def finish_kernel(
    strips_hbm,
    fields_hbm,
    coeffs_hbm,
    upward_hbm,
    ghost_hbm,
    plane_hbm,
    mean_hbm,
    out_hbm,
    avg_hbm,
    strips_ref,
    fields_ref,
    coeffs,
    upward,
    ghost_ref,
    plane_ref,
    mean_ref,
    avg_ref,
    first,
    second,
    share,
    drift,
    staged,
    sems,
    in_sems,
    table_sems,
    avg_sems,
    *,
    slots,
):
    tables = [
        pltpu.make_async_copy(source, target, table_sems.at[order])
        for order, (source, target) in enumerate(
            (
                (strips_hbm, strips_ref),
                (plane_hbm, plane_ref),
                (ghost_hbm, ghost_ref),
                (mean_hbm, mean_ref),
            )
        )
    ]
    start_all(tables)

    def loads(slot):
        return [
            pltpu.make_async_copy(
                source.at[aligned(slot * size, size)],
                target.at[aligned(slot * size, size)],
                in_sems.at[order, slot],
            )
            for order, (source, target, size) in enumerate(
                (
                    (fields_hbm, fields_ref, FIELD_ROWS),
                    (coeffs_hbm, coeffs, COEFF_ROWS),
                    (upward_hbm, upward, UPWARD_ROWS),
                )
            )
        ]

    for slot in range(slots):
        start_all(loads(slot))
    sources = strips_ref.shape[0]
    clear_pads(first)
    clear_pads(second)
    for copy in tables:
        copy.wait()

    gathered = strips_ref[0]
    for source in range(1, sources):
        gathered = gathered + strips_ref[source]
    half = STRIP_ROWS // 2
    gathered = jnp.concatenate(
        [gathered[:half], (gathered[half:] - gathered[:half]) * (1.0 / RATIO)], axis=0
    )
    quarter = AVG_ROWS // FACES
    group_of = lane_ids((quarter, LANES)) // BLK

    def send_out(slot):
        return pltpu.make_async_copy(staged.at[slot], out_hbm.at[slot], sems.at[slot])

    def one_patch(slot, carry):
        for copy in loads(slot):
            copy.wait()
        turned = pltpu.roll(gathered, (LANES - slot * BLK) % LANES, 1)
        stretched = jnp.dot(
            plane_ref[...],
            jnp.concatenate(split_pair(turned), axis=1),
            preferred_element_type=jnp.float32,
        ).astype(jnp.bfloat16)
        base = slot * FIELD_ROWS
        scales = slot * COEFF_ROWS
        for tile in range(TILES):
            ghosts = jnp.dot(
                stretched,
                ghost_ref[:, tile * LANES : (tile + 1) * LANES],
                preferred_element_type=jnp.float32,
            )
            scale = coeffs[aligned(scales + (8 * TILES + tile) * FZ, FZ), :]
            for field in range(SPECIES):
                row = (field * TILES + tile) * FZ
                old = scale * ghosts[field * FZ : (field + 1) * FZ]
                step = scale * ghosts[(SPECIES + field) * FZ : (SPECIES + field + 1) * FZ]
                drift[row : row + FZ, :] = step
                share[row : row + FZ, :] = old + step
                row = padded_at(field * TILES + tile, 0)
                second[row : row + FZ, :] = (
                    fields_ref[aligned(base + row, FZ), :] + DIFFUSE[field] * old
                )

        for step in range(1, RATIO):
            source, target = (second, first) if step % 2 else (first, second)
            for ztile in range(ZTILES):

                def ghosts(field, tile):
                    spot = pl.ds((field * TILES + tile) * FZ + 8 * ztile, 8)
                    value = share[spot, :]
                    if step + 1 < RATIO:
                        share[spot, :] = value + drift[spot, :]
                    return value

                advance(source, target, coeffs, upward, slot, 0, 0, ztile, ghosts)

        for tile in range(TILES):
            for field in range(SPECIES):
                row = padded_at(field * TILES + tile, 0)
                staged[slot, field, :, pl.ds(tile * LANES, LANES)] = first[row : row + FZ, :]
        send_out(slot).start()

        sums = []
        for field in range(SPECIES):
            for plane in range(NZC):
                start = field * TILES * STRIDE + PAD + RATIO * plane
                part = first[pl.ds(start, TILES, stride=STRIDE), :]
                for z in range(1, RATIO):
                    part = part + first[pl.ds(start + z, TILES, stride=STRIDE), :]
                sums.append(part)
        means = jnp.dot(
            jnp.concatenate(split_pair(jnp.concatenate(sums, axis=0)), axis=1),
            mean_ref[...],
            preferred_element_type=jnp.float32,
        )
        chunk = avg_ref[...]
        for part in range(FACES):
            chunk = jnp.where(
                group_of == part * slots + slot,
                means[part * quarter : (part + 1) * quarter],
                chunk,
            )
        avg_ref[...] = chunk
        return carry

    avg_ref[...] = jnp.zeros((quarter, LANES), jnp.float32)
    lax.fori_loop(0, slots, one_patch, 0)
    copies = [
        pltpu.make_async_copy(avg_ref, avg_hbm.at[target], avg_sems.at[target])
        for target in range(sources)
    ]
    start_all(copies)
    for copy in copies:
        copy.wait()
    for slot in range(slots):
        send_out(slot).wait()


def place_kernel(
    place_ref,
    avg_ref,
    new_hbm,
    ylo_ref,
    yhi_ref,
    yl_ref,
    yr_ref,
    out_ref,
    new_ref,
    sem,
    *,
    cells_x,
    cells_y,
    group,
    slots,
):
    fetch = pltpu.make_async_copy(new_hbm, new_ref, sem)
    fetch.start()

    def edge_share(own_ref, other_ref):
        own = own_ref[...]
        other = other_ref[...]
        coeff = face(DT_COARSE, jnp.maximum(own, 0.125), other)
        lane = lane_ids(own.shape)
        spread = jnp.zeros_like(own)
        for field in range(SPECIES):
            moved = roll_lanes(coeff, (field - SPECIES) * NZC)
            spread = jnp.where(lane // NZC == field, DIFFUSE[field] * moved, spread)
        return spread * (other - own)

    lower = edge_share(ylo_ref, yl_ref)
    upper = edge_share(yhi_ref, yr_ref)

    width = slots * BLK
    quarter = AVG_ROWS // FACES
    per_tile = LANES // width
    part = lane_ids((quarter, LANES)) // width
    columns = []
    for tile in range(group * BLK // LANES):
        rows = []
        for index in range(FACES):
            merged = jnp.zeros((quarter, LANES), jnp.float32)
            for place in range(per_tile):
                piece = roll_lanes(avg_ref[tile * per_tile + place], (place - index) * width)
                merged = jnp.where(part == place, piece, merged)
            rows.append(merged)
        columns.append(jnp.concatenate(rows, axis=0))
    high, low = split_pair(jnp.concatenate(columns, axis=1))
    ones = jnp.ones((16, high.shape[1]), jnp.bfloat16)
    stacked = jnp.concatenate([high, low, ones], axis=0)

    fetch.wait()
    lane = lane_ids((BLK, LANES))
    halves = cells_y // LANES
    for column in range(cells_x // BLK):
        placed = lax.dot_general(
            stacked,
            selector(place_ref, column, cells_y),
            (((1,), (1,)), ((), ())),
            preferred_element_type=jnp.float32,
        )
        covered = placed[2 * AVG_ROWS : 2 * AVG_ROWS + 8] > 0.5
        for plane in range(PLANES):
            values = (
                placed[plane * BLK : (plane + 1) * BLK]
                + placed[AVG_ROWS + plane * BLK : AVG_ROWS + (plane + 1) * BLK]
            )
            row = plane * cells_x + column * BLK
            edge_rows = slice(column * BLK, (column + 1) * BLK)
            for half in range(halves):
                cols = slice(half * LANES, (half + 1) * LANES)
                coarse = new_ref[row : row + BLK, cols]
                if half == 0:
                    share = roll_lanes(lower[edge_rows], -plane)
                    coarse = coarse + jnp.where(lane == 0, share, 0.0)
                if half == halves - 1:
                    share = roll_lanes(upper[edge_rows], LANES - 1 - plane)
                    coarse = coarse + jnp.where(lane == LANES - 1, share, 0.0)
                out_ref[row : row + BLK, cols] = jnp.where(
                    covered[:, cols], values[:, cols], coarse
                )


VMEM = pl.BlockSpec(memory_space=pltpu.VMEM)
HBM = pl.BlockSpec(memory_space=pltpu.HBM)
PARAMS = pltpu.CompilerParams(vmem_limit_bytes=40 * 1024 * 1024)


def f32(*shape):
    return jax.ShapeDtypeStruct(shape, jnp.float32)


def hbm32(*shape):
    return pltpu.HBM(shape, jnp.float32)


def pinned(*arrays):
    return [pltpu.with_memory_space_constraint(array, pltpu.HBM) for array in arrays]


def shifted(values, axis, step):
    count = lax.axis_size(axis)
    pairs = [(i, i + step) for i in range(count) if 0 <= i + step < count]
    return lax.ppermute(values, axis, pairs)


def exchange(chunks):
    return lax.all_to_all(chunks, "af", split_axis=0, concat_axis=0, tiled=True)


def per_device(
    coarse_state, coarse_kappa, coarse_rate, fine_state, fine_kappa, fine_rate, boxes, cover
):
    af_count = lax.axis_size("af")
    slots = fine_state.shape[0]
    cells_x, cells_y = coarse_state.shape[2:]
    group = af_count * slots
    lanes = group * BLK
    halves = cells_y // LANES
    rows = PLANES * cells_x
    plain = NZC * cells_x
    sizes = dict(cells_x=cells_x, cells_y=cells_y, group=group)

    state, kappa, rate, place, xlo, xhi, ylo, yhi = pl.pallas_call(
        functools.partial(load_kernel, **sizes),
        out_shape=[f32(rows, cells_y), f32(plain, cells_y), f32(plain, cells_y)]
        + [jax.ShapeDtypeStruct((16, lanes), jnp.int32)]
        + [f32(PLANES + NZC, cells_y)] * 2
        + [f32(cells_x, LANES)] * 2,
        in_specs=[HBM] * 4,
        out_specs=[VMEM] * 8,
        scratch_shapes=[
            pltpu.VMEM((2, boxes.shape[0]), jnp.int32),
            pltpu.SemaphoreType.DMA((4,)),
        ],
        compiler_params=PARAMS,
        name="load",
    )(
        *pinned(
            boxes.T,
            coarse_state.reshape(rows, cells_y),
            coarse_kappa.reshape(plain, cells_y),
            coarse_rate.reshape(plain, cells_y),
        )
    )
    xl = shifted(xhi, "af", 1)
    xr = shifted(xlo, "af", -1)
    yl = shifted(yhi, "col", 1)
    yr = shifted(ylo, "col", -1)

    span = cells_x + 2 * PAD
    new, send = pl.pallas_call(
        functools.partial(coarse_kernel, slots=slots, **sizes),
        out_shape=[hbm32(rows, cells_y), f32(af_count, STRIP_ROWS, LANES)],
        in_specs=[VMEM] * 8,
        out_specs=[HBM, VMEM],
        scratch_shapes=[
            pltpu.VMEM((rows, cells_y), jnp.float32),
            pltpu.VMEM(((SPECIES + 1) * halves * NZC * span, LANES), jnp.float32),
            pltpu.VMEM((rows * halves, LANES), jnp.float32),
            pltpu.SemaphoreType.DMA,
        ],
        compiler_params=PARAMS,
        name="coarse",
    )(place, state, kappa, rate, xl, xr, yl, yr)

    strips = exchange(send)

    kept = [hbm32(slots * size, LANES) for size in (FIELD_ROWS, COEFF_ROWS, UPWARD_ROWS)]
    kept_scratch = [pltpu.VMEM((slots * size, LANES), jnp.float32)
        for size in (FIELD_ROWS, COEFF_ROWS, UPWARD_ROWS)]
    fields, coeffs, upward = pl.pallas_call(
        functools.partial(prepare_kernel, slots=slots),
        out_shape=kept,
        in_specs=[HBM] * 4,
        out_specs=[HBM] * 3,
        scratch_shapes=kept_scratch
        + [
            pltpu.VMEM(fine_state.shape, jnp.float32),
            pltpu.VMEM(fine_kappa.shape, jnp.float32),
            pltpu.VMEM(fine_rate.shape, jnp.float32),
            pltpu.VMEM((FIELD_ROWS, LANES), jnp.float32),
            pltpu.VMEM((UPWARD_ROWS, LANES), jnp.float32),
            pltpu.SemaphoreType.DMA((3, slots)),
            pltpu.SemaphoreType.DMA((3, slots)),
        ],
        compiler_params=PARAMS,
        name="prepare",
    )(*pinned(new, fine_state, fine_kappa, fine_rate))

    tables = [jnp.asarray(table) for table in (ghost_table(), plane_table(), mean_table())]
    chunk = (AVG_ROWS // FACES, LANES)
    fine_out, averages = pl.pallas_call(
        functools.partial(finish_kernel, slots=slots),
        out_shape=[hbm32(*fine_state.shape), hbm32(af_count, *chunk)],
        in_specs=[HBM] * 7,
        out_specs=[HBM, HBM],
        scratch_shapes=[pltpu.VMEM(strips.shape, jnp.float32)]
        + kept_scratch
        + [pltpu.VMEM(table.shape, jnp.bfloat16) for table in tables]
        + [
            pltpu.VMEM(chunk, jnp.float32),
            pltpu.VMEM((FIELD_ROWS, LANES), jnp.float32),
            pltpu.VMEM((FIELD_ROWS, LANES), jnp.float32),
            pltpu.VMEM((SPECIES * TILES * FZ, LANES), jnp.float32),
            pltpu.VMEM((SPECIES * TILES * FZ, LANES), jnp.float32),
            pltpu.VMEM(fine_state.shape, jnp.float32),
            pltpu.SemaphoreType.DMA((slots,)),
            pltpu.SemaphoreType.DMA((3, slots)),
            pltpu.SemaphoreType.DMA((4,)),
            pltpu.SemaphoreType.DMA((af_count,)),
        ],
        compiler_params=PARAMS,
        name="finish",
    )(*pinned(strips, fields, coeffs, upward, *tables))

    arrived = exchange(averages)

    placed = pl.pallas_call(
        functools.partial(place_kernel, slots=slots, **sizes),
        out_shape=f32(rows, cells_y),
        in_specs=[VMEM] * 2 + [HBM] + [VMEM] * 4,
        out_specs=VMEM,
        scratch_shapes=[pltpu.VMEM((rows, cells_y), jnp.float32), pltpu.SemaphoreType.DMA],
        compiler_params=PARAMS,
        name="place",
    )(place, arrived, *pinned(new), ylo, yhi, yl, yr)
    return (placed.reshape(coarse_state.shape), fine_out)


def solution(mesh):
    return jax.shard_map(
        per_device,
        mesh=mesh,
        in_specs=(
            P(None, None, "af", "col"),
            P(None, "af", "col"),
            P(None, "af", "col"),
            P(("col", "af"), None, None, None),
            P(("col", "af"), None, None),
            P(("col", "af"), None, None),
            P(),
            P(),
        ),
        out_specs=(P(None, None, "af", "col"), P(("col", "af"), None, None, None)),
        check_vma=False,
    )
```

```python
import functools

import jax
import jax.numpy as jnp
from jax import lax
from jax.experimental import pallas as pl
from jax.experimental.pallas import tpu as pltpu
from jax.sharding import PartitionSpec as P

NZC = 8
RATIO = 4
BLK = 8
SPECIES = 3
EDGE = BLK * RATIO
FZ = NZC * RATIO
LANES = 128
TILES = EDGE * EDGE // LANES
ZTILES = FZ // 8
STRIDE = 48
PAD = 8
FACES = 4
PLANES = SPECIES * NZC
STRIP_ROWS = 2 * PLANES
AVG_ROWS = PLANES * BLK
KINDS = 9
FIELD_ROWS = SPECIES * TILES * STRIDE
COEFF_ROWS = KINDS * TILES * FZ
UPWARD_ROWS = TILES * STRIDE
EDGE_ROWS = PLANES + NZC
HALO_START = STRIP_ROWS + EDGE_ROWS

DT_COARSE = 1.0 / 28.0
DIFFUSE = (1.0, 0.7, 0.45)
SIGNS = (-1.0, -1.0, 1.0)
FINE_SCALE = RATIO * RATIO * DT_COARSE / RATIO
DT_FINE = DT_COARSE / RATIO


def lane_ids(shape):
    return lax.broadcasted_iota(jnp.int32, shape, len(shape) - 1)


def roll_lanes(values, shift):
    width = values.shape[-1]
    shift = shift % width
    return values if shift == 0 else pltpu.roll(values, shift, values.ndim - 1)


def split_pair(values):
    high = values.astype(jnp.bfloat16)
    low = (values - high.astype(jnp.float32)).astype(jnp.bfloat16)
    return high, low


def face(scale, one, other):
    summed = one + other
    inverse = pl.reciprocal(summed, approx=True)
    inverse = inverse * (2.0 - summed * inverse)
    return (2.0 * scale) * (one * other) * inverse


def start_all(copies):
    for copy in copies:
        copy.start()


def selector(place_ref, column, cells_y):
    wanted = jnp.where(place_ref[0:8, :] == column, place_ref[8:16, :], -1)
    row = lax.broadcasted_iota(jnp.int32, wanted.shape, 0)
    return jnp.concatenate(
        [jnp.where(row + 8 * at == wanted, 1.0, 0.0) for at in range(cells_y // 8)], axis=0
    ).astype(jnp.bfloat16)


def strips_kernel(
    boxes_hbm,
    state_hbm,
    kappa_hbm,
    rate_hbm,
    new_hbm,
    send_ref,
    place_ref,
    xlo_ref,
    xhi_ref,
    ylo_ref,
    yhi_ref,
    boxes_ref,
    state_ref,
    kappa_ref,
    rate_ref,
    new_ref,
    padded,
    fresh,
    sems,
    *,
    cells_x,
    cells_y,
    group,
    slots,
):
    pairs = (
        (boxes_hbm, boxes_ref),
        (kappa_hbm, kappa_ref),
        (state_hbm, state_ref),
        (rate_hbm, rate_ref),
    )
    copies = [
        pltpu.make_async_copy(source, target, sems.at[index])
        for index, (source, target) in enumerate(pairs)
    ]
    start_all(copies)

    patches = boxes_ref.shape[1]
    lanes = group * BLK
    base_patch = lax.axis_index("col") * group
    member = lax.broadcasted_iota(jnp.int32, (patches, lanes), 0) - base_patch
    spread = jnp.where(member == lane_ids((patches, lanes)) // BLK, 1.0, 0.0).astype(jnp.bfloat16)
    first_col = lax.axis_index("af") * (cells_x // BLK)
    first_cell = lax.axis_index("col") * cells_y
    copies[0].wait()
    boxes = boxes_ref[...].astype(jnp.float32)
    stacked = jnp.concatenate(
        [jnp.broadcast_to(boxes[row : row + 1], (8, patches)) for row in range(2)], axis=0
    )
    found = jnp.dot(
        stacked.astype(jnp.bfloat16), spread, preferred_element_type=jnp.float32
    ).astype(jnp.int32)
    place_ref[0:8, :] = found[0:8] - first_col
    place_ref[8:16, :] = found[8:16] * BLK - first_cell + lane_ids((8, lanes)) % BLK

    halves = cells_y // LANES
    span = cells_x + 2 * PAD
    nothing = jnp.zeros((PAD, LANES), jnp.float32)

    def base(field, half, z):
        return ((field * halves + half) * NZC + z) * span

    for copy in copies[1:]:
        copy.wait()
    for field in range(SPECIES + 1):
        for half in range(halves):
            cols = pl.ds(half * LANES, LANES)
            for z in range(NZC):
                if field < SPECIES:
                    start = (field * NZC + z) * cells_x
                    plane = state_ref[start : start + cells_x, cols]
                else:
                    plane = kappa_ref[z * cells_x : (z + 1) * cells_x, cols]
                at = base(field, half, z)
                padded[at : at + PAD, :] = nothing
                padded[at + PAD : at + PAD + cells_x, :] = plane
                padded[at + PAD + cells_x : at + span, :] = nothing

    lane = lane_ids((cells_x, LANES))
    row_id = lax.broadcasted_iota(jnp.int32, (cells_x, LANES), 0)

    low = jnp.zeros((cells_x, LANES), jnp.float32)
    high = jnp.zeros((cells_x, LANES), jnp.float32)
    for plane in range(PLANES + NZC):
        field, z = divmod(plane, NZC)
        at = base(field, 0, z) + PAD
        first = padded[at : at + cells_x, :]
        at = base(field, halves - 1, z) + PAD
        last = padded[at : at + cells_x, :]
        low = jnp.where(lane == plane, roll_lanes(first, plane), low)
        high = jnp.where(lane == plane, roll_lanes(last, plane + 1), high)
    ylo_ref[...] = low
    yhi_ref[...] = high

    def load(field, half, z, shift):
        at = base(field, half, z) + PAD + shift
        return padded[at : at + cells_x, :]

    def neighbours(field, half, z):
        here = load(field, half, z, 0)
        after = roll_lanes(here, -1)
        if half + 1 < halves:
            after = jnp.where(
                lane == LANES - 1, roll_lanes(load(field, half + 1, z, 0), -1), after
            )
        before = roll_lanes(here, 1)
        if half > 0:
            before = jnp.where(lane == 0, roll_lanes(load(field, half - 1, z, 0), 1), before)
        found = [after, before, load(field, half, z, 1), load(field, half, z, -1)]
        if z + 1 < NZC:
            found.append(load(field, half, z + 1, 0))
        if z > 0:
            found.append(load(field, half, z - 1, 0))
        return found

    for z in range(NZC):
        for half in range(halves):
            cols = pl.ds(half * LANES, LANES)
            conduct = load(SPECIES, half, z, 0)
            coeffs = [face(DT_COARSE, conduct, other) for other in neighbours(SPECIES, half, z)]
            if half == halves - 1:
                coeffs[0] = jnp.where(lane == LANES - 1, 0.0, coeffs[0])
            if half == 0:
                coeffs[1] = jnp.where(lane == 0, 0.0, coeffs[1])
            coeffs[2] = jnp.where(row_id == cells_x - 1, 0.0, coeffs[2])
            coeffs[3] = jnp.where(row_id == 0, 0.0, coeffs[3])
            centers = [load(field, half, z, 0) for field in range(SPECIES)]
            forward = (DT_COARSE * rate_ref[z * cells_x : (z + 1) * cells_x, cols]) * (
                centers[0] * centers[1] - centers[2]
            )
            for field in range(SPECIES):
                center = centers[field]
                flux = None
                for coeff, other in zip(coeffs, neighbours(field, half, z)):
                    term = coeff * (other - center)
                    flux = term if flux is None else flux + term
                start = (field * NZC + z) * cells_x
                result = center + DIFFUSE[field] * flux + SIGNS[field] * forward
                new_ref[start : start + cells_x, cols] = result
                start = ((field * halves + half) * NZC + z) * cells_x
                fresh[start : start + cells_x, :] = result

    keep_new = pltpu.make_async_copy(new_ref, new_hbm, sems.at[0])
    keep_new.start()

    def old_row(field, half, row):
        return padded[pl.ds(base(field, half, 0) + PAD + row, NZC, stride=span), :]

    def edge_at(row):
        return jnp.concatenate(
            [
                jnp.concatenate([old_row(field, half, row) for field in range(SPECIES + 1)], axis=0)
                for half in range(halves)
            ],
            axis=1,
        )

    def rows_at(row):
        columns = []
        for half in range(halves):
            pieces = [old_row(field, half, row) for field in range(SPECIES)]
            for field in range(SPECIES):
                start = (field * halves + half) * NZC * cells_x
                pieces.append(fresh[pl.ds(start + row, NZC, stride=cells_x), :])
            columns.append(jnp.concatenate(pieces, axis=0))
        return jnp.concatenate(columns, axis=1)

    block_cols = cells_x // BLK
    spot = lane_ids((STRIP_ROWS, cells_y)) % BLK
    lower_y = []
    upper_y = []
    for column in range(block_cols):
        below = jnp.zeros((STRIP_ROWS, cells_y), jnp.float32)
        above = jnp.zeros((STRIP_ROWS, cells_y), jnp.float32)
        for x in range(BLK):
            strip = rows_at(column * BLK + x)
            below = jnp.where(spot == x, roll_lanes(strip, x + 1), below)
            above = jnp.where(spot == x, roll_lanes(strip, x - BLK), above)
        lower_y.append(below)
        upper_y.append(above)

    first_row = edge_at(0)
    last_row = edge_at(cells_x - 1)
    xlo_ref[...] = first_row
    xhi_ref[...] = last_row
    place = lane_ids((EDGE_ROWS, cells_y)) % BLK

    def corners(row, at):
        below = jnp.where(place == at, roll_lanes(row, at + 1), 0.0)
        return jnp.where(place == at + 1, roll_lanes(row, at + 1 - BLK), below)

    extra_members = {
        -1: [(1, first_row), (2, corners(first_row, 2))],
        0: [(0, first_row), (2, corners(first_row, 0))],
        block_cols - 1: [
            (0, last_row),
            (2, corners(last_row, 0)),
            (3, jnp.ones((EDGE_ROWS, cells_y), jnp.float32)),
        ],
        block_cols: [(1, last_row), (2, corners(last_row, 2))],
    }

    faces = [None] * (2 * FACES)

    def add(index, part):
        faces[index] = part if faces[index] is None else faces[index] + part

    for column in range(-1, block_cols + 1):
        members = []
        if column >= 1:
            members.append((0, rows_at(column * BLK - 1)))
        if column < block_cols - 1:
            members.append((1, rows_at(column * BLK + BLK)))
        if 0 <= column < block_cols:
            members.append((2, lower_y[column]))
            members.append((3, upper_y[column]))
        for index, rows in extra_members.get(column, []):
            members.append((FACES + index, rows))
        operands = []
        for _, rows in members:
            operands.extend(split_pair(rows))
        moved = jnp.dot(
            jnp.concatenate(operands, axis=0),
            selector(place_ref, column, cells_y),
            preferred_element_type=jnp.float32,
        )
        at = 0
        for index, rows in members:
            size = rows.shape[0]
            add(index, moved[at : at + size] + moved[at + size : at + 2 * size])
            at += 2 * size

    width = slots * BLK
    me = lax.axis_index("af")
    for target in range(group // slots):
        first = target * width
        tile = first // LANES * LANES
        for start, size, kind in ((0, STRIP_ROWS, 0), (STRIP_ROWS, EDGE_ROWS, FACES)):
            part = lane_ids((size, LANES)) // width
            chunk = jnp.zeros((size, LANES), jnp.float32)
            for index in range(FACES):
                piece = faces[kind + index][:, tile : tile + LANES]
                chunk = jnp.where(
                    part == index, roll_lanes(piece, index * width - (first - tile)), chunk
                )
            send_ref[target, start : start + size, :] = chunk
        halo = jnp.where(me < target, last_row, first_row)
        for half in range(halves):
            start = HALO_START + half * EDGE_ROWS
            send_ref[target, start : start + EDGE_ROWS, :] = halo[
                :, half * LANES : (half + 1) * LANES
            ]
    keep_new.wait()


def ghost_table(tile):
    lane = lane_ids((BLK, LANES))
    pos = lax.broadcasted_iota(jnp.int32, (BLK, LANES), 0)
    x = tile * (LANES // EDGE) + lane // EDGE
    y = lane % EDGE
    along_y = y // RATIO == pos
    along_x = x // RATIO == pos
    seen = (
        (x == 0) & along_y,
        (x == EDGE - 1) & along_y,
        (y == 0) & along_x,
        (y == EDGE - 1) & along_x,
    )
    nothing = jnp.zeros((LANES // FACES - BLK, LANES), jnp.float32)
    rows = []
    for where in seen:
        rows.extend([jnp.where(where, 1.0, 0.0), nothing])
    return jnp.concatenate(rows + rows, axis=0).astype(jnp.bfloat16)


def plane_table():
    shape = (2 * SPECIES * FZ, STRIP_ROWS)
    rows = lax.broadcasted_iota(jnp.int32, shape, 0)
    return jnp.where(rows // RATIO == lane_ids(shape), 1.0, 0.0).astype(jnp.bfloat16)


def mean_table():
    shape = (2 * LANES, LANES)
    rows = lax.broadcasted_iota(jnp.int32, shape, 0)
    same = rows % EDGE // RATIO == lane_ids(shape) % BLK
    return jnp.where(same, 1.0 / RATIO**3, 0.0).astype(jnp.bfloat16)


def complete_strips(gathered):
    width = LANES // FACES
    beside = [
        gathered[STRIP_ROWS + field * NZC : STRIP_ROWS + (field + 1) * NZC]
        for field in range(SPECIES + 1)
    ]
    lane = lane_ids((NZC, LANES))
    part = lane // width
    pos = lane % BLK
    flag = jnp.where(part == FACES - 1, beside[0], 0.0)
    flag = flag + roll_lanes(flag, width)
    upper = flag + roll_lanes(flag, 2 * width) > 0.5
    conduct = jnp.maximum(beside[SPECIES], 0.125)
    block = face(DT_COARSE, conduct, roll_lanes(conduct, -width))
    corner = face(DT_COARSE, conduct, roll_lanes(conduct, -2))
    nothing = jnp.zeros((NZC, LANES), jnp.float32)
    added = []
    for field in range(SPECIES):
        values = beside[field]
        across = DIFFUSE[field] * block * (values - roll_lanes(values, -width))
        along = DIFFUSE[field] * corner * (roll_lanes(values, -2) - values)
        share = jnp.where((part == 0) & ~upper, across, nothing)
        share = jnp.where((part == 1) & upper, roll_lanes(across, width), share)
        for index in range(2):
            home = 2 + index
            for at, chosen in ((0, ~upper), (BLK - 1, upper)):
                moved = roll_lanes(along, index * width + at - index)
                share = jnp.where((part == home) & (pos == at) & chosen, moved, share)
        added.append(share)
    new = gathered[PLANES:STRIP_ROWS] + jnp.concatenate(added, axis=0)
    return gathered[:PLANES], new


def aligned(start, size):
    return pl.ds(pl.multiple_of(start, 8), size)


def padded_at(block, ztile):
    return block * STRIDE + PAD + 8 * ztile


def advance(source, target, coeffs, upward, slot, from_rows, to_rows, ztile, ghosts):
    lane = lane_ids((8, LANES))

    def value(field, tile, shift):
        return source[pl.ds(from_rows + padded_at(field * TILES + tile, ztile) + shift, 8), :]

    def get(kind, tile):
        return coeffs[
            aligned(slot * COEFF_ROWS + (kind * TILES + tile) * FZ + 8 * ztile, 8), :
        ]

    centers = [value(field, 0, 0) for field in range(SPECIES)]
    down = [roll_lanes(center, -EDGE) for center in centers]
    up = [roll_lanes(center, EDGE) for center in centers]
    up_before = list(up)
    for tile in range(TILES):
        if tile + 1 < TILES:
            centers_after = [value(field, tile + 1, 0) for field in range(SPECIES)]
            down_after = [roll_lanes(center, -EDGE) for center in centers_after]
        next_x, prev_x, next_y, prev_y, rate = [get(kind, tile) for kind in range(5)]
        base = slot * UPWARD_ROWS + padded_at(tile, ztile)
        next_z = upward[pl.ds(base, 8), :]
        prev_z = upward[pl.ds(base - 1, 8), :]
        forward = rate * (centers[0] * centers[1] - centers[2])
        for field in range(SPECIES):
            center = centers[field]
            ahead, behind = down[field], up[field]
            if tile + 1 < TILES:
                ahead = jnp.where(lane < LANES - EDGE, ahead, down_after[field])
            if tile > 0:
                behind = jnp.where(lane >= EDGE, behind, up_before[field])
            flux = (next_x * ahead + prev_x * behind) + (
                next_y * roll_lanes(center, -1) + prev_y * roll_lanes(center, 1)
            )
            flux = flux + (next_z * value(field, tile, 1) + prev_z * value(field, tile, -1))
            share = ghosts(field, tile)
            if share is not None:
                flux = flux + share
            if DIFFUSE[field] != 1.0:
                flux = DIFFUSE[field] * flux
            result = get(5 + field, tile) * center + flux
            result = result - forward if SIGNS[field] < 0 else result + forward
            target[aligned(to_rows + padded_at(field * TILES + tile, ztile), 8), :] = result
        if tile + 1 < TILES:
            up_before = up
            centers, down = centers_after, down_after
            up = [roll_lanes(center, EDGE) for center in centers]


def clear_pads(ref):
    edge = jnp.zeros((PAD, LANES), jnp.float32)

    def body(block, carry):
        ref[aligned(block * STRIDE, PAD), :] = edge
        ref[aligned(block * STRIDE + PAD + FZ, PAD), :] = edge
        return carry

    lax.fori_loop(0, ref.shape[0] // STRIDE, body, 0)


def prepare_kernel(
    after_ref,
    state_hbm,
    kappa_hbm,
    rate_hbm,
    ylo_ref,
    yhi_ref,
    fields_hbm,
    coeffs_hbm,
    upward_hbm,
    ylo_out,
    yhi_out,
    fields_ref,
    coeffs,
    upward,
    state_ref,
    kappa_ref,
    rate_ref,
    first,
    conduct,
    sems,
    out_sems,
    *,
    slots,
):
    def loads(slot):
        return [
            pltpu.make_async_copy(source.at[slot], target.at[slot], sems.at[order, slot])
            for order, (source, target) in enumerate(
                ((kappa_hbm, kappa_ref), (rate_hbm, rate_ref), (state_hbm, state_ref))
            )
        ]

    for slot in range(slots):
        start_all(loads(slot))
    ylo_out[...] = ylo_ref[...]
    yhi_out[...] = yhi_ref[...]

    def stores(slot):
        return [
            pltpu.make_async_copy(
                source.at[aligned(slot * size, size)],
                target.at[aligned(slot * size, size)],
                out_sems.at[order, slot],
            )
            for order, (source, target, size) in enumerate(
                (
                    (fields_ref, fields_hbm, FIELD_ROWS),
                    (coeffs, coeffs_hbm, COEFF_ROWS),
                    (upward, upward_hbm, UPWARD_ROWS),
                )
            )
        ]

    for ref in (fields_ref, upward, first, conduct):
        clear_pads(ref)

    lane = lane_ids((8, LANES))
    column = lane % EDGE
    side_y = jnp.where((column == 0) | (column == EDGE - 1), 1.0, 0.0)

    def one_patch(slot, carry):
        for copy in loads(slot):
            copy.wait()

        for tile in range(TILES):
            cols = pl.ds(tile * LANES, LANES)
            for field in range(SPECIES):
                row = padded_at(field * TILES + tile, 0)
                first[row : row + FZ, :] = state_ref[slot, field, :, cols]
            row = padded_at(tile, 0)
            conduct[row : row + FZ, :] = kappa_ref[slot, :, cols]

        def keep(kind, tile, ztile, values):
            coeffs[
                aligned(slot * COEFF_ROWS + (kind * TILES + tile) * FZ + 8 * ztile, 8), :
            ] = values

        for ztile in range(ZTILES):

            def here(tile, shift):
                return conduct[pl.ds(padded_at(tile, ztile) + shift, 8), :]

            center = here(0, 0)
            turned = roll_lanes(center, -EDGE)
            back_before = None
            for tile in range(TILES):
                other = turned
                if tile + 1 < TILES:
                    center_after = here(tile + 1, 0)
                    turned_after = roll_lanes(center_after, -EDGE)
                    other = jnp.where(lane < LANES - EDGE, turned, turned_after)
                next_x = face(FINE_SCALE, center, other)
                if tile == TILES - 1:
                    next_x = jnp.where(lane < LANES - EDGE, next_x, 0.0)
                back = roll_lanes(next_x, EDGE)
                prev_x = jnp.where(lane >= EDGE, back, 0.0 if tile == 0 else back_before)
                next_y = jnp.where(
                    column < EDGE - 1, face(FINE_SCALE, center, roll_lanes(center, -1)), 0.0
                )
                prev_y = roll_lanes(next_y, 1)
                next_z = face(FINE_SCALE, center, here(tile, 1))
                prev_z = face(FINE_SCALE, center, here(tile, -1))
                sides = side_y
                if tile == 0:
                    sides = sides + jnp.where(lane < EDGE, 1.0, 0.0)
                if tile == TILES - 1:
                    sides = sides + jnp.where(lane >= LANES - EDGE, 1.0, 0.0)
                scale = FINE_SCALE * center
                total = (next_x + prev_x) + (next_y + prev_y) + (next_z + prev_z) + sides * scale
                upward[aligned(slot * UPWARD_ROWS + padded_at(tile, ztile), 8), :] = next_z
                keep(0, tile, ztile, next_x)
                keep(1, tile, ztile, prev_x)
                keep(2, tile, ztile, next_y)
                keep(3, tile, ztile, prev_y)
                rate = rate_ref[slot, pl.ds(8 * ztile, 8), pl.ds(tile * LANES, LANES)]
                keep(4, tile, ztile, DT_FINE * rate)
                for field in range(SPECIES):
                    keep(5 + field, tile, ztile, 1.0 - DIFFUSE[field] * total)
                keep(8, tile, ztile, scale)
                back_before = back
                if tile + 1 < TILES:
                    center, turned = center_after, turned_after

        for ztile in range(ZTILES):
            advance(
                first,
                fields_ref,
                coeffs,
                upward,
                slot,
                0,
                slot * FIELD_ROWS,
                ztile,
                lambda field, tile: None,
            )
        start_all(stores(slot))
        return carry

    lax.fori_loop(0, slots, one_patch, 0)
    for slot in range(slots):
        for copy in stores(slot):
            copy.wait()


def finish_kernel(
    strips_hbm,
    fields_hbm,
    coeffs_hbm,
    upward_hbm,
    yl_ref,
    yr_ref,
    out_hbm,
    avg_hbm,
    strips_ref,
    fields_ref,
    coeffs,
    upward,
    ghost_ref,
    plane_ref,
    mean_ref,
    avg_ref,
    first,
    second,
    share,
    drift,
    staged,
    sems,
    in_sems,
    strips_sem,
    avg_sems,
    *,
    slots,
):
    arrive = pltpu.make_async_copy(strips_hbm.at[:, pl.ds(0, HALO_START)], strips_ref, strips_sem)
    arrive.start()

    def loads(slot):
        return [
            pltpu.make_async_copy(
                source.at[aligned(slot * size, size)],
                target.at[aligned(slot * size, size)],
                in_sems.at[order, slot],
            )
            for order, (source, target, size) in enumerate(
                (
                    (fields_hbm, fields_ref, FIELD_ROWS),
                    (coeffs_hbm, coeffs, COEFF_ROWS),
                    (upward_hbm, upward, UPWARD_ROWS),
                )
            )
        ]

    start_all(loads(0))
    sources = strips_ref.shape[0]
    clear_pads(first)
    clear_pads(second)
    for tile in range(TILES):
        ghost_ref[:, tile * LANES : (tile + 1) * LANES] = ghost_table(tile)
    plane_ref[...] = plane_table()
    mean_ref[...] = mean_table()
    arrive.wait()

    gathered = strips_ref[0]
    for source in range(1, sources):
        gathered = gathered + strips_ref[source]
    old, new = complete_strips(gathered)
    gathered = jnp.concatenate([old, (new - old) * (1.0 / RATIO)], axis=0)
    quarter = AVG_ROWS // FACES
    group_of = lane_ids((quarter, LANES)) // BLK

    def send_out(slot):
        return pltpu.make_async_copy(staged.at[slot], out_hbm.at[slot], sems.at[slot])

    def one_patch(slot, carry):
        for copy in loads(slot):
            copy.wait()

        @pl.when(slot + 1 < slots)
        def _():
            start_all(loads(slot + 1))

        turned = pltpu.roll(gathered, (LANES - slot * BLK) % LANES, 1)
        stretched = jnp.dot(
            plane_ref[...],
            jnp.concatenate(split_pair(turned), axis=1),
            preferred_element_type=jnp.float32,
        ).astype(jnp.bfloat16)
        base = slot * FIELD_ROWS
        scales = slot * COEFF_ROWS
        for tile in range(TILES):
            ghosts = jnp.dot(
                stretched,
                ghost_ref[:, tile * LANES : (tile + 1) * LANES],
                preferred_element_type=jnp.float32,
            )
            scale = coeffs[aligned(scales + (8 * TILES + tile) * FZ, FZ), :]
            for field in range(SPECIES):
                row = (field * TILES + tile) * FZ
                old = scale * ghosts[field * FZ : (field + 1) * FZ]
                step = scale * ghosts[(SPECIES + field) * FZ : (SPECIES + field + 1) * FZ]
                drift[row : row + FZ, :] = step
                share[row : row + FZ, :] = old + step
                row = padded_at(field * TILES + tile, 0)
                second[row : row + FZ, :] = (
                    fields_ref[aligned(base + row, FZ), :] + DIFFUSE[field] * old
                )

        for step in range(1, RATIO):
            source, target = (second, first) if step % 2 else (first, second)
            for ztile in range(ZTILES):

                def ghosts(field, tile):
                    spot = pl.ds((field * TILES + tile) * FZ + 8 * ztile, 8)
                    value = share[spot, :]
                    if step + 1 < RATIO:
                        share[spot, :] = value + drift[spot, :]
                    return value

                advance(source, target, coeffs, upward, slot, 0, 0, ztile, ghosts)

        for tile in range(TILES):
            for field in range(SPECIES):
                row = padded_at(field * TILES + tile, 0)
                staged[slot, field, :, pl.ds(tile * LANES, LANES)] = first[row : row + FZ, :]
        send_out(slot).start()

        sums = []
        for field in range(SPECIES):
            for plane in range(NZC):
                start = field * TILES * STRIDE + PAD + RATIO * plane
                part = first[pl.ds(start, TILES, stride=STRIDE), :]
                for z in range(1, RATIO):
                    part = part + first[pl.ds(start + z, TILES, stride=STRIDE), :]
                sums.append(part)
        means = jnp.dot(
            jnp.concatenate(split_pair(jnp.concatenate(sums, axis=0)), axis=1),
            mean_ref[...],
            preferred_element_type=jnp.float32,
        )
        chunk = avg_ref[...]
        for part in range(FACES):
            chunk = jnp.where(
                group_of == part * slots + slot,
                means[part * quarter : (part + 1) * quarter],
                chunk,
            )
        avg_ref[...] = chunk
        return carry

    avg_ref[...] = jnp.zeros((quarter, LANES), jnp.float32)
    lax.fori_loop(0, slots, one_patch, 0)
    copies = [
        pltpu.make_async_copy(avg_ref, avg_hbm.at[target], avg_sems.at[target])
        for target in range(sources)
    ]
    start_all(copies)
    for copy in copies:
        copy.wait()
    for slot in range(slots):
        send_out(slot).wait()


def place_kernel(
    place_ref,
    avg_ref,
    new_hbm,
    strips_hbm,
    xlo_ref,
    xhi_ref,
    ylo_ref,
    yhi_ref,
    yl_ref,
    yr_ref,
    out_ref,
    new_ref,
    halo_ref,
    sems,
    *,
    cells_x,
    cells_y,
    group,
    slots,
):
    me = lax.axis_index("af")
    last = strips_hbm.shape[0] - 1
    rows = pl.ds(HALO_START, halo_ref.shape[1])
    fetches = [
        pltpu.make_async_copy(
            strips_hbm.at[jnp.maximum(me - 1, 0), rows], halo_ref.at[0], sems.at[0]
        ),
        pltpu.make_async_copy(
            strips_hbm.at[jnp.minimum(me + 1, last), rows], halo_ref.at[1], sems.at[1]
        ),
        pltpu.make_async_copy(new_hbm, new_ref, sems.at[2]),
    ]
    start_all(fetches)

    def edge_share(own_ref, other_ref):
        own = own_ref[...]
        other = other_ref[...]
        coeff = face(DT_COARSE, jnp.maximum(own, 0.125), other)
        lane = lane_ids(own.shape)
        spread = jnp.zeros_like(own)
        for field in range(SPECIES):
            moved = roll_lanes(coeff, (field - SPECIES) * NZC)
            spread = jnp.where(lane // NZC == field, DIFFUSE[field] * moved, spread)
        return spread * (other - own)

    lower = edge_share(ylo_ref, yl_ref)
    upper = edge_share(yhi_ref, yr_ref)

    width = slots * BLK
    quarter = AVG_ROWS // FACES
    per_tile = LANES // width
    part = lane_ids((quarter, LANES)) // width
    columns = []
    for tile in range(group * BLK // LANES):
        rows = []
        for index in range(FACES):
            merged = jnp.zeros((quarter, LANES), jnp.float32)
            for place in range(per_tile):
                piece = roll_lanes(avg_ref[tile * per_tile + place], (place - index) * width)
                merged = jnp.where(part == place, piece, merged)
            rows.append(merged)
        columns.append(jnp.concatenate(rows, axis=0))
    high, low = split_pair(jnp.concatenate(columns, axis=1))
    ones = jnp.ones((16, high.shape[1]), jnp.bfloat16)
    stacked = jnp.concatenate([high, low, ones], axis=0)

    for copy in fetches:
        copy.wait()
    lane = lane_ids((BLK, LANES))
    row_id = lax.broadcasted_iota(jnp.int32, (BLK, LANES), 0)
    halves = cells_y // LANES

    def side_share(own_ref, side, exists):
        shares = []
        for half in range(halves):
            own = own_ref[:, half * LANES : (half + 1) * LANES]
            other = halo_ref[side, half * EDGE_ROWS : (half + 1) * EDGE_ROWS]
            coeff = face(DT_COARSE, own[PLANES:], other[PLANES:])
            coeff = jnp.where(exists, coeff, 0.0)
            shares.append(
                jnp.concatenate(
                    [
                        (DIFFUSE[field] * coeff)
                        * (
                            other[field * NZC : (field + 1) * NZC]
                            - own[field * NZC : (field + 1) * NZC]
                        )
                        for field in range(SPECIES)
                    ],
                    axis=0,
                )
            )
        return shares

    before = side_share(xlo_ref, 0, me > 0)
    after = side_share(xhi_ref, 1, me < last)
    block_cols = cells_x // BLK
    for column in range(block_cols):
        placed = lax.dot_general(
            stacked,
            selector(place_ref, column, cells_y),
            (((1,), (1,)), ((), ())),
            preferred_element_type=jnp.float32,
        )
        covered = placed[2 * AVG_ROWS : 2 * AVG_ROWS + 8] > 0.5
        for plane in range(PLANES):
            values = (
                placed[plane * BLK : (plane + 1) * BLK]
                + placed[AVG_ROWS + plane * BLK : AVG_ROWS + (plane + 1) * BLK]
            )
            row = plane * cells_x + column * BLK
            edge_rows = slice(column * BLK, (column + 1) * BLK)
            for half in range(halves):
                cols = slice(half * LANES, (half + 1) * LANES)
                coarse = new_ref[row : row + BLK, cols]
                if column == 0:
                    share = before[half][plane : plane + 1]
                    coarse = coarse + jnp.where(row_id == 0, share, 0.0)
                if column == block_cols - 1:
                    share = after[half][plane : plane + 1]
                    coarse = coarse + jnp.where(row_id == BLK - 1, share, 0.0)
                if half == 0:
                    share = roll_lanes(lower[edge_rows], -plane)
                    coarse = coarse + jnp.where(lane == 0, share, 0.0)
                if half == halves - 1:
                    share = roll_lanes(upper[edge_rows], LANES - 1 - plane)
                    coarse = coarse + jnp.where(lane == LANES - 1, share, 0.0)
                out_ref[row : row + BLK, cols] = jnp.where(
                    covered[:, cols], values[:, cols], coarse
                )


VMEM = pl.BlockSpec(memory_space=pltpu.VMEM)
HBM = pl.BlockSpec(memory_space=pltpu.HBM)
PARAMS = pltpu.CompilerParams(vmem_limit_bytes=40 * 1024 * 1024)


def f32(*shape):
    return jax.ShapeDtypeStruct(shape, jnp.float32)


def hbm32(*shape):
    return pltpu.HBM(shape, jnp.float32)


def pinned(*arrays):
    return [pltpu.with_memory_space_constraint(array, pltpu.HBM) for array in arrays]


def shifted(values, axis, step):
    count = lax.axis_size(axis)
    pairs = [(i, i + step) for i in range(count) if 0 <= i + step < count]
    return lax.ppermute(values, axis, pairs)


def exchange(chunks):
    return lax.all_to_all(chunks, "af", split_axis=0, concat_axis=0, tiled=True)


def per_device(
    coarse_state, coarse_kappa, coarse_rate, fine_state, fine_kappa, fine_rate, boxes, cover
):
    af_count = lax.axis_size("af")
    slots = fine_state.shape[0]
    cells_x, cells_y = coarse_state.shape[2:]
    group = af_count * slots
    lanes = group * BLK
    halves = cells_y // LANES
    rows = PLANES * cells_x
    plain = NZC * cells_x
    sizes = dict(cells_x=cells_x, cells_y=cells_y, group=group)

    span = cells_x + 2 * PAD
    chunk_rows = HALO_START + halves * EDGE_ROWS
    new, send, place, xlo, xhi, ylo, yhi = pl.pallas_call(
        functools.partial(strips_kernel, slots=slots, **sizes),
        out_shape=[
            hbm32(rows, cells_y),
            f32(af_count, chunk_rows, LANES),
            jax.ShapeDtypeStruct((16, lanes), jnp.int32),
        ]
        + [f32(EDGE_ROWS, cells_y)] * 2
        + [f32(cells_x, LANES)] * 2,
        in_specs=[HBM] * 4,
        out_specs=[HBM] + [VMEM] * 6,
        scratch_shapes=[
            pltpu.VMEM((2, boxes.shape[0]), jnp.int32),
            pltpu.VMEM((rows, cells_y), jnp.float32),
            pltpu.VMEM((plain, cells_y), jnp.float32),
            pltpu.VMEM((plain, cells_y), jnp.float32),
            pltpu.VMEM((rows, cells_y), jnp.float32),
            pltpu.VMEM(((SPECIES + 1) * halves * NZC * span, LANES), jnp.float32),
            pltpu.VMEM((rows * halves, LANES), jnp.float32),
            pltpu.SemaphoreType.DMA((4,)),
        ],
        compiler_params=PARAMS,
        name="strips",
    )(
        *pinned(
            boxes.T,
            coarse_state.reshape(rows, cells_y),
            coarse_kappa.reshape(plain, cells_y),
            coarse_rate.reshape(plain, cells_y),
        )
    )

    strips = exchange(send)

    kept = [hbm32(slots * size, LANES) for size in (FIELD_ROWS, COEFF_ROWS, UPWARD_ROWS)]
    kept_scratch = [pltpu.VMEM((slots * size, LANES), jnp.float32)
        for size in (FIELD_ROWS, COEFF_ROWS, UPWARD_ROWS)]
    fields, coeffs, upward, ylo_sent, yhi_sent = pl.pallas_call(
        functools.partial(prepare_kernel, slots=slots),
        out_shape=kept + [f32(cells_x, LANES)] * 2,
        in_specs=[HBM] * 4 + [VMEM] * 2,
        out_specs=[HBM] * 3 + [VMEM] * 2,
        scratch_shapes=kept_scratch
        + [
            pltpu.VMEM(fine_state.shape, jnp.float32),
            pltpu.VMEM(fine_kappa.shape, jnp.float32),
            pltpu.VMEM(fine_rate.shape, jnp.float32),
            pltpu.VMEM((FIELD_ROWS, LANES), jnp.float32),
            pltpu.VMEM((UPWARD_ROWS, LANES), jnp.float32),
            pltpu.SemaphoreType.DMA((3, slots)),
            pltpu.SemaphoreType.DMA((3, slots)),
        ],
        compiler_params=PARAMS,
        name="prepare",
    )(*pinned(new, fine_state, fine_kappa, fine_rate), ylo, yhi)
    yl = shifted(yhi_sent, "col", 1)
    yr = shifted(ylo_sent, "col", -1)

    chunk = (AVG_ROWS // FACES, LANES)
    fine_out, averages = pl.pallas_call(
        functools.partial(finish_kernel, slots=slots),
        out_shape=[hbm32(*fine_state.shape), hbm32(af_count, *chunk)],
        in_specs=[HBM] * 4 + [VMEM] * 2,
        out_specs=[HBM, HBM],
        scratch_shapes=[pltpu.VMEM((af_count, HALO_START, LANES), jnp.float32)]
        + kept_scratch
        + [
            pltpu.VMEM((2 * LANES, EDGE * EDGE), jnp.bfloat16),
            pltpu.VMEM((2 * SPECIES * FZ, STRIP_ROWS), jnp.bfloat16),
            pltpu.VMEM((2 * LANES, LANES), jnp.bfloat16),
            pltpu.VMEM(chunk, jnp.float32),
            pltpu.VMEM((FIELD_ROWS, LANES), jnp.float32),
            pltpu.VMEM((FIELD_ROWS, LANES), jnp.float32),
            pltpu.VMEM((SPECIES * TILES * FZ, LANES), jnp.float32),
            pltpu.VMEM((SPECIES * TILES * FZ, LANES), jnp.float32),
            pltpu.VMEM(fine_state.shape, jnp.float32),
            pltpu.SemaphoreType.DMA((slots,)),
            pltpu.SemaphoreType.DMA((3, slots)),
            pltpu.SemaphoreType.DMA,
            pltpu.SemaphoreType.DMA((af_count,)),
        ],
        compiler_params=PARAMS,
        name="finish",
    )(*pinned(strips, fields, coeffs, upward), yl, yr)

    arrived = exchange(averages)

    placed = pl.pallas_call(
        functools.partial(place_kernel, slots=slots, **sizes),
        out_shape=f32(rows, cells_y),
        in_specs=[VMEM] * 2 + [HBM] * 2 + [VMEM] * 6,
        out_specs=VMEM,
        scratch_shapes=[
            pltpu.VMEM((rows, cells_y), jnp.float32),
            pltpu.VMEM((2, halves * EDGE_ROWS, LANES), jnp.float32),
            pltpu.SemaphoreType.DMA((3,)),
        ],
        compiler_params=PARAMS,
        name="place",
    )(place, arrived, *pinned(new, strips), xlo, xhi, ylo, yhi, yl, yr)
    return (placed.reshape(coarse_state.shape), fine_out)


def solution(mesh):
    return jax.shard_map(
        per_device,
        mesh=mesh,
        in_specs=(
            P(None, None, "af", "col"),
            P(None, "af", "col"),
            P(None, "af", "col"),
            P(("col", "af"), None, None, None),
            P(("col", "af"), None, None),
            P(("col", "af"), None, None),
            P(),
            P(),
        ),
        out_specs=(P(None, None, "af", "col"), P(("col", "af"), None, None, None)),
        check_vma=False,
    )
```

```python
import functools

import jax
import jax.numpy as jnp
from jax import lax
from jax.experimental import pallas as pl
from jax.experimental.pallas import tpu as pltpu
from jax.sharding import PartitionSpec as P

NZC = 8
RATIO = 4
BLK = 8
SPECIES = 3
EDGE = BLK * RATIO
FZ = NZC * RATIO
LANES = 128
TILES = EDGE * EDGE // LANES
ZTILES = FZ // 8
STRIDE = 48
PAD = 8
FACES = 4
PLANES = SPECIES * NZC
STRIP_ROWS = 2 * PLANES
AVG_ROWS = PLANES * BLK
KINDS = 9
FIELD_ROWS = SPECIES * TILES * STRIDE
COEFF_ROWS = KINDS * TILES * FZ
UPWARD_ROWS = TILES * STRIDE
EDGE_ROWS = PLANES + NZC
BESIDE_ROWS = 2 * NZC
HALO_START = STRIP_ROWS + BESIDE_ROWS

DT_COARSE = 1.0 / 28.0
DIFFUSE = (1.0, 0.7, 0.45)
SIGNS = (-1.0, -1.0, 1.0)
FINE_SCALE = RATIO * RATIO * DT_COARSE / RATIO
DT_FINE = DT_COARSE / RATIO


def lane_ids(shape):
    return lax.broadcasted_iota(jnp.int32, shape, len(shape) - 1)


def roll_lanes(values, shift):
    width = values.shape[-1]
    shift = shift % width
    return values if shift == 0 else pltpu.roll(values, shift, values.ndim - 1)


def split_pair(values):
    high = values.astype(jnp.bfloat16)
    low = (values - high.astype(jnp.float32)).astype(jnp.bfloat16)
    return high, low


def face(scale, one, other):
    summed = one + other
    inverse = pl.reciprocal(summed, approx=True)
    inverse = inverse * (2.0 - summed * inverse)
    return (2.0 * scale) * (one * other) * inverse


def start_all(copies):
    for copy in copies:
        copy.start()


def selector(place_ref, column, cells_y):
    wanted = jnp.where(place_ref[0:8, :] == column, place_ref[8:16, :], -1)
    row = lax.broadcasted_iota(jnp.int32, wanted.shape, 0)
    return jnp.concatenate(
        [jnp.where(row + 8 * at == wanted, 1.0, 0.0) for at in range(cells_y // 8)], axis=0
    ).astype(jnp.bfloat16)


def strips_kernel(
    boxes_hbm,
    state_hbm,
    kappa_hbm,
    rate_hbm,
    new_hbm,
    send_ref,
    place_ref,
    xlo_ref,
    xhi_ref,
    ylo_ref,
    yhi_ref,
    boxes_ref,
    state_ref,
    kappa_ref,
    rate_ref,
    new_ref,
    padded,
    fresh,
    sems,
    *,
    cells_x,
    cells_y,
    group,
    slots,
):
    pairs = (
        (boxes_hbm, boxes_ref),
        (kappa_hbm, kappa_ref),
        (state_hbm, state_ref),
        (rate_hbm, rate_ref),
    )
    copies = [
        pltpu.make_async_copy(source, target, sems.at[index])
        for index, (source, target) in enumerate(pairs)
    ]
    start_all(copies)

    patches = boxes_ref.shape[1]
    lanes = group * BLK
    base_patch = lax.axis_index("col") * group
    member = lax.broadcasted_iota(jnp.int32, (patches, lanes), 0) - base_patch
    spread = jnp.where(member == lane_ids((patches, lanes)) // BLK, 1.0, 0.0).astype(jnp.bfloat16)
    first_col = lax.axis_index("af") * (cells_x // BLK)
    first_cell = lax.axis_index("col") * cells_y
    copies[0].wait()
    boxes = boxes_ref[...].astype(jnp.float32)
    stacked = jnp.concatenate(
        [jnp.broadcast_to(boxes[row : row + 1], (8, patches)) for row in range(2)], axis=0
    )
    found = jnp.dot(
        stacked.astype(jnp.bfloat16), spread, preferred_element_type=jnp.float32
    ).astype(jnp.int32)
    place_ref[0:8, :] = found[0:8] - first_col
    place_ref[8:16, :] = found[8:16] * BLK - first_cell + lane_ids((8, lanes)) % BLK

    halves = cells_y // LANES
    span = cells_x + 2 * PAD
    nothing = jnp.zeros((PAD, LANES), jnp.float32)

    def base(field, half, z):
        return ((field * halves + half) * NZC + z) * span

    for copy in copies[1:]:
        copy.wait()
    for field in range(SPECIES + 1):
        for half in range(halves):
            cols = pl.ds(half * LANES, LANES)
            for z in range(NZC):
                if field < SPECIES:
                    start = (field * NZC + z) * cells_x
                    plane = state_ref[start : start + cells_x, cols]
                else:
                    plane = kappa_ref[z * cells_x : (z + 1) * cells_x, cols]
                at = base(field, half, z)
                padded[at : at + PAD, :] = nothing
                padded[at + PAD : at + PAD + cells_x, :] = plane
                padded[at + PAD + cells_x : at + span, :] = nothing

    lane = lane_ids((cells_x, LANES))
    row_id = lax.broadcasted_iota(jnp.int32, (cells_x, LANES), 0)

    low = jnp.zeros((cells_x, LANES), jnp.float32)
    high = jnp.zeros((cells_x, LANES), jnp.float32)
    for plane in range(PLANES + NZC):
        field, z = divmod(plane, NZC)
        at = base(field, 0, z) + PAD
        first = padded[at : at + cells_x, :]
        at = base(field, halves - 1, z) + PAD
        last = padded[at : at + cells_x, :]
        low = jnp.where(lane == plane, roll_lanes(first, plane), low)
        high = jnp.where(lane == plane, roll_lanes(last, plane + 1), high)
    ylo_ref[...] = low
    yhi_ref[...] = high

    def load(field, half, z, shift):
        at = base(field, half, z) + PAD + shift
        return padded[at : at + cells_x, :]

    def neighbours(field, half, z):
        here = load(field, half, z, 0)
        after = roll_lanes(here, -1)
        if half + 1 < halves:
            after = jnp.where(
                lane == LANES - 1, roll_lanes(load(field, half + 1, z, 0), -1), after
            )
        before = roll_lanes(here, 1)
        if half > 0:
            before = jnp.where(lane == 0, roll_lanes(load(field, half - 1, z, 0), 1), before)
        found = [after, before, load(field, half, z, 1), load(field, half, z, -1)]
        if z + 1 < NZC:
            found.append(load(field, half, z + 1, 0))
        if z > 0:
            found.append(load(field, half, z - 1, 0))
        return found

    for z in range(NZC):
        for half in range(halves):
            cols = pl.ds(half * LANES, LANES)
            conduct = load(SPECIES, half, z, 0)
            coeffs = [face(DT_COARSE, conduct, other) for other in neighbours(SPECIES, half, z)]
            if half == halves - 1:
                coeffs[0] = jnp.where(lane == LANES - 1, 0.0, coeffs[0])
            if half == 0:
                coeffs[1] = jnp.where(lane == 0, 0.0, coeffs[1])
            coeffs[2] = jnp.where(row_id == cells_x - 1, 0.0, coeffs[2])
            coeffs[3] = jnp.where(row_id == 0, 0.0, coeffs[3])
            centers = [load(field, half, z, 0) for field in range(SPECIES)]
            forward = (DT_COARSE * rate_ref[z * cells_x : (z + 1) * cells_x, cols]) * (
                centers[0] * centers[1] - centers[2]
            )
            for field in range(SPECIES):
                center = centers[field]
                flux = None
                for coeff, other in zip(coeffs, neighbours(field, half, z)):
                    term = coeff * (other - center)
                    flux = term if flux is None else flux + term
                start = (field * NZC + z) * cells_x
                result = center + DIFFUSE[field] * flux + SIGNS[field] * forward
                new_ref[start : start + cells_x, cols] = result
                start = ((field * halves + half) * NZC + z) * cells_x
                fresh[start : start + cells_x, :] = result

    keep_new = pltpu.make_async_copy(new_ref, new_hbm, sems.at[0])
    keep_new.start()

    def old_row(field, half, row):
        return padded[pl.ds(base(field, half, 0) + PAD + row, NZC, stride=span), :]

    def edge_at(row):
        return jnp.concatenate(
            [
                jnp.concatenate([old_row(field, half, row) for field in range(SPECIES + 1)], axis=0)
                for half in range(halves)
            ],
            axis=1,
        )

    def rows_at(row):
        columns = []
        for half in range(halves):
            pieces = [old_row(field, half, row) for field in range(SPECIES)]
            for field in range(SPECIES):
                start = (field * halves + half) * NZC * cells_x
                pieces.append(fresh[pl.ds(start + row, NZC, stride=cells_x), :])
            columns.append(jnp.concatenate(pieces, axis=0))
        return jnp.concatenate(columns, axis=1)

    block_cols = cells_x // BLK
    spot = lane_ids((STRIP_ROWS, cells_y)) % BLK
    lower_y = []
    upper_y = []
    for column in range(block_cols):
        below = jnp.zeros((STRIP_ROWS, cells_y), jnp.float32)
        above = jnp.zeros((STRIP_ROWS, cells_y), jnp.float32)
        for x in range(BLK):
            strip = rows_at(column * BLK + x)
            below = jnp.where(spot == x, roll_lanes(strip, x + 1), below)
            above = jnp.where(spot == x, roll_lanes(strip, x - BLK), above)
        lower_y.append(below)
        upper_y.append(above)

    first_row = edge_at(0)
    last_row = edge_at(cells_x - 1)
    xlo_ref[...] = first_row
    xhi_ref[...] = last_row
    place = lane_ids((NZC, cells_y)) % BLK
    ones = jnp.ones((NZC, cells_y), jnp.float32)

    def field_of(row, field):
        return row[field * NZC : (field + 1) * NZC]

    def corners(row, fields, first_at):
        found = jnp.zeros((NZC, cells_y), jnp.float32)
        for order, field in enumerate(fields):
            at = first_at + 2 * order
            values = field_of(row, field)
            found = jnp.where(place == at, roll_lanes(values, at + 1), found)
            found = jnp.where(place == at + 1, roll_lanes(values, at + 1 - BLK), found)
        return found

    every = range(SPECIES)

    def near(row):
        own = [(field, field_of(row, field)) for field in range(SPECIES + 1)]
        return own + [(5, corners(row, [SPECIES], 0))]

    def far(row):
        return [
            (4, field_of(row, SPECIES)),
            (5, corners(row, every, 2)),
            (6, corners(row, [SPECIES], 0)),
        ]

    extra_members = {
        -1: far(first_row),
        0: near(first_row),
        block_cols - 1: near(last_row) + [(7, ones)],
        block_cols: far(last_row),
    }

    faces = [None] * (3 * FACES)

    def add(index, part):
        faces[index] = part if faces[index] is None else faces[index] + part

    for column in range(-1, block_cols + 1):
        members = []
        if column >= 1:
            members.append((0, rows_at(column * BLK - 1)))
        if column < block_cols - 1:
            members.append((1, rows_at(column * BLK + BLK)))
        if 0 <= column < block_cols:
            members.append((2, lower_y[column]))
            members.append((3, upper_y[column]))
        for index, rows in extra_members.get(column, []):
            members.append((FACES + index, rows))
        operands = []
        for _, rows in members:
            operands.extend(split_pair(rows))
        moved = jnp.dot(
            jnp.concatenate(operands, axis=0),
            selector(place_ref, column, cells_y),
            preferred_element_type=jnp.float32,
        )
        at = 0
        for index, rows in members:
            size = rows.shape[0]
            add(index, moved[at : at + size] + moved[at + size : at + 2 * size])
            at += 2 * size

    width = slots * BLK
    me = lax.axis_index("af")
    for target in range(group // slots):
        first = target * width
        tile = first // LANES * LANES
        for start, size, kind in (
            (0, STRIP_ROWS, 0),
            (STRIP_ROWS, NZC, FACES),
            (STRIP_ROWS + NZC, NZC, 2 * FACES),
        ):
            part = lane_ids((size, LANES)) // width
            chunk = jnp.zeros((size, LANES), jnp.float32)
            for index in range(FACES):
                piece = faces[kind + index][:, tile : tile + LANES]
                chunk = jnp.where(
                    part == index, roll_lanes(piece, index * width - (first - tile)), chunk
                )
            send_ref[target, start : start + size, :] = chunk
        halo = jnp.where(me < target, last_row, first_row)
        for half in range(halves):
            start = HALO_START + half * EDGE_ROWS
            send_ref[target, start : start + EDGE_ROWS, :] = halo[
                :, half * LANES : (half + 1) * LANES
            ]
    keep_new.wait()


def ghost_table(tile):
    lane = lane_ids((BLK, LANES))
    pos = lax.broadcasted_iota(jnp.int32, (BLK, LANES), 0)
    x = tile * (LANES // EDGE) + lane // EDGE
    y = lane % EDGE
    along_y = y // RATIO == pos
    along_x = x // RATIO == pos
    seen = (
        (x == 0) & along_y,
        (x == EDGE - 1) & along_y,
        (y == 0) & along_x,
        (y == EDGE - 1) & along_x,
    )
    nothing = jnp.zeros((LANES // FACES - BLK, LANES), jnp.float32)
    rows = []
    for where in seen:
        rows.extend([jnp.where(where, 1.0, 0.0), nothing])
    return jnp.concatenate(rows + rows, axis=0).astype(jnp.bfloat16)


def plane_table():
    shape = (2 * SPECIES * FZ, STRIP_ROWS)
    rows = lax.broadcasted_iota(jnp.int32, shape, 0)
    return jnp.where(rows // RATIO == lane_ids(shape), 1.0, 0.0).astype(jnp.bfloat16)


def mean_table():
    shape = (2 * LANES, LANES)
    rows = lax.broadcasted_iota(jnp.int32, shape, 0)
    same = rows % EDGE // RATIO == lane_ids(shape) % BLK
    return jnp.where(same, 1.0 / RATIO**3, 0.0).astype(jnp.bfloat16)


def complete_strips(gathered):
    width = LANES // FACES
    own = gathered[STRIP_ROWS : STRIP_ROWS + NZC]
    beside = gathered[STRIP_ROWS + NZC : STRIP_ROWS + 2 * NZC]
    lane = lane_ids((NZC, LANES))
    part = lane // width
    pos = lane % BLK
    flag = jnp.where(part == FACES - 1, beside, 0.0)
    flag = flag + roll_lanes(flag, width)
    upper = flag + roll_lanes(flag, 2 * width) > 0.5

    def coefficient(one, other):
        return face(DT_COARSE, jnp.maximum(one, 0.125), jnp.maximum(other, 0.125))

    block = coefficient(roll_lanes(own, width), beside)
    corner = coefficient(beside, roll_lanes(beside, -width))
    added = []
    for field in range(SPECIES):
        old = gathered[field * NZC : (field + 1) * NZC]
        there = jnp.where(upper, roll_lanes(old, -width), old)
        across = DIFFUSE[field] * block * (roll_lanes(own, -field * width) - there)
        below = jnp.where(upper, roll_lanes(old, -width - (BLK - 1)), roll_lanes(old, -width))
        above = jnp.where(
            upper, roll_lanes(old, -2 * width - (BLK - 2)), roll_lanes(old, 1 - 2 * width)
        )
        here = jnp.where(pos == 0, below, above)
        along = DIFFUSE[field] * corner * (roll_lanes(beside, -2 - 2 * field) - here)
        share = jnp.where((part == 0) & ~upper, across, 0.0)
        share = jnp.where((part == 1) & upper, roll_lanes(across, width), share)
        for index in range(2):
            for at, chosen in ((0, ~upper), (BLK - 1, upper)):
                moved = roll_lanes(along, (1 + index) * width + at - index)
                share = jnp.where((part == 2 + index) & (pos == at) & chosen, moved, share)
        added.append(share)
    new = gathered[PLANES:STRIP_ROWS] + jnp.concatenate(added, axis=0)
    return gathered[:PLANES], new


def aligned(start, size):
    return pl.ds(pl.multiple_of(start, 8), size)


def padded_at(block, ztile):
    return block * STRIDE + PAD + 8 * ztile


def advance(source, target, coeffs, upward, slot, from_rows, to_rows, ztile, ghosts):
    lane = lane_ids((8, LANES))

    def value(field, tile, shift):
        start = from_rows + padded_at(field * TILES + tile, ztile) + shift
        return source[aligned(start, 8) if shift == 0 else pl.ds(start, 8), :]

    def get(kind, tile):
        return coeffs[
            aligned(slot * COEFF_ROWS + (kind * TILES + tile) * FZ + 8 * ztile, 8), :
        ]

    centers = [value(field, 0, 0) for field in range(SPECIES)]
    down = [roll_lanes(center, -EDGE) for center in centers]
    up = [roll_lanes(center, EDGE) for center in centers]
    up_before = list(up)
    for tile in range(TILES):
        if tile + 1 < TILES:
            centers_after = [value(field, tile + 1, 0) for field in range(SPECIES)]
            down_after = [roll_lanes(center, -EDGE) for center in centers_after]
        next_x, prev_x, next_y, prev_y, rate = [get(kind, tile) for kind in range(5)]
        base = slot * UPWARD_ROWS + padded_at(tile, ztile)
        next_z = upward[aligned(base, 8), :]
        prev_z = upward[pl.ds(base - 1, 8), :]
        forward = rate * (centers[0] * centers[1] - centers[2])
        for field in range(SPECIES):
            center = centers[field]
            ahead, behind = down[field], up[field]
            if tile + 1 < TILES:
                ahead = jnp.where(lane < LANES - EDGE, ahead, down_after[field])
            if tile > 0:
                behind = jnp.where(lane >= EDGE, behind, up_before[field])
            flux = (next_x * ahead + prev_x * behind) + (
                next_y * roll_lanes(center, -1) + prev_y * roll_lanes(center, 1)
            )
            flux = flux + (next_z * value(field, tile, 1) + prev_z * value(field, tile, -1))
            share = ghosts(field, tile)
            if share is not None:
                flux = flux + share
            if DIFFUSE[field] != 1.0:
                flux = DIFFUSE[field] * flux
            result = get(5 + field, tile) * center + flux
            result = result - forward if SIGNS[field] < 0 else result + forward
            target[aligned(to_rows + padded_at(field * TILES + tile, ztile), 8), :] = result
        if tile + 1 < TILES:
            up_before = up
            centers, down = centers_after, down_after
            up = [roll_lanes(center, EDGE) for center in centers]


def clear_pads(ref):
    edge = jnp.zeros((PAD, LANES), jnp.float32)

    def body(block, carry):
        ref[aligned(block * STRIDE, PAD), :] = edge
        ref[aligned(block * STRIDE + PAD + FZ, PAD), :] = edge
        return carry

    lax.fori_loop(0, ref.shape[0] // STRIDE, body, 0)


def hand_on_kernel(ylo_ref, yhi_ref, ylo_out, yhi_out):
    ylo_out[...] = ylo_ref[...]
    yhi_out[...] = yhi_ref[...]


def prepare_kernel(
    after_ref,
    state_hbm,
    kappa_hbm,
    rate_hbm,
    fields_hbm,
    coeffs_hbm,
    upward_hbm,
    fields_ref,
    coeffs,
    upward,
    state_ref,
    kappa_ref,
    rate_ref,
    first,
    conduct,
    sems,
    out_sems,
    *,
    slots,
):
    def loads(slot):
        return [
            pltpu.make_async_copy(source.at[slot], target.at[slot], sems.at[order, slot])
            for order, (source, target) in enumerate(
                ((kappa_hbm, kappa_ref), (rate_hbm, rate_ref), (state_hbm, state_ref))
            )
        ]

    for slot in range(slots):
        start_all(loads(slot))

    def stores(slot):
        return [
            pltpu.make_async_copy(
                source.at[aligned(slot * size, size)],
                target.at[aligned(slot * size, size)],
                out_sems.at[order, slot],
            )
            for order, (source, target, size) in enumerate(
                (
                    (fields_ref, fields_hbm, FIELD_ROWS),
                    (coeffs, coeffs_hbm, COEFF_ROWS),
                    (upward, upward_hbm, UPWARD_ROWS),
                )
            )
        ]

    for ref in (fields_ref, upward, first, conduct):
        clear_pads(ref)

    lane = lane_ids((8, LANES))
    column = lane % EDGE
    side_y = jnp.where((column == 0) | (column == EDGE - 1), 1.0, 0.0)

    def one_patch(slot, carry):
        for copy in loads(slot):
            copy.wait()

        for tile in range(TILES):
            cols = pl.ds(tile * LANES, LANES)
            for field in range(SPECIES):
                spot = aligned(slot * FIELD_ROWS + padded_at(field * TILES + tile, 0), FZ)
                first[spot, :] = state_ref[slot, field, :, cols]
            spot = aligned(slot * UPWARD_ROWS + padded_at(tile, 0), FZ)
            conduct[spot, :] = kappa_ref[slot, :, cols]

        def keep(kind, tile, ztile, values):
            coeffs[
                aligned(slot * COEFF_ROWS + (kind * TILES + tile) * FZ + 8 * ztile, 8), :
            ] = values

        for ztile in range(ZTILES):

            def here(tile, shift):
                start = slot * UPWARD_ROWS + padded_at(tile, ztile) + shift
                return conduct[aligned(start, 8) if shift == 0 else pl.ds(start, 8), :]

            center = here(0, 0)
            turned = roll_lanes(center, -EDGE)
            back_before = None
            for tile in range(TILES):
                other = turned
                if tile + 1 < TILES:
                    center_after = here(tile + 1, 0)
                    turned_after = roll_lanes(center_after, -EDGE)
                    other = jnp.where(lane < LANES - EDGE, turned, turned_after)
                next_x = face(FINE_SCALE, center, other)
                if tile == TILES - 1:
                    next_x = jnp.where(lane < LANES - EDGE, next_x, 0.0)
                back = roll_lanes(next_x, EDGE)
                prev_x = jnp.where(lane >= EDGE, back, 0.0 if tile == 0 else back_before)
                next_y = jnp.where(
                    column < EDGE - 1, face(FINE_SCALE, center, roll_lanes(center, -1)), 0.0
                )
                prev_y = roll_lanes(next_y, 1)
                next_z = face(FINE_SCALE, center, here(tile, 1))
                prev_z = face(FINE_SCALE, center, here(tile, -1))
                sides = side_y
                if tile == 0:
                    sides = sides + jnp.where(lane < EDGE, 1.0, 0.0)
                if tile == TILES - 1:
                    sides = sides + jnp.where(lane >= LANES - EDGE, 1.0, 0.0)
                scale = FINE_SCALE * center
                total = (next_x + prev_x) + (next_y + prev_y) + (next_z + prev_z) + sides * scale
                upward[aligned(slot * UPWARD_ROWS + padded_at(tile, ztile), 8), :] = next_z
                keep(0, tile, ztile, next_x)
                keep(1, tile, ztile, prev_x)
                keep(2, tile, ztile, next_y)
                keep(3, tile, ztile, prev_y)
                rate = rate_ref[slot, pl.ds(8 * ztile, 8), pl.ds(tile * LANES, LANES)]
                keep(4, tile, ztile, DT_FINE * rate)
                for field in range(SPECIES):
                    keep(5 + field, tile, ztile, 1.0 - DIFFUSE[field] * total)
                keep(8, tile, ztile, scale)
                back_before = back
                if tile + 1 < TILES:
                    center, turned = center_after, turned_after

        for ztile in range(ZTILES):
            advance(
                first,
                fields_ref,
                coeffs,
                upward,
                slot,
                slot * FIELD_ROWS,
                slot * FIELD_ROWS,
                ztile,
                lambda field, tile: None,
            )
        start_all(stores(slot))
        return carry

    lax.fori_loop(0, slots, one_patch, 0)
    for slot in range(slots):
        for copy in stores(slot):
            copy.wait()


def finish_kernel(
    strips_ref,
    fields_hbm,
    coeffs_hbm,
    upward_hbm,
    yl_ref,
    yr_ref,
    out_hbm,
    avg_hbm,
    halo_hbm,
    fields_ref,
    coeffs,
    upward,
    ghost_ref,
    plane_ref,
    mean_ref,
    avg_ref,
    first,
    share,
    drift,
    staged,
    sems,
    in_sems,
    halo_sems,
    avg_sems,
    *,
    slots,
):
    sources = strips_ref.shape[0]
    me = lax.axis_index("af")
    halo_rows = pl.ds(HALO_START, halo_hbm.shape[1])
    halos = [
        pltpu.make_async_copy(
            strips_ref.at[source, halo_rows], halo_hbm.at[side], halo_sems.at[side]
        )
        for side, source in enumerate((jnp.maximum(me - 1, 0), jnp.minimum(me + 1, sources - 1)))
    ]

    def loads(slot):
        return [
            pltpu.make_async_copy(
                source.at[aligned(slot * size, size)],
                target.at[aligned(slot * size, size)],
                in_sems.at[order, slot],
            )
            for order, (source, target, size) in enumerate(
                (
                    (fields_hbm, fields_ref, FIELD_ROWS),
                    (coeffs_hbm, coeffs, COEFF_ROWS),
                    (upward_hbm, upward, UPWARD_ROWS),
                )
            )
        ]

    start_all(loads(0))
    start_all(halos)
    clear_pads(first)
    for tile in range(TILES):
        ghost_ref[:, tile * LANES : (tile + 1) * LANES] = ghost_table(tile)
    plane_ref[...] = plane_table()
    mean_ref[...] = mean_table()

    gathered = strips_ref[0, 0:HALO_START]
    for source in range(1, sources):
        gathered = gathered + strips_ref[source, 0:HALO_START]
    old, new = complete_strips(gathered)
    gathered = jnp.concatenate([old, (new - old) * (1.0 / RATIO)], axis=0)
    quarter = AVG_ROWS // FACES
    group_of = lane_ids((quarter, LANES)) // BLK

    def send_out(slot):
        return pltpu.make_async_copy(staged.at[slot], out_hbm.at[slot], sems.at[slot])

    def one_patch(slot, carry):
        for copy in loads(slot):
            copy.wait()

        @pl.when(slot + 1 < slots)
        def _():
            start_all(loads(slot + 1))

        turned = pltpu.roll(gathered, (LANES - slot * BLK) % LANES, 1)
        stretched = jnp.dot(
            plane_ref[...],
            jnp.concatenate(split_pair(turned), axis=1),
            preferred_element_type=jnp.float32,
        ).astype(jnp.bfloat16)
        base = slot * FIELD_ROWS
        scales = slot * COEFF_ROWS
        for tile in range(TILES):
            ghosts = jnp.dot(
                stretched,
                ghost_ref[:, tile * LANES : (tile + 1) * LANES],
                preferred_element_type=jnp.float32,
            )
            scale = coeffs[aligned(scales + (8 * TILES + tile) * FZ, FZ), :]
            for field in range(SPECIES):
                row = (field * TILES + tile) * FZ
                old = scale * ghosts[field * FZ : (field + 1) * FZ]
                step = scale * ghosts[(SPECIES + field) * FZ : (SPECIES + field + 1) * FZ]
                drift[row : row + FZ, :] = step
                share[row : row + FZ, :] = old + step
                spot = aligned(base + padded_at(field * TILES + tile, 0), FZ)
                fields_ref[spot, :] = fields_ref[spot, :] + DIFFUSE[field] * old

        for step in range(1, RATIO):
            source, target = (fields_ref, first) if step % 2 else (first, fields_ref)
            for ztile in range(ZTILES):

                def ghosts(field, tile):
                    spot = pl.ds((field * TILES + tile) * FZ + 8 * ztile, 8)
                    value = share[spot, :]
                    if step + 1 < RATIO:
                        share[spot, :] = value + drift[spot, :]
                    return value

                advance(source, target, coeffs, upward, slot, base, base, ztile, ghosts)

        for tile in range(TILES):
            for field in range(SPECIES):
                spot = aligned(base + padded_at(field * TILES + tile, 0), FZ)
                staged[slot, field, :, pl.ds(tile * LANES, LANES)] = first[spot, :]
        send_out(slot).start()

        sums = []
        for field in range(SPECIES):
            for plane in range(NZC):
                start = base + field * TILES * STRIDE + PAD + RATIO * plane
                part = first[pl.ds(start, TILES, stride=STRIDE), :]
                for z in range(1, RATIO):
                    part = part + first[pl.ds(start + z, TILES, stride=STRIDE), :]
                sums.append(part)
        means = jnp.dot(
            jnp.concatenate(split_pair(jnp.concatenate(sums, axis=0)), axis=1),
            mean_ref[...],
            preferred_element_type=jnp.float32,
        )
        chunk = avg_ref[...]
        for part in range(FACES):
            chunk = jnp.where(
                group_of == part * slots + slot,
                means[part * quarter : (part + 1) * quarter],
                chunk,
            )
        avg_ref[...] = chunk
        return carry

    avg_ref[...] = jnp.zeros((quarter, LANES), jnp.float32)
    lax.fori_loop(0, slots, one_patch, 0)
    copies = [
        pltpu.make_async_copy(avg_ref, avg_hbm.at[target], avg_sems.at[target])
        for target in range(sources)
    ]
    start_all(copies)
    for copy in copies:
        copy.wait()
    for copy in halos:
        copy.wait()
    for slot in range(slots):
        send_out(slot).wait()


def edges_kernel(
    new_hbm,
    halo_hbm,
    xlo_ref,
    xhi_ref,
    ylo_ref,
    yhi_ref,
    yl_ref,
    yr_ref,
    out_ref,
    new_ref,
    halo_ref,
    sems,
    *,
    cells_x,
    cells_y,
):
    me = lax.axis_index("af")
    last = lax.axis_size("af") - 1
    fetches = [
        pltpu.make_async_copy(halo_hbm, halo_ref, sems.at[0]),
        pltpu.make_async_copy(new_hbm, new_ref, sems.at[1]),
    ]
    start_all(fetches)

    def edge_share(own_ref, other_ref):
        own = own_ref[...]
        other = other_ref[...]
        coeff = face(DT_COARSE, jnp.maximum(own, 0.125), other)
        lane = lane_ids(own.shape)
        spread = jnp.zeros_like(own)
        for field in range(SPECIES):
            moved = roll_lanes(coeff, (field - SPECIES) * NZC)
            spread = jnp.where(lane // NZC == field, DIFFUSE[field] * moved, spread)
        return spread * (other - own)

    lower = edge_share(ylo_ref, yl_ref)
    upper = edge_share(yhi_ref, yr_ref)

    for copy in fetches:
        copy.wait()
    lane = lane_ids((BLK, LANES))
    row_id = lax.broadcasted_iota(jnp.int32, (BLK, LANES), 0)
    halves = cells_y // LANES

    def side_share(own_ref, side, exists):
        shares = []
        for half in range(halves):
            own = own_ref[:, half * LANES : (half + 1) * LANES]
            other = halo_ref[side, half * EDGE_ROWS : (half + 1) * EDGE_ROWS]
            coeff = face(DT_COARSE, own[PLANES:], other[PLANES:])
            coeff = jnp.where(exists, coeff, 0.0)
            shares.append(
                jnp.concatenate(
                    [
                        (DIFFUSE[field] * coeff)
                        * (
                            other[field * NZC : (field + 1) * NZC]
                            - own[field * NZC : (field + 1) * NZC]
                        )
                        for field in range(SPECIES)
                    ],
                    axis=0,
                )
            )
        return shares

    before = side_share(xlo_ref, 0, me > 0)
    after = side_share(xhi_ref, 1, me < last)
    block_cols = cells_x // BLK
    for column in range(block_cols):
        for plane in range(PLANES):
            row = plane * cells_x + column * BLK
            edge_rows = slice(column * BLK, (column + 1) * BLK)
            for half in range(halves):
                cols = slice(half * LANES, (half + 1) * LANES)
                coarse = new_ref[row : row + BLK, cols]
                if column == 0:
                    share = before[half][plane : plane + 1]
                    coarse = coarse + jnp.where(row_id == 0, share, 0.0)
                if column == block_cols - 1:
                    share = after[half][plane : plane + 1]
                    coarse = coarse + jnp.where(row_id == BLK - 1, share, 0.0)
                if half == 0:
                    share = roll_lanes(lower[edge_rows], -plane)
                    coarse = coarse + jnp.where(lane == 0, share, 0.0)
                if half == halves - 1:
                    share = roll_lanes(upper[edge_rows], LANES - 1 - plane)
                    coarse = coarse + jnp.where(lane == LANES - 1, share, 0.0)
                out_ref[row : row + BLK, cols] = coarse


def place_kernel(
    place_ref, avg_ref, new_ref, out_ref, *, cells_x, cells_y, group, slots
):
    width = slots * BLK
    quarter = AVG_ROWS // FACES
    per_tile = LANES // width
    part = lane_ids((quarter, LANES)) // width
    columns = []
    for tile in range(group * BLK // LANES):
        rows = []
        for index in range(FACES):
            merged = jnp.zeros((quarter, LANES), jnp.float32)
            for place in range(per_tile):
                piece = roll_lanes(avg_ref[tile * per_tile + place], (place - index) * width)
                merged = jnp.where(part == place, piece, merged)
            rows.append(merged)
        columns.append(jnp.concatenate(rows, axis=0))
    high, low = split_pair(jnp.concatenate(columns, axis=1))
    ones = jnp.ones((16, high.shape[1]), jnp.bfloat16)
    stacked = jnp.concatenate([high, low, ones], axis=0)

    halves = cells_y // LANES
    for column in range(cells_x // BLK):
        placed = lax.dot_general(
            stacked,
            selector(place_ref, column, cells_y),
            (((1,), (1,)), ((), ())),
            preferred_element_type=jnp.float32,
        )
        covered = placed[2 * AVG_ROWS : 2 * AVG_ROWS + 8] > 0.5
        for plane in range(PLANES):
            values = (
                placed[plane * BLK : (plane + 1) * BLK]
                + placed[AVG_ROWS + plane * BLK : AVG_ROWS + (plane + 1) * BLK]
            )
            row = plane * cells_x + column * BLK
            for half in range(halves):
                cols = slice(half * LANES, (half + 1) * LANES)
                coarse = new_ref[row : row + BLK, cols]
                out_ref[row : row + BLK, cols] = jnp.where(
                    covered[:, cols], values[:, cols], coarse
                )


VMEM = pl.BlockSpec(memory_space=pltpu.VMEM)
HBM = pl.BlockSpec(memory_space=pltpu.HBM)
PARAMS = pltpu.CompilerParams(vmem_limit_bytes=40 * 1024 * 1024)


def f32(*shape):
    return jax.ShapeDtypeStruct(shape, jnp.float32)


def hbm32(*shape):
    return pltpu.HBM(shape, jnp.float32)


def pinned(*arrays):
    return [pltpu.with_memory_space_constraint(array, pltpu.HBM) for array in arrays]


def shifted(values, axis, step):
    count = lax.axis_size(axis)
    pairs = [(i, i + step) for i in range(count) if 0 <= i + step < count]
    return lax.ppermute(values, axis, pairs)


def exchange(chunks):
    return lax.all_to_all(chunks, "af", split_axis=0, concat_axis=0, tiled=True)


def per_device(
    coarse_state, coarse_kappa, coarse_rate, fine_state, fine_kappa, fine_rate, boxes, cover
):
    af_count = lax.axis_size("af")
    slots = fine_state.shape[0]
    cells_x, cells_y = coarse_state.shape[2:]
    group = af_count * slots
    lanes = group * BLK
    halves = cells_y // LANES
    rows = PLANES * cells_x
    plain = NZC * cells_x
    sizes = dict(cells_x=cells_x, cells_y=cells_y, group=group)

    span = cells_x + 2 * PAD
    chunk_rows = HALO_START + halves * EDGE_ROWS
    new, send, place, xlo, xhi, ylo, yhi = pl.pallas_call(
        functools.partial(strips_kernel, slots=slots, **sizes),
        out_shape=[
            hbm32(rows, cells_y),
            f32(af_count, chunk_rows, LANES),
            jax.ShapeDtypeStruct((16, lanes), jnp.int32),
        ]
        + [f32(EDGE_ROWS, cells_y)] * 2
        + [f32(cells_x, LANES)] * 2,
        in_specs=[HBM] * 4,
        out_specs=[HBM] + [VMEM] * 6,
        scratch_shapes=[
            pltpu.VMEM((2, boxes.shape[0]), jnp.int32),
            pltpu.VMEM((rows, cells_y), jnp.float32),
            pltpu.VMEM((plain, cells_y), jnp.float32),
            pltpu.VMEM((plain, cells_y), jnp.float32),
            pltpu.VMEM((rows, cells_y), jnp.float32),
            pltpu.VMEM(((SPECIES + 1) * halves * NZC * span, LANES), jnp.float32),
            pltpu.VMEM((rows * halves, LANES), jnp.float32),
            pltpu.SemaphoreType.DMA((4,)),
        ],
        compiler_params=PARAMS,
        name="strips",
    )(
        *pinned(
            boxes.T,
            coarse_state.reshape(rows, cells_y),
            coarse_kappa.reshape(plain, cells_y),
            coarse_rate.reshape(plain, cells_y),
        )
    )

    strips = exchange(send)

    ylo_sent, yhi_sent = pl.pallas_call(
        hand_on_kernel,
        out_shape=[f32(cells_x, LANES)] * 2,
        in_specs=[VMEM] * 2,
        out_specs=[VMEM] * 2,
        name="hand_on",
    )(ylo, yhi)
    yl = shifted(yhi_sent, "col", 1)
    yr = shifted(ylo_sent, "col", -1)

    kept = [hbm32(slots * size, LANES) for size in (FIELD_ROWS, COEFF_ROWS, UPWARD_ROWS)]
    kept_scratch = [pltpu.VMEM((slots * size, LANES), jnp.float32)
        for size in (FIELD_ROWS, COEFF_ROWS, UPWARD_ROWS)]
    fields, coeffs, upward = pl.pallas_call(
        functools.partial(prepare_kernel, slots=slots),
        out_shape=kept,
        in_specs=[VMEM] + [HBM] * 3,
        out_specs=[HBM] * 3,
        scratch_shapes=kept_scratch
        + [
            pltpu.VMEM(fine_state.shape, jnp.float32),
            pltpu.VMEM(fine_kappa.shape, jnp.float32),
            pltpu.VMEM(fine_rate.shape, jnp.float32),
            pltpu.VMEM((slots * FIELD_ROWS, LANES), jnp.float32),
            pltpu.VMEM((slots * UPWARD_ROWS, LANES), jnp.float32),
            pltpu.SemaphoreType.DMA((3, slots)),
            pltpu.SemaphoreType.DMA((3, slots)),
        ],
        compiler_params=PARAMS,
        name="prepare",
    )(ylo_sent, *pinned(fine_state, fine_kappa, fine_rate))

    chunk = (AVG_ROWS // FACES, LANES)
    halo_shape = (2, halves * EDGE_ROWS, LANES)
    fine_out, averages, halo = pl.pallas_call(
        functools.partial(finish_kernel, slots=slots),
        out_shape=[hbm32(*fine_state.shape), hbm32(af_count, *chunk), hbm32(*halo_shape)],
        in_specs=[VMEM] + [HBM] * 3 + [VMEM] * 2,
        out_specs=[HBM] * 3,
        scratch_shapes=kept_scratch
        + [
            pltpu.VMEM((2 * LANES, EDGE * EDGE), jnp.bfloat16),
            pltpu.VMEM((2 * SPECIES * FZ, STRIP_ROWS), jnp.bfloat16),
            pltpu.VMEM((2 * LANES, LANES), jnp.bfloat16),
            pltpu.VMEM(chunk, jnp.float32),
            pltpu.VMEM((slots * FIELD_ROWS, LANES), jnp.float32),
            pltpu.VMEM((SPECIES * TILES * FZ, LANES), jnp.float32),
            pltpu.VMEM((SPECIES * TILES * FZ, LANES), jnp.float32),
            pltpu.VMEM(fine_state.shape, jnp.float32),
            pltpu.SemaphoreType.DMA((slots,)),
            pltpu.SemaphoreType.DMA((3, slots)),
            pltpu.SemaphoreType.DMA((2,)),
            pltpu.SemaphoreType.DMA((af_count,)),
        ],
        compiler_params=PARAMS,
        name="finish",
    )(strips, *pinned(fields, coeffs, upward), yl, yr)

    arrived = exchange(averages)

    whole = pl.pallas_call(
        functools.partial(edges_kernel, cells_x=cells_x, cells_y=cells_y),
        out_shape=f32(rows, cells_y),
        in_specs=[HBM] * 2 + [VMEM] * 6,
        out_specs=VMEM,
        scratch_shapes=[
            pltpu.VMEM((rows, cells_y), jnp.float32),
            pltpu.VMEM(halo_shape, jnp.float32),
            pltpu.SemaphoreType.DMA((2,)),
        ],
        compiler_params=PARAMS,
        name="edges",
    )(*pinned(new, halo), xlo, xhi, ylo, yhi, yl, yr)

    placed = pl.pallas_call(
        functools.partial(place_kernel, slots=slots, **sizes),
        out_shape=f32(rows, cells_y),
        in_specs=[VMEM] * 3,
        out_specs=VMEM,
        compiler_params=PARAMS,
        name="place",
    )(place, arrived, whole)
    return (placed.reshape(coarse_state.shape), fine_out)


def solution(mesh):
    return jax.shard_map(
        per_device,
        mesh=mesh,
        in_specs=(
            P(None, None, "af", "col"),
            P(None, "af", "col"),
            P(None, "af", "col"),
            P(("col", "af"), None, None, None),
            P(("col", "af"), None, None),
            P(("col", "af"), None, None),
            P(),
            P(),
        ),
        out_specs=(P(None, None, "af", "col"), P(("col", "af"), None, None, None)),
        check_vma=False,
    )
```

```python
import functools

import jax
import jax.numpy as jnp
from jax import lax
from jax.experimental import pallas as pl
from jax.experimental.pallas import tpu as pltpu
from jax.sharding import PartitionSpec as P

NZC = 8
RATIO = 4
BLK = 8
SPECIES = 3
EDGE = BLK * RATIO
FZ = NZC * RATIO
LANES = 128
TILES = EDGE * EDGE // LANES
ZTILES = FZ // 8
STRIDE = 48
PAD = 8
FACES = 4
PLANES = SPECIES * NZC
STRIP_ROWS = 2 * PLANES
AVG_ROWS = PLANES * BLK
KINDS = 9
FIELD_ROWS = SPECIES * TILES * STRIDE
COEFF_ROWS = KINDS * TILES * FZ
UPWARD_ROWS = TILES * STRIDE
EDGE_ROWS = PLANES + NZC
BESIDE_ROWS = 2 * NZC
CHUNK_ROWS = STRIP_ROWS + BESIDE_ROWS

DT_COARSE = 1.0 / 28.0
DIFFUSE = (1.0, 0.7, 0.45)
SIGNS = (-1.0, -1.0, 1.0)
FINE_SCALE = RATIO * RATIO * DT_COARSE / RATIO
DT_FINE = DT_COARSE / RATIO


def lane_ids(shape):
    return lax.broadcasted_iota(jnp.int32, shape, len(shape) - 1)


def roll_lanes(values, shift):
    width = values.shape[-1]
    shift = shift % width
    return values if shift == 0 else pltpu.roll(values, shift, values.ndim - 1)


def split_pair(values):
    high = values.astype(jnp.bfloat16)
    low = (values - high.astype(jnp.float32)).astype(jnp.bfloat16)
    return high, low


def face(scale, one, other):
    summed = one + other
    inverse = pl.reciprocal(summed, approx=True)
    inverse = inverse * (2.0 - summed * inverse)
    return (2.0 * scale) * (one * other) * inverse


def start_all(copies):
    for copy in copies:
        copy.start()


def selector(place_ref, column, cells_y):
    wanted = jnp.where(place_ref[0:8, :] == column, place_ref[8:16, :], -1)
    row = lax.broadcasted_iota(jnp.int32, wanted.shape, 0)
    return jnp.concatenate(
        [jnp.where(row + 8 * at == wanted, 1.0, 0.0) for at in range(cells_y // 8)], axis=0
    ).astype(jnp.bfloat16)


def strips_kernel(
    boxes_hbm,
    state_hbm,
    kappa_hbm,
    rate_hbm,
    new_hbm,
    send_ref,
    place_ref,
    xlo_ref,
    xhi_ref,
    ylo_ref,
    yhi_ref,
    boxes_ref,
    state_ref,
    kappa_ref,
    rate_ref,
    new_ref,
    padded,
    fresh,
    sems,
    *,
    cells_x,
    cells_y,
    group,
    slots,
):
    pairs = (
        (boxes_hbm, boxes_ref),
        (kappa_hbm, kappa_ref),
        (state_hbm, state_ref),
        (rate_hbm, rate_ref),
    )
    copies = [
        pltpu.make_async_copy(source, target, sems.at[index])
        for index, (source, target) in enumerate(pairs)
    ]
    start_all(copies)

    patches = boxes_ref.shape[1]
    lanes = group * BLK
    base_patch = lax.axis_index("col") * group
    member = lax.broadcasted_iota(jnp.int32, (patches, lanes), 0) - base_patch
    spread = jnp.where(member == lane_ids((patches, lanes)) // BLK, 1.0, 0.0).astype(jnp.bfloat16)
    first_col = lax.axis_index("af") * (cells_x // BLK)
    first_cell = lax.axis_index("col") * cells_y
    copies[0].wait()
    boxes = boxes_ref[...].astype(jnp.float32)
    stacked = jnp.concatenate(
        [jnp.broadcast_to(boxes[row : row + 1], (8, patches)) for row in range(2)], axis=0
    )
    found = jnp.dot(
        stacked.astype(jnp.bfloat16), spread, preferred_element_type=jnp.float32
    ).astype(jnp.int32)
    place_ref[0:8, :] = found[0:8] - first_col
    place_ref[8:16, :] = found[8:16] * BLK - first_cell + lane_ids((8, lanes)) % BLK

    halves = cells_y // LANES
    span = cells_x + 2 * PAD
    nothing = jnp.zeros((PAD, LANES), jnp.float32)

    def base(field, half, z):
        return ((field * halves + half) * NZC + z) * span

    for copy in copies[1:]:
        copy.wait()
    for field in range(SPECIES + 1):
        for half in range(halves):
            cols = pl.ds(half * LANES, LANES)
            for z in range(NZC):
                if field < SPECIES:
                    start = (field * NZC + z) * cells_x
                    plane = state_ref[start : start + cells_x, cols]
                else:
                    plane = kappa_ref[z * cells_x : (z + 1) * cells_x, cols]
                at = base(field, half, z)
                padded[at : at + PAD, :] = nothing
                padded[at + PAD : at + PAD + cells_x, :] = plane
                padded[at + PAD + cells_x : at + span, :] = nothing

    lane = lane_ids((cells_x, LANES))
    row_id = lax.broadcasted_iota(jnp.int32, (cells_x, LANES), 0)

    low = jnp.zeros((cells_x, LANES), jnp.float32)
    high = jnp.zeros((cells_x, LANES), jnp.float32)
    for plane in range(PLANES + NZC):
        field, z = divmod(plane, NZC)
        at = base(field, 0, z) + PAD
        first = padded[at : at + cells_x, :]
        at = base(field, halves - 1, z) + PAD
        last = padded[at : at + cells_x, :]
        low = jnp.where(lane == plane, roll_lanes(first, plane), low)
        high = jnp.where(lane == plane, roll_lanes(last, plane + 1), high)
    ylo_ref[...] = low
    yhi_ref[...] = high

    def load(field, half, z, shift):
        at = base(field, half, z) + PAD + shift
        return padded[at : at + cells_x, :]

    def neighbours(field, half, z):
        here = load(field, half, z, 0)
        after = roll_lanes(here, -1)
        if half + 1 < halves:
            after = jnp.where(
                lane == LANES - 1, roll_lanes(load(field, half + 1, z, 0), -1), after
            )
        before = roll_lanes(here, 1)
        if half > 0:
            before = jnp.where(lane == 0, roll_lanes(load(field, half - 1, z, 0), 1), before)
        found = [after, before, load(field, half, z, 1), load(field, half, z, -1)]
        if z + 1 < NZC:
            found.append(load(field, half, z + 1, 0))
        if z > 0:
            found.append(load(field, half, z - 1, 0))
        return found

    for z in range(NZC):
        for half in range(halves):
            cols = pl.ds(half * LANES, LANES)
            conduct = load(SPECIES, half, z, 0)
            coeffs = [face(DT_COARSE, conduct, other) for other in neighbours(SPECIES, half, z)]
            if half == halves - 1:
                coeffs[0] = jnp.where(lane == LANES - 1, 0.0, coeffs[0])
            if half == 0:
                coeffs[1] = jnp.where(lane == 0, 0.0, coeffs[1])
            coeffs[2] = jnp.where(row_id == cells_x - 1, 0.0, coeffs[2])
            coeffs[3] = jnp.where(row_id == 0, 0.0, coeffs[3])
            centers = [load(field, half, z, 0) for field in range(SPECIES)]
            forward = (DT_COARSE * rate_ref[z * cells_x : (z + 1) * cells_x, cols]) * (
                centers[0] * centers[1] - centers[2]
            )
            for field in range(SPECIES):
                center = centers[field]
                flux = None
                for coeff, other in zip(coeffs, neighbours(field, half, z)):
                    term = coeff * (other - center)
                    flux = term if flux is None else flux + term
                start = (field * NZC + z) * cells_x
                result = center + DIFFUSE[field] * flux + SIGNS[field] * forward
                new_ref[start : start + cells_x, cols] = result
                start = ((field * halves + half) * NZC + z) * cells_x
                fresh[start : start + cells_x, :] = result

    keep_new = pltpu.make_async_copy(new_ref, new_hbm, sems.at[0])
    keep_new.start()

    def old_row(field, half, row):
        return padded[pl.ds(base(field, half, 0) + PAD + row, NZC, stride=span), :]

    def edge_at(row):
        return jnp.concatenate(
            [
                jnp.concatenate([old_row(field, half, row) for field in range(SPECIES + 1)], axis=0)
                for half in range(halves)
            ],
            axis=1,
        )

    def rows_at(row):
        columns = []
        for half in range(halves):
            pieces = [old_row(field, half, row) for field in range(SPECIES)]
            for field in range(SPECIES):
                start = (field * halves + half) * NZC * cells_x
                pieces.append(fresh[pl.ds(start + row, NZC, stride=cells_x), :])
            columns.append(jnp.concatenate(pieces, axis=0))
        return jnp.concatenate(columns, axis=1)

    block_cols = cells_x // BLK
    spot = lane_ids((STRIP_ROWS, cells_y)) % BLK
    lower_y = []
    upper_y = []
    for column in range(block_cols):
        below = jnp.zeros((STRIP_ROWS, cells_y), jnp.float32)
        above = jnp.zeros((STRIP_ROWS, cells_y), jnp.float32)
        for x in range(BLK):
            turned = roll_lanes(rows_at(column * BLK + x), x + 1)
            below = jnp.where(spot == x, turned, below)
            above = jnp.where(spot == (x + 1) % BLK, turned, above)
        lower_y.append(below)
        upper_y.append(roll_lanes(above, -1 - BLK))

    first_row = edge_at(0)
    last_row = edge_at(cells_x - 1)
    xlo_ref[...] = first_row
    xhi_ref[...] = last_row
    place = lane_ids((NZC, cells_y)) % BLK
    ones = jnp.ones((NZC, cells_y), jnp.float32)

    def field_of(row, field):
        return row[field * NZC : (field + 1) * NZC]

    def corners(row, fields, first_at):
        found = jnp.zeros((NZC, cells_y), jnp.float32)
        for order, field in enumerate(fields):
            at = first_at + 2 * order
            values = field_of(row, field)
            found = jnp.where(place == at, roll_lanes(values, at + 1), found)
            found = jnp.where(place == at + 1, roll_lanes(values, at + 1 - BLK), found)
        return found

    every = range(SPECIES)

    def near(row):
        own = [(field, field_of(row, field)) for field in range(SPECIES + 1)]
        return own + [(5, corners(row, [SPECIES], 0))]

    def far(row):
        return [
            (4, field_of(row, SPECIES)),
            (5, corners(row, every, 2)),
            (6, corners(row, [SPECIES], 0)),
        ]

    extra_members = {
        -1: far(first_row),
        0: near(first_row),
        block_cols - 1: near(last_row) + [(7, ones)],
        block_cols: far(last_row),
    }

    faces = [None] * (3 * FACES)

    def add(index, part):
        faces[index] = part if faces[index] is None else faces[index] + part

    for column in range(-1, block_cols + 1):
        members = []
        if column >= 1:
            members.append((0, rows_at(column * BLK - 1)))
        if column < block_cols - 1:
            members.append((1, rows_at(column * BLK + BLK)))
        if 0 <= column < block_cols:
            members.append((2, lower_y[column]))
            members.append((3, upper_y[column]))
        for index, rows in extra_members.get(column, []):
            members.append((FACES + index, rows))
        operands = []
        for _, rows in members:
            operands.extend(split_pair(rows))
        moved = jnp.dot(
            jnp.concatenate(operands, axis=0),
            selector(place_ref, column, cells_y),
            preferred_element_type=jnp.float32,
        )
        at = 0
        for index, rows in members:
            size = rows.shape[0]
            add(index, moved[at : at + size] + moved[at + size : at + 2 * size])
            at += 2 * size

    width = slots * BLK
    for target in range(group // slots):
        first = target * width
        tile = first // LANES * LANES
        for start, size, kind in (
            (0, STRIP_ROWS, 0),
            (STRIP_ROWS, NZC, FACES),
            (STRIP_ROWS + NZC, NZC, 2 * FACES),
        ):
            part = lane_ids((size, LANES)) // width
            chunk = jnp.zeros((size, LANES), jnp.float32)
            for index in range(FACES):
                piece = faces[kind + index][:, tile : tile + LANES]
                chunk = jnp.where(
                    part == index, roll_lanes(piece, index * width - (first - tile)), chunk
                )
            send_ref[target, start : start + size, :] = chunk
    keep_new.wait()


def ghost_table(tile):
    lane = lane_ids((BLK, LANES))
    pos = lax.broadcasted_iota(jnp.int32, (BLK, LANES), 0)
    x = tile * (LANES // EDGE) + lane // EDGE
    y = lane % EDGE
    along_y = y // RATIO == pos
    along_x = x // RATIO == pos
    seen = (
        (x == 0) & along_y,
        (x == EDGE - 1) & along_y,
        (y == 0) & along_x,
        (y == EDGE - 1) & along_x,
    )
    nothing = jnp.zeros((LANES // FACES - BLK, LANES), jnp.float32)
    rows = []
    for where in seen:
        rows.extend([jnp.where(where, 1.0, 0.0), nothing])
    return jnp.concatenate(rows + rows, axis=0).astype(jnp.bfloat16)


def plane_table():
    shape = (2 * SPECIES * FZ, STRIP_ROWS)
    rows = lax.broadcasted_iota(jnp.int32, shape, 0)
    return jnp.where(rows // RATIO == lane_ids(shape), 1.0, 0.0).astype(jnp.bfloat16)


def mean_table():
    shape = (2 * LANES, LANES)
    rows = lax.broadcasted_iota(jnp.int32, shape, 0)
    same = rows % EDGE // RATIO == lane_ids(shape) % BLK
    return jnp.where(same, 1.0 / RATIO**3, 0.0).astype(jnp.bfloat16)


def complete_strips(gathered):
    width = LANES // FACES
    own = gathered[STRIP_ROWS : STRIP_ROWS + NZC]
    beside = gathered[STRIP_ROWS + NZC : STRIP_ROWS + 2 * NZC]
    lane = lane_ids((NZC, LANES))
    part = lane // width
    pos = lane % BLK
    flag = jnp.where(part == FACES - 1, beside, 0.0)
    flag = flag + roll_lanes(flag, width)
    upper = flag + roll_lanes(flag, 2 * width) > 0.5

    def coefficient(one, other):
        return face(DT_COARSE, jnp.maximum(one, 0.125), jnp.maximum(other, 0.125))

    block = coefficient(roll_lanes(own, width), beside)
    corner = coefficient(beside, roll_lanes(beside, -width))
    added = []
    for field in range(SPECIES):
        old = gathered[field * NZC : (field + 1) * NZC]
        there = jnp.where(upper, roll_lanes(old, -width), old)
        across = DIFFUSE[field] * block * (roll_lanes(own, -field * width) - there)
        below = jnp.where(upper, roll_lanes(old, -width - (BLK - 1)), roll_lanes(old, -width))
        above = jnp.where(
            upper, roll_lanes(old, -2 * width - (BLK - 2)), roll_lanes(old, 1 - 2 * width)
        )
        here = jnp.where(pos == 0, below, above)
        along = DIFFUSE[field] * corner * (roll_lanes(beside, -2 - 2 * field) - here)
        share = jnp.where((part == 0) & ~upper, across, 0.0)
        share = jnp.where((part == 1) & upper, roll_lanes(across, width), share)
        for index in range(2):
            for at, chosen in ((0, ~upper), (BLK - 1, upper)):
                moved = roll_lanes(along, (1 + index) * width + at - index)
                share = jnp.where((part == 2 + index) & (pos == at) & chosen, moved, share)
        added.append(share)
    new = gathered[PLANES:STRIP_ROWS] + jnp.concatenate(added, axis=0)
    return gathered[:PLANES], new


def aligned(start, size):
    return pl.ds(pl.multiple_of(start, 8), size)


def padded_at(block, ztile):
    return block * STRIDE + PAD + 8 * ztile


def advance(source, target, coeffs, upward, slot, from_rows, to_rows, ztile, ghosts):
    lane = lane_ids((8, LANES))

    def value(field, tile, shift):
        start = from_rows + padded_at(field * TILES + tile, ztile) + shift
        return source[aligned(start, 8) if shift == 0 else pl.ds(start, 8), :]

    def get(kind, tile):
        return coeffs[
            aligned(slot * COEFF_ROWS + (kind * TILES + tile) * FZ + 8 * ztile, 8), :
        ]

    centers = [value(field, 0, 0) for field in range(SPECIES)]
    down = [roll_lanes(center, -EDGE) for center in centers]
    up = [roll_lanes(center, EDGE) for center in centers]
    up_before = list(up)
    for tile in range(TILES):
        if tile + 1 < TILES:
            centers_after = [value(field, tile + 1, 0) for field in range(SPECIES)]
            down_after = [roll_lanes(center, -EDGE) for center in centers_after]
        next_x, prev_x, next_y, prev_y, rate = [get(kind, tile) for kind in range(5)]
        base = slot * UPWARD_ROWS + padded_at(tile, ztile)
        next_z = upward[aligned(base, 8), :]
        prev_z = upward[pl.ds(base - 1, 8), :]
        forward = rate * (centers[0] * centers[1] - centers[2])
        for field in range(SPECIES):
            center = centers[field]
            ahead, behind = down[field], up[field]
            if tile + 1 < TILES:
                ahead = jnp.where(lane < LANES - EDGE, ahead, down_after[field])
            if tile > 0:
                behind = jnp.where(lane >= EDGE, behind, up_before[field])
            flux = (next_x * ahead + prev_x * behind) + (
                next_y * roll_lanes(center, -1) + prev_y * roll_lanes(center, 1)
            )
            flux = flux + (next_z * value(field, tile, 1) + prev_z * value(field, tile, -1))
            share = ghosts(field, tile)
            if share is not None:
                flux = flux + share
            if DIFFUSE[field] != 1.0:
                flux = DIFFUSE[field] * flux
            result = get(5 + field, tile) * center + flux
            result = result - forward if SIGNS[field] < 0 else result + forward
            target[aligned(to_rows + padded_at(field * TILES + tile, ztile), 8), :] = result
        if tile + 1 < TILES:
            up_before = up
            centers, down = centers_after, down_after
            up = [roll_lanes(center, EDGE) for center in centers]


def clear_pads(ref):
    edge = jnp.zeros((PAD, LANES), jnp.float32)

    def body(block, carry):
        ref[aligned(block * STRIDE, PAD), :] = edge
        ref[aligned(block * STRIDE + PAD + FZ, PAD), :] = edge
        return carry

    lax.fori_loop(0, ref.shape[0] // STRIDE, body, 0)


def hand_on_kernel(low_ref, high_ref, low_out, high_out):
    low_out[...] = low_ref[...]
    high_out[...] = high_ref[...]


def prepare_kernel(
    after_ref,
    state_hbm,
    kappa_hbm,
    rate_hbm,
    fields_hbm,
    coeffs_hbm,
    upward_hbm,
    fields_ref,
    coeffs,
    upward,
    state_ref,
    kappa_ref,
    rate_ref,
    first,
    conduct,
    sems,
    out_sems,
    *,
    slots,
):
    def loads(slot):
        return [
            pltpu.make_async_copy(source.at[slot], target.at[slot], sems.at[order, slot])
            for order, (source, target) in enumerate(
                ((kappa_hbm, kappa_ref), (rate_hbm, rate_ref), (state_hbm, state_ref))
            )
        ]

    for slot in range(slots):
        start_all(loads(slot))

    def stores(slot):
        return [
            pltpu.make_async_copy(
                source.at[aligned(slot * size, size)],
                target.at[aligned(slot * size, size)],
                out_sems.at[order, slot],
            )
            for order, (source, target, size) in enumerate(
                (
                    (fields_ref, fields_hbm, FIELD_ROWS),
                    (coeffs, coeffs_hbm, COEFF_ROWS),
                    (upward, upward_hbm, UPWARD_ROWS),
                )
            )
        ]

    for ref in (fields_ref, upward, first, conduct):
        clear_pads(ref)

    lane = lane_ids((8, LANES))
    column = lane % EDGE
    side_y = jnp.where((column == 0) | (column == EDGE - 1), 1.0, 0.0)

    def one_patch(slot, carry):
        for copy in loads(slot):
            copy.wait()

        for tile in range(TILES):
            cols = pl.ds(tile * LANES, LANES)
            for field in range(SPECIES):
                spot = aligned(slot * FIELD_ROWS + padded_at(field * TILES + tile, 0), FZ)
                first[spot, :] = state_ref[slot, field, :, cols]
            spot = aligned(slot * UPWARD_ROWS + padded_at(tile, 0), FZ)
            conduct[spot, :] = kappa_ref[slot, :, cols]

        def keep(kind, tile, ztile, values):
            coeffs[
                aligned(slot * COEFF_ROWS + (kind * TILES + tile) * FZ + 8 * ztile, 8), :
            ] = values

        for ztile in range(ZTILES):

            def here(tile, shift):
                start = slot * UPWARD_ROWS + padded_at(tile, ztile) + shift
                return conduct[aligned(start, 8) if shift == 0 else pl.ds(start, 8), :]

            center = here(0, 0)
            turned = roll_lanes(center, -EDGE)
            back_before = None
            for tile in range(TILES):
                other = turned
                if tile + 1 < TILES:
                    center_after = here(tile + 1, 0)
                    turned_after = roll_lanes(center_after, -EDGE)
                    other = jnp.where(lane < LANES - EDGE, turned, turned_after)
                next_x = face(FINE_SCALE, center, other)
                if tile == TILES - 1:
                    next_x = jnp.where(lane < LANES - EDGE, next_x, 0.0)
                back = roll_lanes(next_x, EDGE)
                prev_x = jnp.where(lane >= EDGE, back, 0.0 if tile == 0 else back_before)
                next_y = jnp.where(
                    column < EDGE - 1, face(FINE_SCALE, center, roll_lanes(center, -1)), 0.0
                )
                prev_y = roll_lanes(next_y, 1)
                next_z = face(FINE_SCALE, center, here(tile, 1))
                prev_z = face(FINE_SCALE, center, here(tile, -1))
                sides = side_y
                if tile == 0:
                    sides = sides + jnp.where(lane < EDGE, 1.0, 0.0)
                if tile == TILES - 1:
                    sides = sides + jnp.where(lane >= LANES - EDGE, 1.0, 0.0)
                scale = FINE_SCALE * center
                total = (next_x + prev_x) + (next_y + prev_y) + (next_z + prev_z) + sides * scale
                upward[aligned(slot * UPWARD_ROWS + padded_at(tile, ztile), 8), :] = next_z
                keep(0, tile, ztile, next_x)
                keep(1, tile, ztile, prev_x)
                keep(2, tile, ztile, next_y)
                keep(3, tile, ztile, prev_y)
                rate = rate_ref[slot, pl.ds(8 * ztile, 8), pl.ds(tile * LANES, LANES)]
                keep(4, tile, ztile, DT_FINE * rate)
                for field in range(SPECIES):
                    keep(5 + field, tile, ztile, 1.0 - DIFFUSE[field] * total)
                keep(8, tile, ztile, scale)
                back_before = back
                if tile + 1 < TILES:
                    center, turned = center_after, turned_after

        for ztile in range(ZTILES):
            advance(
                first,
                fields_ref,
                coeffs,
                upward,
                slot,
                slot * FIELD_ROWS,
                slot * FIELD_ROWS,
                ztile,
                lambda field, tile: None,
            )
        start_all(stores(slot))
        return carry

    lax.fori_loop(0, slots, one_patch, 0)
    for slot in range(slots):
        for copy in stores(slot):
            copy.wait()


def finish_kernel(
    strips_ref,
    fields_hbm,
    coeffs_hbm,
    upward_hbm,
    xl_ref,
    xr_ref,
    out_hbm,
    avg_hbm,
    fields_ref,
    coeffs,
    upward,
    ghost_ref,
    plane_ref,
    mean_ref,
    avg_ref,
    first,
    share,
    drift,
    staged,
    sems,
    in_sems,
    avg_sems,
    *,
    slots,
):
    sources = strips_ref.shape[0]

    def loads(slot):
        return [
            pltpu.make_async_copy(
                source.at[aligned(slot * size, size)],
                target.at[aligned(slot * size, size)],
                in_sems.at[order, slot],
            )
            for order, (source, target, size) in enumerate(
                (
                    (fields_hbm, fields_ref, FIELD_ROWS),
                    (coeffs_hbm, coeffs, COEFF_ROWS),
                    (upward_hbm, upward, UPWARD_ROWS),
                )
            )
        ]

    start_all(loads(0))
    clear_pads(first)
    for tile in range(TILES):
        ghost_ref[:, tile * LANES : (tile + 1) * LANES] = ghost_table(tile)
    plane_ref[...] = plane_table()
    mean_ref[...] = mean_table()

    gathered = strips_ref[0]
    for source in range(1, sources):
        gathered = gathered + strips_ref[source]
    old, new = complete_strips(gathered)
    gathered = jnp.concatenate([old, (new - old) * (1.0 / RATIO)], axis=0)
    quarter = AVG_ROWS // FACES
    group_of = lane_ids((quarter, LANES)) // BLK

    def send_out(slot):
        return pltpu.make_async_copy(staged.at[slot], out_hbm.at[slot], sems.at[slot])

    def one_patch(slot, carry):
        for copy in loads(slot):
            copy.wait()

        @pl.when(slot + 1 < slots)
        def _():
            start_all(loads(slot + 1))

        turned = pltpu.roll(gathered, (LANES - slot * BLK) % LANES, 1)
        stretched = jnp.dot(
            plane_ref[...],
            jnp.concatenate(split_pair(turned), axis=1),
            preferred_element_type=jnp.float32,
        ).astype(jnp.bfloat16)
        base = slot * FIELD_ROWS
        scales = slot * COEFF_ROWS
        for tile in range(TILES):
            ghosts = jnp.dot(
                stretched,
                ghost_ref[:, tile * LANES : (tile + 1) * LANES],
                preferred_element_type=jnp.float32,
            )
            scale = coeffs[aligned(scales + (8 * TILES + tile) * FZ, FZ), :]
            for field in range(SPECIES):
                row = (field * TILES + tile) * FZ
                old = scale * ghosts[field * FZ : (field + 1) * FZ]
                step = scale * ghosts[(SPECIES + field) * FZ : (SPECIES + field + 1) * FZ]
                drift[row : row + FZ, :] = step
                share[row : row + FZ, :] = old + step
                spot = aligned(base + padded_at(field * TILES + tile, 0), FZ)
                fields_ref[spot, :] = fields_ref[spot, :] + DIFFUSE[field] * old

        for step in range(1, RATIO):
            source, target = (fields_ref, first) if step % 2 else (first, fields_ref)
            for ztile in range(ZTILES):

                def ghosts(field, tile):
                    spot = pl.ds((field * TILES + tile) * FZ + 8 * ztile, 8)
                    value = share[spot, :]
                    if step + 1 < RATIO:
                        share[spot, :] = value + drift[spot, :]
                    return value

                advance(source, target, coeffs, upward, slot, base, base, ztile, ghosts)

        for tile in range(TILES):
            for field in range(SPECIES):
                spot = aligned(base + padded_at(field * TILES + tile, 0), FZ)
                staged[slot, field, :, pl.ds(tile * LANES, LANES)] = first[spot, :]
        send_out(slot).start()

        sums = []
        for field in range(SPECIES):
            for plane in range(NZC):
                start = base + field * TILES * STRIDE + PAD + RATIO * plane
                part = first[pl.ds(start, TILES, stride=STRIDE), :]
                for z in range(1, RATIO):
                    part = part + first[pl.ds(start + z, TILES, stride=STRIDE), :]
                sums.append(part)
        means = jnp.dot(
            jnp.concatenate(split_pair(jnp.concatenate(sums, axis=0)), axis=1),
            mean_ref[...],
            preferred_element_type=jnp.float32,
        )
        chunk = avg_ref[...]
        for part in range(FACES):
            chunk = jnp.where(
                group_of == part * slots + slot,
                means[part * quarter : (part + 1) * quarter],
                chunk,
            )
        avg_ref[...] = chunk
        return carry

    avg_ref[...] = jnp.zeros((quarter, LANES), jnp.float32)
    lax.fori_loop(0, slots, one_patch, 0)
    copies = [
        pltpu.make_async_copy(avg_ref, avg_hbm.at[target], avg_sems.at[target])
        for target in range(sources)
    ]
    start_all(copies)
    for copy in copies:
        copy.wait()
    for slot in range(slots):
        send_out(slot).wait()


def edges_kernel(
    new_hbm,
    xlo_ref,
    xhi_ref,
    ylo_ref,
    yhi_ref,
    xl_ref,
    xr_ref,
    yl_ref,
    yr_ref,
    out_ref,
    new_ref,
    sem,
    *,
    cells_x,
    cells_y,
):
    me = lax.axis_index("af")
    last = lax.axis_size("af") - 1
    fetch = pltpu.make_async_copy(new_hbm, new_ref, sem)
    fetch.start()

    def edge_share(own_ref, other_ref):
        own = own_ref[...]
        other = other_ref[...]
        coeff = face(DT_COARSE, jnp.maximum(own, 0.125), other)
        lane = lane_ids(own.shape)
        spread = jnp.zeros_like(own)
        for field in range(SPECIES):
            moved = roll_lanes(coeff, (field - SPECIES) * NZC)
            spread = jnp.where(lane // NZC == field, DIFFUSE[field] * moved, spread)
        return spread * (other - own)

    lower = edge_share(ylo_ref, yl_ref)
    upper = edge_share(yhi_ref, yr_ref)

    lane = lane_ids((BLK, LANES))
    row_id = lax.broadcasted_iota(jnp.int32, (BLK, LANES), 0)
    halves = cells_y // LANES

    def side_share(own_ref, other_ref, exists):
        shares = []
        for half in range(halves):
            own = own_ref[:, half * LANES : (half + 1) * LANES]
            other = other_ref[:, half * LANES : (half + 1) * LANES]
            coeff = face(DT_COARSE, own[PLANES:], other[PLANES:])
            coeff = jnp.where(exists, coeff, 0.0)
            shares.append(
                jnp.concatenate(
                    [
                        (DIFFUSE[field] * coeff)
                        * (
                            other[field * NZC : (field + 1) * NZC]
                            - own[field * NZC : (field + 1) * NZC]
                        )
                        for field in range(SPECIES)
                    ],
                    axis=0,
                )
            )
        return shares

    before = side_share(xlo_ref, xl_ref, me > 0)
    after = side_share(xhi_ref, xr_ref, me < last)
    fetch.wait()
    block_cols = cells_x // BLK
    for column in range(block_cols):
        for plane in range(PLANES):
            row = plane * cells_x + column * BLK
            edge_rows = slice(column * BLK, (column + 1) * BLK)
            for half in range(halves):
                cols = slice(half * LANES, (half + 1) * LANES)
                coarse = new_ref[row : row + BLK, cols]
                if column == 0:
                    share = before[half][plane : plane + 1]
                    coarse = coarse + jnp.where(row_id == 0, share, 0.0)
                if column == block_cols - 1:
                    share = after[half][plane : plane + 1]
                    coarse = coarse + jnp.where(row_id == BLK - 1, share, 0.0)
                if half == 0:
                    share = roll_lanes(lower[edge_rows], -plane)
                    coarse = coarse + jnp.where(lane == 0, share, 0.0)
                if half == halves - 1:
                    share = roll_lanes(upper[edge_rows], LANES - 1 - plane)
                    coarse = coarse + jnp.where(lane == LANES - 1, share, 0.0)
                out_ref[row : row + BLK, cols] = coarse


def place_kernel(
    place_ref, avg_ref, new_ref, out_ref, *, cells_x, cells_y, group, slots
):
    width = slots * BLK
    quarter = AVG_ROWS // FACES
    per_tile = LANES // width
    part = lane_ids((quarter, LANES)) // width
    columns = []
    for tile in range(group * BLK // LANES):
        rows = []
        for index in range(FACES):
            merged = jnp.zeros((quarter, LANES), jnp.float32)
            for place in range(per_tile):
                piece = roll_lanes(avg_ref[tile * per_tile + place], (place - index) * width)
                merged = jnp.where(part == place, piece, merged)
            rows.append(merged)
        columns.append(jnp.concatenate(rows, axis=0))
    high, low = split_pair(jnp.concatenate(columns, axis=1))
    ones = jnp.ones((16, high.shape[1]), jnp.bfloat16)
    stacked = jnp.concatenate([high, low, ones], axis=0)

    halves = cells_y // LANES
    for column in range(cells_x // BLK):
        placed = lax.dot_general(
            stacked,
            selector(place_ref, column, cells_y),
            (((1,), (1,)), ((), ())),
            preferred_element_type=jnp.float32,
        )
        covered = placed[2 * AVG_ROWS : 2 * AVG_ROWS + 8] > 0.5
        for plane in range(PLANES):
            values = (
                placed[plane * BLK : (plane + 1) * BLK]
                + placed[AVG_ROWS + plane * BLK : AVG_ROWS + (plane + 1) * BLK]
            )
            row = plane * cells_x + column * BLK
            for half in range(halves):
                cols = slice(half * LANES, (half + 1) * LANES)
                coarse = new_ref[row : row + BLK, cols]
                out_ref[row : row + BLK, cols] = jnp.where(
                    covered[:, cols], values[:, cols], coarse
                )


VMEM = pl.BlockSpec(memory_space=pltpu.VMEM)
HBM = pl.BlockSpec(memory_space=pltpu.HBM)
PARAMS = pltpu.CompilerParams(vmem_limit_bytes=40 * 1024 * 1024)


def f32(*shape):
    return jax.ShapeDtypeStruct(shape, jnp.float32)


def hbm32(*shape):
    return pltpu.HBM(shape, jnp.float32)


def pinned(*arrays):
    return [pltpu.with_memory_space_constraint(array, pltpu.HBM) for array in arrays]


def shifted(values, axis, step):
    count = lax.axis_size(axis)
    pairs = [(i, i + step) for i in range(count) if 0 <= i + step < count]
    return lax.ppermute(values, axis, pairs)


def exchange(chunks):
    return lax.all_to_all(chunks, "af", split_axis=0, concat_axis=0, tiled=True)


def per_device(
    coarse_state, coarse_kappa, coarse_rate, fine_state, fine_kappa, fine_rate, boxes, cover
):
    af_count = lax.axis_size("af")
    slots = fine_state.shape[0]
    cells_x, cells_y = coarse_state.shape[2:]
    group = af_count * slots
    lanes = group * BLK
    halves = cells_y // LANES
    rows = PLANES * cells_x
    plain = NZC * cells_x
    sizes = dict(cells_x=cells_x, cells_y=cells_y, group=group)

    span = cells_x + 2 * PAD
    new, send, place, xlo, xhi, ylo, yhi = pl.pallas_call(
        functools.partial(strips_kernel, slots=slots, **sizes),
        out_shape=[
            hbm32(rows, cells_y),
            f32(af_count, CHUNK_ROWS, LANES),
            jax.ShapeDtypeStruct((16, lanes), jnp.int32),
        ]
        + [f32(EDGE_ROWS, cells_y)] * 2
        + [f32(cells_x, LANES)] * 2,
        in_specs=[HBM] * 4,
        out_specs=[HBM] + [VMEM] * 6,
        scratch_shapes=[
            pltpu.VMEM((2, boxes.shape[0]), jnp.int32),
            pltpu.VMEM((rows, cells_y), jnp.float32),
            pltpu.VMEM((plain, cells_y), jnp.float32),
            pltpu.VMEM((plain, cells_y), jnp.float32),
            pltpu.VMEM((rows, cells_y), jnp.float32),
            pltpu.VMEM(((SPECIES + 1) * halves * NZC * span, LANES), jnp.float32),
            pltpu.VMEM((rows * halves, LANES), jnp.float32),
            pltpu.SemaphoreType.DMA((4,)),
        ],
        compiler_params=PARAMS,
        name="strips",
    )(
        *pinned(
            boxes.T,
            coarse_state.reshape(rows, cells_y),
            coarse_kappa.reshape(plain, cells_y),
            coarse_rate.reshape(plain, cells_y),
        )
    )

    strips = exchange(send)

    xlo_sent, xhi_sent = pl.pallas_call(
        hand_on_kernel,
        out_shape=[f32(EDGE_ROWS, cells_y)] * 2,
        in_specs=[VMEM] * 2,
        out_specs=[VMEM] * 2,
        compiler_params=pltpu.CompilerParams(vmem_limit_bytes=1024 * 1024),
        name="hand_on",
    )(xlo, xhi)
    xl = shifted(xhi_sent, "af", 1)
    xr = shifted(xlo_sent, "af", -1)

    kept = [hbm32(slots * size, LANES) for size in (FIELD_ROWS, COEFF_ROWS, UPWARD_ROWS)]
    kept_scratch = [pltpu.VMEM((slots * size, LANES), jnp.float32)
        for size in (FIELD_ROWS, COEFF_ROWS, UPWARD_ROWS)]
    fields, coeffs, upward = pl.pallas_call(
        functools.partial(prepare_kernel, slots=slots),
        out_shape=kept,
        in_specs=[VMEM] + [HBM] * 3,
        out_specs=[HBM] * 3,
        scratch_shapes=kept_scratch
        + [
            pltpu.VMEM(fine_state.shape, jnp.float32),
            pltpu.VMEM(fine_kappa.shape, jnp.float32),
            pltpu.VMEM(fine_rate.shape, jnp.float32),
            pltpu.VMEM((slots * FIELD_ROWS, LANES), jnp.float32),
            pltpu.VMEM((slots * UPWARD_ROWS, LANES), jnp.float32),
            pltpu.SemaphoreType.DMA((3, slots)),
            pltpu.SemaphoreType.DMA((3, slots)),
        ],
        compiler_params=PARAMS,
        name="prepare",
    )(xlo_sent, *pinned(fine_state, fine_kappa, fine_rate))

    chunk = (AVG_ROWS // FACES, LANES)
    fine_out, averages = pl.pallas_call(
        functools.partial(finish_kernel, slots=slots),
        out_shape=[hbm32(*fine_state.shape), hbm32(af_count, *chunk)],
        in_specs=[VMEM] + [HBM] * 3 + [VMEM] * 2,
        out_specs=[HBM] * 2,
        scratch_shapes=kept_scratch
        + [
            pltpu.VMEM((2 * LANES, EDGE * EDGE), jnp.bfloat16),
            pltpu.VMEM((2 * SPECIES * FZ, STRIP_ROWS), jnp.bfloat16),
            pltpu.VMEM((2 * LANES, LANES), jnp.bfloat16),
            pltpu.VMEM(chunk, jnp.float32),
            pltpu.VMEM((slots * FIELD_ROWS, LANES), jnp.float32),
            pltpu.VMEM((SPECIES * TILES * FZ, LANES), jnp.float32),
            pltpu.VMEM((SPECIES * TILES * FZ, LANES), jnp.float32),
            pltpu.VMEM(fine_state.shape, jnp.float32),
            pltpu.SemaphoreType.DMA((slots,)),
            pltpu.SemaphoreType.DMA((3, slots)),
            pltpu.SemaphoreType.DMA((af_count,)),
        ],
        compiler_params=PARAMS,
        name="finish",
    )(strips, *pinned(fields, coeffs, upward), xl, xr)

    arrived = exchange(averages)

    yl = shifted(yhi, "col", 1)
    yr = shifted(ylo, "col", -1)
    whole = pl.pallas_call(
        functools.partial(edges_kernel, cells_x=cells_x, cells_y=cells_y),
        out_shape=f32(rows, cells_y),
        in_specs=[HBM] + [VMEM] * 8,
        out_specs=VMEM,
        scratch_shapes=[pltpu.VMEM((rows, cells_y), jnp.float32), pltpu.SemaphoreType.DMA],
        compiler_params=PARAMS,
        name="edges",
    )(*pinned(new), xlo, xhi, ylo, yhi, xl, xr, yl, yr)

    placed = pl.pallas_call(
        functools.partial(place_kernel, slots=slots, **sizes),
        out_shape=f32(rows, cells_y),
        in_specs=[VMEM] * 3,
        out_specs=VMEM,
        compiler_params=PARAMS,
        name="place",
    )(place, arrived, whole)
    return (placed.reshape(coarse_state.shape), fine_out)


def solution(mesh):
    return jax.shard_map(
        per_device,
        mesh=mesh,
        in_specs=(
            P(None, None, "af", "col"),
            P(None, "af", "col"),
            P(None, "af", "col"),
            P(("col", "af"), None, None, None),
            P(("col", "af"), None, None),
            P(("col", "af"), None, None),
            P(),
            P(),
        ),
        out_specs=(P(None, None, "af", "col"), P(("col", "af"), None, None, None)),
        check_vma=False,
    )
```

```python
import functools

import jax
import jax.numpy as jnp
from jax import lax
from jax.experimental import pallas as pl
from jax.experimental.pallas import tpu as pltpu
from jax.sharding import PartitionSpec as P

NZC = 8
RATIO = 4
BLK = 8
SPECIES = 3
EDGE = BLK * RATIO
FZ = NZC * RATIO
LANES = 128
TILES = EDGE * EDGE // LANES
ZTILES = FZ // 8
STRIDE = 48
PAD = 8
FACES = 4
PLANES = SPECIES * NZC
STRIP_ROWS = 2 * PLANES
AVG_ROWS = PLANES * BLK
GROUPS = LANES // EDGE
NEXT_X, NEXT_Y, PREV_Y, RATE, KEEP, SCALE = 0, 9, 17, 25, 33, 57
FIELD_ROWS = SPECIES * TILES * STRIDE
COEFF_ROWS = 65 * FZ
UPWARD_ROWS = TILES * STRIDE
EDGE_ROWS = PLANES + NZC
BESIDE_ROWS = 2 * NZC
CHUNK_ROWS = STRIP_ROWS + BESIDE_ROWS

DT_COARSE = 1.0 / 28.0
DIFFUSE = (1.0, 0.7, 0.45)
SIGNS = (-1.0, -1.0, 1.0)
FINE_SCALE = RATIO * RATIO * DT_COARSE / RATIO
DT_FINE = DT_COARSE / RATIO


def lane_ids(shape):
    return lax.broadcasted_iota(jnp.int32, shape, len(shape) - 1)


def roll_lanes(values, shift):
    width = values.shape[-1]
    shift = shift % width
    return values if shift == 0 else pltpu.roll(values, shift, values.ndim - 1)


def split_pair(values):
    high = values.astype(jnp.bfloat16)
    low = (values - high.astype(jnp.float32)).astype(jnp.bfloat16)
    return high, low


def face(scale, one, other):
    summed = one + other
    inverse = pl.reciprocal(summed, approx=True)
    inverse = inverse * (2.0 - summed * inverse)
    return (2.0 * scale) * (one * other) * inverse


def start_all(copies):
    for copy in copies:
        copy.start()


def selector(place_ref, column, cells_y):
    wanted = jnp.where(place_ref[0:8, :] == column, place_ref[8:16, :], -1)
    row = lax.broadcasted_iota(jnp.int32, wanted.shape, 0)
    return jnp.concatenate(
        [jnp.where(row + 8 * at == wanted, 1.0, 0.0) for at in range(cells_y // 8)], axis=0
    ).astype(jnp.bfloat16)


def strips_kernel(
    boxes_hbm,
    state_hbm,
    kappa_hbm,
    rate_hbm,
    new_hbm,
    send_ref,
    place_ref,
    xlo_ref,
    xhi_ref,
    ylo_ref,
    yhi_ref,
    boxes_ref,
    state_ref,
    kappa_ref,
    rate_ref,
    new_ref,
    padded,
    fresh,
    sems,
    *,
    cells_x,
    cells_y,
    group,
    slots,
):
    pairs = (
        (boxes_hbm, boxes_ref),
        (kappa_hbm, kappa_ref),
        (state_hbm, state_ref),
        (rate_hbm, rate_ref),
    )
    copies = [
        pltpu.make_async_copy(source, target, sems.at[index])
        for index, (source, target) in enumerate(pairs)
    ]
    start_all(copies)

    patches = boxes_ref.shape[1]
    lanes = group * BLK
    base_patch = lax.axis_index("col") * group
    member = lax.broadcasted_iota(jnp.int32, (patches, lanes), 0) - base_patch
    spread = jnp.where(member == lane_ids((patches, lanes)) // BLK, 1.0, 0.0).astype(jnp.bfloat16)
    first_col = lax.axis_index("af") * (cells_x // BLK)
    first_cell = lax.axis_index("col") * cells_y
    copies[0].wait()
    boxes = boxes_ref[...].astype(jnp.float32)
    stacked = jnp.concatenate(
        [jnp.broadcast_to(boxes[row : row + 1], (8, patches)) for row in range(2)], axis=0
    )
    found = jnp.dot(
        stacked.astype(jnp.bfloat16), spread, preferred_element_type=jnp.float32
    ).astype(jnp.int32)
    place_ref[0:8, :] = found[0:8] - first_col
    place_ref[8:16, :] = found[8:16] * BLK - first_cell + lane_ids((8, lanes)) % BLK

    halves = cells_y // LANES
    span = cells_x + 2 * PAD
    nothing = jnp.zeros((PAD, LANES), jnp.float32)

    def base(field, half, z):
        return ((field * halves + half) * NZC + z) * span

    for copy in copies[1:]:
        copy.wait()
    for field in range(SPECIES + 1):
        for half in range(halves):
            cols = pl.ds(half * LANES, LANES)
            for z in range(NZC):
                if field < SPECIES:
                    start = (field * NZC + z) * cells_x
                    plane = state_ref[start : start + cells_x, cols]
                else:
                    plane = kappa_ref[z * cells_x : (z + 1) * cells_x, cols]
                at = base(field, half, z)
                padded[at : at + PAD, :] = nothing
                padded[at + PAD : at + PAD + cells_x, :] = plane
                padded[at + PAD + cells_x : at + span, :] = nothing

    lane = lane_ids((cells_x, LANES))
    row_id = lax.broadcasted_iota(jnp.int32, (cells_x, LANES), 0)

    low = jnp.zeros((cells_x, LANES), jnp.float32)
    high = jnp.zeros((cells_x, LANES), jnp.float32)
    for plane in range(PLANES + NZC):
        field, z = divmod(plane, NZC)
        at = base(field, 0, z) + PAD
        first = padded[at : at + cells_x, :]
        at = base(field, halves - 1, z) + PAD
        last = padded[at : at + cells_x, :]
        low = jnp.where(lane == plane, roll_lanes(first, plane), low)
        high = jnp.where(lane == plane, roll_lanes(last, plane + 1), high)
    ylo_ref[...] = low
    yhi_ref[...] = high

    def load(field, half, z, shift):
        at = base(field, half, z) + PAD + shift
        return padded[at : at + cells_x, :]

    def neighbours(field, half, z):
        here = load(field, half, z, 0)
        after = roll_lanes(here, -1)
        if half + 1 < halves:
            after = jnp.where(
                lane == LANES - 1, roll_lanes(load(field, half + 1, z, 0), -1), after
            )
        before = roll_lanes(here, 1)
        if half > 0:
            before = jnp.where(lane == 0, roll_lanes(load(field, half - 1, z, 0), 1), before)
        found = [after, before, load(field, half, z, 1), load(field, half, z, -1)]
        if z + 1 < NZC:
            found.append(load(field, half, z + 1, 0))
        if z > 0:
            found.append(load(field, half, z - 1, 0))
        return found

    for z in range(NZC):
        for half in range(halves):
            cols = pl.ds(half * LANES, LANES)
            conduct = load(SPECIES, half, z, 0)
            coeffs = [face(DT_COARSE, conduct, other) for other in neighbours(SPECIES, half, z)]
            if half == halves - 1:
                coeffs[0] = jnp.where(lane == LANES - 1, 0.0, coeffs[0])
            if half == 0:
                coeffs[1] = jnp.where(lane == 0, 0.0, coeffs[1])
            coeffs[2] = jnp.where(row_id == cells_x - 1, 0.0, coeffs[2])
            coeffs[3] = jnp.where(row_id == 0, 0.0, coeffs[3])
            centers = [load(field, half, z, 0) for field in range(SPECIES)]
            forward = (DT_COARSE * rate_ref[z * cells_x : (z + 1) * cells_x, cols]) * (
                centers[0] * centers[1] - centers[2]
            )
            for field in range(SPECIES):
                center = centers[field]
                flux = None
                for coeff, other in zip(coeffs, neighbours(field, half, z)):
                    term = coeff * (other - center)
                    flux = term if flux is None else flux + term
                start = (field * NZC + z) * cells_x
                result = center + DIFFUSE[field] * flux + SIGNS[field] * forward
                new_ref[start : start + cells_x, cols] = result
                start = ((field * halves + half) * NZC + z) * cells_x
                fresh[start : start + cells_x, :] = result

    keep_new = pltpu.make_async_copy(new_ref, new_hbm, sems.at[0])
    keep_new.start()

    def old_row(field, half, row):
        return padded[pl.ds(base(field, half, 0) + PAD + row, NZC, stride=span), :]

    def edge_at(row):
        return jnp.concatenate(
            [
                jnp.concatenate([old_row(field, half, row) for field in range(SPECIES + 1)], axis=0)
                for half in range(halves)
            ],
            axis=1,
        )

    def rows_at(row):
        columns = []
        for half in range(halves):
            pieces = [old_row(field, half, row) for field in range(SPECIES)]
            for field in range(SPECIES):
                start = (field * halves + half) * NZC * cells_x
                pieces.append(fresh[pl.ds(start + row, NZC, stride=cells_x), :])
            columns.append(jnp.concatenate(pieces, axis=0))
        return jnp.concatenate(columns, axis=1)

    block_cols = cells_x // BLK
    spot = lane_ids((STRIP_ROWS, cells_y)) % BLK
    lower_y = []
    upper_y = []
    for column in range(block_cols):
        below = jnp.zeros((STRIP_ROWS, cells_y), jnp.float32)
        above = jnp.zeros((STRIP_ROWS, cells_y), jnp.float32)
        for x in range(BLK):
            turned = roll_lanes(rows_at(column * BLK + x), x + 1)
            below = jnp.where(spot == x, turned, below)
            above = jnp.where(spot == (x + 1) % BLK, turned, above)
        lower_y.append(below)
        upper_y.append(roll_lanes(above, -1 - BLK))

    first_row = edge_at(0)
    last_row = edge_at(cells_x - 1)
    xlo_ref[...] = first_row
    xhi_ref[...] = last_row
    place = lane_ids((NZC, cells_y)) % BLK
    ones = jnp.ones((NZC, cells_y), jnp.float32)

    def field_of(row, field):
        return row[field * NZC : (field + 1) * NZC]

    def corners(row, fields, first_at):
        found = jnp.zeros((NZC, cells_y), jnp.float32)
        for order, field in enumerate(fields):
            at = first_at + 2 * order
            values = field_of(row, field)
            found = jnp.where(place == at, roll_lanes(values, at + 1), found)
            found = jnp.where(place == at + 1, roll_lanes(values, at + 1 - BLK), found)
        return found

    every = range(SPECIES)

    def near(row):
        own = [(field, field_of(row, field)) for field in range(SPECIES + 1)]
        return own + [(5, corners(row, [SPECIES], 0))]

    def far(row):
        return [
            (4, field_of(row, SPECIES)),
            (5, corners(row, every, 2)),
            (6, corners(row, [SPECIES], 0)),
        ]

    extra_members = {
        -1: far(first_row),
        0: near(first_row),
        block_cols - 1: near(last_row) + [(7, ones)],
        block_cols: far(last_row),
    }

    faces = [None] * (3 * FACES)

    def add(index, part):
        faces[index] = part if faces[index] is None else faces[index] + part

    for column in range(-1, block_cols + 1):
        members = []
        if column >= 1:
            members.append((0, rows_at(column * BLK - 1)))
        if column < block_cols - 1:
            members.append((1, rows_at(column * BLK + BLK)))
        if 0 <= column < block_cols:
            members.append((2, lower_y[column]))
            members.append((3, upper_y[column]))
        for index, rows in extra_members.get(column, []):
            members.append((FACES + index, rows))
        operands = []
        for _, rows in members:
            operands.extend(split_pair(rows))
        moved = jnp.dot(
            jnp.concatenate(operands, axis=0),
            selector(place_ref, column, cells_y),
            preferred_element_type=jnp.float32,
        )
        at = 0
        for index, rows in members:
            size = rows.shape[0]
            add(index, moved[at : at + size] + moved[at + size : at + 2 * size])
            at += 2 * size

    width = slots * BLK
    for target in range(group // slots):
        first = target * width
        tile = first // LANES * LANES
        for start, size, kind in (
            (0, STRIP_ROWS, 0),
            (STRIP_ROWS, NZC, FACES),
            (STRIP_ROWS + NZC, NZC, 2 * FACES),
        ):
            part = lane_ids((size, LANES)) // width
            chunk = jnp.zeros((size, LANES), jnp.float32)
            for index in range(FACES):
                piece = faces[kind + index][:, tile : tile + LANES]
                chunk = jnp.where(
                    part == index, roll_lanes(piece, index * width - (first - tile)), chunk
                )
            send_ref[target, start : start + size, :] = chunk
    keep_new.wait()


def ghost_table(tile):
    lane = lane_ids((BLK, LANES))
    pos = lax.broadcasted_iota(jnp.int32, (BLK, LANES), 0)
    x = tile + TILES * (lane // EDGE)
    y = lane % EDGE
    along_y = y // RATIO == pos
    along_x = x // RATIO == pos
    seen = (
        (x == 0) & along_y,
        (x == EDGE - 1) & along_y,
        (y == 0) & along_x,
        (y == EDGE - 1) & along_x,
    )
    nothing = jnp.zeros((LANES // FACES - BLK, LANES), jnp.float32)
    rows = []
    for where in seen:
        rows.extend([jnp.where(where, 1.0, 0.0), nothing])
    return jnp.concatenate(rows + rows, axis=0).astype(jnp.bfloat16)


def plane_table():
    shape = (2 * SPECIES * FZ, STRIP_ROWS)
    rows = lax.broadcasted_iota(jnp.int32, shape, 0)
    return jnp.where(rows // RATIO == lane_ids(shape), 1.0, 0.0).astype(jnp.bfloat16)


def mean_table():
    shape = (2 * LANES, LANES)
    rows = lax.broadcasted_iota(jnp.int32, shape, 0) % LANES
    lane = lane_ids(shape)
    same = (rows // EDGE == lane // EDGE) & (rows % EDGE // RATIO == lane % BLK)
    return jnp.where(same, 1.0 / RATIO**3, 0.0).astype(jnp.bfloat16)


def complete_strips(gathered):
    width = LANES // FACES
    own = gathered[STRIP_ROWS : STRIP_ROWS + NZC]
    beside = gathered[STRIP_ROWS + NZC : STRIP_ROWS + 2 * NZC]
    lane = lane_ids((NZC, LANES))
    part = lane // width
    pos = lane % BLK
    flag = jnp.where(part == FACES - 1, beside, 0.0)
    flag = flag + roll_lanes(flag, width)
    upper = flag + roll_lanes(flag, 2 * width) > 0.5

    def coefficient(one, other):
        return face(DT_COARSE, jnp.maximum(one, 0.125), jnp.maximum(other, 0.125))

    block = coefficient(roll_lanes(own, width), beside)
    corner = coefficient(beside, roll_lanes(beside, -width))
    added = []
    for field in range(SPECIES):
        old = gathered[field * NZC : (field + 1) * NZC]
        there = jnp.where(upper, roll_lanes(old, -width), old)
        across = DIFFUSE[field] * block * (roll_lanes(own, -field * width) - there)
        below = jnp.where(upper, roll_lanes(old, -width - (BLK - 1)), roll_lanes(old, -width))
        above = jnp.where(
            upper, roll_lanes(old, -2 * width - (BLK - 2)), roll_lanes(old, 1 - 2 * width)
        )
        here = jnp.where(pos == 0, below, above)
        along = DIFFUSE[field] * corner * (roll_lanes(beside, -2 - 2 * field) - here)
        share = jnp.where((part == 0) & ~upper, across, 0.0)
        share = jnp.where((part == 1) & upper, roll_lanes(across, width), share)
        for index in range(2):
            for at, chosen in ((0, ~upper), (BLK - 1, upper)):
                moved = roll_lanes(along, (1 + index) * width + at - index)
                share = jnp.where((part == 2 + index) & (pos == at) & chosen, moved, share)
        added.append(share)
    new = gathered[PLANES:STRIP_ROWS] + jnp.concatenate(added, axis=0)
    return gathered[:PLANES], new


def aligned(start, size):
    return pl.ds(pl.multiple_of(start, 8), size)


def padded_at(block, ztile):
    return block * STRIDE + PAD + 8 * ztile


def advance(source, target, coeffs, upward, slot, from_rows, to_rows, ztile, ghosts):
    def value(field, tile, shift):
        start = from_rows + padded_at(field * TILES + tile, ztile) + shift
        return source[aligned(start, 8) if shift == 0 else pl.ds(start, 8), :]

    def get(kind, tile):
        return coeffs[aligned(slot * COEFF_ROWS + (kind + tile) * FZ + 8 * ztile, 8), :]

    fields = range(SPECIES)
    center = [value(field, 0, 0) for field in fields]
    behind = [roll_lanes(value(field, TILES - 1, 0), EDGE) for field in fields]
    beyond = [roll_lanes(center[field], -EDGE) for field in fields]
    prev_x = get(NEXT_X, 0)
    for tile in range(TILES):
        if tile + 1 < TILES:
            ahead = [value(field, tile + 1, 0) for field in fields]
        else:
            ahead = beyond
        next_x, next_y, prev_y, rate = [
            get(kind, tile) for kind in (NEXT_X + 1, NEXT_Y, PREV_Y, RATE)
        ]
        base = slot * UPWARD_ROWS + padded_at(tile, ztile)
        next_z = upward[aligned(base, 8), :]
        prev_z = upward[pl.ds(base - 1, 8), :]
        forward = rate * (center[0] * center[1] - center[2])
        for field in fields:
            own = center[field]
            flux = (next_x * ahead[field] + prev_x * behind[field]) + (
                next_y * roll_lanes(own, -1) + prev_y * roll_lanes(own, 1)
            )
            flux = flux + (next_z * value(field, tile, 1) + prev_z * value(field, tile, -1))
            share = ghosts(field, tile)
            if share is not None:
                flux = flux + share
            if DIFFUSE[field] != 1.0:
                flux = DIFFUSE[field] * flux
            result = get(KEEP + field * TILES, tile) * own + flux
            result = result - forward if SIGNS[field] < 0 else result + forward
            target[aligned(to_rows + padded_at(field * TILES + tile, ztile), 8), :] = result
        behind, center, prev_x = center, ahead, next_x


def regroup(tiles):
    lane = lane_ids((8, LANES))
    low = lane < LANES // 2
    even = lane // EDGE % 2 == 0

    def turn(one, two, three, four):
        one, three = (
            jnp.where(low, one, roll_lanes(three, LANES // 2)),
            jnp.where(low, roll_lanes(one, LANES // 2), three),
        )
        two, four = (
            jnp.where(low, two, roll_lanes(four, LANES // 2)),
            jnp.where(low, roll_lanes(two, LANES // 2), four),
        )
        return (
            jnp.where(even, one, roll_lanes(two, EDGE)),
            jnp.where(even, roll_lanes(one, -EDGE), two),
            jnp.where(even, three, roll_lanes(four, EDGE)),
            jnp.where(even, roll_lanes(three, -EDGE), four),
        )

    return turn(*tiles[0::2]) + turn(*tiles[1::2])


def regroup_back(tiles):
    one = regroup([tiles[order] for order in (0, 4, 1, 5, 2, 6, 3, 7)])
    return tuple(one[order] for order in (0, 4, 1, 5, 2, 6, 3, 7))


def clear_pads(ref):
    edge = jnp.zeros((PAD, LANES), jnp.float32)

    def body(block, carry):
        ref[aligned(block * STRIDE, PAD), :] = edge
        ref[aligned(block * STRIDE + PAD + FZ, PAD), :] = edge
        return carry

    lax.fori_loop(0, ref.shape[0] // STRIDE, body, 0)


def hand_on_kernel(low_ref, high_ref, low_out, high_out):
    low_out[...] = low_ref[...]
    high_out[...] = high_ref[...]


def prepare_kernel(
    after_ref,
    state_hbm,
    kappa_hbm,
    rate_hbm,
    fields_hbm,
    coeffs_hbm,
    upward_hbm,
    fields_ref,
    coeffs,
    upward,
    state_ref,
    kappa_ref,
    rate_ref,
    first,
    conduct,
    sems,
    out_sems,
    *,
    slots,
):
    def loads(slot):
        return [
            pltpu.make_async_copy(source.at[slot], target.at[slot], sems.at[order, slot])
            for order, (source, target) in enumerate(
                ((kappa_hbm, kappa_ref), (rate_hbm, rate_ref), (state_hbm, state_ref))
            )
        ]

    for slot in range(slots):
        start_all(loads(slot))

    def stores(slot):
        return [
            pltpu.make_async_copy(
                source.at[aligned(slot * size, size)],
                target.at[aligned(slot * size, size)],
                out_sems.at[order, slot],
            )
            for order, (source, target, size) in enumerate(
                (
                    (fields_ref, fields_hbm, FIELD_ROWS),
                    (coeffs, coeffs_hbm, COEFF_ROWS),
                    (upward, upward_hbm, UPWARD_ROWS),
                )
            )
        ]

    for ref in (fields_ref, upward, first, conduct):
        clear_pads(ref)

    lane = lane_ids((8, LANES))
    column = lane % EDGE
    side_y = jnp.where((column == 0) | (column == EDGE - 1), 1.0, 0.0)

    def one_patch(slot, carry):
        for copy in loads(slot):
            copy.wait()

        def regrouped(ref, index, ztile):
            rows = pl.ds(8 * ztile, 8)
            return regroup(
                [ref[(*index, rows, pl.ds(tile * LANES, LANES))] for tile in range(TILES)]
            )

        for ztile in range(ZTILES):
            for field in range(SPECIES):
                for tile, values in enumerate(regrouped(state_ref, (slot, field), ztile)):
                    start = slot * FIELD_ROWS + padded_at(field * TILES + tile, ztile)
                    first[aligned(start, 8), :] = values
            for tile, values in enumerate(regrouped(kappa_ref, (slot,), ztile)):
                conduct[aligned(slot * UPWARD_ROWS + padded_at(tile, ztile), 8), :] = values

        def keep(kind, tile, ztile, values):
            row = slot * COEFF_ROWS + (kind + tile) * FZ + 8 * ztile
            coeffs[aligned(row, 8), :] = values

        for ztile in range(ZTILES):

            def here(tile, shift):
                start = slot * UPWARD_ROWS + padded_at(tile, ztile) + shift
                return conduct[aligned(start, 8) if shift == 0 else pl.ds(start, 8), :]

            center = here(0, 0)
            beyond = roll_lanes(center, -EDGE)
            wrapped = face(FINE_SCALE, here(TILES - 1, 0), beyond)
            wrapped = jnp.where(lane < LANES - EDGE, wrapped, 0.0)
            prev_x = roll_lanes(wrapped, EDGE)
            keep(NEXT_X, 0, ztile, prev_x)
            rates = regrouped(rate_ref, (slot,), ztile)
            for tile in range(TILES):
                if tile + 1 < TILES:
                    ahead = here(tile + 1, 0)
                    next_x = face(FINE_SCALE, center, ahead)
                else:
                    ahead, next_x = beyond, wrapped
                next_y = jnp.where(
                    column < EDGE - 1, face(FINE_SCALE, center, roll_lanes(center, -1)), 0.0
                )
                prev_y = roll_lanes(next_y, 1)
                next_z = face(FINE_SCALE, center, here(tile, 1))
                prev_z = face(FINE_SCALE, center, here(tile, -1))
                sides = side_y
                if tile == 0:
                    sides = sides + jnp.where(lane < EDGE, 1.0, 0.0)
                if tile == TILES - 1:
                    sides = sides + jnp.where(lane >= LANES - EDGE, 1.0, 0.0)
                scale = FINE_SCALE * center
                total = (next_x + prev_x) + (next_y + prev_y) + (next_z + prev_z) + sides * scale
                upward[aligned(slot * UPWARD_ROWS + padded_at(tile, ztile), 8), :] = next_z
                keep(NEXT_X + 1, tile, ztile, next_x)
                keep(NEXT_Y, tile, ztile, next_y)
                keep(PREV_Y, tile, ztile, prev_y)
                keep(RATE, tile, ztile, DT_FINE * rates[tile])
                for field in range(SPECIES):
                    keep(KEEP + field * TILES, tile, ztile, 1.0 - DIFFUSE[field] * total)
                keep(SCALE, tile, ztile, scale)
                center, prev_x = ahead, next_x

        for ztile in range(ZTILES):
            advance(
                first,
                fields_ref,
                coeffs,
                upward,
                slot,
                slot * FIELD_ROWS,
                slot * FIELD_ROWS,
                ztile,
                lambda field, tile: None,
            )
        start_all(stores(slot))
        return carry

    lax.fori_loop(0, slots, one_patch, 0)
    for slot in range(slots):
        for copy in stores(slot):
            copy.wait()


def finish_kernel(
    strips_ref,
    fields_hbm,
    coeffs_hbm,
    upward_hbm,
    xl_ref,
    xr_ref,
    out_hbm,
    avg_hbm,
    fields_ref,
    coeffs,
    upward,
    ghost_ref,
    plane_ref,
    mean_ref,
    avg_ref,
    first,
    share,
    drift,
    staged,
    sums,
    sems,
    in_sems,
    avg_sems,
    *,
    slots,
):
    sources = strips_ref.shape[0]

    def loads(slot):
        return [
            pltpu.make_async_copy(
                source.at[aligned(slot * size, size)],
                target.at[aligned(slot * size, size)],
                in_sems.at[order, slot],
            )
            for order, (source, target, size) in enumerate(
                (
                    (fields_hbm, fields_ref, FIELD_ROWS),
                    (coeffs_hbm, coeffs, COEFF_ROWS),
                    (upward_hbm, upward, UPWARD_ROWS),
                )
            )
        ]

    start_all(loads(0))
    clear_pads(first)
    for tile in range(TILES):
        ghost_ref[:, tile * LANES : (tile + 1) * LANES] = ghost_table(tile)
    plane_ref[...] = plane_table()
    mean_ref[...] = mean_table()

    gathered = strips_ref[0]
    for source in range(1, sources):
        gathered = gathered + strips_ref[source]
    old, new = complete_strips(gathered)
    gathered = jnp.concatenate([old, (new - old) * (1.0 / RATIO)], axis=0)
    quarter = AVG_ROWS // FACES
    slot_of = lane_ids((quarter, LANES)) // BLK % slots

    def send_out(slot):
        return pltpu.make_async_copy(staged.at[slot], out_hbm.at[slot], sems.at[slot])

    def one_patch(slot, carry):
        for copy in loads(slot):
            copy.wait()

        @pl.when(slot + 1 < slots)
        def _():
            start_all(loads(slot + 1))

        turned = pltpu.roll(gathered, (LANES - slot * BLK) % LANES, 1)
        stretched = jnp.dot(
            plane_ref[...],
            jnp.concatenate(split_pair(turned), axis=1),
            preferred_element_type=jnp.float32,
        ).astype(jnp.bfloat16)
        base = slot * FIELD_ROWS
        scales = slot * COEFF_ROWS
        for tile in range(TILES):
            ghosts = jnp.dot(
                stretched,
                ghost_ref[:, tile * LANES : (tile + 1) * LANES],
                preferred_element_type=jnp.float32,
            )
            scale = coeffs[aligned(scales + (SCALE + tile) * FZ, FZ), :]
            for field in range(SPECIES):
                row = (field * TILES + tile) * FZ
                old = scale * ghosts[field * FZ : (field + 1) * FZ]
                step = scale * ghosts[(SPECIES + field) * FZ : (SPECIES + field + 1) * FZ]
                drift[row : row + FZ, :] = step
                share[row : row + FZ, :] = old + step
                spot = aligned(base + padded_at(field * TILES + tile, 0), FZ)
                fields_ref[spot, :] = fields_ref[spot, :] + DIFFUSE[field] * old

        for step in range(1, RATIO):
            source, target = (fields_ref, first) if step % 2 else (first, fields_ref)
            for ztile in range(ZTILES):

                def ghosts(field, tile):
                    spot = pl.ds((field * TILES + tile) * FZ + 8 * ztile, 8)
                    value = share[spot, :]
                    if step + 1 < RATIO:
                        share[spot, :] = value + drift[spot, :]
                    return value

                advance(source, target, coeffs, upward, slot, base, base, ztile, ghosts)

        for field in range(SPECIES):
            for ztile in range(ZTILES):
                values = [
                    first[aligned(base + padded_at(field * TILES + tile, ztile), 8), :]
                    for tile in range(TILES)
                ]
                for tile, native in enumerate(regroup_back(values)):
                    staged[slot, field, pl.ds(8 * ztile, 8), pl.ds(tile * LANES, LANES)] = native
        send_out(slot).start()

        for field in range(SPECIES):
            for part in range(2):
                pieces = [
                    first[aligned(base + padded_at(field * TILES + part * RATIO + x, 0), FZ), :]
                    for x in range(RATIO)
                ]
                row = (field * 2 + part) * FZ
                sums[row : row + FZ, :] = (pieces[0] + pieces[1]) + (pieces[2] + pieces[3])
        parts = []
        for index in range(SPECIES * 2):
            pieces = [
                sums[pl.ds(index * FZ + z, NZC, stride=RATIO), :] for z in range(RATIO)
            ]
            parts.append((pieces[0] + pieces[1]) + (pieces[2] + pieces[3]))
        means = jnp.dot(
            jnp.concatenate(split_pair(jnp.concatenate(parts, axis=0)), axis=1),
            mean_ref[...],
            preferred_element_type=jnp.float32,
        )
        chunk = jnp.where(slot_of == slot, means, avg_ref[...])
        avg_ref[...] = chunk
        return carry

    avg_ref[...] = jnp.zeros((quarter, LANES), jnp.float32)
    lax.fori_loop(0, slots, one_patch, 0)
    copies = [
        pltpu.make_async_copy(avg_ref, avg_hbm.at[target], avg_sems.at[target])
        for target in range(sources)
    ]
    start_all(copies)
    for copy in copies:
        copy.wait()
    for slot in range(slots):
        send_out(slot).wait()


def edges_kernel(
    new_hbm,
    xlo_ref,
    xhi_ref,
    ylo_ref,
    yhi_ref,
    xl_ref,
    xr_ref,
    yl_ref,
    yr_ref,
    out_ref,
    new_ref,
    sem,
    *,
    cells_x,
    cells_y,
):
    me = lax.axis_index("af")
    last = lax.axis_size("af") - 1
    fetch = pltpu.make_async_copy(new_hbm, new_ref, sem)
    fetch.start()

    def edge_share(own_ref, other_ref):
        own = own_ref[...]
        other = other_ref[...]
        coeff = face(DT_COARSE, jnp.maximum(own, 0.125), other)
        lane = lane_ids(own.shape)
        spread = jnp.zeros_like(own)
        for field in range(SPECIES):
            moved = roll_lanes(coeff, (field - SPECIES) * NZC)
            spread = jnp.where(lane // NZC == field, DIFFUSE[field] * moved, spread)
        return spread * (other - own)

    lower = edge_share(ylo_ref, yl_ref)
    upper = edge_share(yhi_ref, yr_ref)

    lane = lane_ids((BLK, LANES))
    row_id = lax.broadcasted_iota(jnp.int32, (BLK, LANES), 0)
    halves = cells_y // LANES

    def side_share(own_ref, other_ref, exists):
        shares = []
        for half in range(halves):
            own = own_ref[:, half * LANES : (half + 1) * LANES]
            other = other_ref[:, half * LANES : (half + 1) * LANES]
            coeff = face(DT_COARSE, own[PLANES:], other[PLANES:])
            coeff = jnp.where(exists, coeff, 0.0)
            shares.append(
                jnp.concatenate(
                    [
                        (DIFFUSE[field] * coeff)
                        * (
                            other[field * NZC : (field + 1) * NZC]
                            - own[field * NZC : (field + 1) * NZC]
                        )
                        for field in range(SPECIES)
                    ],
                    axis=0,
                )
            )
        return shares

    before = side_share(xlo_ref, xl_ref, me > 0)
    after = side_share(xhi_ref, xr_ref, me < last)
    fetch.wait()
    block_cols = cells_x // BLK
    for column in range(block_cols):
        for plane in range(PLANES):
            row = plane * cells_x + column * BLK
            edge_rows = slice(column * BLK, (column + 1) * BLK)
            for half in range(halves):
                cols = slice(half * LANES, (half + 1) * LANES)
                coarse = new_ref[row : row + BLK, cols]
                if column == 0:
                    share = before[half][plane : plane + 1]
                    coarse = coarse + jnp.where(row_id == 0, share, 0.0)
                if column == block_cols - 1:
                    share = after[half][plane : plane + 1]
                    coarse = coarse + jnp.where(row_id == BLK - 1, share, 0.0)
                if half == 0:
                    share = roll_lanes(lower[edge_rows], -plane)
                    coarse = coarse + jnp.where(lane == 0, share, 0.0)
                if half == halves - 1:
                    share = roll_lanes(upper[edge_rows], LANES - 1 - plane)
                    coarse = coarse + jnp.where(lane == LANES - 1, share, 0.0)
                out_ref[row : row + BLK, cols] = coarse


def place_kernel(
    place_ref, avg_ref, new_ref, out_ref, placed_ref, *, cells_x, cells_y, group, slots
):
    width = slots * BLK
    quarter = AVG_ROWS // FACES
    per_tile = LANES // width
    part = lane_ids((quarter, LANES)) // width
    columns = []
    for tile in range(group * BLK // LANES):
        rows = []
        for index in range(FACES):
            merged = jnp.zeros((quarter, LANES), jnp.float32)
            for place in range(per_tile):
                piece = roll_lanes(avg_ref[tile * per_tile + place], (place - index) * width)
                merged = jnp.where(part == place, piece, merged)
            rows.append(merged)
        ordered = []
        for field in range(SPECIES):
            for x in range(BLK):
                at = (field * 2 + x % 2) * NZC
                ordered.append(rows[x // 2][at : at + NZC])
        columns.append(jnp.concatenate(ordered, axis=0))
    high, low = split_pair(jnp.concatenate(columns, axis=1))
    ones = jnp.ones((16, high.shape[1]), jnp.bfloat16)
    stacked = jnp.concatenate([high, low, ones], axis=0)

    halves = cells_y // LANES
    for column in range(cells_x // BLK):
        placed = lax.dot_general(
            stacked,
            selector(place_ref, column, cells_y),
            (((1,), (1,)), ((), ())),
            preferred_element_type=jnp.float32,
        )
        covered = placed[2 * AVG_ROWS : 2 * AVG_ROWS + 8] > 0.5
        values = placed[:AVG_ROWS] + placed[AVG_ROWS : 2 * AVG_ROWS]
        for half in range(halves):
            cols = slice(half * LANES, (half + 1) * LANES)
            start = (column * halves + half) * AVG_ROWS
            placed_ref[start : start + AVG_ROWS, :] = values[:, cols]
            for plane in range(PLANES):
                field, z = divmod(plane, NZC)
                chosen = placed_ref[pl.ds(start + field * BLK * NZC + z, BLK, stride=NZC), :]
                row = plane * cells_x + column * BLK
                coarse = new_ref[row : row + BLK, cols]
                out_ref[row : row + BLK, cols] = jnp.where(covered[:, cols], chosen, coarse)


VMEM = pl.BlockSpec(memory_space=pltpu.VMEM)
HBM = pl.BlockSpec(memory_space=pltpu.HBM)
PARAMS = pltpu.CompilerParams(vmem_limit_bytes=40 * 1024 * 1024)


def f32(*shape):
    return jax.ShapeDtypeStruct(shape, jnp.float32)


def hbm32(*shape):
    return pltpu.HBM(shape, jnp.float32)


def pinned(*arrays):
    return [pltpu.with_memory_space_constraint(array, pltpu.HBM) for array in arrays]


def shifted(values, axis, step):
    count = lax.axis_size(axis)
    pairs = [(i, i + step) for i in range(count) if 0 <= i + step < count]
    return lax.ppermute(values, axis, pairs)


def exchange(chunks):
    return lax.all_to_all(chunks, "af", split_axis=0, concat_axis=0, tiled=True)


def per_device(
    coarse_state, coarse_kappa, coarse_rate, fine_state, fine_kappa, fine_rate, boxes, cover
):
    af_count = lax.axis_size("af")
    slots = fine_state.shape[0]
    cells_x, cells_y = coarse_state.shape[2:]
    group = af_count * slots
    lanes = group * BLK
    halves = cells_y // LANES
    rows = PLANES * cells_x
    plain = NZC * cells_x
    sizes = dict(cells_x=cells_x, cells_y=cells_y, group=group)

    span = cells_x + 2 * PAD
    new, send, place, xlo, xhi, ylo, yhi = pl.pallas_call(
        functools.partial(strips_kernel, slots=slots, **sizes),
        out_shape=[
            hbm32(rows, cells_y),
            f32(af_count, CHUNK_ROWS, LANES),
            jax.ShapeDtypeStruct((16, lanes), jnp.int32),
        ]
        + [f32(EDGE_ROWS, cells_y)] * 2
        + [f32(cells_x, LANES)] * 2,
        in_specs=[HBM] * 4,
        out_specs=[HBM] + [VMEM] * 6,
        scratch_shapes=[
            pltpu.VMEM((2, boxes.shape[0]), jnp.int32),
            pltpu.VMEM((rows, cells_y), jnp.float32),
            pltpu.VMEM((plain, cells_y), jnp.float32),
            pltpu.VMEM((plain, cells_y), jnp.float32),
            pltpu.VMEM((rows, cells_y), jnp.float32),
            pltpu.VMEM(((SPECIES + 1) * halves * NZC * span, LANES), jnp.float32),
            pltpu.VMEM((rows * halves, LANES), jnp.float32),
            pltpu.SemaphoreType.DMA((4,)),
        ],
        compiler_params=PARAMS,
        name="strips",
    )(
        *pinned(
            boxes.T,
            coarse_state.reshape(rows, cells_y),
            coarse_kappa.reshape(plain, cells_y),
            coarse_rate.reshape(plain, cells_y),
        )
    )

    strips = exchange(send)

    xlo_sent, xhi_sent = pl.pallas_call(
        hand_on_kernel,
        out_shape=[f32(EDGE_ROWS, cells_y)] * 2,
        in_specs=[VMEM] * 2,
        out_specs=[VMEM] * 2,
        compiler_params=pltpu.CompilerParams(vmem_limit_bytes=1024 * 1024),
        name="hand_on",
    )(xlo, xhi)
    xl = shifted(xhi_sent, "af", 1)
    xr = shifted(xlo_sent, "af", -1)

    kept = [hbm32(slots * size, LANES) for size in (FIELD_ROWS, COEFF_ROWS, UPWARD_ROWS)]
    kept_scratch = [pltpu.VMEM((slots * size, LANES), jnp.float32)
        for size in (FIELD_ROWS, COEFF_ROWS, UPWARD_ROWS)]
    fields, coeffs, upward = pl.pallas_call(
        functools.partial(prepare_kernel, slots=slots),
        out_shape=kept,
        in_specs=[VMEM] + [HBM] * 3,
        out_specs=[HBM] * 3,
        scratch_shapes=kept_scratch
        + [
            pltpu.VMEM(fine_state.shape, jnp.float32),
            pltpu.VMEM(fine_kappa.shape, jnp.float32),
            pltpu.VMEM(fine_rate.shape, jnp.float32),
            pltpu.VMEM((slots * FIELD_ROWS, LANES), jnp.float32),
            pltpu.VMEM((slots * UPWARD_ROWS, LANES), jnp.float32),
            pltpu.SemaphoreType.DMA((3, slots)),
            pltpu.SemaphoreType.DMA((3, slots)),
        ],
        compiler_params=PARAMS,
        name="prepare",
    )(xlo_sent, *pinned(fine_state, fine_kappa, fine_rate))

    chunk = (AVG_ROWS // FACES, LANES)
    fine_out, averages = pl.pallas_call(
        functools.partial(finish_kernel, slots=slots),
        out_shape=[hbm32(*fine_state.shape), hbm32(af_count, *chunk)],
        in_specs=[VMEM] + [HBM] * 3 + [VMEM] * 2,
        out_specs=[HBM] * 2,
        scratch_shapes=kept_scratch
        + [
            pltpu.VMEM((2 * LANES, EDGE * EDGE), jnp.bfloat16),
            pltpu.VMEM((2 * SPECIES * FZ, STRIP_ROWS), jnp.bfloat16),
            pltpu.VMEM((2 * LANES, LANES), jnp.bfloat16),
            pltpu.VMEM(chunk, jnp.float32),
            pltpu.VMEM((slots * FIELD_ROWS, LANES), jnp.float32),
            pltpu.VMEM((SPECIES * TILES * FZ, LANES), jnp.float32),
            pltpu.VMEM((SPECIES * TILES * FZ, LANES), jnp.float32),
            pltpu.VMEM(fine_state.shape, jnp.float32),
            pltpu.VMEM((SPECIES * 2 * FZ, LANES), jnp.float32),
            pltpu.SemaphoreType.DMA((slots,)),
            pltpu.SemaphoreType.DMA((3, slots)),
            pltpu.SemaphoreType.DMA((af_count,)),
        ],
        compiler_params=PARAMS,
        name="finish",
    )(strips, *pinned(fields, coeffs, upward), xl, xr)

    arrived = exchange(averages)

    yl = shifted(yhi, "col", 1)
    yr = shifted(ylo, "col", -1)
    whole = pl.pallas_call(
        functools.partial(edges_kernel, cells_x=cells_x, cells_y=cells_y),
        out_shape=f32(rows, cells_y),
        in_specs=[HBM] + [VMEM] * 8,
        out_specs=VMEM,
        scratch_shapes=[pltpu.VMEM((rows, cells_y), jnp.float32), pltpu.SemaphoreType.DMA],
        compiler_params=PARAMS,
        name="edges",
    )(*pinned(new), xlo, xhi, ylo, yhi, xl, xr, yl, yr)

    placed = pl.pallas_call(
        functools.partial(place_kernel, slots=slots, **sizes),
        out_shape=f32(rows, cells_y),
        in_specs=[VMEM] * 3,
        out_specs=VMEM,
        scratch_shapes=[
            pltpu.VMEM((cells_x // BLK * halves * AVG_ROWS, LANES), jnp.float32),
        ],
        compiler_params=PARAMS,
        name="place",
    )(place, arrived, whole)
    return (placed.reshape(coarse_state.shape), fine_out)


def solution(mesh):
    return jax.shard_map(
        per_device,
        mesh=mesh,
        in_specs=(
            P(None, None, "af", "col"),
            P(None, "af", "col"),
            P(None, "af", "col"),
            P(("col", "af"), None, None, None),
            P(("col", "af"), None, None),
            P(("col", "af"), None, None),
            P(),
            P(),
        ),
        out_specs=(P(None, None, "af", "col"), P(("col", "af"), None, None, None)),
        check_vma=False,
    )
```

```python
import functools

import jax
import jax.numpy as jnp
from jax import lax
from jax.experimental import pallas as pl
from jax.experimental.pallas import tpu as pltpu
from jax.sharding import PartitionSpec as P

NZC = 8
RATIO = 4
BLK = 8
SPECIES = 3
EDGE = BLK * RATIO
FZ = NZC * RATIO
LANES = 128
TILES = EDGE * EDGE // LANES
ZTILES = FZ // 8
STRIDE = 48
PAD = 8
FACES = 4
PLANES = SPECIES * NZC
STRIP_ROWS = 2 * PLANES
AVG_ROWS = PLANES * BLK
KINDS = 9
FIELD_ROWS = SPECIES * TILES * STRIDE
COEFF_ROWS = KINDS * TILES * FZ
UPWARD_ROWS = TILES * STRIDE
EDGE_ROWS = PLANES + NZC
BESIDE_ROWS = 2 * NZC
CHUNK_ROWS = STRIP_ROWS + BESIDE_ROWS

DT_COARSE = 1.0 / 28.0
DIFFUSE = (1.0, 0.7, 0.45)
SIGNS = (-1.0, -1.0, 1.0)
FINE_SCALE = RATIO * RATIO * DT_COARSE / RATIO
DT_FINE = DT_COARSE / RATIO


def lane_ids(shape):
    return lax.broadcasted_iota(jnp.int32, shape, len(shape) - 1)


def roll_lanes(values, shift):
    width = values.shape[-1]
    shift = shift % width
    return values if shift == 0 else pltpu.roll(values, shift, values.ndim - 1)


def split_pair(values):
    high = values.astype(jnp.bfloat16)
    low = (values - high.astype(jnp.float32)).astype(jnp.bfloat16)
    return high, low


def face(scale, one, other):
    summed = one + other
    inverse = pl.reciprocal(summed, approx=True)
    inverse = inverse * (2.0 - summed * inverse)
    return (2.0 * scale) * (one * other) * inverse


def start_all(copies):
    for copy in copies:
        copy.start()


def selector(place_ref, column, cells_y):
    wanted = jnp.where(place_ref[0:8, :] == column, place_ref[8:16, :], -1)
    row = lax.broadcasted_iota(jnp.int32, wanted.shape, 0)
    return jnp.concatenate(
        [jnp.where(row + 8 * at == wanted, 1.0, 0.0) for at in range(cells_y // 8)], axis=0
    ).astype(jnp.bfloat16)


def strips_kernel(
    boxes_hbm,
    state_hbm,
    kappa_hbm,
    rate_hbm,
    new_hbm,
    send_hbm,
    place_ref,
    xlo_ref,
    xhi_ref,
    ylo_ref,
    yhi_ref,
    boxes_ref,
    state_ref,
    kappa_ref,
    rate_ref,
    new_ref,
    padded,
    fresh,
    send_ref,
    sems,
    send_sems,
    *,
    cells_x,
    cells_y,
    group,
    slots,
):
    pairs = (
        (boxes_hbm, boxes_ref),
        (kappa_hbm, kappa_ref),
        (state_hbm, state_ref),
        (rate_hbm, rate_ref),
    )
    copies = [
        pltpu.make_async_copy(source, target, sems.at[index])
        for index, (source, target) in enumerate(pairs)
    ]
    start_all(copies)

    patches = boxes_ref.shape[1]
    lanes = group * BLK
    base_patch = lax.axis_index("col") * group
    member = lax.broadcasted_iota(jnp.int32, (patches, lanes), 0) - base_patch
    spread = jnp.where(member == lane_ids((patches, lanes)) // BLK, 1.0, 0.0).astype(jnp.bfloat16)
    first_col = lax.axis_index("af") * (cells_x // BLK)
    first_cell = lax.axis_index("col") * cells_y
    copies[0].wait()
    boxes = boxes_ref[...].astype(jnp.float32)
    stacked = jnp.concatenate(
        [jnp.broadcast_to(boxes[row : row + 1], (8, patches)) for row in range(2)], axis=0
    )
    found = jnp.dot(
        stacked.astype(jnp.bfloat16), spread, preferred_element_type=jnp.float32
    ).astype(jnp.int32)
    place_ref[0:8, :] = found[0:8] - first_col
    place_ref[8:16, :] = found[8:16] * BLK - first_cell + lane_ids((8, lanes)) % BLK

    halves = cells_y // LANES
    span = cells_x + 2 * PAD
    nothing = jnp.zeros((PAD, LANES), jnp.float32)

    def base(field, half, z):
        return ((field * halves + half) * NZC + z) * span

    for copy in copies[1:]:
        copy.wait()
    for field in range(SPECIES + 1):
        for half in range(halves):
            cols = pl.ds(half * LANES, LANES)
            for z in range(NZC):
                if field < SPECIES:
                    start = (field * NZC + z) * cells_x
                    plane = state_ref[start : start + cells_x, cols]
                else:
                    plane = kappa_ref[z * cells_x : (z + 1) * cells_x, cols]
                at = base(field, half, z)
                padded[at : at + PAD, :] = nothing
                padded[at + PAD : at + PAD + cells_x, :] = plane
                padded[at + PAD + cells_x : at + span, :] = nothing

    lane = lane_ids((cells_x, LANES))
    row_id = lax.broadcasted_iota(jnp.int32, (cells_x, LANES), 0)

    low = jnp.zeros((cells_x, LANES), jnp.float32)
    high = jnp.zeros((cells_x, LANES), jnp.float32)
    for plane in range(PLANES + NZC):
        field, z = divmod(plane, NZC)
        at = base(field, 0, z) + PAD
        first = padded[at : at + cells_x, :]
        at = base(field, halves - 1, z) + PAD
        last = padded[at : at + cells_x, :]
        low = jnp.where(lane == plane, roll_lanes(first, plane), low)
        high = jnp.where(lane == plane, roll_lanes(last, plane + 1), high)
    ylo_ref[...] = low
    yhi_ref[...] = high

    def load(field, half, z, shift):
        at = base(field, half, z) + PAD + shift
        return padded[at : at + cells_x, :]

    def neighbours(field, half, z):
        here = load(field, half, z, 0)
        after = roll_lanes(here, -1)
        if half + 1 < halves:
            after = jnp.where(
                lane == LANES - 1, roll_lanes(load(field, half + 1, z, 0), -1), after
            )
        before = roll_lanes(here, 1)
        if half > 0:
            before = jnp.where(lane == 0, roll_lanes(load(field, half - 1, z, 0), 1), before)
        found = [after, before, load(field, half, z, 1), load(field, half, z, -1)]
        if z + 1 < NZC:
            found.append(load(field, half, z + 1, 0))
        if z > 0:
            found.append(load(field, half, z - 1, 0))
        return found

    for z in range(NZC):
        for half in range(halves):
            cols = pl.ds(half * LANES, LANES)
            conduct = load(SPECIES, half, z, 0)
            coeffs = [face(DT_COARSE, conduct, other) for other in neighbours(SPECIES, half, z)]
            if half == halves - 1:
                coeffs[0] = jnp.where(lane == LANES - 1, 0.0, coeffs[0])
            if half == 0:
                coeffs[1] = jnp.where(lane == 0, 0.0, coeffs[1])
            coeffs[2] = jnp.where(row_id == cells_x - 1, 0.0, coeffs[2])
            coeffs[3] = jnp.where(row_id == 0, 0.0, coeffs[3])
            centers = [load(field, half, z, 0) for field in range(SPECIES)]
            forward = (DT_COARSE * rate_ref[z * cells_x : (z + 1) * cells_x, cols]) * (
                centers[0] * centers[1] - centers[2]
            )
            for field in range(SPECIES):
                center = centers[field]
                flux = None
                for coeff, other in zip(coeffs, neighbours(field, half, z)):
                    term = coeff * (other - center)
                    flux = term if flux is None else flux + term
                start = (field * NZC + z) * cells_x
                result = center + DIFFUSE[field] * flux + SIGNS[field] * forward
                new_ref[start : start + cells_x, cols] = result
                start = ((field * halves + half) * NZC + z) * cells_x
                fresh[start : start + cells_x, :] = result

    keep_new = pltpu.make_async_copy(new_ref, new_hbm, sems.at[0])
    keep_new.start()

    def old_row(field, half, row):
        return padded[pl.ds(base(field, half, 0) + PAD + row, NZC, stride=span), :]

    def edge_at(row):
        return jnp.concatenate(
            [
                jnp.concatenate([old_row(field, half, row) for field in range(SPECIES + 1)], axis=0)
                for half in range(halves)
            ],
            axis=1,
        )

    def rows_at(row):
        columns = []
        for half in range(halves):
            pieces = [old_row(field, half, row) for field in range(SPECIES)]
            for field in range(SPECIES):
                start = (field * halves + half) * NZC * cells_x
                pieces.append(fresh[pl.ds(start + row, NZC, stride=cells_x), :])
            columns.append(jnp.concatenate(pieces, axis=0))
        return jnp.concatenate(columns, axis=1)

    block_cols = cells_x // BLK
    spot = lane_ids((STRIP_ROWS, cells_y)) % BLK
    lower_y = []
    upper_y = []
    for column in range(block_cols):
        below = jnp.zeros((STRIP_ROWS, cells_y), jnp.float32)
        above = jnp.zeros((STRIP_ROWS, cells_y), jnp.float32)
        for x in range(BLK):
            turned = roll_lanes(rows_at(column * BLK + x), x + 1)
            below = jnp.where(spot == x, turned, below)
            above = jnp.where(spot == (x + 1) % BLK, turned, above)
        lower_y.append(below)
        upper_y.append(roll_lanes(above, -1 - BLK))

    first_row = edge_at(0)
    last_row = edge_at(cells_x - 1)
    xlo_ref[...] = first_row
    xhi_ref[...] = last_row
    place = lane_ids((NZC, cells_y)) % BLK
    ones = jnp.ones((NZC, cells_y), jnp.float32)

    def field_of(row, field):
        return row[field * NZC : (field + 1) * NZC]

    def corners(row, fields, first_at):
        found = jnp.zeros((NZC, cells_y), jnp.float32)
        for order, field in enumerate(fields):
            at = first_at + 2 * order
            values = field_of(row, field)
            found = jnp.where(place == at, roll_lanes(values, at + 1), found)
            found = jnp.where(place == at + 1, roll_lanes(values, at + 1 - BLK), found)
        return found

    every = range(SPECIES)

    def near(row):
        own = [(field, field_of(row, field)) for field in range(SPECIES + 1)]
        return own + [(5, corners(row, [SPECIES], 0))]

    def far(row):
        return [
            (4, field_of(row, SPECIES)),
            (5, corners(row, every, 2)),
            (6, corners(row, [SPECIES], 0)),
        ]

    extra_members = {
        -1: far(first_row),
        0: near(first_row),
        block_cols - 1: near(last_row) + [(7, ones)],
        block_cols: far(last_row),
    }

    faces = [None] * (3 * FACES)

    def add(index, part):
        faces[index] = part if faces[index] is None else faces[index] + part

    for column in range(-1, block_cols + 1):
        members = []
        if column >= 1:
            members.append((0, rows_at(column * BLK - 1)))
        if column < block_cols - 1:
            members.append((1, rows_at(column * BLK + BLK)))
        if 0 <= column < block_cols:
            members.append((2, lower_y[column]))
            members.append((3, upper_y[column]))
        for index, rows in extra_members.get(column, []):
            members.append((FACES + index, rows))
        operands = []
        for _, rows in members:
            operands.extend(split_pair(rows))
        moved = jnp.dot(
            jnp.concatenate(operands, axis=0),
            selector(place_ref, column, cells_y),
            preferred_element_type=jnp.float32,
        )
        at = 0
        for index, rows in members:
            size = rows.shape[0]
            add(index, moved[at : at + size] + moved[at + size : at + 2 * size])
            at += 2 * size

    width = slots * BLK
    outgoing = [
        pltpu.make_async_copy(send_ref.at[target], send_hbm.at[target], send_sems.at[target])
        for target in range(group // slots)
    ]
    for target in range(group // slots):
        first = target * width
        tile = first // LANES * LANES
        for start, size, kind in (
            (0, STRIP_ROWS, 0),
            (STRIP_ROWS, NZC, FACES),
            (STRIP_ROWS + NZC, NZC, 2 * FACES),
        ):
            part = lane_ids((size, LANES)) // width
            chunk = jnp.zeros((size, LANES), jnp.float32)
            for index in range(FACES):
                piece = faces[kind + index][:, tile : tile + LANES]
                chunk = jnp.where(
                    part == index, roll_lanes(piece, index * width - (first - tile)), chunk
                )
            send_ref[target, start : start + size, :] = chunk
        outgoing[target].start()
    for copy in outgoing:
        copy.wait()
    keep_new.wait()


def ghost_table(tile):
    lane = lane_ids((BLK, LANES))
    pos = lax.broadcasted_iota(jnp.int32, (BLK, LANES), 0)
    x = tile * (LANES // EDGE) + lane // EDGE
    y = lane % EDGE
    along_y = y // RATIO == pos
    along_x = x // RATIO == pos
    seen = (
        (x == 0) & along_y,
        (x == EDGE - 1) & along_y,
        (y == 0) & along_x,
        (y == EDGE - 1) & along_x,
    )
    nothing = jnp.zeros((LANES // FACES - BLK, LANES), jnp.float32)
    rows = []
    for where in seen:
        rows.extend([jnp.where(where, 1.0, 0.0), nothing])
    return jnp.concatenate(rows + rows, axis=0).astype(jnp.bfloat16)


def plane_table():
    shape = (2 * SPECIES * FZ, STRIP_ROWS)
    rows = lax.broadcasted_iota(jnp.int32, shape, 0)
    return jnp.where(rows // RATIO == lane_ids(shape), 1.0, 0.0).astype(jnp.bfloat16)


def mean_table():
    shape = (2 * LANES, LANES)
    rows = lax.broadcasted_iota(jnp.int32, shape, 0)
    same = rows % EDGE // RATIO == lane_ids(shape) % BLK
    return jnp.where(same, 1.0 / RATIO**3, 0.0).astype(jnp.bfloat16)


def complete_strips(gathered):
    width = LANES // FACES
    own = gathered[STRIP_ROWS : STRIP_ROWS + NZC]
    beside = gathered[STRIP_ROWS + NZC : STRIP_ROWS + 2 * NZC]
    lane = lane_ids((NZC, LANES))
    part = lane // width
    pos = lane % BLK
    flag = jnp.where(part == FACES - 1, beside, 0.0)
    flag = flag + roll_lanes(flag, width)
    upper = flag + roll_lanes(flag, 2 * width) > 0.5

    def coefficient(one, other):
        return face(DT_COARSE, jnp.maximum(one, 0.125), jnp.maximum(other, 0.125))

    block = coefficient(roll_lanes(own, width), beside)
    corner = coefficient(beside, roll_lanes(beside, -width))
    added = []
    for field in range(SPECIES):
        old = gathered[field * NZC : (field + 1) * NZC]
        there = jnp.where(upper, roll_lanes(old, -width), old)
        across = DIFFUSE[field] * block * (roll_lanes(own, -field * width) - there)
        below = jnp.where(upper, roll_lanes(old, -width - (BLK - 1)), roll_lanes(old, -width))
        above = jnp.where(
            upper, roll_lanes(old, -2 * width - (BLK - 2)), roll_lanes(old, 1 - 2 * width)
        )
        here = jnp.where(pos == 0, below, above)
        along = DIFFUSE[field] * corner * (roll_lanes(beside, -2 - 2 * field) - here)
        share = jnp.where((part == 0) & ~upper, across, 0.0)
        share = jnp.where((part == 1) & upper, roll_lanes(across, width), share)
        for index in range(2):
            for at, chosen in ((0, ~upper), (BLK - 1, upper)):
                moved = roll_lanes(along, (1 + index) * width + at - index)
                share = jnp.where((part == 2 + index) & (pos == at) & chosen, moved, share)
        added.append(share)
    new = gathered[PLANES:STRIP_ROWS] + jnp.concatenate(added, axis=0)
    return gathered[:PLANES], new


def aligned(start, size):
    return pl.ds(pl.multiple_of(start, 8), size)


def padded_at(block, ztile):
    return block * STRIDE + PAD + 8 * ztile


def advance(source, target, coeffs, upward, slot, from_rows, to_rows, ztile, ghosts):
    lane = lane_ids((8, LANES))

    def value(field, tile, shift):
        start = from_rows + padded_at(field * TILES + tile, ztile) + shift
        return source[aligned(start, 8) if shift == 0 else pl.ds(start, 8), :]

    def get(kind, tile):
        return coeffs[
            aligned(slot * COEFF_ROWS + (kind * TILES + tile) * FZ + 8 * ztile, 8), :
        ]

    centers = [value(field, 0, 0) for field in range(SPECIES)]
    down = [roll_lanes(center, -EDGE) for center in centers]
    up = [roll_lanes(center, EDGE) for center in centers]
    up_before = list(up)
    for tile in range(TILES):
        if tile + 1 < TILES:
            centers_after = [value(field, tile + 1, 0) for field in range(SPECIES)]
            down_after = [roll_lanes(center, -EDGE) for center in centers_after]
        next_x, prev_x, next_y, prev_y, rate = [get(kind, tile) for kind in range(5)]
        base = slot * UPWARD_ROWS + padded_at(tile, ztile)
        next_z = upward[aligned(base, 8), :]
        prev_z = upward[pl.ds(base - 1, 8), :]
        forward = rate * (centers[0] * centers[1] - centers[2])
        for field in range(SPECIES):
            center = centers[field]
            ahead, behind = down[field], up[field]
            if tile + 1 < TILES:
                ahead = jnp.where(lane < LANES - EDGE, ahead, down_after[field])
            if tile > 0:
                behind = jnp.where(lane >= EDGE, behind, up_before[field])
            flux = (next_x * ahead + prev_x * behind) + (
                next_y * roll_lanes(center, -1) + prev_y * roll_lanes(center, 1)
            )
            flux = flux + (next_z * value(field, tile, 1) + prev_z * value(field, tile, -1))
            share = ghosts(field, tile)
            if share is not None:
                flux = flux + share
            if DIFFUSE[field] != 1.0:
                flux = DIFFUSE[field] * flux
            result = get(5 + field, tile) * center + flux
            result = result - forward if SIGNS[field] < 0 else result + forward
            target[aligned(to_rows + padded_at(field * TILES + tile, ztile), 8), :] = result
        if tile + 1 < TILES:
            up_before = up
            centers, down = centers_after, down_after
            up = [roll_lanes(center, EDGE) for center in centers]


def clear_pads(ref):
    edge = jnp.zeros((PAD, LANES), jnp.float32)

    def body(block, carry):
        ref[aligned(block * STRIDE, PAD), :] = edge
        ref[aligned(block * STRIDE + PAD + FZ, PAD), :] = edge
        return carry

    lax.fori_loop(0, ref.shape[0] // STRIDE, body, 0)


def hand_on_kernel(low_ref, high_ref, low_out, high_out):
    low_out[...] = low_ref[...]
    high_out[...] = high_ref[...]


def prepare_kernel(
    after_ref,
    state_hbm,
    kappa_hbm,
    rate_hbm,
    fields_hbm,
    coeffs_hbm,
    upward_hbm,
    fields_ref,
    coeffs,
    upward,
    state_ref,
    kappa_ref,
    rate_ref,
    first,
    conduct,
    sems,
    out_sems,
    *,
    slots,
):
    def loads(slot):
        return [
            pltpu.make_async_copy(source.at[slot], target.at[slot], sems.at[order, slot])
            for order, (source, target) in enumerate(
                ((kappa_hbm, kappa_ref), (rate_hbm, rate_ref), (state_hbm, state_ref))
            )
        ]

    for slot in range(slots):
        start_all(loads(slot))

    def stores(slot):
        return [
            pltpu.make_async_copy(
                source.at[aligned(slot * size, size)],
                target.at[aligned(slot * size, size)],
                out_sems.at[order, slot],
            )
            for order, (source, target, size) in enumerate(
                (
                    (fields_ref, fields_hbm, FIELD_ROWS),
                    (coeffs, coeffs_hbm, COEFF_ROWS),
                    (upward, upward_hbm, UPWARD_ROWS),
                )
            )
        ]

    for ref in (fields_ref, upward, first, conduct):
        clear_pads(ref)

    lane = lane_ids((8, LANES))
    column = lane % EDGE
    side_y = jnp.where((column == 0) | (column == EDGE - 1), 1.0, 0.0)

    def one_patch(slot, carry):
        for copy in loads(slot):
            copy.wait()

        for tile in range(TILES):
            cols = pl.ds(tile * LANES, LANES)
            for field in range(SPECIES):
                spot = aligned(slot * FIELD_ROWS + padded_at(field * TILES + tile, 0), FZ)
                first[spot, :] = state_ref[slot, field, :, cols]
            spot = aligned(slot * UPWARD_ROWS + padded_at(tile, 0), FZ)
            conduct[spot, :] = kappa_ref[slot, :, cols]

        def keep(kind, tile, ztile, values):
            coeffs[
                aligned(slot * COEFF_ROWS + (kind * TILES + tile) * FZ + 8 * ztile, 8), :
            ] = values

        def prepare_tile(ztile, inner):
            def here(tile, shift):
                start = slot * UPWARD_ROWS + padded_at(tile, ztile) + shift
                return conduct[aligned(start, 8) if shift == 0 else pl.ds(start, 8), :]

            center = here(0, 0)
            turned = roll_lanes(center, -EDGE)
            back_before = None
            for tile in range(TILES):
                other = turned
                if tile + 1 < TILES:
                    center_after = here(tile + 1, 0)
                    turned_after = roll_lanes(center_after, -EDGE)
                    other = jnp.where(lane < LANES - EDGE, turned, turned_after)
                next_x = face(FINE_SCALE, center, other)
                if tile == TILES - 1:
                    next_x = jnp.where(lane < LANES - EDGE, next_x, 0.0)
                back = roll_lanes(next_x, EDGE)
                prev_x = jnp.where(lane >= EDGE, back, 0.0 if tile == 0 else back_before)
                next_y = jnp.where(
                    column < EDGE - 1, face(FINE_SCALE, center, roll_lanes(center, -1)), 0.0
                )
                prev_y = roll_lanes(next_y, 1)
                next_z = face(FINE_SCALE, center, here(tile, 1))
                prev_z = face(FINE_SCALE, center, here(tile, -1))
                sides = side_y
                if tile == 0:
                    sides = sides + jnp.where(lane < EDGE, 1.0, 0.0)
                if tile == TILES - 1:
                    sides = sides + jnp.where(lane >= LANES - EDGE, 1.0, 0.0)
                scale = FINE_SCALE * center
                total = (next_x + prev_x) + (next_y + prev_y) + (next_z + prev_z) + sides * scale
                upward[aligned(slot * UPWARD_ROWS + padded_at(tile, ztile), 8), :] = next_z
                keep(0, tile, ztile, next_x)
                keep(1, tile, ztile, prev_x)
                keep(2, tile, ztile, next_y)
                keep(3, tile, ztile, prev_y)
                rate = rate_ref[slot, aligned(8 * ztile, 8), pl.ds(tile * LANES, LANES)]
                keep(4, tile, ztile, DT_FINE * rate)
                for field in range(SPECIES):
                    keep(5 + field, tile, ztile, 1.0 - DIFFUSE[field] * total)
                keep(8, tile, ztile, scale)
                back_before = back
                if tile + 1 < TILES:
                    center, turned = center_after, turned_after
            return inner

        lax.fori_loop(0, ZTILES, prepare_tile, 0)

        def first_step(ztile, inner):
            advance(
                first,
                fields_ref,
                coeffs,
                upward,
                slot,
                slot * FIELD_ROWS,
                slot * FIELD_ROWS,
                ztile,
                lambda field, tile: None,
            )
            return inner

        lax.fori_loop(0, ZTILES, first_step, 0)
        start_all(stores(slot))
        return carry

    lax.fori_loop(0, slots, one_patch, 0)
    for slot in range(slots):
        for copy in stores(slot):
            copy.wait()


def finish_kernel(
    strips_ref,
    fields_hbm,
    coeffs_hbm,
    upward_hbm,
    xl_ref,
    xr_ref,
    out_hbm,
    avg_hbm,
    fields_ref,
    coeffs,
    upward,
    ghost_ref,
    plane_ref,
    mean_ref,
    avg_ref,
    first,
    share,
    drift,
    staged,
    sems,
    in_sems,
    avg_sems,
    *,
    slots,
):
    sources = strips_ref.shape[0]

    def loads(slot):
        return [
            pltpu.make_async_copy(
                source.at[aligned(slot * size, size)],
                target.at[aligned(slot * size, size)],
                in_sems.at[order, slot],
            )
            for order, (source, target, size) in enumerate(
                (
                    (fields_hbm, fields_ref, FIELD_ROWS),
                    (coeffs_hbm, coeffs, COEFF_ROWS),
                    (upward_hbm, upward, UPWARD_ROWS),
                )
            )
        ]

    start_all(loads(0))
    clear_pads(first)
    for tile in range(TILES):
        ghost_ref[:, tile * LANES : (tile + 1) * LANES] = ghost_table(tile)
    plane_ref[...] = plane_table()
    mean_ref[...] = mean_table()

    gathered = strips_ref[0]
    for source in range(1, sources):
        gathered = gathered + strips_ref[source]
    old, new = complete_strips(gathered)
    gathered = jnp.concatenate([old, (new - old) * (1.0 / RATIO)], axis=0)
    quarter = AVG_ROWS // FACES
    group_of = lane_ids((quarter, LANES)) // BLK

    def send_out(slot):
        return pltpu.make_async_copy(staged.at[slot], out_hbm.at[slot], sems.at[slot])

    def one_patch(slot, carry):
        for copy in loads(slot):
            copy.wait()

        @pl.when(slot + 1 < slots)
        def _():
            start_all(loads(slot + 1))

        turned = pltpu.roll(gathered, (LANES - slot * BLK) % LANES, 1)
        stretched = jnp.dot(
            plane_ref[...],
            jnp.concatenate(split_pair(turned), axis=1),
            preferred_element_type=jnp.float32,
        ).astype(jnp.bfloat16)
        base = slot * FIELD_ROWS
        scales = slot * COEFF_ROWS
        for tile in range(TILES):
            ghosts = jnp.dot(
                stretched,
                ghost_ref[:, tile * LANES : (tile + 1) * LANES],
                preferred_element_type=jnp.float32,
            )
            scale = coeffs[aligned(scales + (8 * TILES + tile) * FZ, FZ), :]
            for field in range(SPECIES):
                row = (field * TILES + tile) * FZ
                old = scale * ghosts[field * FZ : (field + 1) * FZ]
                step = scale * ghosts[(SPECIES + field) * FZ : (SPECIES + field + 1) * FZ]
                drift[row : row + FZ, :] = step
                share[row : row + FZ, :] = old
                spot = aligned(base + padded_at(field * TILES + tile, 0), FZ)
                fields_ref[spot, :] = fields_ref[spot, :] + DIFFUSE[field] * old

        for step in range(1, RATIO):
            source, target = (fields_ref, first) if step % 2 else (first, fields_ref)

            def one_tile(ztile, inner, step=step, source=source, target=target):
                def ghosts(field, tile):
                    spot = aligned((field * TILES + tile) * FZ + 8 * ztile, 8)
                    return share[spot, :] + float(step) * drift[spot, :]

                advance(source, target, coeffs, upward, slot, base, base, ztile, ghosts)
                return inner

            lax.fori_loop(0, ZTILES, one_tile, 0)

        for tile in range(TILES):
            for field in range(SPECIES):
                spot = aligned(base + padded_at(field * TILES + tile, 0), FZ)
                staged[slot, field, :, pl.ds(tile * LANES, LANES)] = first[spot, :]
        send_out(slot).start()

        sums = []
        for field in range(SPECIES):
            for plane in range(NZC):
                start = base + field * TILES * STRIDE + PAD + RATIO * plane
                part = first[pl.ds(start, TILES, stride=STRIDE), :]
                for z in range(1, RATIO):
                    part = part + first[pl.ds(start + z, TILES, stride=STRIDE), :]
                sums.append(part)
        means = jnp.dot(
            jnp.concatenate(split_pair(jnp.concatenate(sums, axis=0)), axis=1),
            mean_ref[...],
            preferred_element_type=jnp.float32,
        )
        chunk = avg_ref[...]
        for part in range(FACES):
            chunk = jnp.where(
                group_of == part * slots + slot,
                means[part * quarter : (part + 1) * quarter],
                chunk,
            )
        avg_ref[...] = chunk
        return carry

    avg_ref[...] = jnp.zeros((quarter, LANES), jnp.float32)
    lax.fori_loop(0, slots, one_patch, 0)
    copies = [
        pltpu.make_async_copy(avg_ref, avg_hbm.at[target], avg_sems.at[target])
        for target in range(sources)
    ]
    start_all(copies)
    for copy in copies:
        copy.wait()
    for slot in range(slots):
        send_out(slot).wait()


def edges_kernel(
    new_hbm,
    xlo_ref,
    xhi_ref,
    ylo_ref,
    yhi_ref,
    xl_ref,
    xr_ref,
    yl_ref,
    yr_ref,
    out_ref,
    new_ref,
    sem,
    *,
    cells_x,
    cells_y,
):
    me = lax.axis_index("af")
    last = lax.axis_size("af") - 1
    fetch = pltpu.make_async_copy(new_hbm, new_ref, sem)
    fetch.start()

    def edge_share(own_ref, other_ref):
        own = own_ref[...]
        other = other_ref[...]
        coeff = face(DT_COARSE, jnp.maximum(own, 0.125), other)
        lane = lane_ids(own.shape)
        spread = jnp.zeros_like(own)
        for field in range(SPECIES):
            moved = roll_lanes(coeff, (field - SPECIES) * NZC)
            spread = jnp.where(lane // NZC == field, DIFFUSE[field] * moved, spread)
        return spread * (other - own)

    lower = edge_share(ylo_ref, yl_ref)
    upper = edge_share(yhi_ref, yr_ref)

    lane = lane_ids((BLK, LANES))
    row_id = lax.broadcasted_iota(jnp.int32, (BLK, LANES), 0)
    halves = cells_y // LANES

    def side_share(own_ref, other_ref, exists):
        shares = []
        for half in range(halves):
            own = own_ref[:, half * LANES : (half + 1) * LANES]
            other = other_ref[:, half * LANES : (half + 1) * LANES]
            coeff = face(DT_COARSE, own[PLANES:], other[PLANES:])
            coeff = jnp.where(exists, coeff, 0.0)
            shares.append(
                jnp.concatenate(
                    [
                        (DIFFUSE[field] * coeff)
                        * (
                            other[field * NZC : (field + 1) * NZC]
                            - own[field * NZC : (field + 1) * NZC]
                        )
                        for field in range(SPECIES)
                    ],
                    axis=0,
                )
            )
        return shares

    before = side_share(xlo_ref, xl_ref, me > 0)
    after = side_share(xhi_ref, xr_ref, me < last)
    fetch.wait()
    block_cols = cells_x // BLK
    for column in range(block_cols):
        for plane in range(PLANES):
            row = plane * cells_x + column * BLK
            edge_rows = slice(column * BLK, (column + 1) * BLK)
            for half in range(halves):
                cols = slice(half * LANES, (half + 1) * LANES)
                coarse = new_ref[row : row + BLK, cols]
                if column == 0:
                    share = before[half][plane : plane + 1]
                    coarse = coarse + jnp.where(row_id == 0, share, 0.0)
                if column == block_cols - 1:
                    share = after[half][plane : plane + 1]
                    coarse = coarse + jnp.where(row_id == BLK - 1, share, 0.0)
                if half == 0:
                    share = roll_lanes(lower[edge_rows], -plane)
                    coarse = coarse + jnp.where(lane == 0, share, 0.0)
                if half == halves - 1:
                    share = roll_lanes(upper[edge_rows], LANES - 1 - plane)
                    coarse = coarse + jnp.where(lane == LANES - 1, share, 0.0)
                out_ref[row : row + BLK, cols] = coarse


def place_kernel(
    place_ref, avg_ref, new_ref, out_ref, *, cells_x, cells_y, group, slots
):
    width = slots * BLK
    quarter = AVG_ROWS // FACES
    per_tile = LANES // width
    part = lane_ids((quarter, LANES)) // width
    columns = []
    for tile in range(group * BLK // LANES):
        rows = []
        for index in range(FACES):
            merged = jnp.zeros((quarter, LANES), jnp.float32)
            for place in range(per_tile):
                piece = roll_lanes(avg_ref[tile * per_tile + place], (place - index) * width)
                merged = jnp.where(part == place, piece, merged)
            rows.append(merged)
        columns.append(jnp.concatenate(rows, axis=0))
    high, low = split_pair(jnp.concatenate(columns, axis=1))
    ones = jnp.ones((16, high.shape[1]), jnp.bfloat16)
    stacked = jnp.concatenate([high, low, ones], axis=0)

    halves = cells_y // LANES
    for column in range(cells_x // BLK):
        placed = lax.dot_general(
            stacked,
            selector(place_ref, column, cells_y),
            (((1,), (1,)), ((), ())),
            preferred_element_type=jnp.float32,
        )
        covered = placed[2 * AVG_ROWS : 2 * AVG_ROWS + 8] > 0.5
        for plane in range(PLANES):
            values = (
                placed[plane * BLK : (plane + 1) * BLK]
                + placed[AVG_ROWS + plane * BLK : AVG_ROWS + (plane + 1) * BLK]
            )
            row = plane * cells_x + column * BLK
            for half in range(halves):
                cols = slice(half * LANES, (half + 1) * LANES)
                coarse = new_ref[row : row + BLK, cols]
                out_ref[row : row + BLK, cols] = jnp.where(
                    covered[:, cols], values[:, cols], coarse
                )


VMEM = pl.BlockSpec(memory_space=pltpu.VMEM)
HBM = pl.BlockSpec(memory_space=pltpu.HBM)
PARAMS = pltpu.CompilerParams(vmem_limit_bytes=40 * 1024 * 1024)


def f32(*shape):
    return jax.ShapeDtypeStruct(shape, jnp.float32)


def hbm32(*shape):
    return pltpu.HBM(shape, jnp.float32)


def pinned(*arrays):
    return [pltpu.with_memory_space_constraint(array, pltpu.HBM) for array in arrays]


def shifted(values, axis, step):
    count = lax.axis_size(axis)
    pairs = [(i, i + step) for i in range(count) if 0 <= i + step < count]
    return lax.ppermute(values, axis, pairs)


def exchange(chunks):
    return lax.all_to_all(chunks, "af", split_axis=0, concat_axis=0, tiled=True)


def per_device(
    coarse_state, coarse_kappa, coarse_rate, fine_state, fine_kappa, fine_rate, boxes, cover
):
    af_count = lax.axis_size("af")
    slots = fine_state.shape[0]
    cells_x, cells_y = coarse_state.shape[2:]
    group = af_count * slots
    lanes = group * BLK
    halves = cells_y // LANES
    rows = PLANES * cells_x
    plain = NZC * cells_x
    sizes = dict(cells_x=cells_x, cells_y=cells_y, group=group)

    span = cells_x + 2 * PAD
    new, send, place, xlo, xhi, ylo, yhi = pl.pallas_call(
        functools.partial(strips_kernel, slots=slots, **sizes),
        out_shape=[
            hbm32(rows, cells_y),
            hbm32(af_count, CHUNK_ROWS, LANES),
            jax.ShapeDtypeStruct((16, lanes), jnp.int32),
        ]
        + [f32(EDGE_ROWS, cells_y)] * 2
        + [f32(cells_x, LANES)] * 2,
        in_specs=[HBM] * 4,
        out_specs=[HBM] * 2 + [VMEM] * 5,
        scratch_shapes=[
            pltpu.VMEM((2, boxes.shape[0]), jnp.int32),
            pltpu.VMEM((rows, cells_y), jnp.float32),
            pltpu.VMEM((plain, cells_y), jnp.float32),
            pltpu.VMEM((plain, cells_y), jnp.float32),
            pltpu.VMEM((rows, cells_y), jnp.float32),
            pltpu.VMEM(((SPECIES + 1) * halves * NZC * span, LANES), jnp.float32),
            pltpu.VMEM((rows * halves, LANES), jnp.float32),
            pltpu.VMEM((af_count, CHUNK_ROWS, LANES), jnp.float32),
            pltpu.SemaphoreType.DMA((4,)),
            pltpu.SemaphoreType.DMA((af_count,)),
        ],
        compiler_params=PARAMS,
        name="strips",
    )(
        *pinned(
            boxes.T,
            coarse_state.reshape(rows, cells_y),
            coarse_kappa.reshape(plain, cells_y),
            coarse_rate.reshape(plain, cells_y),
        )
    )

    strips = exchange(send)

    xlo_sent, xhi_sent = pl.pallas_call(
        hand_on_kernel,
        out_shape=[f32(EDGE_ROWS, cells_y)] * 2,
        in_specs=[VMEM] * 2,
        out_specs=[VMEM] * 2,
        compiler_params=pltpu.CompilerParams(vmem_limit_bytes=1024 * 1024),
        name="hand_on",
    )(xlo, xhi)
    xl = shifted(xhi_sent, "af", 1)
    xr = shifted(xlo_sent, "af", -1)

    kept = [hbm32(slots * size, LANES) for size in (FIELD_ROWS, COEFF_ROWS, UPWARD_ROWS)]
    kept_scratch = [pltpu.VMEM((slots * size, LANES), jnp.float32)
        for size in (FIELD_ROWS, COEFF_ROWS, UPWARD_ROWS)]
    fields, coeffs, upward = pl.pallas_call(
        functools.partial(prepare_kernel, slots=slots),
        out_shape=kept,
        in_specs=[VMEM] + [HBM] * 3,
        out_specs=[HBM] * 3,
        scratch_shapes=kept_scratch
        + [
            pltpu.VMEM(fine_state.shape, jnp.float32),
            pltpu.VMEM(fine_kappa.shape, jnp.float32),
            pltpu.VMEM(fine_rate.shape, jnp.float32),
            pltpu.VMEM((slots * FIELD_ROWS, LANES), jnp.float32),
            pltpu.VMEM((slots * UPWARD_ROWS, LANES), jnp.float32),
            pltpu.SemaphoreType.DMA((3, slots)),
            pltpu.SemaphoreType.DMA((3, slots)),
        ],
        compiler_params=PARAMS,
        name="prepare",
    )(xlo_sent, *pinned(fine_state, fine_kappa, fine_rate))

    chunk = (AVG_ROWS // FACES, LANES)
    fine_out, averages = pl.pallas_call(
        functools.partial(finish_kernel, slots=slots),
        out_shape=[hbm32(*fine_state.shape), hbm32(af_count, *chunk)],
        in_specs=[VMEM] + [HBM] * 3 + [VMEM] * 2,
        out_specs=[HBM] * 2,
        scratch_shapes=kept_scratch
        + [
            pltpu.VMEM((2 * LANES, EDGE * EDGE), jnp.bfloat16),
            pltpu.VMEM((2 * SPECIES * FZ, STRIP_ROWS), jnp.bfloat16),
            pltpu.VMEM((2 * LANES, LANES), jnp.bfloat16),
            pltpu.VMEM(chunk, jnp.float32),
            pltpu.VMEM((slots * FIELD_ROWS, LANES), jnp.float32),
            pltpu.VMEM((SPECIES * TILES * FZ, LANES), jnp.float32),
            pltpu.VMEM((SPECIES * TILES * FZ, LANES), jnp.float32),
            pltpu.VMEM(fine_state.shape, jnp.float32),
            pltpu.SemaphoreType.DMA((slots,)),
            pltpu.SemaphoreType.DMA((3, slots)),
            pltpu.SemaphoreType.DMA((af_count,)),
        ],
        compiler_params=PARAMS,
        name="finish",
    )(strips, *pinned(fields, coeffs, upward), xl, xr)

    arrived = exchange(averages)

    yl = shifted(yhi, "col", 1)
    yr = shifted(ylo, "col", -1)
    whole = pl.pallas_call(
        functools.partial(edges_kernel, cells_x=cells_x, cells_y=cells_y),
        out_shape=f32(rows, cells_y),
        in_specs=[HBM] + [VMEM] * 8,
        out_specs=VMEM,
        scratch_shapes=[pltpu.VMEM((rows, cells_y), jnp.float32), pltpu.SemaphoreType.DMA],
        compiler_params=PARAMS,
        name="edges",
    )(*pinned(new), xlo, xhi, ylo, yhi, xl, xr, yl, yr)

    placed = pl.pallas_call(
        functools.partial(place_kernel, slots=slots, **sizes),
        out_shape=f32(rows, cells_y),
        in_specs=[VMEM] * 3,
        out_specs=VMEM,
        compiler_params=PARAMS,
        name="place",
    )(place, arrived, whole)
    return (placed.reshape(coarse_state.shape), fine_out)


def solution(mesh):
    return jax.shard_map(
        per_device,
        mesh=mesh,
        in_specs=(
            P(None, None, "af", "col"),
            P(None, "af", "col"),
            P(None, "af", "col"),
            P(("col", "af"), None, None, None),
            P(("col", "af"), None, None),
            P(("col", "af"), None, None),
            P(),
            P(),
        ),
        out_specs=(P(None, None, "af", "col"), P(("col", "af"), None, None, None)),
        check_vma=False,
    )
```

```python
import functools

import jax
import jax.numpy as jnp
from jax import lax
from jax.experimental import pallas as pl
from jax.experimental.pallas import tpu as pltpu
from jax.sharding import PartitionSpec as P

NZC = 8
RATIO = 4
BLK = 8
SPECIES = 3
EDGE = BLK * RATIO
FZ = NZC * RATIO
LANES = 128
TILES = EDGE * EDGE // LANES
DEPTH = 16
ZTILES = FZ // DEPTH
STRIDE = 48
PAD = 8
FACES = 4
PLANES = SPECIES * NZC
STRIP_ROWS = 2 * PLANES
AVG_ROWS = PLANES * BLK
KINDS = 9
FIELD_ROWS = SPECIES * TILES * STRIDE
COEFF_ROWS = KINDS * TILES * FZ
UPWARD_ROWS = TILES * STRIDE
EDGE_ROWS = PLANES + NZC
BESIDE_ROWS = 2 * NZC
CHUNK_ROWS = STRIP_ROWS + BESIDE_ROWS

DT_COARSE = 1.0 / 28.0
DIFFUSE = (1.0, 0.7, 0.45)
SIGNS = (-1.0, -1.0, 1.0)
FINE_SCALE = RATIO * RATIO * DT_COARSE / RATIO
DT_FINE = DT_COARSE / RATIO


def lane_ids(shape):
    return lax.broadcasted_iota(jnp.int32, shape, len(shape) - 1)


def roll_lanes(values, shift):
    width = values.shape[-1]
    shift = shift % width
    return values if shift == 0 else pltpu.roll(values, shift, values.ndim - 1)


def split_pair(values):
    high = values.astype(jnp.bfloat16)
    low = (values - high.astype(jnp.float32)).astype(jnp.bfloat16)
    return high, low


def face(scale, one, other):
    summed = one + other
    inverse = pl.reciprocal(summed, approx=True)
    inverse = inverse * (2.0 - summed * inverse)
    return (2.0 * scale) * (one * other) * inverse


def start_all(copies):
    for copy in copies:
        copy.start()


def selector(place_ref, column, cells_y):
    wanted = jnp.where(place_ref[0:8, :] == column, place_ref[8:16, :], -1)
    row = lax.broadcasted_iota(jnp.int32, wanted.shape, 0)
    return jnp.concatenate(
        [jnp.where(row + 8 * at == wanted, 1.0, 0.0) for at in range(cells_y // 8)], axis=0
    ).astype(jnp.bfloat16)


def strips_kernel(
    boxes_hbm,
    state_hbm,
    kappa_hbm,
    rate_hbm,
    new_hbm,
    send_hbm,
    place_ref,
    xlo_ref,
    xhi_ref,
    ylo_ref,
    yhi_ref,
    boxes_ref,
    state_ref,
    kappa_ref,
    rate_ref,
    new_ref,
    padded,
    fresh,
    send_ref,
    sems,
    send_sems,
    *,
    cells_x,
    cells_y,
    group,
    slots,
):
    pairs = (
        (boxes_hbm, boxes_ref),
        (kappa_hbm, kappa_ref),
        (state_hbm, state_ref),
        (rate_hbm, rate_ref),
    )
    copies = [
        pltpu.make_async_copy(source, target, sems.at[index])
        for index, (source, target) in enumerate(pairs)
    ]
    start_all(copies)

    patches = boxes_ref.shape[1]
    lanes = group * BLK
    base_patch = lax.axis_index("col") * group
    member = lax.broadcasted_iota(jnp.int32, (patches, lanes), 0) - base_patch
    spread = jnp.where(member == lane_ids((patches, lanes)) // BLK, 1.0, 0.0).astype(jnp.bfloat16)
    first_col = lax.axis_index("af") * (cells_x // BLK)
    first_cell = lax.axis_index("col") * cells_y
    copies[0].wait()
    boxes = boxes_ref[...].astype(jnp.float32)
    stacked = jnp.concatenate(
        [jnp.broadcast_to(boxes[row : row + 1], (8, patches)) for row in range(2)], axis=0
    )
    found = jnp.dot(
        stacked.astype(jnp.bfloat16), spread, preferred_element_type=jnp.float32
    ).astype(jnp.int32)
    place_ref[0:8, :] = found[0:8] - first_col
    place_ref[8:16, :] = found[8:16] * BLK - first_cell + lane_ids((8, lanes)) % BLK

    halves = cells_y // LANES
    span = cells_x + 2 * PAD
    nothing = jnp.zeros((PAD, LANES), jnp.float32)

    def base(field, half, z):
        return ((field * halves + half) * NZC + z) * span

    for copy in copies[1:]:
        copy.wait()
    for field in range(SPECIES + 1):
        for half in range(halves):
            cols = pl.ds(half * LANES, LANES)
            for z in range(NZC):
                if field < SPECIES:
                    start = (field * NZC + z) * cells_x
                    plane = state_ref[start : start + cells_x, cols]
                else:
                    plane = kappa_ref[z * cells_x : (z + 1) * cells_x, cols]
                at = base(field, half, z)
                padded[at : at + PAD, :] = nothing
                padded[at + PAD : at + PAD + cells_x, :] = plane
                padded[at + PAD + cells_x : at + span, :] = nothing

    lane = lane_ids((cells_x, LANES))
    row_id = lax.broadcasted_iota(jnp.int32, (cells_x, LANES), 0)

    low = jnp.zeros((cells_x, LANES), jnp.float32)
    high = jnp.zeros((cells_x, LANES), jnp.float32)
    for plane in range(PLANES + NZC):
        field, z = divmod(plane, NZC)
        at = base(field, 0, z) + PAD
        first = padded[at : at + cells_x, :]
        at = base(field, halves - 1, z) + PAD
        last = padded[at : at + cells_x, :]
        low = jnp.where(lane == plane, roll_lanes(first, plane), low)
        high = jnp.where(lane == plane, roll_lanes(last, plane + 1), high)
    ylo_ref[...] = low
    yhi_ref[...] = high

    def load(field, half, z, shift):
        at = base(field, half, z) + PAD + shift
        return padded[at : at + cells_x, :]

    def neighbours(field, half, z):
        here = load(field, half, z, 0)
        after = roll_lanes(here, -1)
        if half + 1 < halves:
            after = jnp.where(
                lane == LANES - 1, roll_lanes(load(field, half + 1, z, 0), -1), after
            )
        before = roll_lanes(here, 1)
        if half > 0:
            before = jnp.where(lane == 0, roll_lanes(load(field, half - 1, z, 0), 1), before)
        found = [after, before, load(field, half, z, 1), load(field, half, z, -1)]
        if z + 1 < NZC:
            found.append(load(field, half, z + 1, 0))
        if z > 0:
            found.append(load(field, half, z - 1, 0))
        return found

    for z in range(NZC):
        for half in range(halves):
            cols = pl.ds(half * LANES, LANES)
            conduct = load(SPECIES, half, z, 0)
            coeffs = [face(DT_COARSE, conduct, other) for other in neighbours(SPECIES, half, z)]
            if half == halves - 1:
                coeffs[0] = jnp.where(lane == LANES - 1, 0.0, coeffs[0])
            if half == 0:
                coeffs[1] = jnp.where(lane == 0, 0.0, coeffs[1])
            coeffs[2] = jnp.where(row_id == cells_x - 1, 0.0, coeffs[2])
            coeffs[3] = jnp.where(row_id == 0, 0.0, coeffs[3])
            centers = [load(field, half, z, 0) for field in range(SPECIES)]
            forward = (DT_COARSE * rate_ref[z * cells_x : (z + 1) * cells_x, cols]) * (
                centers[0] * centers[1] - centers[2]
            )
            for field in range(SPECIES):
                center = centers[field]
                flux = None
                for coeff, other in zip(coeffs, neighbours(field, half, z)):
                    term = coeff * (other - center)
                    flux = term if flux is None else flux + term
                start = (field * NZC + z) * cells_x
                result = center + DIFFUSE[field] * flux + SIGNS[field] * forward
                new_ref[start : start + cells_x, cols] = result
                start = ((field * halves + half) * NZC + z) * cells_x
                fresh[start : start + cells_x, :] = result

    keep_new = pltpu.make_async_copy(new_ref, new_hbm, sems.at[0])
    keep_new.start()

    def old_row(field, half, row):
        return padded[pl.ds(base(field, half, 0) + PAD + row, NZC, stride=span), :]

    def edge_at(row):
        return jnp.concatenate(
            [
                jnp.concatenate([old_row(field, half, row) for field in range(SPECIES + 1)], axis=0)
                for half in range(halves)
            ],
            axis=1,
        )

    def rows_at(row):
        columns = []
        for half in range(halves):
            pieces = [old_row(field, half, row) for field in range(SPECIES)]
            for field in range(SPECIES):
                start = (field * halves + half) * NZC * cells_x
                pieces.append(fresh[pl.ds(start + row, NZC, stride=cells_x), :])
            columns.append(jnp.concatenate(pieces, axis=0))
        return jnp.concatenate(columns, axis=1)

    block_cols = cells_x // BLK
    spot = lane_ids((STRIP_ROWS, cells_y)) % BLK
    lower_y = []
    upper_y = []
    for column in range(block_cols):
        below = jnp.zeros((STRIP_ROWS, cells_y), jnp.float32)
        above = jnp.zeros((STRIP_ROWS, cells_y), jnp.float32)
        for x in range(BLK):
            turned = roll_lanes(rows_at(column * BLK + x), x + 1)
            below = jnp.where(spot == x, turned, below)
            above = jnp.where(spot == (x + 1) % BLK, turned, above)
        lower_y.append(below)
        upper_y.append(roll_lanes(above, -1 - BLK))

    first_row = edge_at(0)
    last_row = edge_at(cells_x - 1)
    xlo_ref[...] = first_row
    xhi_ref[...] = last_row
    place = lane_ids((NZC, cells_y)) % BLK
    ones = jnp.ones((NZC, cells_y), jnp.float32)

    def field_of(row, field):
        return row[field * NZC : (field + 1) * NZC]

    def corners(row, fields, first_at):
        found = jnp.zeros((NZC, cells_y), jnp.float32)
        for order, field in enumerate(fields):
            at = first_at + 2 * order
            values = field_of(row, field)
            found = jnp.where(place == at, roll_lanes(values, at + 1), found)
            found = jnp.where(place == at + 1, roll_lanes(values, at + 1 - BLK), found)
        return found

    every = range(SPECIES)

    def near(row):
        own = [(field, field_of(row, field)) for field in range(SPECIES + 1)]
        return own + [(5, corners(row, [SPECIES], 0))]

    def far(row):
        return [
            (4, field_of(row, SPECIES)),
            (5, corners(row, every, 2)),
            (6, corners(row, [SPECIES], 0)),
        ]

    extra_members = {
        -1: far(first_row),
        0: near(first_row),
        block_cols - 1: near(last_row) + [(7, ones)],
        block_cols: far(last_row),
    }

    faces = [None] * (3 * FACES)

    def add(index, part):
        faces[index] = part if faces[index] is None else faces[index] + part

    for column in range(-1, block_cols + 1):
        members = []
        if column >= 1:
            members.append((0, rows_at(column * BLK - 1)))
        if column < block_cols - 1:
            members.append((1, rows_at(column * BLK + BLK)))
        if 0 <= column < block_cols:
            members.append((2, lower_y[column]))
            members.append((3, upper_y[column]))
        for index, rows in extra_members.get(column, []):
            members.append((FACES + index, rows))
        operands = []
        for _, rows in members:
            operands.extend(split_pair(rows))
        moved = jnp.dot(
            jnp.concatenate(operands, axis=0),
            selector(place_ref, column, cells_y),
            preferred_element_type=jnp.float32,
        )
        at = 0
        for index, rows in members:
            size = rows.shape[0]
            add(index, moved[at : at + size] + moved[at + size : at + 2 * size])
            at += 2 * size

    width = slots * BLK
    outgoing = [
        pltpu.make_async_copy(send_ref.at[target], send_hbm.at[target], send_sems.at[target])
        for target in range(group // slots)
    ]
    for target in range(group // slots):
        first = target * width
        tile = first // LANES * LANES
        for start, size, kind in (
            (0, STRIP_ROWS, 0),
            (STRIP_ROWS, NZC, FACES),
            (STRIP_ROWS + NZC, NZC, 2 * FACES),
        ):
            part = lane_ids((size, LANES)) // width
            chunk = jnp.zeros((size, LANES), jnp.float32)
            for index in range(FACES):
                piece = faces[kind + index][:, tile : tile + LANES]
                chunk = jnp.where(
                    part == index, roll_lanes(piece, index * width - (first - tile)), chunk
                )
            send_ref[target, start : start + size, :] = chunk
        outgoing[target].start()
    for copy in outgoing:
        copy.wait()
    keep_new.wait()


def ghost_table(tile):
    lane = lane_ids((BLK, LANES))
    pos = lax.broadcasted_iota(jnp.int32, (BLK, LANES), 0)
    x = tile * (LANES // EDGE) + lane // EDGE
    y = lane % EDGE
    along_y = y // RATIO == pos
    along_x = x // RATIO == pos
    seen = (
        (x == 0) & along_y,
        (x == EDGE - 1) & along_y,
        (y == 0) & along_x,
        (y == EDGE - 1) & along_x,
    )
    nothing = jnp.zeros((LANES // FACES - BLK, LANES), jnp.float32)
    rows = []
    for where in seen:
        rows.extend([jnp.where(where, 1.0, 0.0), nothing])
    return jnp.concatenate(rows + rows, axis=0).astype(jnp.bfloat16)


def plane_table():
    shape = (2 * SPECIES * FZ, STRIP_ROWS)
    rows = lax.broadcasted_iota(jnp.int32, shape, 0)
    return jnp.where(rows // RATIO == lane_ids(shape), 1.0, 0.0).astype(jnp.bfloat16)


def mean_table():
    shape = (2 * LANES, LANES)
    rows = lax.broadcasted_iota(jnp.int32, shape, 0)
    same = rows % EDGE // RATIO == lane_ids(shape) % BLK
    return jnp.where(same, 1.0 / RATIO**3, 0.0).astype(jnp.bfloat16)


def complete_strips(gathered):
    width = LANES // FACES
    own = gathered[STRIP_ROWS : STRIP_ROWS + NZC]
    beside = gathered[STRIP_ROWS + NZC : STRIP_ROWS + 2 * NZC]
    lane = lane_ids((NZC, LANES))
    part = lane // width
    pos = lane % BLK
    flag = jnp.where(part == FACES - 1, beside, 0.0)
    flag = flag + roll_lanes(flag, width)
    upper = flag + roll_lanes(flag, 2 * width) > 0.5

    def coefficient(one, other):
        return face(DT_COARSE, jnp.maximum(one, 0.125), jnp.maximum(other, 0.125))

    block = coefficient(roll_lanes(own, width), beside)
    corner = coefficient(beside, roll_lanes(beside, -width))
    added = []
    for field in range(SPECIES):
        old = gathered[field * NZC : (field + 1) * NZC]
        there = jnp.where(upper, roll_lanes(old, -width), old)
        across = DIFFUSE[field] * block * (roll_lanes(own, -field * width) - there)
        below = jnp.where(upper, roll_lanes(old, -width - (BLK - 1)), roll_lanes(old, -width))
        above = jnp.where(
            upper, roll_lanes(old, -2 * width - (BLK - 2)), roll_lanes(old, 1 - 2 * width)
        )
        here = jnp.where(pos == 0, below, above)
        along = DIFFUSE[field] * corner * (roll_lanes(beside, -2 - 2 * field) - here)
        share = jnp.where((part == 0) & ~upper, across, 0.0)
        share = jnp.where((part == 1) & upper, roll_lanes(across, width), share)
        for index in range(2):
            for at, chosen in ((0, ~upper), (BLK - 1, upper)):
                moved = roll_lanes(along, (1 + index) * width + at - index)
                share = jnp.where((part == 2 + index) & (pos == at) & chosen, moved, share)
        added.append(share)
    new = gathered[PLANES:STRIP_ROWS] + jnp.concatenate(added, axis=0)
    return gathered[:PLANES], new


def aligned(start, size):
    return pl.ds(pl.multiple_of(start, 8), size)


def padded_at(block, ztile):
    return block * STRIDE + PAD + DEPTH * ztile


def advance(source, target, coeffs, upward, slot, from_rows, to_rows, ztile, ghosts):
    lane = lane_ids((DEPTH, LANES))

    def value(field, tile, shift):
        start = from_rows + padded_at(field * TILES + tile, ztile) + shift
        return source[aligned(start, DEPTH) if shift == 0 else pl.ds(start, DEPTH), :]

    def get(kind, tile):
        return coeffs[
            aligned(slot * COEFF_ROWS + (kind * TILES + tile) * FZ + DEPTH * ztile, DEPTH), :
        ]

    centers = [value(field, 0, 0) for field in range(SPECIES)]
    down = [roll_lanes(center, -EDGE) for center in centers]
    up = [roll_lanes(center, EDGE) for center in centers]
    up_before = list(up)
    for tile in range(TILES):
        if tile + 1 < TILES:
            centers_after = [value(field, tile + 1, 0) for field in range(SPECIES)]
            down_after = [roll_lanes(center, -EDGE) for center in centers_after]
        next_x, prev_x, next_y, prev_y, rate = [get(kind, tile) for kind in range(5)]
        base = slot * UPWARD_ROWS + padded_at(tile, ztile)
        next_z = upward[aligned(base, DEPTH), :]
        prev_z = upward[pl.ds(base - 1, DEPTH), :]
        forward = rate * (centers[0] * centers[1] - centers[2])
        for field in range(SPECIES):
            center = centers[field]
            ahead, behind = down[field], up[field]
            if tile + 1 < TILES:
                ahead = jnp.where(lane < LANES - EDGE, ahead, down_after[field])
            if tile > 0:
                behind = jnp.where(lane >= EDGE, behind, up_before[field])
            flux = (next_x * ahead + prev_x * behind) + (
                next_y * roll_lanes(center, -1) + prev_y * roll_lanes(center, 1)
            )
            flux = flux + (next_z * value(field, tile, 1) + prev_z * value(field, tile, -1))
            share = ghosts(field, tile)
            if share is not None:
                flux = flux + share
            if DIFFUSE[field] != 1.0:
                flux = DIFFUSE[field] * flux
            result = get(5 + field, tile) * center + flux
            result = result - forward if SIGNS[field] < 0 else result + forward
            target[aligned(to_rows + padded_at(field * TILES + tile, ztile), DEPTH), :] = result
        if tile + 1 < TILES:
            up_before = up
            centers, down = centers_after, down_after
            up = [roll_lanes(center, EDGE) for center in centers]


def clear_pads(ref):
    edge = jnp.zeros((PAD, LANES), jnp.float32)

    def body(block, carry):
        ref[aligned(block * STRIDE, PAD), :] = edge
        ref[aligned(block * STRIDE + PAD + FZ, PAD), :] = edge
        return carry

    lax.fori_loop(0, ref.shape[0] // STRIDE, body, 0)


def hand_on_kernel(low_ref, high_ref, low_out, high_out):
    low_out[...] = low_ref[...]
    high_out[...] = high_ref[...]


def prepare_kernel(
    after_ref,
    state_hbm,
    kappa_hbm,
    rate_hbm,
    fields_hbm,
    coeffs_hbm,
    upward_hbm,
    fields_ref,
    coeffs,
    upward,
    state_ref,
    kappa_ref,
    rate_ref,
    first,
    conduct,
    sems,
    out_sems,
    *,
    slots,
):
    def loads(slot):
        return [
            pltpu.make_async_copy(source.at[slot], target.at[slot], sems.at[order, slot])
            for order, (source, target) in enumerate(
                ((kappa_hbm, kappa_ref), (rate_hbm, rate_ref), (state_hbm, state_ref))
            )
        ]

    for slot in range(slots):
        start_all(loads(slot))

    def stores(slot):
        return [
            pltpu.make_async_copy(
                source.at[aligned(slot * size, size)],
                target.at[aligned(slot * size, size)],
                out_sems.at[order, slot],
            )
            for order, (source, target, size) in enumerate(
                (
                    (fields_ref, fields_hbm, FIELD_ROWS),
                    (coeffs, coeffs_hbm, COEFF_ROWS),
                    (upward, upward_hbm, UPWARD_ROWS),
                )
            )
        ]

    for ref in (fields_ref, upward, first, conduct):
        clear_pads(ref)

    lane = lane_ids((DEPTH, LANES))
    column = lane % EDGE
    side_y = jnp.where((column == 0) | (column == EDGE - 1), 1.0, 0.0)

    def one_patch(slot, carry):
        for copy in loads(slot):
            copy.wait()

        for tile in range(TILES):
            cols = pl.ds(tile * LANES, LANES)
            for field in range(SPECIES):
                spot = aligned(slot * FIELD_ROWS + padded_at(field * TILES + tile, 0), FZ)
                first[spot, :] = state_ref[slot, field, :, cols]
            spot = aligned(slot * UPWARD_ROWS + padded_at(tile, 0), FZ)
            conduct[spot, :] = kappa_ref[slot, :, cols]

        def keep(kind, tile, ztile, values):
            coeffs[
                aligned(slot * COEFF_ROWS + (kind * TILES + tile) * FZ + DEPTH * ztile, DEPTH), :
            ] = values

        for ztile in range(ZTILES):

            def here(tile, shift):
                start = slot * UPWARD_ROWS + padded_at(tile, ztile) + shift
                return conduct[aligned(start, DEPTH) if shift == 0 else pl.ds(start, DEPTH), :]

            center = here(0, 0)
            turned = roll_lanes(center, -EDGE)
            back_before = None
            for tile in range(TILES):
                other = turned
                if tile + 1 < TILES:
                    center_after = here(tile + 1, 0)
                    turned_after = roll_lanes(center_after, -EDGE)
                    other = jnp.where(lane < LANES - EDGE, turned, turned_after)
                next_x = face(FINE_SCALE, center, other)
                if tile == TILES - 1:
                    next_x = jnp.where(lane < LANES - EDGE, next_x, 0.0)
                back = roll_lanes(next_x, EDGE)
                prev_x = jnp.where(lane >= EDGE, back, 0.0 if tile == 0 else back_before)
                next_y = jnp.where(
                    column < EDGE - 1, face(FINE_SCALE, center, roll_lanes(center, -1)), 0.0
                )
                prev_y = roll_lanes(next_y, 1)
                next_z = face(FINE_SCALE, center, here(tile, 1))
                prev_z = face(FINE_SCALE, center, here(tile, -1))
                sides = side_y
                if tile == 0:
                    sides = sides + jnp.where(lane < EDGE, 1.0, 0.0)
                if tile == TILES - 1:
                    sides = sides + jnp.where(lane >= LANES - EDGE, 1.0, 0.0)
                scale = FINE_SCALE * center
                total = (next_x + prev_x) + (next_y + prev_y) + (next_z + prev_z) + sides * scale
                upward[aligned(slot * UPWARD_ROWS + padded_at(tile, ztile), DEPTH), :] = next_z
                keep(0, tile, ztile, next_x)
                keep(1, tile, ztile, prev_x)
                keep(2, tile, ztile, next_y)
                keep(3, tile, ztile, prev_y)
                rate = rate_ref[slot, pl.ds(DEPTH * ztile, DEPTH), pl.ds(tile * LANES, LANES)]
                keep(4, tile, ztile, DT_FINE * rate)
                for field in range(SPECIES):
                    keep(5 + field, tile, ztile, 1.0 - DIFFUSE[field] * total)
                keep(8, tile, ztile, scale)
                back_before = back
                if tile + 1 < TILES:
                    center, turned = center_after, turned_after

        for ztile in range(ZTILES):
            advance(
                first,
                fields_ref,
                coeffs,
                upward,
                slot,
                slot * FIELD_ROWS,
                slot * FIELD_ROWS,
                ztile,
                lambda field, tile: None,
            )
        start_all(stores(slot))
        return carry

    lax.fori_loop(0, slots, one_patch, 0)
    for slot in range(slots):
        for copy in stores(slot):
            copy.wait()


def finish_kernel(
    strips_ref,
    fields_hbm,
    coeffs_hbm,
    upward_hbm,
    xl_ref,
    xr_ref,
    out_hbm,
    avg_hbm,
    fields_ref,
    coeffs,
    upward,
    ghost_ref,
    plane_ref,
    mean_ref,
    avg_ref,
    first,
    share,
    drift,
    staged,
    sems,
    in_sems,
    avg_sems,
    *,
    slots,
):
    sources = strips_ref.shape[0]

    def loads(slot):
        return [
            pltpu.make_async_copy(
                source.at[aligned(slot * size, size)],
                target.at[aligned(slot * size, size)],
                in_sems.at[order, slot],
            )
            for order, (source, target, size) in enumerate(
                (
                    (fields_hbm, fields_ref, FIELD_ROWS),
                    (coeffs_hbm, coeffs, COEFF_ROWS),
                    (upward_hbm, upward, UPWARD_ROWS),
                )
            )
        ]

    start_all(loads(0))
    clear_pads(first)
    for tile in range(TILES):
        ghost_ref[:, tile * LANES : (tile + 1) * LANES] = ghost_table(tile)
    plane_ref[...] = plane_table()
    mean_ref[...] = mean_table()

    gathered = strips_ref[0]
    for source in range(1, sources):
        gathered = gathered + strips_ref[source]
    old, new = complete_strips(gathered)
    gathered = jnp.concatenate([old, (new - old) * (1.0 / RATIO)], axis=0)
    quarter = AVG_ROWS // FACES
    group_of = lane_ids((quarter, LANES)) // BLK

    def send_out(slot):
        return pltpu.make_async_copy(staged.at[slot], out_hbm.at[slot], sems.at[slot])

    def one_patch(slot, carry):
        for copy in loads(slot):
            copy.wait()

        @pl.when(slot + 1 < slots)
        def _():
            start_all(loads(slot + 1))

        turned = pltpu.roll(gathered, (LANES - slot * BLK) % LANES, 1)
        stretched = jnp.dot(
            plane_ref[...],
            jnp.concatenate(split_pair(turned), axis=1),
            preferred_element_type=jnp.float32,
        ).astype(jnp.bfloat16)
        base = slot * FIELD_ROWS
        scales = slot * COEFF_ROWS
        for tile in range(TILES):
            ghosts = jnp.dot(
                stretched,
                ghost_ref[:, tile * LANES : (tile + 1) * LANES],
                preferred_element_type=jnp.float32,
            )
            scale = coeffs[aligned(scales + (8 * TILES + tile) * FZ, FZ), :]
            for field in range(SPECIES):
                row = (field * TILES + tile) * FZ
                old = scale * ghosts[field * FZ : (field + 1) * FZ]
                step = scale * ghosts[(SPECIES + field) * FZ : (SPECIES + field + 1) * FZ]
                drift[row : row + FZ, :] = step
                share[row : row + FZ, :] = old + step
                spot = aligned(base + padded_at(field * TILES + tile, 0), FZ)
                fields_ref[spot, :] = fields_ref[spot, :] + DIFFUSE[field] * old

        for step in range(1, RATIO):
            source, target = (fields_ref, first) if step % 2 else (first, fields_ref)
            for ztile in range(ZTILES):

                def ghosts(field, tile):
                    spot = pl.ds((field * TILES + tile) * FZ + DEPTH * ztile, DEPTH)
                    value = share[spot, :]
                    if step + 1 < RATIO:
                        share[spot, :] = value + drift[spot, :]
                    return value

                advance(source, target, coeffs, upward, slot, base, base, ztile, ghosts)

        for tile in range(TILES):
            for field in range(SPECIES):
                spot = aligned(base + padded_at(field * TILES + tile, 0), FZ)
                staged[slot, field, :, pl.ds(tile * LANES, LANES)] = first[spot, :]
        send_out(slot).start()

        sums = []
        for field in range(SPECIES):
            for plane in range(NZC):
                start = base + field * TILES * STRIDE + PAD + RATIO * plane
                part = first[pl.ds(start, TILES, stride=STRIDE), :]
                for z in range(1, RATIO):
                    part = part + first[pl.ds(start + z, TILES, stride=STRIDE), :]
                sums.append(part)
        means = jnp.dot(
            jnp.concatenate(split_pair(jnp.concatenate(sums, axis=0)), axis=1),
            mean_ref[...],
            preferred_element_type=jnp.float32,
        )
        chunk = avg_ref[...]
        for part in range(FACES):
            chunk = jnp.where(
                group_of == part * slots + slot,
                means[part * quarter : (part + 1) * quarter],
                chunk,
            )
        avg_ref[...] = chunk
        return carry

    avg_ref[...] = jnp.zeros((quarter, LANES), jnp.float32)
    lax.fori_loop(0, slots, one_patch, 0)
    copies = [
        pltpu.make_async_copy(avg_ref, avg_hbm.at[target], avg_sems.at[target])
        for target in range(sources)
    ]
    start_all(copies)
    for copy in copies:
        copy.wait()
    for slot in range(slots):
        send_out(slot).wait()


def edges_kernel(
    new_hbm,
    xlo_ref,
    xhi_ref,
    ylo_ref,
    yhi_ref,
    xl_ref,
    xr_ref,
    yl_ref,
    yr_ref,
    out_ref,
    new_ref,
    sem,
    *,
    cells_x,
    cells_y,
):
    me = lax.axis_index("af")
    last = lax.axis_size("af") - 1
    fetch = pltpu.make_async_copy(new_hbm, new_ref, sem)
    fetch.start()

    def edge_share(own_ref, other_ref):
        own = own_ref[...]
        other = other_ref[...]
        coeff = face(DT_COARSE, jnp.maximum(own, 0.125), other)
        lane = lane_ids(own.shape)
        spread = jnp.zeros_like(own)
        for field in range(SPECIES):
            moved = roll_lanes(coeff, (field - SPECIES) * NZC)
            spread = jnp.where(lane // NZC == field, DIFFUSE[field] * moved, spread)
        return spread * (other - own)

    lower = edge_share(ylo_ref, yl_ref)
    upper = edge_share(yhi_ref, yr_ref)

    lane = lane_ids((BLK, LANES))
    row_id = lax.broadcasted_iota(jnp.int32, (BLK, LANES), 0)
    halves = cells_y // LANES

    def side_share(own_ref, other_ref, exists):
        shares = []
        for half in range(halves):
            own = own_ref[:, half * LANES : (half + 1) * LANES]
            other = other_ref[:, half * LANES : (half + 1) * LANES]
            coeff = face(DT_COARSE, own[PLANES:], other[PLANES:])
            coeff = jnp.where(exists, coeff, 0.0)
            shares.append(
                jnp.concatenate(
                    [
                        (DIFFUSE[field] * coeff)
                        * (
                            other[field * NZC : (field + 1) * NZC]
                            - own[field * NZC : (field + 1) * NZC]
                        )
                        for field in range(SPECIES)
                    ],
                    axis=0,
                )
            )
        return shares

    before = side_share(xlo_ref, xl_ref, me > 0)
    after = side_share(xhi_ref, xr_ref, me < last)
    fetch.wait()
    block_cols = cells_x // BLK
    for column in range(block_cols):
        for plane in range(PLANES):
            row = plane * cells_x + column * BLK
            edge_rows = slice(column * BLK, (column + 1) * BLK)
            for half in range(halves):
                cols = slice(half * LANES, (half + 1) * LANES)
                coarse = new_ref[row : row + BLK, cols]
                if column == 0:
                    share = before[half][plane : plane + 1]
                    coarse = coarse + jnp.where(row_id == 0, share, 0.0)
                if column == block_cols - 1:
                    share = after[half][plane : plane + 1]
                    coarse = coarse + jnp.where(row_id == BLK - 1, share, 0.0)
                if half == 0:
                    share = roll_lanes(lower[edge_rows], -plane)
                    coarse = coarse + jnp.where(lane == 0, share, 0.0)
                if half == halves - 1:
                    share = roll_lanes(upper[edge_rows], LANES - 1 - plane)
                    coarse = coarse + jnp.where(lane == LANES - 1, share, 0.0)
                out_ref[row : row + BLK, cols] = coarse


def place_kernel(
    place_ref, avg_ref, new_ref, out_ref, *, cells_x, cells_y, group, slots
):
    width = slots * BLK
    quarter = AVG_ROWS // FACES
    per_tile = LANES // width
    part = lane_ids((quarter, LANES)) // width
    columns = []
    for tile in range(group * BLK // LANES):
        rows = []
        for index in range(FACES):
            merged = jnp.zeros((quarter, LANES), jnp.float32)
            for place in range(per_tile):
                piece = roll_lanes(avg_ref[tile * per_tile + place], (place - index) * width)
                merged = jnp.where(part == place, piece, merged)
            rows.append(merged)
        columns.append(jnp.concatenate(rows, axis=0))
    high, low = split_pair(jnp.concatenate(columns, axis=1))
    ones = jnp.ones((16, high.shape[1]), jnp.bfloat16)
    stacked = jnp.concatenate([high, low, ones], axis=0)

    halves = cells_y // LANES
    for column in range(cells_x // BLK):
        placed = lax.dot_general(
            stacked,
            selector(place_ref, column, cells_y),
            (((1,), (1,)), ((), ())),
            preferred_element_type=jnp.float32,
        )
        covered = placed[2 * AVG_ROWS : 2 * AVG_ROWS + 8] > 0.5
        for plane in range(PLANES):
            values = (
                placed[plane * BLK : (plane + 1) * BLK]
                + placed[AVG_ROWS + plane * BLK : AVG_ROWS + (plane + 1) * BLK]
            )
            row = plane * cells_x + column * BLK
            for half in range(halves):
                cols = slice(half * LANES, (half + 1) * LANES)
                coarse = new_ref[row : row + BLK, cols]
                out_ref[row : row + BLK, cols] = jnp.where(
                    covered[:, cols], values[:, cols], coarse
                )


VMEM = pl.BlockSpec(memory_space=pltpu.VMEM)
HBM = pl.BlockSpec(memory_space=pltpu.HBM)
PARAMS = pltpu.CompilerParams(vmem_limit_bytes=40 * 1024 * 1024)


def f32(*shape):
    return jax.ShapeDtypeStruct(shape, jnp.float32)


def hbm32(*shape):
    return pltpu.HBM(shape, jnp.float32)


def pinned(*arrays):
    return [pltpu.with_memory_space_constraint(array, pltpu.HBM) for array in arrays]


def shifted(values, axis, step):
    count = lax.axis_size(axis)
    pairs = [(i, i + step) for i in range(count) if 0 <= i + step < count]
    return lax.ppermute(values, axis, pairs)


def exchange(chunks):
    return lax.all_to_all(chunks, "af", split_axis=0, concat_axis=0, tiled=True)


def per_device(
    coarse_state, coarse_kappa, coarse_rate, fine_state, fine_kappa, fine_rate, boxes, cover
):
    af_count = lax.axis_size("af")
    slots = fine_state.shape[0]
    cells_x, cells_y = coarse_state.shape[2:]
    group = af_count * slots
    lanes = group * BLK
    halves = cells_y // LANES
    rows = PLANES * cells_x
    plain = NZC * cells_x
    sizes = dict(cells_x=cells_x, cells_y=cells_y, group=group)

    span = cells_x + 2 * PAD
    new, send, place, xlo, xhi, ylo, yhi = pl.pallas_call(
        functools.partial(strips_kernel, slots=slots, **sizes),
        out_shape=[
            hbm32(rows, cells_y),
            hbm32(af_count, CHUNK_ROWS, LANES),
            jax.ShapeDtypeStruct((16, lanes), jnp.int32),
        ]
        + [f32(EDGE_ROWS, cells_y)] * 2
        + [f32(cells_x, LANES)] * 2,
        in_specs=[HBM] * 4,
        out_specs=[HBM] * 2 + [VMEM] * 5,
        scratch_shapes=[
            pltpu.VMEM((2, boxes.shape[0]), jnp.int32),
            pltpu.VMEM((rows, cells_y), jnp.float32),
            pltpu.VMEM((plain, cells_y), jnp.float32),
            pltpu.VMEM((plain, cells_y), jnp.float32),
            pltpu.VMEM((rows, cells_y), jnp.float32),
            pltpu.VMEM(((SPECIES + 1) * halves * NZC * span, LANES), jnp.float32),
            pltpu.VMEM((rows * halves, LANES), jnp.float32),
            pltpu.VMEM((af_count, CHUNK_ROWS, LANES), jnp.float32),
            pltpu.SemaphoreType.DMA((4,)),
            pltpu.SemaphoreType.DMA((af_count,)),
        ],
        compiler_params=PARAMS,
        name="strips",
    )(
        *pinned(
            boxes.T,
            coarse_state.reshape(rows, cells_y),
            coarse_kappa.reshape(plain, cells_y),
            coarse_rate.reshape(plain, cells_y),
        )
    )

    strips = exchange(send)

    xlo_sent, xhi_sent = pl.pallas_call(
        hand_on_kernel,
        out_shape=[f32(EDGE_ROWS, cells_y)] * 2,
        in_specs=[VMEM] * 2,
        out_specs=[VMEM] * 2,
        compiler_params=pltpu.CompilerParams(vmem_limit_bytes=1024 * 1024),
        name="hand_on",
    )(xlo, xhi)
    xl = shifted(xhi_sent, "af", 1)
    xr = shifted(xlo_sent, "af", -1)

    kept = [hbm32(slots * size, LANES) for size in (FIELD_ROWS, COEFF_ROWS, UPWARD_ROWS)]
    kept_scratch = [pltpu.VMEM((slots * size, LANES), jnp.float32)
        for size in (FIELD_ROWS, COEFF_ROWS, UPWARD_ROWS)]
    fields, coeffs, upward = pl.pallas_call(
        functools.partial(prepare_kernel, slots=slots),
        out_shape=kept,
        in_specs=[VMEM] + [HBM] * 3,
        out_specs=[HBM] * 3,
        scratch_shapes=kept_scratch
        + [
            pltpu.VMEM(fine_state.shape, jnp.float32),
            pltpu.VMEM(fine_kappa.shape, jnp.float32),
            pltpu.VMEM(fine_rate.shape, jnp.float32),
            pltpu.VMEM((slots * FIELD_ROWS, LANES), jnp.float32),
            pltpu.VMEM((slots * UPWARD_ROWS, LANES), jnp.float32),
            pltpu.SemaphoreType.DMA((3, slots)),
            pltpu.SemaphoreType.DMA((3, slots)),
        ],
        compiler_params=PARAMS,
        name="prepare",
    )(xlo_sent, *pinned(fine_state, fine_kappa, fine_rate))

    chunk = (AVG_ROWS // FACES, LANES)
    fine_out, averages = pl.pallas_call(
        functools.partial(finish_kernel, slots=slots),
        out_shape=[hbm32(*fine_state.shape), hbm32(af_count, *chunk)],
        in_specs=[VMEM] + [HBM] * 3 + [VMEM] * 2,
        out_specs=[HBM] * 2,
        scratch_shapes=kept_scratch
        + [
            pltpu.VMEM((2 * LANES, EDGE * EDGE), jnp.bfloat16),
            pltpu.VMEM((2 * SPECIES * FZ, STRIP_ROWS), jnp.bfloat16),
            pltpu.VMEM((2 * LANES, LANES), jnp.bfloat16),
            pltpu.VMEM(chunk, jnp.float32),
            pltpu.VMEM((slots * FIELD_ROWS, LANES), jnp.float32),
            pltpu.VMEM((SPECIES * TILES * FZ, LANES), jnp.float32),
            pltpu.VMEM((SPECIES * TILES * FZ, LANES), jnp.float32),
            pltpu.VMEM(fine_state.shape, jnp.float32),
            pltpu.SemaphoreType.DMA((slots,)),
            pltpu.SemaphoreType.DMA((3, slots)),
            pltpu.SemaphoreType.DMA((af_count,)),
        ],
        compiler_params=PARAMS,
        name="finish",
    )(strips, *pinned(fields, coeffs, upward), xl, xr)

    arrived = exchange(averages)

    yl = shifted(yhi, "col", 1)
    yr = shifted(ylo, "col", -1)
    whole = pl.pallas_call(
        functools.partial(edges_kernel, cells_x=cells_x, cells_y=cells_y),
        out_shape=f32(rows, cells_y),
        in_specs=[HBM] + [VMEM] * 8,
        out_specs=VMEM,
        scratch_shapes=[pltpu.VMEM((rows, cells_y), jnp.float32), pltpu.SemaphoreType.DMA],
        compiler_params=PARAMS,
        name="edges",
    )(*pinned(new), xlo, xhi, ylo, yhi, xl, xr, yl, yr)

    placed = pl.pallas_call(
        functools.partial(place_kernel, slots=slots, **sizes),
        out_shape=f32(rows, cells_y),
        in_specs=[VMEM] * 3,
        out_specs=VMEM,
        compiler_params=PARAMS,
        name="place",
    )(place, arrived, whole)
    return (placed.reshape(coarse_state.shape), fine_out)


def solution(mesh):
    return jax.shard_map(
        per_device,
        mesh=mesh,
        in_specs=(
            P(None, None, "af", "col"),
            P(None, "af", "col"),
            P(None, "af", "col"),
            P(("col", "af"), None, None, None),
            P(("col", "af"), None, None),
            P(("col", "af"), None, None),
            P(),
            P(),
        ),
        out_specs=(P(None, None, "af", "col"), P(("col", "af"), None, None, None)),
        check_vma=False,
    )
```

```python
import functools

import jax
import jax.numpy as jnp
from jax import lax
from jax.experimental import pallas as pl
from jax.experimental.pallas import tpu as pltpu
from jax.sharding import PartitionSpec as P

NZC = 8
RATIO = 4
BLK = 8
SPECIES = 3
EDGE = BLK * RATIO
FZ = NZC * RATIO
LANES = 128
TILES = EDGE * EDGE // LANES
DEPTH = 8
ZTILES = FZ // DEPTH
STRIDE = 48
PAD = 8
FACES = 4
PLANES = SPECIES * NZC
STRIP_ROWS = 2 * PLANES
AVG_ROWS = PLANES * BLK
KINDS = 8
FIELD_ROWS = SPECIES * TILES * STRIDE
COEFF_ROWS = KINDS * TILES * FZ
UPWARD_ROWS = TILES * STRIDE
EDGE_ROWS = PLANES + NZC
BESIDE_ROWS = 2 * NZC
CHUNK_ROWS = STRIP_ROWS + BESIDE_ROWS

DT_COARSE = 1.0 / 28.0
DIFFUSE = (1.0, 0.7, 0.45)
SIGNS = (-1.0, -1.0, 1.0)
FINE_SCALE = RATIO * RATIO * DT_COARSE / RATIO
DT_FINE = DT_COARSE / RATIO


def lane_ids(shape):
    return lax.broadcasted_iota(jnp.int32, shape, len(shape) - 1)


def roll_lanes(values, shift):
    width = values.shape[-1]
    shift = shift % width
    return values if shift == 0 else pltpu.roll(values, shift, values.ndim - 1)


def split_pair(values):
    high = values.astype(jnp.bfloat16)
    low = (values - high.astype(jnp.float32)).astype(jnp.bfloat16)
    return high, low


def face(scale, one, other):
    summed = one + other
    inverse = pl.reciprocal(summed, approx=True)
    inverse = inverse * (2.0 - summed * inverse)
    return (2.0 * scale) * (one * other) * inverse


def start_all(copies):
    for copy in copies:
        copy.start()


def selector(place_ref, column, cells_y):
    wanted = jnp.where(place_ref[0:8, :] == column, place_ref[8:16, :], -1)
    row = lax.broadcasted_iota(jnp.int32, wanted.shape, 0)
    return jnp.concatenate(
        [jnp.where(row + 8 * at == wanted, 1.0, 0.0) for at in range(cells_y // 8)], axis=0
    ).astype(jnp.bfloat16)


def strips_kernel(
    boxes_hbm,
    state_hbm,
    kappa_hbm,
    rate_hbm,
    new_hbm,
    send_hbm,
    place_ref,
    xlo_ref,
    xhi_ref,
    ylo_ref,
    yhi_ref,
    boxes_ref,
    state_ref,
    kappa_ref,
    rate_ref,
    new_ref,
    padded,
    fresh,
    send_ref,
    sems,
    send_sems,
    *,
    cells_x,
    cells_y,
    group,
    slots,
):
    pairs = (
        (boxes_hbm, boxes_ref),
        (kappa_hbm, kappa_ref),
        (state_hbm, state_ref),
        (rate_hbm, rate_ref),
    )
    copies = [
        pltpu.make_async_copy(source, target, sems.at[index])
        for index, (source, target) in enumerate(pairs)
    ]
    start_all(copies)

    patches = boxes_ref.shape[1]
    lanes = group * BLK
    base_patch = lax.axis_index("col") * group
    member = lax.broadcasted_iota(jnp.int32, (patches, lanes), 0) - base_patch
    spread = jnp.where(member == lane_ids((patches, lanes)) // BLK, 1.0, 0.0).astype(jnp.bfloat16)
    first_col = lax.axis_index("af") * (cells_x // BLK)
    first_cell = lax.axis_index("col") * cells_y
    copies[0].wait()
    boxes = boxes_ref[...].astype(jnp.float32)
    stacked = jnp.concatenate(
        [jnp.broadcast_to(boxes[row : row + 1], (8, patches)) for row in range(2)], axis=0
    )
    found = jnp.dot(
        stacked.astype(jnp.bfloat16), spread, preferred_element_type=jnp.float32
    ).astype(jnp.int32)
    place_ref[0:8, :] = found[0:8] - first_col
    place_ref[8:16, :] = found[8:16] * BLK - first_cell + lane_ids((8, lanes)) % BLK

    halves = cells_y // LANES
    span = cells_x + 2 * PAD
    nothing = jnp.zeros((PAD, LANES), jnp.float32)

    def base(field, half, z):
        return ((field * halves + half) * NZC + z) * span

    for copy in copies[1:]:
        copy.wait()
    for field in range(SPECIES + 1):
        for half in range(halves):
            cols = pl.ds(half * LANES, LANES)
            for z in range(NZC):
                if field < SPECIES:
                    start = (field * NZC + z) * cells_x
                    plane = state_ref[start : start + cells_x, cols]
                else:
                    plane = kappa_ref[z * cells_x : (z + 1) * cells_x, cols]
                at = base(field, half, z)
                padded[at : at + PAD, :] = nothing
                padded[at + PAD : at + PAD + cells_x, :] = plane
                padded[at + PAD + cells_x : at + span, :] = nothing

    lane = lane_ids((cells_x, LANES))
    row_id = lax.broadcasted_iota(jnp.int32, (cells_x, LANES), 0)

    low = jnp.zeros((cells_x, LANES), jnp.float32)
    high = jnp.zeros((cells_x, LANES), jnp.float32)
    for plane in range(PLANES + NZC):
        field, z = divmod(plane, NZC)
        at = base(field, 0, z) + PAD
        first = padded[at : at + cells_x, :]
        at = base(field, halves - 1, z) + PAD
        last = padded[at : at + cells_x, :]
        low = jnp.where(lane == plane, roll_lanes(first, plane), low)
        high = jnp.where(lane == plane, roll_lanes(last, plane + 1), high)
    ylo_ref[...] = low
    yhi_ref[...] = high

    def load(field, half, z, shift):
        at = base(field, half, z) + PAD + shift
        return padded[at : at + cells_x, :]

    def neighbours(field, half, z):
        here = load(field, half, z, 0)
        after = roll_lanes(here, -1)
        if half + 1 < halves:
            after = jnp.where(
                lane == LANES - 1, roll_lanes(load(field, half + 1, z, 0), -1), after
            )
        before = roll_lanes(here, 1)
        if half > 0:
            before = jnp.where(lane == 0, roll_lanes(load(field, half - 1, z, 0), 1), before)
        found = [after, before, load(field, half, z, 1), load(field, half, z, -1)]
        if z + 1 < NZC:
            found.append(load(field, half, z + 1, 0))
        if z > 0:
            found.append(load(field, half, z - 1, 0))
        return found

    for z in range(NZC):
        for half in range(halves):
            cols = pl.ds(half * LANES, LANES)
            conduct = load(SPECIES, half, z, 0)
            coeffs = [face(DT_COARSE, conduct, other) for other in neighbours(SPECIES, half, z)]
            if half == halves - 1:
                coeffs[0] = jnp.where(lane == LANES - 1, 0.0, coeffs[0])
            if half == 0:
                coeffs[1] = jnp.where(lane == 0, 0.0, coeffs[1])
            coeffs[2] = jnp.where(row_id == cells_x - 1, 0.0, coeffs[2])
            coeffs[3] = jnp.where(row_id == 0, 0.0, coeffs[3])
            centers = [load(field, half, z, 0) for field in range(SPECIES)]
            forward = (DT_COARSE * rate_ref[z * cells_x : (z + 1) * cells_x, cols]) * (
                centers[0] * centers[1] - centers[2]
            )
            for field in range(SPECIES):
                center = centers[field]
                flux = None
                for coeff, other in zip(coeffs, neighbours(field, half, z)):
                    term = coeff * (other - center)
                    flux = term if flux is None else flux + term
                start = (field * NZC + z) * cells_x
                result = center + DIFFUSE[field] * flux + SIGNS[field] * forward
                new_ref[start : start + cells_x, cols] = result
                start = ((field * halves + half) * NZC + z) * cells_x
                fresh[start : start + cells_x, :] = result

    keep_new = pltpu.make_async_copy(new_ref, new_hbm, sems.at[0])
    keep_new.start()

    def old_row(field, half, row):
        return padded[pl.ds(base(field, half, 0) + PAD + row, NZC, stride=span), :]

    def edge_at(row):
        return jnp.concatenate(
            [
                jnp.concatenate([old_row(field, half, row) for field in range(SPECIES + 1)], axis=0)
                for half in range(halves)
            ],
            axis=1,
        )

    def rows_at(row):
        columns = []
        for half in range(halves):
            pieces = [old_row(field, half, row) for field in range(SPECIES)]
            for field in range(SPECIES):
                start = (field * halves + half) * NZC * cells_x
                pieces.append(fresh[pl.ds(start + row, NZC, stride=cells_x), :])
            columns.append(jnp.concatenate(pieces, axis=0))
        return jnp.concatenate(columns, axis=1)

    block_cols = cells_x // BLK
    spot = lane_ids((STRIP_ROWS, cells_y)) % BLK
    lower_y = []
    upper_y = []
    for column in range(block_cols):
        below = jnp.zeros((STRIP_ROWS, cells_y), jnp.float32)
        above = jnp.zeros((STRIP_ROWS, cells_y), jnp.float32)
        for x in range(BLK):
            turned = roll_lanes(rows_at(column * BLK + x), x + 1)
            below = jnp.where(spot == x, turned, below)
            above = jnp.where(spot == (x + 1) % BLK, turned, above)
        lower_y.append(below)
        upper_y.append(roll_lanes(above, -1 - BLK))

    first_row = edge_at(0)
    last_row = edge_at(cells_x - 1)
    xlo_ref[...] = first_row
    xhi_ref[...] = last_row
    place = lane_ids((NZC, cells_y)) % BLK
    ones = jnp.ones((NZC, cells_y), jnp.float32)

    def field_of(row, field):
        return row[field * NZC : (field + 1) * NZC]

    def corners(row, fields, first_at):
        found = jnp.zeros((NZC, cells_y), jnp.float32)
        for order, field in enumerate(fields):
            at = first_at + 2 * order
            values = field_of(row, field)
            found = jnp.where(place == at, roll_lanes(values, at + 1), found)
            found = jnp.where(place == at + 1, roll_lanes(values, at + 1 - BLK), found)
        return found

    every = range(SPECIES)

    def near(row):
        own = [(field, field_of(row, field)) for field in range(SPECIES + 1)]
        return own + [(5, corners(row, [SPECIES], 0))]

    def far(row):
        return [
            (4, field_of(row, SPECIES)),
            (5, corners(row, every, 2)),
            (6, corners(row, [SPECIES], 0)),
        ]

    extra_members = {
        -1: far(first_row),
        0: near(first_row),
        block_cols - 1: near(last_row) + [(7, ones)],
        block_cols: far(last_row),
    }

    faces = [None] * (3 * FACES)

    def add(index, part):
        faces[index] = part if faces[index] is None else faces[index] + part

    for column in range(-1, block_cols + 1):
        members = []
        if column >= 1:
            members.append((0, rows_at(column * BLK - 1)))
        if column < block_cols - 1:
            members.append((1, rows_at(column * BLK + BLK)))
        if 0 <= column < block_cols:
            members.append((2, lower_y[column]))
            members.append((3, upper_y[column]))
        for index, rows in extra_members.get(column, []):
            members.append((FACES + index, rows))
        operands = []
        for _, rows in members:
            operands.extend(split_pair(rows))
        moved = jnp.dot(
            jnp.concatenate(operands, axis=0),
            selector(place_ref, column, cells_y),
            preferred_element_type=jnp.float32,
        )
        at = 0
        for index, rows in members:
            size = rows.shape[0]
            add(index, moved[at : at + size] + moved[at + size : at + 2 * size])
            at += 2 * size

    width = slots * BLK
    outgoing = [
        pltpu.make_async_copy(send_ref.at[target], send_hbm.at[target], send_sems.at[target])
        for target in range(group // slots)
    ]
    for target in range(group // slots):
        first = target * width
        tile = first // LANES * LANES
        for start, size, kind in (
            (0, STRIP_ROWS, 0),
            (STRIP_ROWS, NZC, FACES),
            (STRIP_ROWS + NZC, NZC, 2 * FACES),
        ):
            part = lane_ids((size, LANES)) // width
            chunk = jnp.zeros((size, LANES), jnp.float32)
            for index in range(FACES):
                piece = faces[kind + index][:, tile : tile + LANES]
                chunk = jnp.where(
                    part == index, roll_lanes(piece, index * width - (first - tile)), chunk
                )
            send_ref[target, start : start + size, :] = chunk
        outgoing[target].start()
    for copy in outgoing:
        copy.wait()
    keep_new.wait()


def ghost_table(tile):
    lane = lane_ids((BLK, LANES))
    pos = lax.broadcasted_iota(jnp.int32, (BLK, LANES), 0)
    x = tile * (LANES // EDGE) + lane // EDGE
    y = lane % EDGE
    along_y = y // RATIO == pos
    along_x = x // RATIO == pos
    seen = (
        (x == 0) & along_y,
        (x == EDGE - 1) & along_y,
        (y == 0) & along_x,
        (y == EDGE - 1) & along_x,
    )
    nothing = jnp.zeros((LANES // FACES - BLK, LANES), jnp.float32)
    rows = []
    for where in seen:
        rows.extend([jnp.where(where, 1.0, 0.0), nothing])
    return jnp.concatenate(rows + rows, axis=0).astype(jnp.bfloat16)


def plane_table():
    shape = (2 * SPECIES * FZ, STRIP_ROWS)
    rows = lax.broadcasted_iota(jnp.int32, shape, 0)
    return jnp.where(rows // RATIO == lane_ids(shape), 1.0, 0.0).astype(jnp.bfloat16)


def mean_table():
    shape = (2 * LANES, LANES)
    rows = lax.broadcasted_iota(jnp.int32, shape, 0)
    same = rows % EDGE // RATIO == lane_ids(shape) % BLK
    return jnp.where(same, 1.0 / RATIO**3, 0.0).astype(jnp.bfloat16)


def complete_strips(gathered):
    width = LANES // FACES
    own = gathered[STRIP_ROWS : STRIP_ROWS + NZC]
    beside = gathered[STRIP_ROWS + NZC : STRIP_ROWS + 2 * NZC]
    lane = lane_ids((NZC, LANES))
    part = lane // width
    pos = lane % BLK
    flag = jnp.where(part == FACES - 1, beside, 0.0)
    flag = flag + roll_lanes(flag, width)
    upper = flag + roll_lanes(flag, 2 * width) > 0.5

    def coefficient(one, other):
        return face(DT_COARSE, jnp.maximum(one, 0.125), jnp.maximum(other, 0.125))

    block = coefficient(roll_lanes(own, width), beside)
    corner = coefficient(beside, roll_lanes(beside, -width))
    added = []
    for field in range(SPECIES):
        old = gathered[field * NZC : (field + 1) * NZC]
        there = jnp.where(upper, roll_lanes(old, -width), old)
        across = DIFFUSE[field] * block * (roll_lanes(own, -field * width) - there)
        below = jnp.where(upper, roll_lanes(old, -width - (BLK - 1)), roll_lanes(old, -width))
        above = jnp.where(
            upper, roll_lanes(old, -2 * width - (BLK - 2)), roll_lanes(old, 1 - 2 * width)
        )
        here = jnp.where(pos == 0, below, above)
        along = DIFFUSE[field] * corner * (roll_lanes(beside, -2 - 2 * field) - here)
        share = jnp.where((part == 0) & ~upper, across, 0.0)
        share = jnp.where((part == 1) & upper, roll_lanes(across, width), share)
        for index in range(2):
            for at, chosen in ((0, ~upper), (BLK - 1, upper)):
                moved = roll_lanes(along, (1 + index) * width + at - index)
                share = jnp.where((part == 2 + index) & (pos == at) & chosen, moved, share)
        added.append(share)
    new = gathered[PLANES:STRIP_ROWS] + jnp.concatenate(added, axis=0)
    return gathered[:PLANES], new


def aligned(start, size):
    return pl.ds(pl.multiple_of(start, 8), size)


def padded_at(block, ztile):
    return block * STRIDE + PAD + DEPTH * ztile


def advance(source, target, coeffs, upward, slot, from_rows, to_rows, ztile, ghosts):
    lane = lane_ids((DEPTH, LANES))

    def value(field, tile, shift):
        start = from_rows + padded_at(field * TILES + tile, ztile) + shift
        return source[aligned(start, DEPTH) if shift == 0 else pl.ds(start, DEPTH), :]

    def get(kind, tile):
        return coeffs[
            aligned(slot * COEFF_ROWS + (kind * TILES + tile) * FZ + DEPTH * ztile, DEPTH), :
        ]

    centers = [value(field, 0, 0) for field in range(SPECIES)]
    down = [roll_lanes(center, -EDGE) for center in centers]
    up = [roll_lanes(center, EDGE) for center in centers]
    up_before = list(up)
    for tile in range(TILES):
        if tile + 1 < TILES:
            centers_after = [value(field, tile + 1, 0) for field in range(SPECIES)]
            down_after = [roll_lanes(center, -EDGE) for center in centers_after]
        next_x, prev_x, next_y, rate = [get(kind, tile) for kind in range(4)]
        prev_y = roll_lanes(next_y, 1)
        base = slot * UPWARD_ROWS + padded_at(tile, ztile)
        next_z = upward[aligned(base, DEPTH), :]
        prev_z = upward[pl.ds(base - 1, DEPTH), :]
        forward = rate * (centers[0] * centers[1] - centers[2])
        for field in range(SPECIES):
            center = centers[field]
            ahead, behind = down[field], up[field]
            if tile + 1 < TILES:
                ahead = jnp.where(lane < LANES - EDGE, ahead, down_after[field])
            if tile > 0:
                behind = jnp.where(lane >= EDGE, behind, up_before[field])
            flux = (next_x * ahead + prev_x * behind) + (
                next_y * roll_lanes(center, -1) + prev_y * roll_lanes(center, 1)
            )
            flux = flux + (next_z * value(field, tile, 1) + prev_z * value(field, tile, -1))
            share = ghosts(field, tile)
            if share is not None:
                flux = flux + share
            if DIFFUSE[field] != 1.0:
                flux = DIFFUSE[field] * flux
            result = get(4 + field, tile) * center + flux
            result = result - forward if SIGNS[field] < 0 else result + forward
            target[aligned(to_rows + padded_at(field * TILES + tile, ztile), DEPTH), :] = result
        if tile + 1 < TILES:
            up_before = up
            centers, down = centers_after, down_after
            up = [roll_lanes(center, EDGE) for center in centers]


def clear_pads(ref):
    edge = jnp.zeros((PAD, LANES), jnp.float32)

    def body(block, carry):
        ref[aligned(block * STRIDE, PAD), :] = edge
        ref[aligned(block * STRIDE + PAD + FZ, PAD), :] = edge
        return carry

    lax.fori_loop(0, ref.shape[0] // STRIDE, body, 0)


def hand_on_kernel(low_ref, high_ref, low_out, high_out):
    low_out[...] = low_ref[...]
    high_out[...] = high_ref[...]


def prepare_kernel(
    after_ref,
    state_hbm,
    kappa_hbm,
    rate_hbm,
    fields_hbm,
    coeffs_hbm,
    upward_hbm,
    fields_ref,
    coeffs,
    upward,
    state_ref,
    kappa_ref,
    rate_ref,
    first,
    conduct,
    sems,
    out_sems,
    *,
    slots,
):
    def loads(slot):
        return [
            pltpu.make_async_copy(source.at[slot], target.at[slot], sems.at[order, slot])
            for order, (source, target) in enumerate(
                ((kappa_hbm, kappa_ref), (rate_hbm, rate_ref), (state_hbm, state_ref))
            )
        ]

    for slot in range(slots):
        start_all(loads(slot))

    def stores(slot):
        return [
            pltpu.make_async_copy(
                source.at[aligned(slot * size, size)],
                target.at[aligned(slot * size, size)],
                out_sems.at[order, slot],
            )
            for order, (source, target, size) in enumerate(
                (
                    (fields_ref, fields_hbm, FIELD_ROWS),
                    (coeffs, coeffs_hbm, COEFF_ROWS),
                    (upward, upward_hbm, UPWARD_ROWS),
                )
            )
        ]

    for ref in (fields_ref, upward, first, conduct):
        clear_pads(ref)

    lane = lane_ids((DEPTH, LANES))
    column = lane % EDGE
    side_y = jnp.where((column == 0) | (column == EDGE - 1), 1.0, 0.0)

    def one_patch(slot, carry):
        for copy in loads(slot):
            copy.wait()

        for tile in range(TILES):
            cols = pl.ds(tile * LANES, LANES)
            for field in range(SPECIES):
                spot = aligned(slot * FIELD_ROWS + padded_at(field * TILES + tile, 0), FZ)
                first[spot, :] = state_ref[slot, field, :, cols]
            spot = aligned(slot * UPWARD_ROWS + padded_at(tile, 0), FZ)
            conduct[spot, :] = kappa_ref[slot, :, cols]

        def keep(kind, tile, ztile, values):
            coeffs[
                aligned(slot * COEFF_ROWS + (kind * TILES + tile) * FZ + DEPTH * ztile, DEPTH), :
            ] = values

        for ztile in range(ZTILES):

            def here(tile, shift):
                start = slot * UPWARD_ROWS + padded_at(tile, ztile) + shift
                return conduct[aligned(start, DEPTH) if shift == 0 else pl.ds(start, DEPTH), :]

            center = here(0, 0)
            turned = roll_lanes(center, -EDGE)
            back_before = None
            for tile in range(TILES):
                other = turned
                if tile + 1 < TILES:
                    center_after = here(tile + 1, 0)
                    turned_after = roll_lanes(center_after, -EDGE)
                    other = jnp.where(lane < LANES - EDGE, turned, turned_after)
                next_x = face(FINE_SCALE, center, other)
                if tile == TILES - 1:
                    next_x = jnp.where(lane < LANES - EDGE, next_x, 0.0)
                back = roll_lanes(next_x, EDGE)
                prev_x = jnp.where(lane >= EDGE, back, 0.0 if tile == 0 else back_before)
                next_y = jnp.where(
                    column < EDGE - 1, face(FINE_SCALE, center, roll_lanes(center, -1)), 0.0
                )
                prev_y = roll_lanes(next_y, 1)
                next_z = face(FINE_SCALE, center, here(tile, 1))
                spot = slot * UPWARD_ROWS + padded_at(tile, ztile)
                upward[aligned(spot, DEPTH), :] = next_z
                prev_z = upward[pl.ds(spot - 1, DEPTH), :]
                sides = side_y
                if tile == 0:
                    sides = sides + jnp.where(lane < EDGE, 1.0, 0.0)
                if tile == TILES - 1:
                    sides = sides + jnp.where(lane >= LANES - EDGE, 1.0, 0.0)
                scale = FINE_SCALE * center
                total = (next_x + prev_x) + (next_y + prev_y) + (next_z + prev_z) + sides * scale
                keep(0, tile, ztile, next_x)
                keep(1, tile, ztile, prev_x)
                keep(2, tile, ztile, next_y)
                rate = rate_ref[slot, pl.ds(DEPTH * ztile, DEPTH), pl.ds(tile * LANES, LANES)]
                keep(3, tile, ztile, DT_FINE * rate)
                for field in range(SPECIES):
                    keep(4 + field, tile, ztile, 1.0 - DIFFUSE[field] * total)
                keep(7, tile, ztile, scale)
                back_before = back
                if tile + 1 < TILES:
                    center, turned = center_after, turned_after

        for ztile in range(ZTILES):
            advance(
                first,
                fields_ref,
                coeffs,
                upward,
                slot,
                slot * FIELD_ROWS,
                slot * FIELD_ROWS,
                ztile,
                lambda field, tile: None,
            )
        start_all(stores(slot))
        return carry

    lax.fori_loop(0, slots, one_patch, 0)
    for slot in range(slots):
        for copy in stores(slot):
            copy.wait()


def finish_kernel(
    strips_ref,
    fields_hbm,
    coeffs_hbm,
    upward_hbm,
    xl_ref,
    xr_ref,
    out_hbm,
    avg_hbm,
    fields_ref,
    coeffs,
    upward,
    ghost_ref,
    plane_ref,
    mean_ref,
    avg_ref,
    first,
    share,
    staged,
    sems,
    in_sems,
    avg_sems,
    *,
    slots,
):
    sources = strips_ref.shape[0]

    def loads(slot):
        return [
            pltpu.make_async_copy(
                source.at[aligned(slot * size, size)],
                target.at[aligned(slot * size, size)],
                in_sems.at[order, slot],
            )
            for order, (source, target, size) in enumerate(
                (
                    (fields_hbm, fields_ref, FIELD_ROWS),
                    (coeffs_hbm, coeffs, COEFF_ROWS),
                    (upward_hbm, upward, UPWARD_ROWS),
                )
            )
        ]

    start_all(loads(0))
    clear_pads(first)
    for tile in range(TILES):
        ghost_ref[:, tile * LANES : (tile + 1) * LANES] = ghost_table(tile)
    plane_ref[...] = plane_table()
    mean_ref[...] = mean_table()

    gathered = strips_ref[0]
    for source in range(1, sources):
        gathered = gathered + strips_ref[source]
    old, new = complete_strips(gathered)
    gathered = jnp.concatenate([old, (new - old) * (1.0 / RATIO)], axis=0)
    quarter = AVG_ROWS // FACES
    group_of = lane_ids((quarter, LANES)) // BLK

    def send_out(slot):
        return pltpu.make_async_copy(staged.at[slot], out_hbm.at[slot], sems.at[slot])

    def one_patch(slot, carry):
        for copy in loads(slot):
            copy.wait()

        @pl.when(slot + 1 < slots)
        def _():
            start_all(loads(slot + 1))

        turned = pltpu.roll(gathered, (LANES - slot * BLK) % LANES, 1)
        stretched = jnp.dot(
            plane_ref[...],
            jnp.concatenate(split_pair(turned), axis=1),
            preferred_element_type=jnp.float32,
        ).astype(jnp.bfloat16)
        base = slot * FIELD_ROWS
        scales = slot * COEFF_ROWS
        for tile in range(TILES):
            ghosts = jnp.dot(
                stretched,
                ghost_ref[:, tile * LANES : (tile + 1) * LANES],
                preferred_element_type=jnp.float32,
            )
            scale = coeffs[aligned(scales + (7 * TILES + tile) * FZ, FZ), :]
            for field in range(SPECIES):
                row = (field * TILES + tile) * FZ
                old = scale * ghosts[field * FZ : (field + 1) * FZ]
                drift = scale * ghosts[(SPECIES + field) * FZ : (SPECIES + field + 1) * FZ]
                later = old
                for step in range(1, RATIO):
                    later = later + drift
                    share[step - 1, row : row + FZ, :] = later
                spot = aligned(base + padded_at(field * TILES + tile, 0), FZ)
                fields_ref[spot, :] = fields_ref[spot, :] + DIFFUSE[field] * old

        for step in range(1, RATIO):
            source, target = (fields_ref, first) if step % 2 else (first, fields_ref)
            for ztile in range(ZTILES):

                def ghosts(field, tile):
                    spot = pl.ds((field * TILES + tile) * FZ + DEPTH * ztile, DEPTH)
                    return share[step - 1, spot, :]

                advance(source, target, coeffs, upward, slot, base, base, ztile, ghosts)

        for tile in range(TILES):
            for field in range(SPECIES):
                spot = aligned(base + padded_at(field * TILES + tile, 0), FZ)
                staged[slot, field, :, pl.ds(tile * LANES, LANES)] = first[spot, :]
        send_out(slot).start()

        sums = []
        for field in range(SPECIES):
            for plane in range(NZC):
                start = base + field * TILES * STRIDE + PAD + RATIO * plane
                part = first[pl.ds(start, TILES, stride=STRIDE), :]
                for z in range(1, RATIO):
                    part = part + first[pl.ds(start + z, TILES, stride=STRIDE), :]
                sums.append(part)
        means = jnp.dot(
            jnp.concatenate(split_pair(jnp.concatenate(sums, axis=0)), axis=1),
            mean_ref[...],
            preferred_element_type=jnp.float32,
        )
        chunk = avg_ref[...]
        for part in range(FACES):
            chunk = jnp.where(
                group_of == part * slots + slot,
                means[part * quarter : (part + 1) * quarter],
                chunk,
            )
        avg_ref[...] = chunk
        return carry

    avg_ref[...] = jnp.zeros((quarter, LANES), jnp.float32)
    lax.fori_loop(0, slots, one_patch, 0)
    copies = [
        pltpu.make_async_copy(avg_ref, avg_hbm.at[target], avg_sems.at[target])
        for target in range(sources)
    ]
    start_all(copies)
    for copy in copies:
        copy.wait()
    for slot in range(slots):
        send_out(slot).wait()


def edges_kernel(
    new_hbm,
    xlo_ref,
    xhi_ref,
    ylo_ref,
    yhi_ref,
    xl_ref,
    xr_ref,
    yl_ref,
    yr_ref,
    out_ref,
    new_ref,
    sem,
    *,
    cells_x,
    cells_y,
):
    me = lax.axis_index("af")
    last = lax.axis_size("af") - 1
    fetch = pltpu.make_async_copy(new_hbm, new_ref, sem)
    fetch.start()

    def edge_share(own_ref, other_ref):
        own = own_ref[...]
        other = other_ref[...]
        coeff = face(DT_COARSE, jnp.maximum(own, 0.125), other)
        lane = lane_ids(own.shape)
        spread = jnp.zeros_like(own)
        for field in range(SPECIES):
            moved = roll_lanes(coeff, (field - SPECIES) * NZC)
            spread = jnp.where(lane // NZC == field, DIFFUSE[field] * moved, spread)
        return spread * (other - own)

    lower = edge_share(ylo_ref, yl_ref)
    upper = edge_share(yhi_ref, yr_ref)

    lane = lane_ids((BLK, LANES))
    row_id = lax.broadcasted_iota(jnp.int32, (BLK, LANES), 0)
    halves = cells_y // LANES

    def side_share(own_ref, other_ref, exists):
        shares = []
        for half in range(halves):
            own = own_ref[:, half * LANES : (half + 1) * LANES]
            other = other_ref[:, half * LANES : (half + 1) * LANES]
            coeff = face(DT_COARSE, own[PLANES:], other[PLANES:])
            coeff = jnp.where(exists, coeff, 0.0)
            shares.append(
                jnp.concatenate(
                    [
                        (DIFFUSE[field] * coeff)
                        * (
                            other[field * NZC : (field + 1) * NZC]
                            - own[field * NZC : (field + 1) * NZC]
                        )
                        for field in range(SPECIES)
                    ],
                    axis=0,
                )
            )
        return shares

    before = side_share(xlo_ref, xl_ref, me > 0)
    after = side_share(xhi_ref, xr_ref, me < last)
    fetch.wait()
    block_cols = cells_x // BLK
    for column in range(block_cols):
        for plane in range(PLANES):
            row = plane * cells_x + column * BLK
            edge_rows = slice(column * BLK, (column + 1) * BLK)
            for half in range(halves):
                cols = slice(half * LANES, (half + 1) * LANES)
                coarse = new_ref[row : row + BLK, cols]
                if column == 0:
                    share = before[half][plane : plane + 1]
                    coarse = coarse + jnp.where(row_id == 0, share, 0.0)
                if column == block_cols - 1:
                    share = after[half][plane : plane + 1]
                    coarse = coarse + jnp.where(row_id == BLK - 1, share, 0.0)
                if half == 0:
                    share = roll_lanes(lower[edge_rows], -plane)
                    coarse = coarse + jnp.where(lane == 0, share, 0.0)
                if half == halves - 1:
                    share = roll_lanes(upper[edge_rows], LANES - 1 - plane)
                    coarse = coarse + jnp.where(lane == LANES - 1, share, 0.0)
                out_ref[row : row + BLK, cols] = coarse


def place_kernel(
    place_ref, avg_ref, new_ref, out_ref, *, cells_x, cells_y, group, slots
):
    width = slots * BLK
    quarter = AVG_ROWS // FACES
    per_tile = LANES // width
    part = lane_ids((quarter, LANES)) // width
    columns = []
    for tile in range(group * BLK // LANES):
        rows = []
        for index in range(FACES):
            merged = jnp.zeros((quarter, LANES), jnp.float32)
            for place in range(per_tile):
                piece = roll_lanes(avg_ref[tile * per_tile + place], (place - index) * width)
                merged = jnp.where(part == place, piece, merged)
            rows.append(merged)
        columns.append(jnp.concatenate(rows, axis=0))
    high, low = split_pair(jnp.concatenate(columns, axis=1))
    ones = jnp.ones((16, high.shape[1]), jnp.bfloat16)
    stacked = jnp.concatenate([high, low, ones], axis=0)

    halves = cells_y // LANES
    for column in range(cells_x // BLK):
        placed = lax.dot_general(
            stacked,
            selector(place_ref, column, cells_y),
            (((1,), (1,)), ((), ())),
            preferred_element_type=jnp.float32,
        )
        covered = placed[2 * AVG_ROWS : 2 * AVG_ROWS + 8] > 0.5
        for plane in range(PLANES):
            values = (
                placed[plane * BLK : (plane + 1) * BLK]
                + placed[AVG_ROWS + plane * BLK : AVG_ROWS + (plane + 1) * BLK]
            )
            row = plane * cells_x + column * BLK
            for half in range(halves):
                cols = slice(half * LANES, (half + 1) * LANES)
                coarse = new_ref[row : row + BLK, cols]
                out_ref[row : row + BLK, cols] = jnp.where(
                    covered[:, cols], values[:, cols], coarse
                )


VMEM = pl.BlockSpec(memory_space=pltpu.VMEM)
HBM = pl.BlockSpec(memory_space=pltpu.HBM)
PARAMS = pltpu.CompilerParams(vmem_limit_bytes=40 * 1024 * 1024)


def f32(*shape):
    return jax.ShapeDtypeStruct(shape, jnp.float32)


def hbm32(*shape):
    return pltpu.HBM(shape, jnp.float32)


def pinned(*arrays):
    return [pltpu.with_memory_space_constraint(array, pltpu.HBM) for array in arrays]


def shifted(values, axis, step):
    count = lax.axis_size(axis)
    pairs = [(i, i + step) for i in range(count) if 0 <= i + step < count]
    return lax.ppermute(values, axis, pairs)


def exchange(chunks):
    return lax.all_to_all(chunks, "af", split_axis=0, concat_axis=0, tiled=True)


def per_device(
    coarse_state, coarse_kappa, coarse_rate, fine_state, fine_kappa, fine_rate, boxes, cover
):
    af_count = lax.axis_size("af")
    slots = fine_state.shape[0]
    cells_x, cells_y = coarse_state.shape[2:]
    group = af_count * slots
    lanes = group * BLK
    halves = cells_y // LANES
    rows = PLANES * cells_x
    plain = NZC * cells_x
    sizes = dict(cells_x=cells_x, cells_y=cells_y, group=group)

    span = cells_x + 2 * PAD
    new, send, place, xlo, xhi, ylo, yhi = pl.pallas_call(
        functools.partial(strips_kernel, slots=slots, **sizes),
        out_shape=[
            hbm32(rows, cells_y),
            hbm32(af_count, CHUNK_ROWS, LANES),
            jax.ShapeDtypeStruct((16, lanes), jnp.int32),
        ]
        + [f32(EDGE_ROWS, cells_y)] * 2
        + [f32(cells_x, LANES)] * 2,
        in_specs=[HBM] * 4,
        out_specs=[HBM] * 2 + [VMEM] * 5,
        scratch_shapes=[
            pltpu.VMEM((2, boxes.shape[0]), jnp.int32),
            pltpu.VMEM((rows, cells_y), jnp.float32),
            pltpu.VMEM((plain, cells_y), jnp.float32),
            pltpu.VMEM((plain, cells_y), jnp.float32),
            pltpu.VMEM((rows, cells_y), jnp.float32),
            pltpu.VMEM(((SPECIES + 1) * halves * NZC * span, LANES), jnp.float32),
            pltpu.VMEM((rows * halves, LANES), jnp.float32),
            pltpu.VMEM((af_count, CHUNK_ROWS, LANES), jnp.float32),
            pltpu.SemaphoreType.DMA((4,)),
            pltpu.SemaphoreType.DMA((af_count,)),
        ],
        compiler_params=PARAMS,
        name="strips",
    )(
        *pinned(
            boxes.T,
            coarse_state.reshape(rows, cells_y),
            coarse_kappa.reshape(plain, cells_y),
            coarse_rate.reshape(plain, cells_y),
        )
    )

    strips = exchange(send)

    xlo_sent, xhi_sent = pl.pallas_call(
        hand_on_kernel,
        out_shape=[f32(EDGE_ROWS, cells_y)] * 2,
        in_specs=[VMEM] * 2,
        out_specs=[VMEM] * 2,
        compiler_params=pltpu.CompilerParams(vmem_limit_bytes=1024 * 1024),
        name="hand_on",
    )(xlo, xhi)
    xl = shifted(xhi_sent, "af", 1)
    xr = shifted(xlo_sent, "af", -1)

    kept = [hbm32(slots * size, LANES) for size in (FIELD_ROWS, COEFF_ROWS, UPWARD_ROWS)]
    kept_scratch = [pltpu.VMEM((slots * size, LANES), jnp.float32)
        for size in (FIELD_ROWS, COEFF_ROWS, UPWARD_ROWS)]
    fields, coeffs, upward = pl.pallas_call(
        functools.partial(prepare_kernel, slots=slots),
        out_shape=kept,
        in_specs=[VMEM] + [HBM] * 3,
        out_specs=[HBM] * 3,
        scratch_shapes=kept_scratch
        + [
            pltpu.VMEM(fine_state.shape, jnp.float32),
            pltpu.VMEM(fine_kappa.shape, jnp.float32),
            pltpu.VMEM(fine_rate.shape, jnp.float32),
            pltpu.VMEM((slots * FIELD_ROWS, LANES), jnp.float32),
            pltpu.VMEM((slots * UPWARD_ROWS, LANES), jnp.float32),
            pltpu.SemaphoreType.DMA((3, slots)),
            pltpu.SemaphoreType.DMA((3, slots)),
        ],
        compiler_params=PARAMS,
        name="prepare",
    )(xlo_sent, *pinned(fine_state, fine_kappa, fine_rate))

    chunk = (AVG_ROWS // FACES, LANES)
    fine_out, averages = pl.pallas_call(
        functools.partial(finish_kernel, slots=slots),
        out_shape=[hbm32(*fine_state.shape), hbm32(af_count, *chunk)],
        in_specs=[VMEM] + [HBM] * 3 + [VMEM] * 2,
        out_specs=[HBM] * 2,
        scratch_shapes=kept_scratch
        + [
            pltpu.VMEM((2 * LANES, EDGE * EDGE), jnp.bfloat16),
            pltpu.VMEM((2 * SPECIES * FZ, STRIP_ROWS), jnp.bfloat16),
            pltpu.VMEM((2 * LANES, LANES), jnp.bfloat16),
            pltpu.VMEM(chunk, jnp.float32),
            pltpu.VMEM((slots * FIELD_ROWS, LANES), jnp.float32),
            pltpu.VMEM((RATIO - 1, SPECIES * TILES * FZ, LANES), jnp.float32),
            pltpu.VMEM(fine_state.shape, jnp.float32),
            pltpu.SemaphoreType.DMA((slots,)),
            pltpu.SemaphoreType.DMA((3, slots)),
            pltpu.SemaphoreType.DMA((af_count,)),
        ],
        compiler_params=PARAMS,
        name="finish",
    )(strips, *pinned(fields, coeffs, upward), xl, xr)

    arrived = exchange(averages)

    yl = shifted(yhi, "col", 1)
    yr = shifted(ylo, "col", -1)
    whole = pl.pallas_call(
        functools.partial(edges_kernel, cells_x=cells_x, cells_y=cells_y),
        out_shape=f32(rows, cells_y),
        in_specs=[HBM] + [VMEM] * 8,
        out_specs=VMEM,
        scratch_shapes=[pltpu.VMEM((rows, cells_y), jnp.float32), pltpu.SemaphoreType.DMA],
        compiler_params=PARAMS,
        name="edges",
    )(*pinned(new), xlo, xhi, ylo, yhi, xl, xr, yl, yr)

    placed = pl.pallas_call(
        functools.partial(place_kernel, slots=slots, **sizes),
        out_shape=f32(rows, cells_y),
        in_specs=[VMEM] * 3,
        out_specs=VMEM,
        compiler_params=PARAMS,
        name="place",
    )(place, arrived, whole)
    return (placed.reshape(coarse_state.shape), fine_out)


def solution(mesh):
    return jax.shard_map(
        per_device,
        mesh=mesh,
        in_specs=(
            P(None, None, "af", "col"),
            P(None, "af", "col"),
            P(None, "af", "col"),
            P(("col", "af"), None, None, None),
            P(("col", "af"), None, None),
            P(("col", "af"), None, None),
            P(),
            P(),
        ),
        out_specs=(P(None, None, "af", "col"), P(("col", "af"), None, None, None)),
        check_vma=False,
    )
```

```python
import functools

import jax
import jax.numpy as jnp
from jax import lax
from jax.experimental import pallas as pl
from jax.experimental.pallas import tpu as pltpu
from jax.sharding import PartitionSpec as P

NZC = 8
RATIO = 4
BLK = 8
SPECIES = 3
EDGE = BLK * RATIO
FZ = NZC * RATIO
LANES = 128
TILES = EDGE * EDGE // LANES
DEPTH = 8
ZTILES = FZ // DEPTH
STRIDE = 48
PAD = 8
FACES = 4
PLANES = SPECIES * NZC
STRIP_ROWS = 2 * PLANES
AVG_ROWS = PLANES * BLK
KINDS = 8
FIELD_ROWS = SPECIES * TILES * STRIDE
COEFF_ROWS = KINDS * TILES * FZ
UPWARD_ROWS = TILES * STRIDE
EDGE_ROWS = PLANES + NZC
BESIDE_ROWS = 2 * NZC
CHUNK_ROWS = STRIP_ROWS + BESIDE_ROWS

DT_COARSE = 1.0 / 28.0
DIFFUSE = (1.0, 0.7, 0.45)
SIGNS = (-1.0, -1.0, 1.0)
FINE_SCALE = RATIO * RATIO * DT_COARSE / RATIO
DT_FINE = DT_COARSE / RATIO


def lane_ids(shape):
    return lax.broadcasted_iota(jnp.int32, shape, len(shape) - 1)


def roll_lanes(values, shift):
    width = values.shape[-1]
    shift = shift % width
    return values if shift == 0 else pltpu.roll(values, shift, values.ndim - 1)


def split_pair(values):
    high = values.astype(jnp.bfloat16)
    low = (values - high.astype(jnp.float32)).astype(jnp.bfloat16)
    return high, low


def face(scale, one, other):
    summed = one + other
    inverse = pl.reciprocal(summed, approx=True)
    inverse = inverse * (2.0 - summed * inverse)
    return (2.0 * scale) * (one * other) * inverse


def start_all(copies):
    for copy in copies:
        copy.start()


def selector(place_ref, column, cells_y):
    wanted = jnp.where(place_ref[0:8, :] == column, place_ref[8:16, :], -1)
    row = lax.broadcasted_iota(jnp.int32, wanted.shape, 0)
    return jnp.concatenate(
        [jnp.where(row + 8 * at == wanted, 1.0, 0.0) for at in range(cells_y // 8)], axis=0
    ).astype(jnp.bfloat16)


def block_place(shift):
    return (lax.axis_index("col") + shift) % 2, (lax.axis_index("af") + shift) % 2


def block_exchange(chunks, shift):
    cols, afs = lax.axis_size("col"), lax.axis_size("af")
    groups = [
        [
            (2 * col + shift + in_col) % cols * afs + (2 * af + shift + in_af) % afs
            for in_col in range(2)
            for in_af in range(2)
        ]
        for col in range(cols // 2)
        for af in range(afs // 2)
    ]
    return lax.all_to_all(
        chunks, ("col", "af"), 0, 0, axis_index_groups=groups, tiled=True
    )


def strips_kernel(
    boxes_hbm,
    state_hbm,
    kappa_hbm,
    rate_hbm,
    new_hbm,
    send_hbm,
    place_ref,
    xlo_ref,
    xhi_ref,
    ylo_ref,
    yhi_ref,
    even_ref,
    odd_ref,
    boxes_ref,
    state_ref,
    kappa_ref,
    rate_ref,
    new_ref,
    padded,
    fresh,
    send_ref,
    sems,
    send_sems,
    *,
    cells_x,
    cells_y,
    group,
    slots,
):
    pairs = (
        (boxes_hbm, boxes_ref),
        (kappa_hbm, kappa_ref),
        (state_hbm, state_ref),
        (rate_hbm, rate_ref),
    )
    copies = [
        pltpu.make_async_copy(source, target, sems.at[index])
        for index, (source, target) in enumerate(pairs)
    ]
    start_all(copies)

    patches = boxes_ref.shape[1]
    lanes = group * BLK
    base_patch = lax.axis_index("col") * group
    member = lax.broadcasted_iota(jnp.int32, (patches, lanes), 0) - base_patch
    spread = jnp.where(member == lane_ids((patches, lanes)) // BLK, 1.0, 0.0).astype(jnp.bfloat16)
    first_col = lax.axis_index("af") * (cells_x // BLK)
    first_cell = lax.axis_index("col") * cells_y
    copies[0].wait()
    boxes = boxes_ref[...].astype(jnp.float32)
    stacked = jnp.concatenate(
        [jnp.broadcast_to(boxes[row : row + 1], (8, patches)) for row in range(2)], axis=0
    )
    found = jnp.dot(
        stacked.astype(jnp.bfloat16), spread, preferred_element_type=jnp.float32
    ).astype(jnp.int32)
    place_ref[0:8, :] = found[0:8] - first_col
    place_ref[8:16, :] = found[8:16] * BLK - first_cell + lane_ids((8, lanes)) % BLK

    halves = cells_y // LANES
    span = cells_x + 2 * PAD
    nothing = jnp.zeros((PAD, LANES), jnp.float32)

    def base(field, half, z):
        return ((field * halves + half) * NZC + z) * span

    for copy in copies[1:]:
        copy.wait()
    for field in range(SPECIES + 1):
        for half in range(halves):
            cols = pl.ds(half * LANES, LANES)
            for z in range(NZC):
                if field < SPECIES:
                    start = (field * NZC + z) * cells_x
                    plane = state_ref[start : start + cells_x, cols]
                else:
                    plane = kappa_ref[z * cells_x : (z + 1) * cells_x, cols]
                at = base(field, half, z)
                padded[at : at + PAD, :] = nothing
                padded[at + PAD : at + PAD + cells_x, :] = plane
                padded[at + PAD + cells_x : at + span, :] = nothing

    lane = lane_ids((cells_x, LANES))
    row_id = lax.broadcasted_iota(jnp.int32, (cells_x, LANES), 0)

    low = jnp.zeros((cells_x, LANES), jnp.float32)
    high = jnp.zeros((cells_x, LANES), jnp.float32)
    for plane in range(PLANES + NZC):
        field, z = divmod(plane, NZC)
        at = base(field, 0, z) + PAD
        first = padded[at : at + cells_x, :]
        at = base(field, halves - 1, z) + PAD
        last = padded[at : at + cells_x, :]
        low = jnp.where(lane == plane, roll_lanes(first, plane), low)
        high = jnp.where(lane == plane, roll_lanes(last, plane + 1), high)
    ylo_ref[...] = low
    yhi_ref[...] = high

    def load(field, half, z, shift):
        at = base(field, half, z) + PAD + shift
        return padded[at : at + cells_x, :]

    def neighbours(field, half, z):
        here = load(field, half, z, 0)
        after = roll_lanes(here, -1)
        if half + 1 < halves:
            after = jnp.where(
                lane == LANES - 1, roll_lanes(load(field, half + 1, z, 0), -1), after
            )
        before = roll_lanes(here, 1)
        if half > 0:
            before = jnp.where(lane == 0, roll_lanes(load(field, half - 1, z, 0), 1), before)
        found = [after, before, load(field, half, z, 1), load(field, half, z, -1)]
        if z + 1 < NZC:
            found.append(load(field, half, z + 1, 0))
        if z > 0:
            found.append(load(field, half, z - 1, 0))
        return found

    for z in range(NZC):
        for half in range(halves):
            cols = pl.ds(half * LANES, LANES)
            conduct = load(SPECIES, half, z, 0)
            coeffs = [face(DT_COARSE, conduct, other) for other in neighbours(SPECIES, half, z)]
            if half == halves - 1:
                coeffs[0] = jnp.where(lane == LANES - 1, 0.0, coeffs[0])
            if half == 0:
                coeffs[1] = jnp.where(lane == 0, 0.0, coeffs[1])
            coeffs[2] = jnp.where(row_id == cells_x - 1, 0.0, coeffs[2])
            coeffs[3] = jnp.where(row_id == 0, 0.0, coeffs[3])
            centers = [load(field, half, z, 0) for field in range(SPECIES)]
            forward = (DT_COARSE * rate_ref[z * cells_x : (z + 1) * cells_x, cols]) * (
                centers[0] * centers[1] - centers[2]
            )
            for field in range(SPECIES):
                center = centers[field]
                flux = None
                for coeff, other in zip(coeffs, neighbours(field, half, z)):
                    term = coeff * (other - center)
                    flux = term if flux is None else flux + term
                start = (field * NZC + z) * cells_x
                result = center + DIFFUSE[field] * flux + SIGNS[field] * forward
                new_ref[start : start + cells_x, cols] = result
                start = ((field * halves + half) * NZC + z) * cells_x
                fresh[start : start + cells_x, :] = result

    keep_new = pltpu.make_async_copy(new_ref, new_hbm, sems.at[0])
    keep_new.start()

    def old_row(field, half, row):
        return padded[pl.ds(base(field, half, 0) + PAD + row, NZC, stride=span), :]

    def edge_at(row):
        return jnp.concatenate(
            [
                jnp.concatenate([old_row(field, half, row) for field in range(SPECIES + 1)], axis=0)
                for half in range(halves)
            ],
            axis=1,
        )

    def rows_at(row):
        columns = []
        for half in range(halves):
            pieces = [old_row(field, half, row) for field in range(SPECIES)]
            for field in range(SPECIES):
                start = (field * halves + half) * NZC * cells_x
                pieces.append(fresh[pl.ds(start + row, NZC, stride=cells_x), :])
            columns.append(jnp.concatenate(pieces, axis=0))
        return jnp.concatenate(columns, axis=1)

    block_cols = cells_x // BLK
    spot = lane_ids((STRIP_ROWS, cells_y)) % BLK
    lower_y = []
    upper_y = []
    for column in range(block_cols):
        below = jnp.zeros((STRIP_ROWS, cells_y), jnp.float32)
        above = jnp.zeros((STRIP_ROWS, cells_y), jnp.float32)
        for x in range(BLK):
            turned = roll_lanes(rows_at(column * BLK + x), x + 1)
            below = jnp.where(spot == x, turned, below)
            above = jnp.where(spot == (x + 1) % BLK, turned, above)
        lower_y.append(below)
        upper_y.append(roll_lanes(above, -1 - BLK))

    first_row = edge_at(0)
    last_row = edge_at(cells_x - 1)
    xlo_ref[...] = first_row
    xhi_ref[...] = last_row
    cut = cells_x, LANES
    for ref, shift in ((even_ref, 0), (odd_ref, 1)):
        along_col, along_af = block_place(shift)
        ref[...] = jnp.zeros_like(ref)
        for member in range(4):
            if_x = along_col == member // 2
            if_y = along_af == member % 2
            edge = jnp.where(along_af == 0, last_row, first_row)

            @pl.when(if_x)
            def _(ref=ref, member=member, edge=edge):
                ref[member] = edge

            @pl.when(if_y & ~if_x)
            def _(ref=ref, member=member, along_col=along_col):
                ref[member, : cut[0], : cut[1]] = jnp.where(along_col == 0, high, low)

    place = lane_ids((NZC, cells_y)) % BLK
    ones = jnp.ones((NZC, cells_y), jnp.float32)

    def field_of(row, field):
        return row[field * NZC : (field + 1) * NZC]

    def corners(row, fields, first_at):
        found = jnp.zeros((NZC, cells_y), jnp.float32)
        for order, field in enumerate(fields):
            at = first_at + 2 * order
            values = field_of(row, field)
            found = jnp.where(place == at, roll_lanes(values, at + 1), found)
            found = jnp.where(place == at + 1, roll_lanes(values, at + 1 - BLK), found)
        return found

    every = range(SPECIES)

    def near(row):
        own = [(field, field_of(row, field)) for field in range(SPECIES + 1)]
        return own + [(5, corners(row, [SPECIES], 0))]

    def far(row):
        return [
            (4, field_of(row, SPECIES)),
            (5, corners(row, every, 2)),
            (6, corners(row, [SPECIES], 0)),
        ]

    extra_members = {
        -1: far(first_row),
        0: near(first_row),
        block_cols - 1: near(last_row) + [(7, ones)],
        block_cols: far(last_row),
    }

    faces = [None] * (3 * FACES)

    def add(index, part):
        faces[index] = part if faces[index] is None else faces[index] + part

    for column in range(-1, block_cols + 1):
        members = []
        if column >= 1:
            members.append((0, rows_at(column * BLK - 1)))
        if column < block_cols - 1:
            members.append((1, rows_at(column * BLK + BLK)))
        if 0 <= column < block_cols:
            members.append((2, lower_y[column]))
            members.append((3, upper_y[column]))
        for index, rows in extra_members.get(column, []):
            members.append((FACES + index, rows))
        operands = []
        for _, rows in members:
            operands.extend(split_pair(rows))
        moved = jnp.dot(
            jnp.concatenate(operands, axis=0),
            selector(place_ref, column, cells_y),
            preferred_element_type=jnp.float32,
        )
        at = 0
        for index, rows in members:
            size = rows.shape[0]
            add(index, moved[at : at + size] + moved[at + size : at + 2 * size])
            at += 2 * size

    width = slots * BLK
    outgoing = [
        pltpu.make_async_copy(send_ref.at[target], send_hbm.at[target], send_sems.at[target])
        for target in range(group // slots)
    ]
    for target in range(group // slots):
        first = target * width
        tile = first // LANES * LANES
        for start, size, kind in (
            (0, STRIP_ROWS, 0),
            (STRIP_ROWS, NZC, FACES),
            (STRIP_ROWS + NZC, NZC, 2 * FACES),
        ):
            part = lane_ids((size, LANES)) // width
            chunk = jnp.zeros((size, LANES), jnp.float32)
            for index in range(FACES):
                piece = faces[kind + index][:, tile : tile + LANES]
                chunk = jnp.where(
                    part == index, roll_lanes(piece, index * width - (first - tile)), chunk
                )
            send_ref[target, start : start + size, :] = chunk
        outgoing[target].start()
    for copy in outgoing:
        copy.wait()
    keep_new.wait()


def ghost_table(tile):
    lane = lane_ids((BLK, LANES))
    pos = lax.broadcasted_iota(jnp.int32, (BLK, LANES), 0)
    x = tile * (LANES // EDGE) + lane // EDGE
    y = lane % EDGE
    along_y = y // RATIO == pos
    along_x = x // RATIO == pos
    seen = (
        (x == 0) & along_y,
        (x == EDGE - 1) & along_y,
        (y == 0) & along_x,
        (y == EDGE - 1) & along_x,
    )
    nothing = jnp.zeros((LANES // FACES - BLK, LANES), jnp.float32)
    rows = []
    for where in seen:
        rows.extend([jnp.where(where, 1.0, 0.0), nothing])
    return jnp.concatenate(rows + rows, axis=0).astype(jnp.bfloat16)


def plane_table():
    shape = (2 * SPECIES * FZ, STRIP_ROWS)
    rows = lax.broadcasted_iota(jnp.int32, shape, 0)
    return jnp.where(rows // RATIO == lane_ids(shape), 1.0, 0.0).astype(jnp.bfloat16)


def mean_table():
    shape = (2 * LANES, LANES)
    rows = lax.broadcasted_iota(jnp.int32, shape, 0)
    same = rows % EDGE // RATIO == lane_ids(shape) % BLK
    return jnp.where(same, 1.0 / RATIO**3, 0.0).astype(jnp.bfloat16)


def complete_strips(gathered):
    width = LANES // FACES
    own = gathered[STRIP_ROWS : STRIP_ROWS + NZC]
    beside = gathered[STRIP_ROWS + NZC : STRIP_ROWS + 2 * NZC]
    lane = lane_ids((NZC, LANES))
    part = lane // width
    pos = lane % BLK
    flag = jnp.where(part == FACES - 1, beside, 0.0)
    flag = flag + roll_lanes(flag, width)
    upper = flag + roll_lanes(flag, 2 * width) > 0.5

    def coefficient(one, other):
        return face(DT_COARSE, jnp.maximum(one, 0.125), jnp.maximum(other, 0.125))

    block = coefficient(roll_lanes(own, width), beside)
    corner = coefficient(beside, roll_lanes(beside, -width))
    added = []
    for field in range(SPECIES):
        old = gathered[field * NZC : (field + 1) * NZC]
        there = jnp.where(upper, roll_lanes(old, -width), old)
        across = DIFFUSE[field] * block * (roll_lanes(own, -field * width) - there)
        below = jnp.where(upper, roll_lanes(old, -width - (BLK - 1)), roll_lanes(old, -width))
        above = jnp.where(
            upper, roll_lanes(old, -2 * width - (BLK - 2)), roll_lanes(old, 1 - 2 * width)
        )
        here = jnp.where(pos == 0, below, above)
        along = DIFFUSE[field] * corner * (roll_lanes(beside, -2 - 2 * field) - here)
        share = jnp.where((part == 0) & ~upper, across, 0.0)
        share = jnp.where((part == 1) & upper, roll_lanes(across, width), share)
        for index in range(2):
            for at, chosen in ((0, ~upper), (BLK - 1, upper)):
                moved = roll_lanes(along, (1 + index) * width + at - index)
                share = jnp.where((part == 2 + index) & (pos == at) & chosen, moved, share)
        added.append(share)
    new = gathered[PLANES:STRIP_ROWS] + jnp.concatenate(added, axis=0)
    return gathered[:PLANES], new


def aligned(start, size):
    return pl.ds(pl.multiple_of(start, 8), size)


def padded_at(block, ztile):
    return block * STRIDE + PAD + DEPTH * ztile


def advance(source, target, coeffs, upward, slot, from_rows, to_rows, ztile, ghosts):
    lane = lane_ids((DEPTH, LANES))

    def value(field, tile, shift):
        start = from_rows + padded_at(field * TILES + tile, ztile) + shift
        return source[aligned(start, DEPTH) if shift == 0 else pl.ds(start, DEPTH), :]

    def get(kind, tile):
        return coeffs[
            aligned(slot * COEFF_ROWS + (kind * TILES + tile) * FZ + DEPTH * ztile, DEPTH), :
        ]

    centers = [value(field, 0, 0) for field in range(SPECIES)]
    down = [roll_lanes(center, -EDGE) for center in centers]
    up = [roll_lanes(center, EDGE) for center in centers]
    up_before = list(up)
    for tile in range(TILES):
        if tile + 1 < TILES:
            centers_after = [value(field, tile + 1, 0) for field in range(SPECIES)]
            down_after = [roll_lanes(center, -EDGE) for center in centers_after]
        next_x, prev_x, next_y, rate = [get(kind, tile) for kind in range(4)]
        prev_y = roll_lanes(next_y, 1)
        base = slot * UPWARD_ROWS + padded_at(tile, ztile)
        next_z = upward[aligned(base, DEPTH), :]
        prev_z = upward[pl.ds(base - 1, DEPTH), :]
        forward = rate * (centers[0] * centers[1] - centers[2])
        for field in range(SPECIES):
            center = centers[field]
            ahead, behind = down[field], up[field]
            if tile + 1 < TILES:
                ahead = jnp.where(lane < LANES - EDGE, ahead, down_after[field])
            if tile > 0:
                behind = jnp.where(lane >= EDGE, behind, up_before[field])
            flux = (next_x * ahead + prev_x * behind) + (
                next_y * roll_lanes(center, -1) + prev_y * roll_lanes(center, 1)
            )
            flux = flux + (next_z * value(field, tile, 1) + prev_z * value(field, tile, -1))
            share = ghosts(field, tile)
            if share is not None:
                flux = flux + share
            if DIFFUSE[field] != 1.0:
                flux = DIFFUSE[field] * flux
            result = get(4 + field, tile) * center + flux
            result = result - forward if SIGNS[field] < 0 else result + forward
            target[aligned(to_rows + padded_at(field * TILES + tile, ztile), DEPTH), :] = result
        if tile + 1 < TILES:
            up_before = up
            centers, down = centers_after, down_after
            up = [roll_lanes(center, EDGE) for center in centers]


def clear_pads(ref):
    edge = jnp.zeros((PAD, LANES), jnp.float32)

    def body(block, carry):
        ref[aligned(block * STRIDE, PAD), :] = edge
        ref[aligned(block * STRIDE + PAD + FZ, PAD), :] = edge
        return carry

    lax.fori_loop(0, ref.shape[0] // STRIDE, body, 0)


PIECES = SPECIES + 1 + KINDS


def pieces(slot, *refs):
    sources, targets = refs[:3], refs[3:]
    found = []
    for order, parts, size in ((0, SPECIES, FIELD_ROWS), (2, 1, UPWARD_ROWS), (1, KINDS, COEFF_ROWS)):
        for part in range(parts):
            rows = aligned(slot * size + part * (size // parts), size // parts)
            found.append((sources[order].at[rows], targets[order].at[rows]))
    return found


def hand_on_kernel(given_ref, out_ref):
    out_ref[...] = given_ref[...]


def prepare_kernel(
    after_ref,
    state_hbm,
    kappa_hbm,
    rate_hbm,
    fields_hbm,
    coeffs_hbm,
    upward_hbm,
    fields_ref,
    coeffs,
    upward,
    state_ref,
    kappa_ref,
    rate_ref,
    first,
    conduct,
    sems,
    out_sems,
    *,
    slots,
):
    def loads(slot):
        return [
            pltpu.make_async_copy(source.at[slot], target.at[slot], sems.at[order, slot])
            for order, (source, target) in enumerate(
                ((kappa_hbm, kappa_ref), (rate_hbm, rate_ref), (state_hbm, state_ref))
            )
        ]

    for slot in range(slots):
        start_all(loads(slot))

    def stores(slot, start, stop):
        made = pieces(slot, fields_ref, coeffs, upward, fields_hbm, coeffs_hbm, upward_hbm)
        return [
            pltpu.make_async_copy(*made[order], out_sems.at[order, slot])
            for order in range(start, stop)
        ]

    for ref in (fields_ref, upward, first, conduct):
        clear_pads(ref)

    lane = lane_ids((DEPTH, LANES))
    column = lane % EDGE
    side_y = jnp.where((column == 0) | (column == EDGE - 1), 1.0, 0.0)

    def one_patch(slot, carry):
        for copy in loads(slot):
            copy.wait()

        for tile in range(TILES):
            cols = pl.ds(tile * LANES, LANES)
            for field in range(SPECIES):
                spot = aligned(slot * FIELD_ROWS + padded_at(field * TILES + tile, 0), FZ)
                first[spot, :] = state_ref[slot, field, :, cols]
            spot = aligned(slot * UPWARD_ROWS + padded_at(tile, 0), FZ)
            conduct[spot, :] = kappa_ref[slot, :, cols]

        def keep(kind, tile, ztile, values):
            coeffs[
                aligned(slot * COEFF_ROWS + (kind * TILES + tile) * FZ + DEPTH * ztile, DEPTH), :
            ] = values

        for ztile in range(ZTILES):

            def here(tile, shift):
                start = slot * UPWARD_ROWS + padded_at(tile, ztile) + shift
                return conduct[aligned(start, DEPTH) if shift == 0 else pl.ds(start, DEPTH), :]

            center = here(0, 0)
            turned = roll_lanes(center, -EDGE)
            back_before = None
            for tile in range(TILES):
                other = turned
                if tile + 1 < TILES:
                    center_after = here(tile + 1, 0)
                    turned_after = roll_lanes(center_after, -EDGE)
                    other = jnp.where(lane < LANES - EDGE, turned, turned_after)
                next_x = face(FINE_SCALE, center, other)
                if tile == TILES - 1:
                    next_x = jnp.where(lane < LANES - EDGE, next_x, 0.0)
                back = roll_lanes(next_x, EDGE)
                prev_x = jnp.where(lane >= EDGE, back, 0.0 if tile == 0 else back_before)
                next_y = jnp.where(
                    column < EDGE - 1, face(FINE_SCALE, center, roll_lanes(center, -1)), 0.0
                )
                prev_y = roll_lanes(next_y, 1)
                next_z = face(FINE_SCALE, center, here(tile, 1))
                spot = slot * UPWARD_ROWS + padded_at(tile, ztile)
                upward[aligned(spot, DEPTH), :] = next_z
                prev_z = upward[pl.ds(spot - 1, DEPTH), :]
                sides = side_y
                if tile == 0:
                    sides = sides + jnp.where(lane < EDGE, 1.0, 0.0)
                if tile == TILES - 1:
                    sides = sides + jnp.where(lane >= LANES - EDGE, 1.0, 0.0)
                scale = FINE_SCALE * center
                total = (next_x + prev_x) + (next_y + prev_y) + (next_z + prev_z) + sides * scale
                keep(0, tile, ztile, next_x)
                keep(1, tile, ztile, prev_x)
                keep(2, tile, ztile, next_y)
                rate = rate_ref[slot, pl.ds(DEPTH * ztile, DEPTH), pl.ds(tile * LANES, LANES)]
                keep(3, tile, ztile, DT_FINE * rate)
                for field in range(SPECIES):
                    keep(4 + field, tile, ztile, 1.0 - DIFFUSE[field] * total)
                keep(7, tile, ztile, scale)
                back_before = back
                if tile + 1 < TILES:
                    center, turned = center_after, turned_after

        start_all(stores(slot, SPECIES, PIECES))
        for ztile in range(ZTILES):
            advance(
                first,
                fields_ref,
                coeffs,
                upward,
                slot,
                slot * FIELD_ROWS,
                slot * FIELD_ROWS,
                ztile,
                lambda field, tile: None,
            )
        start_all(stores(slot, 0, SPECIES))
        return carry

    lax.fori_loop(0, slots, one_patch, 0)
    for slot in range(slots):
        for copy in stores(slot, 0, PIECES):
            copy.wait()


def finish_kernel(
    strips_ref,
    fields_hbm,
    coeffs_hbm,
    upward_hbm,
    even_ref,
    out_hbm,
    avg_hbm,
    fields_ref,
    coeffs,
    upward,
    ghost_ref,
    plane_ref,
    mean_ref,
    avg_ref,
    first,
    share,
    staged,
    sems,
    in_sems,
    avg_sems,
    *,
    slots,
):
    sources = strips_ref.shape[0]

    def loads(slot):
        made = pieces(slot, fields_hbm, coeffs_hbm, upward_hbm, fields_ref, coeffs, upward)
        return [
            pltpu.make_async_copy(source, target, in_sems.at[order, slot])
            for order, (source, target) in enumerate(made)
        ]

    start_all(loads(0))
    clear_pads(first)
    for tile in range(TILES):
        ghost_ref[:, tile * LANES : (tile + 1) * LANES] = ghost_table(tile)
    plane_ref[...] = plane_table()
    mean_ref[...] = mean_table()

    gathered = strips_ref[0]
    for source in range(1, sources):
        gathered = gathered + strips_ref[source]
    old, new = complete_strips(gathered)
    gathered = jnp.concatenate([old, (new - old) * (1.0 / RATIO)], axis=0)
    quarter = AVG_ROWS // FACES
    group_of = lane_ids((quarter, LANES)) // BLK

    def send_out(slot):
        return pltpu.make_async_copy(staged.at[slot], out_hbm.at[slot], sems.at[slot])

    def one_patch(slot, carry):
        for copy in loads(slot):
            copy.wait()

        @pl.when(slot + 1 < slots)
        def _():
            start_all(loads(slot + 1))

        turned = pltpu.roll(gathered, (LANES - slot * BLK) % LANES, 1)
        stretched = jnp.dot(
            plane_ref[...],
            jnp.concatenate(split_pair(turned), axis=1),
            preferred_element_type=jnp.float32,
        ).astype(jnp.bfloat16)
        base = slot * FIELD_ROWS
        scales = slot * COEFF_ROWS
        for tile in range(TILES):
            ghosts = jnp.dot(
                stretched,
                ghost_ref[:, tile * LANES : (tile + 1) * LANES],
                preferred_element_type=jnp.float32,
            )
            scale = coeffs[aligned(scales + (7 * TILES + tile) * FZ, FZ), :]
            for field in range(SPECIES):
                row = (field * TILES + tile) * FZ
                old = scale * ghosts[field * FZ : (field + 1) * FZ]
                drift = scale * ghosts[(SPECIES + field) * FZ : (SPECIES + field + 1) * FZ]
                later = old
                for step in range(1, RATIO):
                    later = later + drift
                    share[step - 1, row : row + FZ, :] = later
                spot = aligned(base + padded_at(field * TILES + tile, 0), FZ)
                fields_ref[spot, :] = fields_ref[spot, :] + DIFFUSE[field] * old

        for step in range(1, RATIO):
            source, target = (fields_ref, first) if step % 2 else (first, fields_ref)
            for ztile in range(ZTILES):

                def ghosts(field, tile):
                    spot = pl.ds((field * TILES + tile) * FZ + DEPTH * ztile, DEPTH)
                    return share[step - 1, spot, :]

                advance(source, target, coeffs, upward, slot, base, base, ztile, ghosts)

        for tile in range(TILES):
            for field in range(SPECIES):
                spot = aligned(base + padded_at(field * TILES + tile, 0), FZ)
                staged[slot, field, :, pl.ds(tile * LANES, LANES)] = first[spot, :]
        send_out(slot).start()

        sums = []
        for field in range(SPECIES):
            for plane in range(NZC):
                start = base + field * TILES * STRIDE + PAD + RATIO * plane
                part = first[pl.ds(start, TILES, stride=STRIDE), :]
                for z in range(1, RATIO):
                    part = part + first[pl.ds(start + z, TILES, stride=STRIDE), :]
                sums.append(part)
        means = jnp.dot(
            jnp.concatenate(split_pair(jnp.concatenate(sums, axis=0)), axis=1),
            mean_ref[...],
            preferred_element_type=jnp.float32,
        )
        chunk = avg_ref[...]
        for part in range(FACES):
            chunk = jnp.where(
                group_of == part * slots + slot,
                means[part * quarter : (part + 1) * quarter],
                chunk,
            )
        avg_ref[...] = chunk
        return carry

    avg_ref[...] = jnp.zeros((quarter, LANES), jnp.float32)
    lax.fori_loop(0, slots, one_patch, 0)
    copies = [
        pltpu.make_async_copy(avg_ref, avg_hbm.at[target], avg_sems.at[target])
        for target in range(sources)
    ]
    start_all(copies)
    for copy in copies:
        copy.wait()
    for slot in range(slots):
        send_out(slot).wait()


def edges_kernel(
    new_hbm,
    xlo_ref,
    xhi_ref,
    ylo_ref,
    yhi_ref,
    even_ref,
    odd_ref,
    out_ref,
    new_ref,
    sem,
    *,
    cells_x,
    cells_y,
):
    me = lax.axis_index("af")
    last = lax.axis_size("af") - 1
    fetch = pltpu.make_async_copy(new_hbm, new_ref, sem)
    fetch.start()

    col = lax.axis_index("col")
    in_col, in_af = block_place(0)
    even_x = even_ref[2 * in_col + 1 - in_af]
    odd_x = odd_ref[2 * (1 - in_col) + in_af]
    even_y = even_ref[2 * (1 - in_col) + in_af, :cells_x, :LANES]
    odd_y = odd_ref[2 * in_col + 1 - in_af, :cells_x, :LANES]
    xl, xr = jnp.where(in_af == 0, odd_x, even_x), jnp.where(in_af == 0, even_x, odd_x)
    yl, yr = jnp.where(in_col == 0, odd_y, even_y), jnp.where(in_col == 0, even_y, odd_y)

    def edge_share(own_ref, other, exists):
        own = own_ref[...]
        coeff = face(DT_COARSE, jnp.maximum(own, 0.125), other)
        coeff = jnp.where(exists, coeff, 0.0)
        lane = lane_ids(own.shape)
        spread = jnp.zeros_like(own)
        for field in range(SPECIES):
            moved = roll_lanes(coeff, (field - SPECIES) * NZC)
            spread = jnp.where(lane // NZC == field, DIFFUSE[field] * moved, spread)
        return spread * (other - own)

    lower = edge_share(ylo_ref, yl, col > 0)
    upper = edge_share(yhi_ref, yr, col < lax.axis_size("col") - 1)

    lane = lane_ids((BLK, LANES))
    row_id = lax.broadcasted_iota(jnp.int32, (BLK, LANES), 0)
    halves = cells_y // LANES

    def side_share(own_ref, beyond, exists):
        shares = []
        for half in range(halves):
            own = own_ref[:, half * LANES : (half + 1) * LANES]
            other = beyond[:, half * LANES : (half + 1) * LANES]
            coeff = face(DT_COARSE, own[PLANES:], other[PLANES:])
            coeff = jnp.where(exists, coeff, 0.0)
            shares.append(
                jnp.concatenate(
                    [
                        (DIFFUSE[field] * coeff)
                        * (
                            other[field * NZC : (field + 1) * NZC]
                            - own[field * NZC : (field + 1) * NZC]
                        )
                        for field in range(SPECIES)
                    ],
                    axis=0,
                )
            )
        return shares

    before = side_share(xlo_ref, xl, me > 0)
    after = side_share(xhi_ref, xr, me < last)
    fetch.wait()
    block_cols = cells_x // BLK
    for column in range(block_cols):
        for plane in range(PLANES):
            row = plane * cells_x + column * BLK
            edge_rows = slice(column * BLK, (column + 1) * BLK)
            for half in range(halves):
                cols = slice(half * LANES, (half + 1) * LANES)
                coarse = new_ref[row : row + BLK, cols]
                if column == 0:
                    share = before[half][plane : plane + 1]
                    coarse = coarse + jnp.where(row_id == 0, share, 0.0)
                if column == block_cols - 1:
                    share = after[half][plane : plane + 1]
                    coarse = coarse + jnp.where(row_id == BLK - 1, share, 0.0)
                if half == 0:
                    share = roll_lanes(lower[edge_rows], -plane)
                    coarse = coarse + jnp.where(lane == 0, share, 0.0)
                if half == halves - 1:
                    share = roll_lanes(upper[edge_rows], LANES - 1 - plane)
                    coarse = coarse + jnp.where(lane == LANES - 1, share, 0.0)
                out_ref[row : row + BLK, cols] = coarse


def place_kernel(
    place_ref, avg_ref, new_ref, out_ref, *, cells_x, cells_y, group, slots
):
    width = slots * BLK
    quarter = AVG_ROWS // FACES
    per_tile = LANES // width
    part = lane_ids((quarter, LANES)) // width
    columns = []
    for tile in range(group * BLK // LANES):
        rows = []
        for index in range(FACES):
            merged = jnp.zeros((quarter, LANES), jnp.float32)
            for place in range(per_tile):
                piece = roll_lanes(avg_ref[tile * per_tile + place], (place - index) * width)
                merged = jnp.where(part == place, piece, merged)
            rows.append(merged)
        columns.append(jnp.concatenate(rows, axis=0))
    high, low = split_pair(jnp.concatenate(columns, axis=1))
    ones = jnp.ones((16, high.shape[1]), jnp.bfloat16)
    stacked = jnp.concatenate([high, low, ones], axis=0)

    halves = cells_y // LANES
    for column in range(cells_x // BLK):
        placed = lax.dot_general(
            stacked,
            selector(place_ref, column, cells_y),
            (((1,), (1,)), ((), ())),
            preferred_element_type=jnp.float32,
        )
        covered = placed[2 * AVG_ROWS : 2 * AVG_ROWS + 8] > 0.5
        for plane in range(PLANES):
            values = (
                placed[plane * BLK : (plane + 1) * BLK]
                + placed[AVG_ROWS + plane * BLK : AVG_ROWS + (plane + 1) * BLK]
            )
            row = plane * cells_x + column * BLK
            for half in range(halves):
                cols = slice(half * LANES, (half + 1) * LANES)
                coarse = new_ref[row : row + BLK, cols]
                out_ref[row : row + BLK, cols] = jnp.where(
                    covered[:, cols], values[:, cols], coarse
                )


VMEM = pl.BlockSpec(memory_space=pltpu.VMEM)
HBM = pl.BlockSpec(memory_space=pltpu.HBM)
PARAMS = pltpu.CompilerParams(vmem_limit_bytes=40 * 1024 * 1024)


def f32(*shape):
    return jax.ShapeDtypeStruct(shape, jnp.float32)


def hbm32(*shape):
    return pltpu.HBM(shape, jnp.float32)


def pinned(*arrays):
    return [pltpu.with_memory_space_constraint(array, pltpu.HBM) for array in arrays]


def exchange(chunks):
    return lax.all_to_all(chunks, "af", split_axis=0, concat_axis=0, tiled=True)


def per_device(
    coarse_state, coarse_kappa, coarse_rate, fine_state, fine_kappa, fine_rate, boxes, cover
):
    af_count = lax.axis_size("af")
    slots = fine_state.shape[0]
    cells_x, cells_y = coarse_state.shape[2:]
    group = af_count * slots
    lanes = group * BLK
    halves = cells_y // LANES
    rows = PLANES * cells_x
    plain = NZC * cells_x
    sizes = dict(cells_x=cells_x, cells_y=cells_y, group=group)

    span = cells_x + 2 * PAD
    new, send, place, xlo, xhi, ylo, yhi, even_sent, odd = pl.pallas_call(
        functools.partial(strips_kernel, slots=slots, **sizes),
        out_shape=[
            hbm32(rows, cells_y),
            hbm32(af_count, CHUNK_ROWS, LANES),
            jax.ShapeDtypeStruct((16, lanes), jnp.int32),
        ]
        + [f32(EDGE_ROWS, cells_y)] * 2
        + [f32(cells_x, LANES)] * 2
        + [f32(4, EDGE_ROWS, cells_y)] * 2,
        in_specs=[HBM] * 4,
        out_specs=[HBM] * 2 + [VMEM] * 7,
        scratch_shapes=[
            pltpu.VMEM((2, boxes.shape[0]), jnp.int32),
            pltpu.VMEM((rows, cells_y), jnp.float32),
            pltpu.VMEM((plain, cells_y), jnp.float32),
            pltpu.VMEM((plain, cells_y), jnp.float32),
            pltpu.VMEM((rows, cells_y), jnp.float32),
            pltpu.VMEM(((SPECIES + 1) * halves * NZC * span, LANES), jnp.float32),
            pltpu.VMEM((rows * halves, LANES), jnp.float32),
            pltpu.VMEM((af_count, CHUNK_ROWS, LANES), jnp.float32),
            pltpu.SemaphoreType.DMA((4,)),
            pltpu.SemaphoreType.DMA((af_count,)),
        ],
        compiler_params=PARAMS,
        name="strips",
    )(
        *pinned(
            boxes.T,
            coarse_state.reshape(rows, cells_y),
            coarse_kappa.reshape(plain, cells_y),
            coarse_rate.reshape(plain, cells_y),
        )
    )

    strips = exchange(send)

    even = pl.pallas_call(
        hand_on_kernel,
        out_shape=f32(4, EDGE_ROWS, cells_y),
        in_specs=[VMEM],
        out_specs=VMEM,
        compiler_params=pltpu.CompilerParams(vmem_limit_bytes=1024 * 1024),
        name="hand_on",
    )(even_sent)
    even_arrived = block_exchange(even, 0)

    kept = [hbm32(slots * size, LANES) for size in (FIELD_ROWS, COEFF_ROWS, UPWARD_ROWS)]
    kept_scratch = [pltpu.VMEM((slots * size, LANES), jnp.float32)
        for size in (FIELD_ROWS, COEFF_ROWS, UPWARD_ROWS)]
    fields, coeffs, upward = pl.pallas_call(
        functools.partial(prepare_kernel, slots=slots),
        out_shape=kept,
        in_specs=[VMEM] + [HBM] * 3,
        out_specs=[HBM] * 3,
        scratch_shapes=kept_scratch
        + [
            pltpu.VMEM(fine_state.shape, jnp.float32),
            pltpu.VMEM(fine_kappa.shape, jnp.float32),
            pltpu.VMEM(fine_rate.shape, jnp.float32),
            pltpu.VMEM((slots * FIELD_ROWS, LANES), jnp.float32),
            pltpu.VMEM((slots * UPWARD_ROWS, LANES), jnp.float32),
            pltpu.SemaphoreType.DMA((3, slots)),
            pltpu.SemaphoreType.DMA((PIECES, slots)),
        ],
        compiler_params=PARAMS,
        name="prepare",
    )(even, *pinned(fine_state, fine_kappa, fine_rate))

    chunk = (AVG_ROWS // FACES, LANES)
    fine_out, averages = pl.pallas_call(
        functools.partial(finish_kernel, slots=slots),
        out_shape=[hbm32(*fine_state.shape), hbm32(af_count, *chunk)],
        in_specs=[VMEM] + [HBM] * 3 + [VMEM],
        out_specs=[HBM] * 2,
        scratch_shapes=kept_scratch
        + [
            pltpu.VMEM((2 * LANES, EDGE * EDGE), jnp.bfloat16),
            pltpu.VMEM((2 * SPECIES * FZ, STRIP_ROWS), jnp.bfloat16),
            pltpu.VMEM((2 * LANES, LANES), jnp.bfloat16),
            pltpu.VMEM(chunk, jnp.float32),
            pltpu.VMEM((slots * FIELD_ROWS, LANES), jnp.float32),
            pltpu.VMEM((RATIO - 1, SPECIES * TILES * FZ, LANES), jnp.float32),
            pltpu.VMEM(fine_state.shape, jnp.float32),
            pltpu.SemaphoreType.DMA((slots,)),
            pltpu.SemaphoreType.DMA((PIECES, slots)),
            pltpu.SemaphoreType.DMA((af_count,)),
        ],
        compiler_params=PARAMS,
        name="finish",
    )(strips, *pinned(fields, coeffs, upward), even_arrived)

    arrived = exchange(averages)

    odd_arrived = block_exchange(odd, 1)
    whole = pl.pallas_call(
        functools.partial(edges_kernel, cells_x=cells_x, cells_y=cells_y),
        out_shape=f32(rows, cells_y),
        in_specs=[HBM] + [VMEM] * 6,
        out_specs=VMEM,
        scratch_shapes=[pltpu.VMEM((rows, cells_y), jnp.float32), pltpu.SemaphoreType.DMA],
        compiler_params=PARAMS,
        name="edges",
    )(*pinned(new), xlo, xhi, ylo, yhi, even_arrived, odd_arrived)

    placed = pl.pallas_call(
        functools.partial(place_kernel, slots=slots, **sizes),
        out_shape=f32(rows, cells_y),
        in_specs=[VMEM] * 3,
        out_specs=VMEM,
        compiler_params=PARAMS,
        name="place",
    )(place, arrived, whole)
    return (placed.reshape(coarse_state.shape), fine_out)


def solution(mesh):
    return jax.shard_map(
        per_device,
        mesh=mesh,
        in_specs=(
            P(None, None, "af", "col"),
            P(None, "af", "col"),
            P(None, "af", "col"),
            P(("col", "af"), None, None, None),
            P(("col", "af"), None, None),
            P(("col", "af"), None, None),
            P(),
            P(),
        ),
        out_specs=(P(None, None, "af", "col"), P(("col", "af"), None, None, None)),
        check_vma=False,
    )
```

```python
import functools

import jax
import jax.numpy as jnp
from jax import lax
from jax.experimental import pallas as pl
from jax.experimental.pallas import tpu as pltpu
from jax.sharding import PartitionSpec as P

NZC = 8
RATIO = 4
BLK = 8
SPECIES = 3
EDGE = BLK * RATIO
FZ = NZC * RATIO
LANES = 128
TILES = EDGE * EDGE // LANES
DEPTH = 8
ZTILES = FZ // DEPTH
STRIDE = 40
PAD = 8
FACES = 4
PLANES = SPECIES * NZC
STRIP_ROWS = 2 * PLANES
AVG_ROWS = PLANES * BLK
KINDS = 8
FIELD_ROWS = SPECIES * TILES * STRIDE + PAD
COEFF_ROWS = KINDS * TILES * FZ
UPWARD_ROWS = TILES * STRIDE + PAD
EDGE_ROWS = PLANES + NZC
BESIDE_ROWS = 2 * NZC
CHUNK_ROWS = STRIP_ROWS + BESIDE_ROWS

DT_COARSE = 1.0 / 28.0
DIFFUSE = (1.0, 0.7, 0.45)
SIGNS = (-1.0, -1.0, 1.0)
FINE_SCALE = RATIO * RATIO * DT_COARSE / RATIO
DT_FINE = DT_COARSE / RATIO


def lane_ids(shape):
    return lax.broadcasted_iota(jnp.int32, shape, len(shape) - 1)


def roll_lanes(values, shift):
    width = values.shape[-1]
    shift = shift % width
    return values if shift == 0 else pltpu.roll(values, shift, values.ndim - 1)


def split_pair(values):
    high = values.astype(jnp.bfloat16)
    low = (values - high.astype(jnp.float32)).astype(jnp.bfloat16)
    return high, low


def face(scale, one, other):
    summed = one + other
    inverse = pl.reciprocal(summed, approx=True)
    inverse = inverse * (2.0 - summed * inverse)
    return (2.0 * scale) * (one * other) * inverse


def start_all(copies):
    for copy in copies:
        copy.start()


def selector(place_ref, column, cells_y):
    wanted = jnp.where(place_ref[0:8, :] == column, place_ref[8:16, :], -1)
    row = lax.broadcasted_iota(jnp.int32, wanted.shape, 0)
    return jnp.concatenate(
        [jnp.where(row + 8 * at == wanted, 1.0, 0.0) for at in range(cells_y // 8)], axis=0
    ).astype(jnp.bfloat16)


def strips_kernel(
    boxes_hbm,
    state_hbm,
    kappa_hbm,
    rate_hbm,
    new_hbm,
    send_hbm,
    place_ref,
    xlo_ref,
    xhi_ref,
    ylo_ref,
    yhi_ref,
    boxes_ref,
    state_ref,
    kappa_ref,
    rate_ref,
    new_ref,
    padded,
    fresh,
    send_ref,
    sems,
    send_sems,
    *,
    cells_x,
    cells_y,
    group,
    slots,
):
    pairs = (
        (boxes_hbm, boxes_ref),
        (kappa_hbm, kappa_ref),
        (state_hbm, state_ref),
        (rate_hbm, rate_ref),
    )
    copies = [
        pltpu.make_async_copy(source, target, sems.at[index])
        for index, (source, target) in enumerate(pairs)
    ]
    start_all(copies)

    patches = boxes_ref.shape[1]
    lanes = group * BLK
    base_patch = lax.axis_index("col") * group
    member = lax.broadcasted_iota(jnp.int32, (patches, lanes), 0) - base_patch
    spread = jnp.where(member == lane_ids((patches, lanes)) // BLK, 1.0, 0.0).astype(jnp.bfloat16)
    first_col = lax.axis_index("af") * (cells_x // BLK)
    first_cell = lax.axis_index("col") * cells_y
    copies[0].wait()
    boxes = boxes_ref[...].astype(jnp.float32)
    stacked = jnp.concatenate(
        [jnp.broadcast_to(boxes[row : row + 1], (8, patches)) for row in range(2)], axis=0
    )
    found = jnp.dot(
        stacked.astype(jnp.bfloat16), spread, preferred_element_type=jnp.float32
    ).astype(jnp.int32)
    place_ref[0:8, :] = found[0:8] - first_col
    place_ref[8:16, :] = found[8:16] * BLK - first_cell + lane_ids((8, lanes)) % BLK

    halves = cells_y // LANES
    span = cells_x + 2 * PAD
    nothing = jnp.zeros((PAD, LANES), jnp.float32)

    def base(field, half, z):
        return ((field * halves + half) * NZC + z) * span

    for copy in copies[1:]:
        copy.wait()
    for field in range(SPECIES + 1):
        for half in range(halves):
            cols = pl.ds(half * LANES, LANES)
            for z in range(NZC):
                if field < SPECIES:
                    start = (field * NZC + z) * cells_x
                    plane = state_ref[start : start + cells_x, cols]
                else:
                    plane = kappa_ref[z * cells_x : (z + 1) * cells_x, cols]
                at = base(field, half, z)
                padded[at : at + PAD, :] = nothing
                padded[at + PAD : at + PAD + cells_x, :] = plane
                padded[at + PAD + cells_x : at + span, :] = nothing

    lane = lane_ids((cells_x, LANES))
    row_id = lax.broadcasted_iota(jnp.int32, (cells_x, LANES), 0)

    low = jnp.zeros((cells_x, LANES), jnp.float32)
    high = jnp.zeros((cells_x, LANES), jnp.float32)
    for plane in range(PLANES + NZC):
        field, z = divmod(plane, NZC)
        at = base(field, 0, z) + PAD
        first = padded[at : at + cells_x, :]
        at = base(field, halves - 1, z) + PAD
        last = padded[at : at + cells_x, :]
        low = jnp.where(lane == plane, roll_lanes(first, plane), low)
        high = jnp.where(lane == plane, roll_lanes(last, plane + 1), high)
    ylo_ref[...] = low
    yhi_ref[...] = high

    def load(field, half, z, shift):
        at = base(field, half, z) + PAD + shift
        return padded[at : at + cells_x, :]

    def neighbours(field, half, z):
        here = load(field, half, z, 0)
        after = roll_lanes(here, -1)
        if half + 1 < halves:
            after = jnp.where(
                lane == LANES - 1, roll_lanes(load(field, half + 1, z, 0), -1), after
            )
        before = roll_lanes(here, 1)
        if half > 0:
            before = jnp.where(lane == 0, roll_lanes(load(field, half - 1, z, 0), 1), before)
        found = [after, before, load(field, half, z, 1), load(field, half, z, -1)]
        if z + 1 < NZC:
            found.append(load(field, half, z + 1, 0))
        if z > 0:
            found.append(load(field, half, z - 1, 0))
        return found

    for z in range(NZC):
        for half in range(halves):
            cols = pl.ds(half * LANES, LANES)
            conduct = load(SPECIES, half, z, 0)
            coeffs = [face(DT_COARSE, conduct, other) for other in neighbours(SPECIES, half, z)]
            if half == halves - 1:
                coeffs[0] = jnp.where(lane == LANES - 1, 0.0, coeffs[0])
            if half == 0:
                coeffs[1] = jnp.where(lane == 0, 0.0, coeffs[1])
            coeffs[2] = jnp.where(row_id == cells_x - 1, 0.0, coeffs[2])
            coeffs[3] = jnp.where(row_id == 0, 0.0, coeffs[3])
            centers = [load(field, half, z, 0) for field in range(SPECIES)]
            forward = (DT_COARSE * rate_ref[z * cells_x : (z + 1) * cells_x, cols]) * (
                centers[0] * centers[1] - centers[2]
            )
            for field in range(SPECIES):
                center = centers[field]
                flux = None
                for coeff, other in zip(coeffs, neighbours(field, half, z)):
                    term = coeff * (other - center)
                    flux = term if flux is None else flux + term
                start = (field * NZC + z) * cells_x
                result = center + DIFFUSE[field] * flux + SIGNS[field] * forward
                new_ref[start : start + cells_x, cols] = result
                start = ((field * halves + half) * NZC + z) * cells_x
                fresh[start : start + cells_x, :] = result

    keep_new = pltpu.make_async_copy(new_ref, new_hbm, sems.at[0])
    keep_new.start()

    def old_row(field, half, row):
        return padded[pl.ds(base(field, half, 0) + PAD + row, NZC, stride=span), :]

    def edge_at(row):
        return jnp.concatenate(
            [
                jnp.concatenate([old_row(field, half, row) for field in range(SPECIES + 1)], axis=0)
                for half in range(halves)
            ],
            axis=1,
        )

    def rows_at(row):
        columns = []
        for half in range(halves):
            pieces = [old_row(field, half, row) for field in range(SPECIES)]
            for field in range(SPECIES):
                start = (field * halves + half) * NZC * cells_x
                pieces.append(fresh[pl.ds(start + row, NZC, stride=cells_x), :])
            columns.append(jnp.concatenate(pieces, axis=0))
        return jnp.concatenate(columns, axis=1)

    block_cols = cells_x // BLK
    spot = lane_ids((STRIP_ROWS, cells_y)) % BLK
    lower_y = []
    upper_y = []
    for column in range(block_cols):
        below = jnp.zeros((STRIP_ROWS, cells_y), jnp.float32)
        above = jnp.zeros((STRIP_ROWS, cells_y), jnp.float32)
        for x in range(BLK):
            turned = roll_lanes(rows_at(column * BLK + x), x + 1)
            below = jnp.where(spot == x, turned, below)
            above = jnp.where(spot == (x + 1) % BLK, turned, above)
        lower_y.append(below)
        upper_y.append(roll_lanes(above, -1 - BLK))

    first_row = edge_at(0)
    last_row = edge_at(cells_x - 1)
    xlo_ref[...] = first_row
    xhi_ref[...] = last_row
    place = lane_ids((NZC, cells_y)) % BLK
    ones = jnp.ones((NZC, cells_y), jnp.float32)

    def field_of(row, field):
        return row[field * NZC : (field + 1) * NZC]

    def corners(row, fields, first_at):
        found = jnp.zeros((NZC, cells_y), jnp.float32)
        for order, field in enumerate(fields):
            at = first_at + 2 * order
            values = field_of(row, field)
            found = jnp.where(place == at, roll_lanes(values, at + 1), found)
            found = jnp.where(place == at + 1, roll_lanes(values, at + 1 - BLK), found)
        return found

    every = range(SPECIES)

    def near(row):
        own = [(field, field_of(row, field)) for field in range(SPECIES + 1)]
        return own + [(5, corners(row, [SPECIES], 0))]

    def far(row):
        return [
            (4, field_of(row, SPECIES)),
            (5, corners(row, every, 2)),
            (6, corners(row, [SPECIES], 0)),
        ]

    extra_members = {
        -1: far(first_row),
        0: near(first_row),
        block_cols - 1: near(last_row) + [(7, ones)],
        block_cols: far(last_row),
    }

    faces = [None] * (3 * FACES)

    def add(index, part):
        faces[index] = part if faces[index] is None else faces[index] + part

    for column in range(-1, block_cols + 1):
        members = []
        if column >= 1:
            members.append((0, rows_at(column * BLK - 1)))
        if column < block_cols - 1:
            members.append((1, rows_at(column * BLK + BLK)))
        if 0 <= column < block_cols:
            members.append((2, lower_y[column]))
            members.append((3, upper_y[column]))
        for index, rows in extra_members.get(column, []):
            members.append((FACES + index, rows))
        operands = []
        for _, rows in members:
            operands.extend(split_pair(rows))
        moved = jnp.dot(
            jnp.concatenate(operands, axis=0),
            selector(place_ref, column, cells_y),
            preferred_element_type=jnp.float32,
        )
        at = 0
        for index, rows in members:
            size = rows.shape[0]
            add(index, moved[at : at + size] + moved[at + size : at + 2 * size])
            at += 2 * size

    width = slots * BLK
    outgoing = [
        pltpu.make_async_copy(send_ref.at[target], send_hbm.at[target], send_sems.at[target])
        for target in range(group // slots)
    ]
    for target in range(group // slots):
        first = target * width
        tile = first // LANES * LANES
        for start, size, kind in (
            (0, STRIP_ROWS, 0),
            (STRIP_ROWS, NZC, FACES),
            (STRIP_ROWS + NZC, NZC, 2 * FACES),
        ):
            part = lane_ids((size, LANES)) // width
            chunk = jnp.zeros((size, LANES), jnp.float32)
            for index in range(FACES):
                piece = faces[kind + index][:, tile : tile + LANES]
                chunk = jnp.where(
                    part == index, roll_lanes(piece, index * width - (first - tile)), chunk
                )
            send_ref[target, start : start + size, :] = chunk
        outgoing[target].start()
    for copy in outgoing:
        copy.wait()
    keep_new.wait()


def ghost_table(tile):
    lane = lane_ids((BLK, LANES))
    pos = lax.broadcasted_iota(jnp.int32, (BLK, LANES), 0)
    x = tile * (LANES // EDGE) + lane // EDGE
    y = lane % EDGE
    along_y = y // RATIO == pos
    along_x = x // RATIO == pos
    seen = (
        (x == 0) & along_y,
        (x == EDGE - 1) & along_y,
        (y == 0) & along_x,
        (y == EDGE - 1) & along_x,
    )
    nothing = jnp.zeros((LANES // FACES - BLK, LANES), jnp.float32)
    rows = []
    for where in seen:
        rows.extend([jnp.where(where, 1.0, 0.0), nothing])
    return jnp.concatenate(rows + rows, axis=0).astype(jnp.bfloat16)


def plane_table():
    shape = (2 * SPECIES * FZ, STRIP_ROWS)
    rows = lax.broadcasted_iota(jnp.int32, shape, 0)
    return jnp.where(rows // RATIO == lane_ids(shape), 1.0, 0.0).astype(jnp.bfloat16)


def mean_table():
    shape = (2 * LANES, LANES)
    rows = lax.broadcasted_iota(jnp.int32, shape, 0)
    same = rows % EDGE // RATIO == lane_ids(shape) % BLK
    return jnp.where(same, 1.0 / RATIO**3, 0.0).astype(jnp.bfloat16)


def complete_strips(gathered):
    width = LANES // FACES
    own = gathered[STRIP_ROWS : STRIP_ROWS + NZC]
    beside = gathered[STRIP_ROWS + NZC : STRIP_ROWS + 2 * NZC]
    lane = lane_ids((NZC, LANES))
    part = lane // width
    pos = lane % BLK
    flag = jnp.where(part == FACES - 1, beside, 0.0)
    flag = flag + roll_lanes(flag, width)
    upper = flag + roll_lanes(flag, 2 * width) > 0.5

    def coefficient(one, other):
        return face(DT_COARSE, jnp.maximum(one, 0.125), jnp.maximum(other, 0.125))

    block = coefficient(roll_lanes(own, width), beside)
    corner = coefficient(beside, roll_lanes(beside, -width))
    added = []
    for field in range(SPECIES):
        old = gathered[field * NZC : (field + 1) * NZC]
        there = jnp.where(upper, roll_lanes(old, -width), old)
        across = DIFFUSE[field] * block * (roll_lanes(own, -field * width) - there)
        below = jnp.where(upper, roll_lanes(old, -width - (BLK - 1)), roll_lanes(old, -width))
        above = jnp.where(
            upper, roll_lanes(old, -2 * width - (BLK - 2)), roll_lanes(old, 1 - 2 * width)
        )
        here = jnp.where(pos == 0, below, above)
        along = DIFFUSE[field] * corner * (roll_lanes(beside, -2 - 2 * field) - here)
        share = jnp.where((part == 0) & ~upper, across, 0.0)
        share = jnp.where((part == 1) & upper, roll_lanes(across, width), share)
        for index in range(2):
            for at, chosen in ((0, ~upper), (BLK - 1, upper)):
                moved = roll_lanes(along, (1 + index) * width + at - index)
                share = jnp.where((part == 2 + index) & (pos == at) & chosen, moved, share)
        added.append(share)
    new = gathered[PLANES:STRIP_ROWS] + jnp.concatenate(added, axis=0)
    return gathered[:PLANES], new


def aligned(start, size):
    return pl.ds(pl.multiple_of(start, 8), size)


def padded_at(block, ztile):
    return block * STRIDE + PAD + DEPTH * ztile


def advance(source, target, coeffs, upward, slot, from_rows, to_rows, ztile, ghosts):
    lane = lane_ids((DEPTH, LANES))

    def value(field, tile, shift):
        start = from_rows + padded_at(field * TILES + tile, ztile) + shift
        return source[aligned(start, DEPTH) if shift == 0 else pl.ds(start, DEPTH), :]

    def get(kind, tile):
        return coeffs[
            aligned(slot * COEFF_ROWS + (kind * TILES + tile) * FZ + DEPTH * ztile, DEPTH), :
        ]

    centers = [value(field, 0, 0) for field in range(SPECIES)]
    down = [roll_lanes(center, -EDGE) for center in centers]
    up = [roll_lanes(center, EDGE) for center in centers]
    up_before = list(up)
    for tile in range(TILES):
        if tile + 1 < TILES:
            centers_after = [value(field, tile + 1, 0) for field in range(SPECIES)]
            down_after = [roll_lanes(center, -EDGE) for center in centers_after]
        next_x, prev_x, next_y, rate = [get(kind, tile) for kind in range(4)]
        prev_y = roll_lanes(next_y, 1)
        base = slot * UPWARD_ROWS + padded_at(tile, ztile)
        next_z = upward[aligned(base, DEPTH), :]
        prev_z = upward[pl.ds(base - 1, DEPTH), :]
        forward = rate * (centers[0] * centers[1] - centers[2])
        for field in range(SPECIES):
            center = centers[field]
            ahead, behind = down[field], up[field]
            if tile + 1 < TILES:
                ahead = jnp.where(lane < LANES - EDGE, ahead, down_after[field])
            if tile > 0:
                behind = jnp.where(lane >= EDGE, behind, up_before[field])
            flux = (next_x * ahead + prev_x * behind) + (
                next_y * roll_lanes(center, -1) + prev_y * roll_lanes(center, 1)
            )
            flux = flux + (next_z * value(field, tile, 1) + prev_z * value(field, tile, -1))
            share = ghosts(field, tile)
            if share is not None:
                flux = flux + share
            if DIFFUSE[field] != 1.0:
                flux = DIFFUSE[field] * flux
            result = get(4 + field, tile) * center + flux
            result = result - forward if SIGNS[field] < 0 else result + forward
            target[aligned(to_rows + padded_at(field * TILES + tile, ztile), DEPTH), :] = result
        if tile + 1 < TILES:
            up_before = up
            centers, down = centers_after, down_after
            up = [roll_lanes(center, EDGE) for center in centers]


def clear_pads(ref, size):
    edge = jnp.zeros((PAD, LANES), jnp.float32)
    for start in range(0, ref.shape[0], size):
        for row in range(start, start + size, STRIDE):
            ref[row : row + PAD, :] = edge


def hand_on_kernel(low_ref, high_ref, low_out, high_out):
    low_out[...] = low_ref[...]
    high_out[...] = high_ref[...]


def prepare_kernel(
    after_ref,
    state_hbm,
    kappa_hbm,
    rate_hbm,
    fields_hbm,
    coeffs_hbm,
    upward_hbm,
    fields_ref,
    coeffs,
    upward,
    state_ref,
    kappa_ref,
    rate_ref,
    first,
    conduct,
    sems,
    out_sems,
    *,
    slots,
):
    def loads(slot):
        return [
            pltpu.make_async_copy(source.at[slot], target.at[slot], sems.at[order, slot])
            for order, (source, target) in enumerate(
                ((kappa_hbm, kappa_ref), (rate_hbm, rate_ref), (state_hbm, state_ref))
            )
        ]

    for slot in range(slots):
        start_all(loads(slot))

    def stores(slot):
        return [
            pltpu.make_async_copy(
                source.at[aligned(slot * size, size)],
                target.at[aligned(slot * size, size)],
                out_sems.at[order, slot],
            )
            for order, (source, target, size) in enumerate(
                (
                    (fields_ref, fields_hbm, FIELD_ROWS),
                    (coeffs, coeffs_hbm, COEFF_ROWS),
                    (upward, upward_hbm, UPWARD_ROWS),
                )
            )
        ]

    for ref, size in (
        (conduct, UPWARD_ROWS),
        (upward, UPWARD_ROWS),
        (first, FIELD_ROWS),
        (fields_ref, FIELD_ROWS),
    ):
        clear_pads(ref, size)

    lane = lane_ids((DEPTH, LANES))
    column = lane % EDGE
    side_y = jnp.where((column == 0) | (column == EDGE - 1), 1.0, 0.0)

    def one_patch(slot, carry):
        for copy in loads(slot):
            copy.wait()

        for tile in range(TILES):
            cols = pl.ds(tile * LANES, LANES)
            for field in range(SPECIES):
                spot = aligned(slot * FIELD_ROWS + padded_at(field * TILES + tile, 0), FZ)
                first[spot, :] = state_ref[slot, field, :, cols]
            spot = aligned(slot * UPWARD_ROWS + padded_at(tile, 0), FZ)
            conduct[spot, :] = kappa_ref[slot, :, cols]

        def keep(kind, tile, ztile, values):
            coeffs[
                aligned(slot * COEFF_ROWS + (kind * TILES + tile) * FZ + DEPTH * ztile, DEPTH), :
            ] = values

        for ztile in range(ZTILES):

            def here(tile, shift):
                start = slot * UPWARD_ROWS + padded_at(tile, ztile) + shift
                return conduct[aligned(start, DEPTH) if shift == 0 else pl.ds(start, DEPTH), :]

            center = here(0, 0)
            turned = roll_lanes(center, -EDGE)
            back_before = None
            for tile in range(TILES):
                other = turned
                if tile + 1 < TILES:
                    center_after = here(tile + 1, 0)
                    turned_after = roll_lanes(center_after, -EDGE)
                    other = jnp.where(lane < LANES - EDGE, turned, turned_after)
                next_x = face(FINE_SCALE, center, other)
                if tile == TILES - 1:
                    next_x = jnp.where(lane < LANES - EDGE, next_x, 0.0)
                back = roll_lanes(next_x, EDGE)
                prev_x = jnp.where(lane >= EDGE, back, 0.0 if tile == 0 else back_before)
                next_y = jnp.where(
                    column < EDGE - 1, face(FINE_SCALE, center, roll_lanes(center, -1)), 0.0
                )
                prev_y = roll_lanes(next_y, 1)
                next_z = face(FINE_SCALE, center, here(tile, 1))
                spot = slot * UPWARD_ROWS + padded_at(tile, ztile)
                upward[aligned(spot, DEPTH), :] = next_z
                prev_z = upward[pl.ds(spot - 1, DEPTH), :]
                sides = side_y
                if tile == 0:
                    sides = sides + jnp.where(lane < EDGE, 1.0, 0.0)
                if tile == TILES - 1:
                    sides = sides + jnp.where(lane >= LANES - EDGE, 1.0, 0.0)
                scale = FINE_SCALE * center
                total = (next_x + prev_x) + (next_y + prev_y) + (next_z + prev_z) + sides * scale
                keep(0, tile, ztile, next_x)
                keep(1, tile, ztile, prev_x)
                keep(2, tile, ztile, next_y)
                rate = rate_ref[slot, pl.ds(DEPTH * ztile, DEPTH), pl.ds(tile * LANES, LANES)]
                keep(3, tile, ztile, DT_FINE * rate)
                for field in range(SPECIES):
                    keep(4 + field, tile, ztile, 1.0 - DIFFUSE[field] * total)
                keep(7, tile, ztile, scale)
                back_before = back
                if tile + 1 < TILES:
                    center, turned = center_after, turned_after

        for ztile in range(ZTILES):
            advance(
                first,
                fields_ref,
                coeffs,
                upward,
                slot,
                slot * FIELD_ROWS,
                slot * FIELD_ROWS,
                ztile,
                lambda field, tile: None,
            )
        start_all(stores(slot))
        return carry

    lax.fori_loop(0, slots, one_patch, 0)
    for slot in range(slots):
        for copy in stores(slot):
            copy.wait()


def finish_kernel(
    strips_ref,
    fields_hbm,
    coeffs_hbm,
    upward_hbm,
    xl_ref,
    xr_ref,
    out_hbm,
    avg_hbm,
    fields_ref,
    coeffs,
    upward,
    ghost_ref,
    plane_ref,
    mean_ref,
    avg_ref,
    ghosts_ref,
    first,
    share,
    staged,
    sems,
    in_sems,
    avg_sems,
    *,
    slots,
):
    sources = strips_ref.shape[0]

    def loads(slot):
        return [
            pltpu.make_async_copy(
                source.at[aligned(slot * size, size)],
                target.at[aligned(slot * size, size)],
                in_sems.at[order, slot],
            )
            for order, (source, target, size) in enumerate(
                (
                    (fields_hbm, fields_ref, FIELD_ROWS),
                    (coeffs_hbm, coeffs, COEFF_ROWS),
                    (upward_hbm, upward, UPWARD_ROWS),
                )
            )
        ]

    start_all(loads(0))
    clear_pads(first, FIELD_ROWS)
    for tile in range(TILES):
        ghost_ref[:, tile * LANES : (tile + 1) * LANES] = ghost_table(tile)
    plane_ref[...] = plane_table()
    mean_ref[...] = mean_table()

    gathered = strips_ref[0]
    for source in range(1, sources):
        gathered = gathered + strips_ref[source]
    old, new = complete_strips(gathered)
    gathered = jnp.concatenate([old, (new - old) * (1.0 / RATIO)], axis=0)
    quarter = AVG_ROWS // FACES
    group_of = lane_ids((quarter, LANES)) // BLK

    def send_out(slot):
        return pltpu.make_async_copy(staged.at[slot], out_hbm.at[slot], sems.at[slot])

    stretched = [
        jnp.dot(
            plane_ref[...],
            jnp.concatenate(split_pair(roll_lanes(gathered, -slot * BLK)), axis=1),
            preferred_element_type=jnp.float32,
        ).astype(jnp.bfloat16)
        for slot in range(slots)
    ]
    ghost_rows = 2 * SPECIES * FZ
    for pair in range(TILES // 2):
        cols = slice(2 * pair * LANES, 2 * (pair + 1) * LANES)
        for slot in range(slots):
            ghosts_ref[slot * ghost_rows : (slot + 1) * ghost_rows, cols] = jnp.dot(
                stretched[slot], ghost_ref[:, cols], preferred_element_type=jnp.float32
            )

    def one_patch(slot, carry):
        for copy in loads(slot):
            copy.wait()

        @pl.when(slot + 1 < slots)
        def _():
            start_all(loads(slot + 1))

        base = slot * FIELD_ROWS
        scales = slot * COEFF_ROWS
        for tile in range(TILES):
            cols = pl.ds(tile * LANES, LANES)
            scale = coeffs[aligned(scales + (7 * TILES + tile) * FZ, FZ), :]
            for field in range(SPECIES):
                row = (field * TILES + tile) * FZ
                ghost = slot * ghost_rows + field * FZ
                old = scale * ghosts_ref[aligned(ghost, FZ), cols]
                drift = scale * ghosts_ref[aligned(ghost + SPECIES * FZ, FZ), cols]
                later = old
                for step in range(1, RATIO):
                    later = later + drift
                    share[step - 1, row : row + FZ, :] = later
                spot = aligned(base + padded_at(field * TILES + tile, 0), FZ)
                fields_ref[spot, :] = fields_ref[spot, :] + DIFFUSE[field] * old

        for step in range(1, RATIO):
            source, target = (fields_ref, first) if step % 2 else (first, fields_ref)
            for ztile in range(ZTILES):

                def ghosts(field, tile):
                    spot = pl.ds((field * TILES + tile) * FZ + DEPTH * ztile, DEPTH)
                    return share[step - 1, spot, :]

                advance(source, target, coeffs, upward, slot, base, base, ztile, ghosts)

        for tile in range(TILES):
            for field in range(SPECIES):
                spot = aligned(base + padded_at(field * TILES + tile, 0), FZ)
                staged[slot, field, :, pl.ds(tile * LANES, LANES)] = first[spot, :]
        send_out(slot).start()

        return carry

    lax.fori_loop(0, slots, one_patch, 0)
    sums = []
    for slot in range(slots):
        for field in range(SPECIES):
            for plane in range(NZC):
                start = slot * FIELD_ROWS + field * TILES * STRIDE + PAD + RATIO * plane
                part = [first[pl.ds(start + z, TILES, stride=STRIDE), :] for z in range(RATIO)]
                sums.append((part[0] + part[1]) + (part[2] + part[3]))
    means = jnp.dot(
        jnp.concatenate(split_pair(jnp.concatenate(sums, axis=0)), axis=1),
        mean_ref[...],
        preferred_element_type=jnp.float32,
    )
    chunk = jnp.zeros((quarter, LANES), jnp.float32)
    for slot in range(slots):
        for part in range(FACES):
            row = slot * AVG_ROWS + part * quarter
            chunk = jnp.where(group_of == part * slots + slot, means[row : row + quarter], chunk)
    avg_ref[...] = chunk
    copies = [
        pltpu.make_async_copy(avg_ref, avg_hbm.at[target], avg_sems.at[target])
        for target in range(sources)
    ]
    start_all(copies)
    for copy in copies:
        copy.wait()
    for slot in range(slots):
        send_out(slot).wait()


def edges_kernel(
    new_hbm,
    xlo_ref,
    xhi_ref,
    ylo_ref,
    yhi_ref,
    xl_ref,
    xr_ref,
    yl_ref,
    yr_ref,
    out_ref,
    new_ref,
    sem,
    *,
    cells_x,
    cells_y,
):
    me = lax.axis_index("af")
    last = lax.axis_size("af") - 1
    fetch = pltpu.make_async_copy(new_hbm, new_ref, sem)
    fetch.start()

    def edge_share(own_ref, other_ref):
        own = own_ref[...]
        other = other_ref[...]
        coeff = face(DT_COARSE, jnp.maximum(own, 0.125), other)
        lane = lane_ids(own.shape)
        spread = jnp.zeros_like(own)
        for field in range(SPECIES):
            moved = roll_lanes(coeff, (field - SPECIES) * NZC)
            spread = jnp.where(lane // NZC == field, DIFFUSE[field] * moved, spread)
        return spread * (other - own)

    lower = edge_share(ylo_ref, yl_ref)
    upper = edge_share(yhi_ref, yr_ref)

    lane = lane_ids((BLK, LANES))
    row_id = lax.broadcasted_iota(jnp.int32, (BLK, LANES), 0)
    halves = cells_y // LANES

    def side_share(own_ref, other_ref, exists):
        shares = []
        for half in range(halves):
            own = own_ref[:, half * LANES : (half + 1) * LANES]
            other = other_ref[:, half * LANES : (half + 1) * LANES]
            coeff = face(DT_COARSE, own[PLANES:], other[PLANES:])
            coeff = jnp.where(exists, coeff, 0.0)
            shares.append(
                jnp.concatenate(
                    [
                        (DIFFUSE[field] * coeff)
                        * (
                            other[field * NZC : (field + 1) * NZC]
                            - own[field * NZC : (field + 1) * NZC]
                        )
                        for field in range(SPECIES)
                    ],
                    axis=0,
                )
            )
        return shares

    before = side_share(xlo_ref, xl_ref, me > 0)
    after = side_share(xhi_ref, xr_ref, me < last)
    fetch.wait()
    block_cols = cells_x // BLK
    for column in range(block_cols):
        for plane in range(PLANES):
            row = plane * cells_x + column * BLK
            edge_rows = slice(column * BLK, (column + 1) * BLK)
            for half in range(halves):
                cols = slice(half * LANES, (half + 1) * LANES)
                coarse = new_ref[row : row + BLK, cols]
                if column == 0:
                    share = before[half][plane : plane + 1]
                    coarse = coarse + jnp.where(row_id == 0, share, 0.0)
                if column == block_cols - 1:
                    share = after[half][plane : plane + 1]
                    coarse = coarse + jnp.where(row_id == BLK - 1, share, 0.0)
                if half == 0:
                    share = roll_lanes(lower[edge_rows], -plane)
                    coarse = coarse + jnp.where(lane == 0, share, 0.0)
                if half == halves - 1:
                    share = roll_lanes(upper[edge_rows], LANES - 1 - plane)
                    coarse = coarse + jnp.where(lane == LANES - 1, share, 0.0)
                out_ref[row : row + BLK, cols] = coarse


def place_kernel(
    place_ref, avg_ref, new_ref, out_ref, *, cells_x, cells_y, group, slots
):
    width = slots * BLK
    quarter = AVG_ROWS // FACES
    per_tile = LANES // width
    part = lane_ids((quarter, LANES)) // width
    columns = []
    for tile in range(group * BLK // LANES):
        rows = []
        for index in range(FACES):
            merged = jnp.zeros((quarter, LANES), jnp.float32)
            for place in range(per_tile):
                piece = roll_lanes(avg_ref[tile * per_tile + place], (place - index) * width)
                merged = jnp.where(part == place, piece, merged)
            rows.append(merged)
        columns.append(jnp.concatenate(rows, axis=0))
    high, low = split_pair(jnp.concatenate(columns, axis=1))
    ones = jnp.ones((16, high.shape[1]), jnp.bfloat16)
    stacked = jnp.concatenate([high, low, ones], axis=0)

    halves = cells_y // LANES
    for column in range(cells_x // BLK):
        placed = lax.dot_general(
            stacked,
            selector(place_ref, column, cells_y),
            (((1,), (1,)), ((), ())),
            preferred_element_type=jnp.float32,
        )
        covered = placed[2 * AVG_ROWS : 2 * AVG_ROWS + 8] > 0.5
        for plane in range(PLANES):
            values = (
                placed[plane * BLK : (plane + 1) * BLK]
                + placed[AVG_ROWS + plane * BLK : AVG_ROWS + (plane + 1) * BLK]
            )
            row = plane * cells_x + column * BLK
            for half in range(halves):
                cols = slice(half * LANES, (half + 1) * LANES)
                coarse = new_ref[row : row + BLK, cols]
                out_ref[row : row + BLK, cols] = jnp.where(
                    covered[:, cols], values[:, cols], coarse
                )


VMEM = pl.BlockSpec(memory_space=pltpu.VMEM)
HBM = pl.BlockSpec(memory_space=pltpu.HBM)
PARAMS = pltpu.CompilerParams(vmem_limit_bytes=40 * 1024 * 1024)


def f32(*shape):
    return jax.ShapeDtypeStruct(shape, jnp.float32)


def hbm32(*shape):
    return pltpu.HBM(shape, jnp.float32)


def pinned(*arrays):
    return [pltpu.with_memory_space_constraint(array, pltpu.HBM) for array in arrays]


def shifted(values, axis, step):
    count = lax.axis_size(axis)
    pairs = [(i, i + step) for i in range(count) if 0 <= i + step < count]
    return lax.ppermute(values, axis, pairs)


def exchange(chunks):
    return lax.all_to_all(chunks, "af", split_axis=0, concat_axis=0, tiled=True)


def per_device(
    coarse_state, coarse_kappa, coarse_rate, fine_state, fine_kappa, fine_rate, boxes, cover
):
    af_count = lax.axis_size("af")
    slots = fine_state.shape[0]
    cells_x, cells_y = coarse_state.shape[2:]
    group = af_count * slots
    lanes = group * BLK
    halves = cells_y // LANES
    rows = PLANES * cells_x
    plain = NZC * cells_x
    sizes = dict(cells_x=cells_x, cells_y=cells_y, group=group)

    span = cells_x + 2 * PAD
    new, send, place, xlo, xhi, ylo, yhi = pl.pallas_call(
        functools.partial(strips_kernel, slots=slots, **sizes),
        out_shape=[
            hbm32(rows, cells_y),
            hbm32(af_count, CHUNK_ROWS, LANES),
            jax.ShapeDtypeStruct((16, lanes), jnp.int32),
        ]
        + [f32(EDGE_ROWS, cells_y)] * 2
        + [f32(cells_x, LANES)] * 2,
        in_specs=[HBM] * 4,
        out_specs=[HBM] * 2 + [VMEM] * 5,
        scratch_shapes=[
            pltpu.VMEM((2, boxes.shape[0]), jnp.int32),
            pltpu.VMEM((rows, cells_y), jnp.float32),
            pltpu.VMEM((plain, cells_y), jnp.float32),
            pltpu.VMEM((plain, cells_y), jnp.float32),
            pltpu.VMEM((rows, cells_y), jnp.float32),
            pltpu.VMEM(((SPECIES + 1) * halves * NZC * span, LANES), jnp.float32),
            pltpu.VMEM((rows * halves, LANES), jnp.float32),
            pltpu.VMEM((af_count, CHUNK_ROWS, LANES), jnp.float32),
            pltpu.SemaphoreType.DMA((4,)),
            pltpu.SemaphoreType.DMA((af_count,)),
        ],
        compiler_params=PARAMS,
        name="strips",
    )(
        *pinned(
            boxes.T,
            coarse_state.reshape(rows, cells_y),
            coarse_kappa.reshape(plain, cells_y),
            coarse_rate.reshape(plain, cells_y),
        )
    )

    strips = exchange(send)

    xlo_sent, xhi_sent = pl.pallas_call(
        hand_on_kernel,
        out_shape=[f32(EDGE_ROWS, cells_y)] * 2,
        in_specs=[VMEM] * 2,
        out_specs=[VMEM] * 2,
        compiler_params=pltpu.CompilerParams(vmem_limit_bytes=1024 * 1024),
        name="hand_on",
    )(xlo, xhi)
    xl = shifted(xhi_sent, "af", 1)
    xr = shifted(xlo_sent, "af", -1)

    kept = [hbm32(slots * size, LANES) for size in (FIELD_ROWS, COEFF_ROWS, UPWARD_ROWS)]
    kept_scratch = [pltpu.VMEM((slots * size, LANES), jnp.float32)
        for size in (FIELD_ROWS, COEFF_ROWS, UPWARD_ROWS)]
    fields, coeffs, upward = pl.pallas_call(
        functools.partial(prepare_kernel, slots=slots),
        out_shape=kept,
        in_specs=[VMEM] + [HBM] * 3,
        out_specs=[HBM] * 3,
        scratch_shapes=kept_scratch
        + [
            pltpu.VMEM(fine_state.shape, jnp.float32),
            pltpu.VMEM(fine_kappa.shape, jnp.float32),
            pltpu.VMEM(fine_rate.shape, jnp.float32),
            pltpu.VMEM((slots * FIELD_ROWS, LANES), jnp.float32),
            pltpu.VMEM((slots * UPWARD_ROWS, LANES), jnp.float32),
            pltpu.SemaphoreType.DMA((3, slots)),
            pltpu.SemaphoreType.DMA((3, slots)),
        ],
        compiler_params=PARAMS,
        name="prepare",
    )(xlo_sent, *pinned(fine_state, fine_kappa, fine_rate))

    chunk = (AVG_ROWS // FACES, LANES)
    fine_out, averages = pl.pallas_call(
        functools.partial(finish_kernel, slots=slots),
        out_shape=[hbm32(*fine_state.shape), hbm32(af_count, *chunk)],
        in_specs=[VMEM] + [HBM] * 3 + [VMEM] * 2,
        out_specs=[HBM] * 2,
        scratch_shapes=kept_scratch
        + [
            pltpu.VMEM((2 * LANES, EDGE * EDGE), jnp.bfloat16),
            pltpu.VMEM((2 * SPECIES * FZ, STRIP_ROWS), jnp.bfloat16),
            pltpu.VMEM((2 * LANES, LANES), jnp.bfloat16),
            pltpu.VMEM(chunk, jnp.float32),
            pltpu.VMEM((slots * 2 * SPECIES * FZ, EDGE * EDGE), jnp.float32),
            pltpu.VMEM((slots * FIELD_ROWS, LANES), jnp.float32),
            pltpu.VMEM((RATIO - 1, SPECIES * TILES * FZ, LANES), jnp.float32),
            pltpu.VMEM(fine_state.shape, jnp.float32),
            pltpu.SemaphoreType.DMA((slots,)),
            pltpu.SemaphoreType.DMA((3, slots)),
            pltpu.SemaphoreType.DMA((af_count,)),
        ],
        compiler_params=PARAMS,
        name="finish",
    )(strips, *pinned(fields, coeffs, upward), xl, xr)

    arrived = exchange(averages)

    yl = shifted(yhi, "col", 1)
    yr = shifted(ylo, "col", -1)
    whole = pl.pallas_call(
        functools.partial(edges_kernel, cells_x=cells_x, cells_y=cells_y),
        out_shape=f32(rows, cells_y),
        in_specs=[HBM] + [VMEM] * 8,
        out_specs=VMEM,
        scratch_shapes=[pltpu.VMEM((rows, cells_y), jnp.float32), pltpu.SemaphoreType.DMA],
        compiler_params=PARAMS,
        name="edges",
    )(*pinned(new), xlo, xhi, ylo, yhi, xl, xr, yl, yr)

    placed = pl.pallas_call(
        functools.partial(place_kernel, slots=slots, **sizes),
        out_shape=f32(rows, cells_y),
        in_specs=[VMEM] * 3,
        out_specs=VMEM,
        compiler_params=PARAMS,
        name="place",
    )(place, arrived, whole)
    return (placed.reshape(coarse_state.shape), fine_out)


def solution(mesh):
    return jax.shard_map(
        per_device,
        mesh=mesh,
        in_specs=(
            P(None, None, "af", "col"),
            P(None, "af", "col"),
            P(None, "af", "col"),
            P(("col", "af"), None, None, None),
            P(("col", "af"), None, None),
            P(("col", "af"), None, None),
            P(),
            P(),
        ),
        out_specs=(P(None, None, "af", "col"), P(("col", "af"), None, None, None)),
        check_vma=False,
    )
```

```python
import functools

import jax
import jax.numpy as jnp
from jax import lax
from jax.experimental import pallas as pl
from jax.experimental.pallas import tpu as pltpu
from jax.sharding import PartitionSpec as P

NZC = 8
RATIO = 4
BLK = 8
SPECIES = 3
EDGE = BLK * RATIO
FZ = NZC * RATIO
LANES = 128
TILES = EDGE * EDGE // LANES
DEPTH = 8
ZTILES = FZ // DEPTH
STRIDE = 40
PAD = 8
FACES = 4
PLANES = SPECIES * NZC
STRIP_ROWS = 2 * PLANES
AVG_ROWS = PLANES * BLK
KINDS = 8
FIELD_ROWS = SPECIES * TILES * STRIDE + PAD
COEFF_ROWS = KINDS * TILES * FZ
UPWARD_ROWS = TILES * STRIDE + PAD
EDGE_ROWS = PLANES + NZC
BESIDE_ROWS = 2 * NZC
CHUNK_ROWS = STRIP_ROWS + BESIDE_ROWS

DT_COARSE = 1.0 / 28.0
DIFFUSE = (1.0, 0.7, 0.45)
SIGNS = (-1.0, -1.0, 1.0)
FINE_SCALE = RATIO * RATIO * DT_COARSE / RATIO
DT_FINE = DT_COARSE / RATIO


def lane_ids(shape):
    return lax.broadcasted_iota(jnp.int32, shape, len(shape) - 1)


def roll_lanes(values, shift):
    width = values.shape[-1]
    shift = shift % width
    return values if shift == 0 else pltpu.roll(values, shift, values.ndim - 1)


def split_pair(values):
    high = values.astype(jnp.bfloat16)
    low = (values - high.astype(jnp.float32)).astype(jnp.bfloat16)
    return high, low


def face(scale, one, other):
    summed = one + other
    inverse = pl.reciprocal(summed, approx=True)
    inverse = inverse * (2.0 - summed * inverse)
    return (2.0 * scale) * (one * other) * inverse


def start_all(copies):
    for copy in copies:
        copy.start()


def selector(place_ref, column, cells_y):
    wanted = jnp.where(place_ref[0:8, :] == column, place_ref[8:16, :], -1)
    row = lax.broadcasted_iota(jnp.int32, wanted.shape, 0)
    return jnp.concatenate(
        [jnp.where(row + 8 * at == wanted, 1.0, 0.0) for at in range(cells_y // 8)], axis=0
    ).astype(jnp.bfloat16)


def strips_kernel(
    boxes_hbm,
    state_hbm,
    kappa_hbm,
    rate_hbm,
    new_hbm,
    send_hbm,
    place_ref,
    xlo_ref,
    xhi_ref,
    ylo_ref,
    yhi_ref,
    boxes_ref,
    state_ref,
    kappa_ref,
    rate_ref,
    new_ref,
    padded,
    fresh,
    send_ref,
    sems,
    send_sems,
    *,
    cells_x,
    cells_y,
    group,
    slots,
):
    pairs = (
        (boxes_hbm, boxes_ref),
        (kappa_hbm, kappa_ref),
        (state_hbm, state_ref),
        (rate_hbm, rate_ref),
    )
    copies = [
        pltpu.make_async_copy(source, target, sems.at[index])
        for index, (source, target) in enumerate(pairs)
    ]
    start_all(copies)

    patches = boxes_ref.shape[1]
    lanes = group * BLK
    base_patch = lax.axis_index("col") * group
    member = lax.broadcasted_iota(jnp.int32, (patches, lanes), 0) - base_patch
    spread = jnp.where(member == lane_ids((patches, lanes)) // BLK, 1.0, 0.0).astype(jnp.bfloat16)
    first_col = lax.axis_index("af") * (cells_x // BLK)
    first_cell = lax.axis_index("col") * cells_y
    copies[0].wait()
    boxes = boxes_ref[...].astype(jnp.float32)
    stacked = jnp.concatenate(
        [jnp.broadcast_to(boxes[row : row + 1], (8, patches)) for row in range(2)], axis=0
    )
    found = jnp.dot(
        stacked.astype(jnp.bfloat16), spread, preferred_element_type=jnp.float32
    ).astype(jnp.int32)
    place_ref[0:8, :] = found[0:8] - first_col
    place_ref[8:16, :] = found[8:16] * BLK - first_cell + lane_ids((8, lanes)) % BLK

    halves = cells_y // LANES
    span = cells_x + 2 * PAD
    nothing = jnp.zeros((PAD, LANES), jnp.float32)

    def base(field, half, z):
        return ((field * halves + half) * NZC + z) * span

    for copy in copies[1:]:
        copy.wait()
    for field in range(SPECIES + 1):
        for half in range(halves):
            cols = pl.ds(half * LANES, LANES)
            for z in range(NZC):
                if field < SPECIES:
                    start = (field * NZC + z) * cells_x
                    plane = state_ref[start : start + cells_x, cols]
                else:
                    plane = kappa_ref[z * cells_x : (z + 1) * cells_x, cols]
                at = base(field, half, z)
                padded[at : at + PAD, :] = nothing
                padded[at + PAD : at + PAD + cells_x, :] = plane
                padded[at + PAD + cells_x : at + span, :] = nothing

    lane = lane_ids((cells_x, LANES))
    row_id = lax.broadcasted_iota(jnp.int32, (cells_x, LANES), 0)

    low = jnp.zeros((cells_x, LANES), jnp.float32)
    high = jnp.zeros((cells_x, LANES), jnp.float32)
    for plane in range(PLANES + NZC):
        field, z = divmod(plane, NZC)
        at = base(field, 0, z) + PAD
        first = padded[at : at + cells_x, :]
        at = base(field, halves - 1, z) + PAD
        last = padded[at : at + cells_x, :]
        low = jnp.where(lane == plane, roll_lanes(first, plane), low)
        high = jnp.where(lane == plane, roll_lanes(last, plane + 1), high)
    ylo_ref[...] = low
    yhi_ref[...] = high

    def load(field, half, z, shift):
        at = base(field, half, z) + PAD + shift
        return padded[at : at + cells_x, :]

    def neighbours(field, half, z):
        here = load(field, half, z, 0)
        after = roll_lanes(here, -1)
        if half + 1 < halves:
            after = jnp.where(
                lane == LANES - 1, roll_lanes(load(field, half + 1, z, 0), -1), after
            )
        before = roll_lanes(here, 1)
        if half > 0:
            before = jnp.where(lane == 0, roll_lanes(load(field, half - 1, z, 0), 1), before)
        found = [after, before, load(field, half, z, 1), load(field, half, z, -1)]
        if z + 1 < NZC:
            found.append(load(field, half, z + 1, 0))
        if z > 0:
            found.append(load(field, half, z - 1, 0))
        return found

    for z in range(NZC):
        for half in range(halves):
            cols = pl.ds(half * LANES, LANES)
            conduct = load(SPECIES, half, z, 0)
            coeffs = [face(DT_COARSE, conduct, other) for other in neighbours(SPECIES, half, z)]
            if half == halves - 1:
                coeffs[0] = jnp.where(lane == LANES - 1, 0.0, coeffs[0])
            if half == 0:
                coeffs[1] = jnp.where(lane == 0, 0.0, coeffs[1])
            coeffs[2] = jnp.where(row_id == cells_x - 1, 0.0, coeffs[2])
            coeffs[3] = jnp.where(row_id == 0, 0.0, coeffs[3])
            centers = [load(field, half, z, 0) for field in range(SPECIES)]
            forward = (DT_COARSE * rate_ref[z * cells_x : (z + 1) * cells_x, cols]) * (
                centers[0] * centers[1] - centers[2]
            )
            for field in range(SPECIES):
                center = centers[field]
                flux = None
                for coeff, other in zip(coeffs, neighbours(field, half, z)):
                    term = coeff * (other - center)
                    flux = term if flux is None else flux + term
                start = (field * NZC + z) * cells_x
                result = center + DIFFUSE[field] * flux + SIGNS[field] * forward
                new_ref[start : start + cells_x, cols] = result
                start = ((field * halves + half) * NZC + z) * cells_x
                fresh[start : start + cells_x, :] = result

    keep_new = pltpu.make_async_copy(new_ref, new_hbm, sems.at[0])
    keep_new.start()

    def old_row(field, half, row):
        return padded[pl.ds(base(field, half, 0) + PAD + row, NZC, stride=span), :]

    def edge_at(row):
        return jnp.concatenate(
            [
                jnp.concatenate([old_row(field, half, row) for field in range(SPECIES + 1)], axis=0)
                for half in range(halves)
            ],
            axis=1,
        )

    def rows_at(row):
        columns = []
        for half in range(halves):
            pieces = [old_row(field, half, row) for field in range(SPECIES)]
            for field in range(SPECIES):
                start = (field * halves + half) * NZC * cells_x
                pieces.append(fresh[pl.ds(start + row, NZC, stride=cells_x), :])
            columns.append(jnp.concatenate(pieces, axis=0))
        return jnp.concatenate(columns, axis=1)

    block_cols = cells_x // BLK
    spot = lane_ids((STRIP_ROWS, cells_y)) % BLK
    lower_y = []
    upper_y = []
    for column in range(block_cols):
        below = jnp.zeros((STRIP_ROWS, cells_y), jnp.float32)
        above = jnp.zeros((STRIP_ROWS, cells_y), jnp.float32)
        for x in range(BLK):
            turned = roll_lanes(rows_at(column * BLK + x), x + 1)
            below = jnp.where(spot == x, turned, below)
            above = jnp.where(spot == (x + 1) % BLK, turned, above)
        lower_y.append(below)
        upper_y.append(roll_lanes(above, -1 - BLK))

    first_row = edge_at(0)
    last_row = edge_at(cells_x - 1)
    xlo_ref[...] = first_row
    xhi_ref[...] = last_row
    place = lane_ids((NZC, cells_y)) % BLK
    ones = jnp.ones((NZC, cells_y), jnp.float32)

    def field_of(row, field):
        return row[field * NZC : (field + 1) * NZC]

    def corners(row, fields, first_at):
        found = jnp.zeros((NZC, cells_y), jnp.float32)
        for order, field in enumerate(fields):
            at = first_at + 2 * order
            values = field_of(row, field)
            found = jnp.where(place == at, roll_lanes(values, at + 1), found)
            found = jnp.where(place == at + 1, roll_lanes(values, at + 1 - BLK), found)
        return found

    every = range(SPECIES)

    def near(row):
        own = [(field, field_of(row, field)) for field in range(SPECIES + 1)]
        return own + [(5, corners(row, [SPECIES], 0))]

    def far(row):
        return [
            (4, field_of(row, SPECIES)),
            (5, corners(row, every, 2)),
            (6, corners(row, [SPECIES], 0)),
        ]

    extra_members = {
        -1: far(first_row),
        0: near(first_row),
        block_cols - 1: near(last_row) + [(7, ones)],
        block_cols: far(last_row),
    }

    faces = [None] * (3 * FACES)

    def add(index, part):
        faces[index] = part if faces[index] is None else faces[index] + part

    for column in range(-1, block_cols + 1):
        members = []
        if column >= 1:
            members.append((0, rows_at(column * BLK - 1)))
        if column < block_cols - 1:
            members.append((1, rows_at(column * BLK + BLK)))
        if 0 <= column < block_cols:
            members.append((2, lower_y[column]))
            members.append((3, upper_y[column]))
        for index, rows in extra_members.get(column, []):
            members.append((FACES + index, rows))
        operands = []
        for _, rows in members:
            operands.extend(split_pair(rows))
        moved = jnp.dot(
            jnp.concatenate(operands, axis=0),
            selector(place_ref, column, cells_y),
            preferred_element_type=jnp.float32,
        )
        at = 0
        for index, rows in members:
            size = rows.shape[0]
            add(index, moved[at : at + size] + moved[at + size : at + 2 * size])
            at += 2 * size

    width = slots * BLK
    outgoing = [
        pltpu.make_async_copy(send_ref.at[target], send_hbm.at[target], send_sems.at[target])
        for target in range(group // slots)
    ]
    for target in range(group // slots):
        first = target * width
        tile = first // LANES * LANES
        for start, size, kind in (
            (0, STRIP_ROWS, 0),
            (STRIP_ROWS, NZC, FACES),
            (STRIP_ROWS + NZC, NZC, 2 * FACES),
        ):
            part = lane_ids((size, LANES)) // width
            chunk = jnp.zeros((size, LANES), jnp.float32)
            for index in range(FACES):
                piece = faces[kind + index][:, tile : tile + LANES]
                chunk = jnp.where(
                    part == index, roll_lanes(piece, index * width - (first - tile)), chunk
                )
            send_ref[target, start : start + size, :] = chunk
        outgoing[target].start()
    for copy in outgoing:
        copy.wait()
    keep_new.wait()


def ghost_table(tile):
    lane = lane_ids((BLK, LANES))
    pos = lax.broadcasted_iota(jnp.int32, (BLK, LANES), 0)
    x = tile * (LANES // EDGE) + lane // EDGE
    y = lane % EDGE
    along_y = y // RATIO == pos
    along_x = x // RATIO == pos
    seen = (
        (x == 0) & along_y,
        (x == EDGE - 1) & along_y,
        (y == 0) & along_x,
        (y == EDGE - 1) & along_x,
    )
    nothing = jnp.zeros((LANES // FACES - BLK, LANES), jnp.float32)
    rows = []
    for where in seen:
        rows.extend([jnp.where(where, 1.0, 0.0), nothing])
    return jnp.concatenate(rows + rows, axis=0).astype(jnp.bfloat16)


def plane_table():
    shape = (2 * SPECIES * FZ, STRIP_ROWS)
    rows = lax.broadcasted_iota(jnp.int32, shape, 0)
    return jnp.where(rows // RATIO == lane_ids(shape), 1.0, 0.0).astype(jnp.bfloat16)


def mean_table():
    shape = (2 * LANES, LANES)
    rows = lax.broadcasted_iota(jnp.int32, shape, 0)
    same = rows % EDGE // RATIO == lane_ids(shape) % BLK
    return jnp.where(same, 1.0 / RATIO**3, 0.0).astype(jnp.bfloat16)


def complete_strips(gathered):
    width = LANES // FACES
    own = gathered[STRIP_ROWS : STRIP_ROWS + NZC]
    beside = gathered[STRIP_ROWS + NZC : STRIP_ROWS + 2 * NZC]
    lane = lane_ids((NZC, LANES))
    part = lane // width
    pos = lane % BLK
    flag = jnp.where(part == FACES - 1, beside, 0.0)
    flag = flag + roll_lanes(flag, width)
    upper = flag + roll_lanes(flag, 2 * width) > 0.5

    def coefficient(one, other):
        return face(DT_COARSE, jnp.maximum(one, 0.125), jnp.maximum(other, 0.125))

    block = coefficient(roll_lanes(own, width), beside)
    corner = coefficient(beside, roll_lanes(beside, -width))
    added = []
    for field in range(SPECIES):
        old = gathered[field * NZC : (field + 1) * NZC]
        there = jnp.where(upper, roll_lanes(old, -width), old)
        across = DIFFUSE[field] * block * (roll_lanes(own, -field * width) - there)
        below = jnp.where(upper, roll_lanes(old, -width - (BLK - 1)), roll_lanes(old, -width))
        above = jnp.where(
            upper, roll_lanes(old, -2 * width - (BLK - 2)), roll_lanes(old, 1 - 2 * width)
        )
        here = jnp.where(pos == 0, below, above)
        along = DIFFUSE[field] * corner * (roll_lanes(beside, -2 - 2 * field) - here)
        share = jnp.where((part == 0) & ~upper, across, 0.0)
        share = jnp.where((part == 1) & upper, roll_lanes(across, width), share)
        for index in range(2):
            for at, chosen in ((0, ~upper), (BLK - 1, upper)):
                moved = roll_lanes(along, (1 + index) * width + at - index)
                share = jnp.where((part == 2 + index) & (pos == at) & chosen, moved, share)
        added.append(share)
    new = gathered[PLANES:STRIP_ROWS] + jnp.concatenate(added, axis=0)
    return gathered[:PLANES], new


def aligned(start, size):
    return pl.ds(start if isinstance(start, int) else pl.multiple_of(start, 8), size)


def padded_at(block, ztile):
    return block * STRIDE + PAD + DEPTH * ztile


def advance(source, target, coeffs, upward, slot, from_rows, to_rows, ztile, ghosts):
    lane = lane_ids((DEPTH, LANES))

    def value(field, tile, shift):
        start = from_rows + padded_at(field * TILES + tile, ztile) + shift
        return source[aligned(start, DEPTH) if shift == 0 else pl.ds(start, DEPTH), :]

    def get(kind, tile):
        return coeffs[
            aligned(slot * COEFF_ROWS + (kind * TILES + tile) * FZ + DEPTH * ztile, DEPTH), :
        ]

    centers = [value(field, 0, 0) for field in range(SPECIES)]
    down = [roll_lanes(center, -EDGE) for center in centers]
    up = [roll_lanes(center, EDGE) for center in centers]
    up_before = list(up)
    for tile in range(TILES):
        if tile + 1 < TILES:
            centers_after = [value(field, tile + 1, 0) for field in range(SPECIES)]
            down_after = [roll_lanes(center, -EDGE) for center in centers_after]
        next_x, prev_x, next_y, rate = [get(kind, tile) for kind in range(4)]
        prev_y = roll_lanes(next_y, 1)
        base = slot * UPWARD_ROWS + padded_at(tile, ztile)
        next_z = upward[aligned(base, DEPTH), :]
        prev_z = upward[pl.ds(base - 1, DEPTH), :]
        forward = rate * (centers[0] * centers[1] - centers[2])
        for field in range(SPECIES):
            center = centers[field]
            ahead, behind = down[field], up[field]
            if tile + 1 < TILES:
                ahead = jnp.where(lane < LANES - EDGE, ahead, down_after[field])
            if tile > 0:
                behind = jnp.where(lane >= EDGE, behind, up_before[field])
            flux = (next_x * ahead + prev_x * behind) + (
                next_y * roll_lanes(center, -1) + prev_y * roll_lanes(center, 1)
            )
            flux = flux + (next_z * value(field, tile, 1) + prev_z * value(field, tile, -1))
            share = ghosts(field, tile)
            if share is not None:
                flux = flux + share
            if DIFFUSE[field] != 1.0:
                flux = DIFFUSE[field] * flux
            result = get(4 + field, tile) * center + flux
            result = result - forward if SIGNS[field] < 0 else result + forward
            target[aligned(to_rows + padded_at(field * TILES + tile, ztile), DEPTH), :] = result
        if tile + 1 < TILES:
            up_before = up
            centers, down = centers_after, down_after
            up = [roll_lanes(center, EDGE) for center in centers]


def clear_pads(ref, size):
    edge = jnp.zeros((PAD, LANES), jnp.float32)
    for start in range(0, ref.shape[0], size):
        for row in range(start, start + size, STRIDE):
            ref[row : row + PAD, :] = edge


def hand_on_kernel(low_ref, high_ref, low_out, high_out):
    low_out[...] = low_ref[...]
    high_out[...] = high_ref[...]


def prepare_kernel(
    after_ref,
    state_hbm,
    kappa_hbm,
    rate_hbm,
    fields_hbm,
    coeffs_hbm,
    upward_hbm,
    fields_ref,
    coeffs,
    upward,
    state_ref,
    kappa_ref,
    rate_ref,
    first,
    conduct,
    sems,
    out_sems,
    *,
    slots,
):
    def loads(slot):
        return [
            pltpu.make_async_copy(source.at[slot], target.at[slot], sems.at[order, slot])
            for order, (source, target) in enumerate(
                ((kappa_hbm, kappa_ref), (rate_hbm, rate_ref), (state_hbm, state_ref))
            )
        ]

    for slot in range(slots):
        start_all(loads(slot))

    def stores(slot, start, stop):
        return [
            pltpu.make_async_copy(
                source.at[aligned(slot * size, size)],
                target.at[aligned(slot * size, size)],
                out_sems.at[order, slot],
            )
            for order, (source, target, size) in enumerate(
                (
                    (fields_ref, fields_hbm, FIELD_ROWS),
                    (coeffs, coeffs_hbm, COEFF_ROWS),
                    (upward, upward_hbm, UPWARD_ROWS),
                )
            )
            if start <= order < stop
        ]

    for ref, size in (
        (conduct, UPWARD_ROWS),
        (upward, UPWARD_ROWS),
        (first, FIELD_ROWS),
        (fields_ref, FIELD_ROWS),
    ):
        clear_pads(ref, size)

    lane = lane_ids((DEPTH, LANES))
    column = lane % EDGE
    side_y = jnp.where((column == 0) | (column == EDGE - 1), 1.0, 0.0)

    def one_patch(slot):
        for copy in loads(slot):
            copy.wait()

        for tile in range(TILES):
            cols = pl.ds(tile * LANES, LANES)
            for field in range(SPECIES):
                spot = aligned(slot * FIELD_ROWS + padded_at(field * TILES + tile, 0), FZ)
                first[spot, :] = state_ref[slot, field, :, cols]
            spot = aligned(slot * UPWARD_ROWS + padded_at(tile, 0), FZ)
            conduct[spot, :] = kappa_ref[slot, :, cols]

        def keep(kind, tile, ztile, values):
            coeffs[
                aligned(slot * COEFF_ROWS + (kind * TILES + tile) * FZ + DEPTH * ztile, DEPTH), :
            ] = values

        for ztile in range(ZTILES):

            def here(tile, shift):
                start = slot * UPWARD_ROWS + padded_at(tile, ztile) + shift
                return conduct[aligned(start, DEPTH) if shift == 0 else pl.ds(start, DEPTH), :]

            center = here(0, 0)
            turned = roll_lanes(center, -EDGE)
            back_before = None
            for tile in range(TILES):
                other = turned
                if tile + 1 < TILES:
                    center_after = here(tile + 1, 0)
                    turned_after = roll_lanes(center_after, -EDGE)
                    other = jnp.where(lane < LANES - EDGE, turned, turned_after)
                next_x = face(FINE_SCALE, center, other)
                if tile == TILES - 1:
                    next_x = jnp.where(lane < LANES - EDGE, next_x, 0.0)
                back = roll_lanes(next_x, EDGE)
                prev_x = jnp.where(lane >= EDGE, back, 0.0 if tile == 0 else back_before)
                next_y = jnp.where(
                    column < EDGE - 1, face(FINE_SCALE, center, roll_lanes(center, -1)), 0.0
                )
                prev_y = roll_lanes(next_y, 1)
                next_z = face(FINE_SCALE, center, here(tile, 1))
                spot = slot * UPWARD_ROWS + padded_at(tile, ztile)
                upward[aligned(spot, DEPTH), :] = next_z
                prev_z = upward[pl.ds(spot - 1, DEPTH), :]
                sides = side_y
                if tile == 0:
                    sides = sides + jnp.where(lane < EDGE, 1.0, 0.0)
                if tile == TILES - 1:
                    sides = sides + jnp.where(lane >= LANES - EDGE, 1.0, 0.0)
                scale = FINE_SCALE * center
                total = (next_x + prev_x) + (next_y + prev_y) + (next_z + prev_z) + sides * scale
                keep(0, tile, ztile, next_x)
                keep(1, tile, ztile, prev_x)
                keep(2, tile, ztile, next_y)
                rate = rate_ref[slot, pl.ds(DEPTH * ztile, DEPTH), pl.ds(tile * LANES, LANES)]
                keep(3, tile, ztile, DT_FINE * rate)
                for field in range(SPECIES):
                    keep(4 + field, tile, ztile, 1.0 - DIFFUSE[field] * total)
                keep(7, tile, ztile, scale)
                back_before = back
                if tile + 1 < TILES:
                    center, turned = center_after, turned_after

        start_all(stores(slot, 1, 3))
        for ztile in range(ZTILES):
            advance(
                first,
                fields_ref,
                coeffs,
                upward,
                slot,
                slot * FIELD_ROWS,
                slot * FIELD_ROWS,
                ztile,
                lambda field, tile: None,
            )
        start_all(stores(slot, 0, 1))

    for slot in range(slots):
        one_patch(slot)
    for slot in range(slots):
        for copy in stores(slot, 0, 3):
            copy.wait()


def finish_kernel(
    strips_ref,
    fields_hbm,
    coeffs_hbm,
    upward_hbm,
    xl_ref,
    xr_ref,
    out_hbm,
    avg_hbm,
    fields_ref,
    coeffs,
    upward,
    ghost_ref,
    plane_ref,
    mean_ref,
    avg_ref,
    ghosts_ref,
    first,
    share,
    staged,
    sems,
    in_sems,
    avg_sems,
    *,
    slots,
):
    sources = strips_ref.shape[0]

    def loads(slot):
        return [
            pltpu.make_async_copy(
                source.at[aligned(slot * size, size)],
                target.at[aligned(slot * size, size)],
                in_sems.at[order, slot],
            )
            for order, (source, target, size) in enumerate(
                (
                    (fields_hbm, fields_ref, FIELD_ROWS),
                    (coeffs_hbm, coeffs, COEFF_ROWS),
                    (upward_hbm, upward, UPWARD_ROWS),
                )
            )
        ]

    start_all(loads(0))
    clear_pads(first, FIELD_ROWS)
    for tile in range(TILES):
        ghost_ref[:, tile * LANES : (tile + 1) * LANES] = ghost_table(tile)
    plane_ref[...] = plane_table()
    mean_ref[...] = mean_table()

    gathered = strips_ref[0]
    for source in range(1, sources):
        gathered = gathered + strips_ref[source]
    old, new = complete_strips(gathered)
    gathered = jnp.concatenate([old, (new - old) * (1.0 / RATIO)], axis=0)
    quarter = AVG_ROWS // FACES
    group_of = lane_ids((quarter, LANES)) // BLK

    def send_out(slot):
        return pltpu.make_async_copy(staged.at[slot], out_hbm.at[slot], sems.at[slot])

    stretched = [
        jnp.dot(
            plane_ref[...],
            jnp.concatenate(split_pair(roll_lanes(gathered, -slot * BLK)), axis=1),
            preferred_element_type=jnp.float32,
        ).astype(jnp.bfloat16)
        for slot in range(slots)
    ]
    ghost_rows = 2 * SPECIES * FZ
    for pair in range(TILES // 2):
        cols = slice(2 * pair * LANES, 2 * (pair + 1) * LANES)
        for slot in range(slots):
            ghosts_ref[slot * ghost_rows : (slot + 1) * ghost_rows, cols] = jnp.dot(
                stretched[slot], ghost_ref[:, cols], preferred_element_type=jnp.float32
            )

    def one_patch(slot):
        for copy in loads(slot):
            copy.wait()
        if slot + 1 < slots:
            start_all(loads(slot + 1))
        base = slot * FIELD_ROWS
        scales = slot * COEFF_ROWS
        for tile in range(TILES):
            cols = pl.ds(tile * LANES, LANES)
            scale = coeffs[aligned(scales + (7 * TILES + tile) * FZ, FZ), :]
            for field in range(SPECIES):
                row = (field * TILES + tile) * FZ
                ghost = slot * ghost_rows + field * FZ
                old = scale * ghosts_ref[aligned(ghost, FZ), cols]
                drift = scale * ghosts_ref[aligned(ghost + SPECIES * FZ, FZ), cols]
                later = old
                for step in range(1, RATIO):
                    later = later + drift
                    share[step - 1, row : row + FZ, :] = later
                spot = aligned(base + padded_at(field * TILES + tile, 0), FZ)
                fields_ref[spot, :] = fields_ref[spot, :] + DIFFUSE[field] * old

        for step in range(1, RATIO):
            source, target = (fields_ref, first) if step % 2 else (first, fields_ref)
            for ztile in range(ZTILES):

                def ghosts(field, tile):
                    spot = pl.ds((field * TILES + tile) * FZ + DEPTH * ztile, DEPTH)
                    return share[step - 1, spot, :]

                advance(source, target, coeffs, upward, slot, base, base, ztile, ghosts)

        for tile in range(TILES):
            for field in range(SPECIES):
                spot = aligned(base + padded_at(field * TILES + tile, 0), FZ)
                staged[slot, field, :, pl.ds(tile * LANES, LANES)] = first[spot, :]
        send_out(slot).start()

    for slot in range(slots):
        one_patch(slot)
    sums = []
    for slot in range(slots):
        for field in range(SPECIES):
            for plane in range(NZC):
                start = slot * FIELD_ROWS + field * TILES * STRIDE + PAD + RATIO * plane
                part = [first[pl.ds(start + z, TILES, stride=STRIDE), :] for z in range(RATIO)]
                sums.append((part[0] + part[1]) + (part[2] + part[3]))
    means = jnp.dot(
        jnp.concatenate(split_pair(jnp.concatenate(sums, axis=0)), axis=1),
        mean_ref[...],
        preferred_element_type=jnp.float32,
    )
    chunk = jnp.zeros((quarter, LANES), jnp.float32)
    for slot in range(slots):
        for part in range(FACES):
            row = slot * AVG_ROWS + part * quarter
            chunk = jnp.where(group_of == part * slots + slot, means[row : row + quarter], chunk)
    avg_ref[...] = chunk
    copies = [
        pltpu.make_async_copy(avg_ref, avg_hbm.at[target], avg_sems.at[target])
        for target in range(sources)
    ]
    start_all(copies)
    for copy in copies:
        copy.wait()
    for slot in range(slots):
        send_out(slot).wait()


def edges_kernel(
    new_hbm,
    xlo_ref,
    xhi_ref,
    ylo_ref,
    yhi_ref,
    xl_ref,
    xr_ref,
    yl_ref,
    yr_ref,
    out_ref,
    new_ref,
    sem,
    *,
    cells_x,
    cells_y,
):
    me = lax.axis_index("af")
    last = lax.axis_size("af") - 1
    fetch = pltpu.make_async_copy(new_hbm, new_ref, sem)
    fetch.start()

    def edge_share(own_ref, other_ref):
        own = own_ref[...]
        other = other_ref[...]
        coeff = face(DT_COARSE, jnp.maximum(own, 0.125), other)
        lane = lane_ids(own.shape)
        spread = jnp.zeros_like(own)
        for field in range(SPECIES):
            moved = roll_lanes(coeff, (field - SPECIES) * NZC)
            spread = jnp.where(lane // NZC == field, DIFFUSE[field] * moved, spread)
        return spread * (other - own)

    lower = edge_share(ylo_ref, yl_ref)
    upper = edge_share(yhi_ref, yr_ref)

    lane = lane_ids((BLK, LANES))
    row_id = lax.broadcasted_iota(jnp.int32, (BLK, LANES), 0)
    halves = cells_y // LANES

    def side_share(own_ref, other_ref, exists):
        shares = []
        for half in range(halves):
            own = own_ref[:, half * LANES : (half + 1) * LANES]
            other = other_ref[:, half * LANES : (half + 1) * LANES]
            coeff = face(DT_COARSE, own[PLANES:], other[PLANES:])
            coeff = jnp.where(exists, coeff, 0.0)
            shares.append(
                jnp.concatenate(
                    [
                        (DIFFUSE[field] * coeff)
                        * (
                            other[field * NZC : (field + 1) * NZC]
                            - own[field * NZC : (field + 1) * NZC]
                        )
                        for field in range(SPECIES)
                    ],
                    axis=0,
                )
            )
        return shares

    before = side_share(xlo_ref, xl_ref, me > 0)
    after = side_share(xhi_ref, xr_ref, me < last)
    fetch.wait()
    block_cols = cells_x // BLK
    for column in range(block_cols):
        for plane in range(PLANES):
            row = plane * cells_x + column * BLK
            edge_rows = slice(column * BLK, (column + 1) * BLK)
            for half in range(halves):
                cols = slice(half * LANES, (half + 1) * LANES)
                coarse = new_ref[row : row + BLK, cols]
                if column == 0:
                    share = before[half][plane : plane + 1]
                    coarse = coarse + jnp.where(row_id == 0, share, 0.0)
                if column == block_cols - 1:
                    share = after[half][plane : plane + 1]
                    coarse = coarse + jnp.where(row_id == BLK - 1, share, 0.0)
                if half == 0:
                    share = roll_lanes(lower[edge_rows], -plane)
                    coarse = coarse + jnp.where(lane == 0, share, 0.0)
                if half == halves - 1:
                    share = roll_lanes(upper[edge_rows], LANES - 1 - plane)
                    coarse = coarse + jnp.where(lane == LANES - 1, share, 0.0)
                out_ref[row : row + BLK, cols] = coarse


def place_kernel(
    place_ref, avg_ref, new_ref, out_ref, *, cells_x, cells_y, group, slots
):
    width = slots * BLK
    quarter = AVG_ROWS // FACES
    per_tile = LANES // width
    part = lane_ids((quarter, LANES)) // width
    columns = []
    for tile in range(group * BLK // LANES):
        rows = []
        for index in range(FACES):
            merged = jnp.zeros((quarter, LANES), jnp.float32)
            for place in range(per_tile):
                piece = roll_lanes(avg_ref[tile * per_tile + place], (place - index) * width)
                merged = jnp.where(part == place, piece, merged)
            rows.append(merged)
        columns.append(jnp.concatenate(rows, axis=0))
    high, low = split_pair(jnp.concatenate(columns, axis=1))
    ones = jnp.ones((16, high.shape[1]), jnp.bfloat16)
    stacked = jnp.concatenate([high, low, ones], axis=0)

    halves = cells_y // LANES
    for column in range(cells_x // BLK):
        placed = lax.dot_general(
            stacked,
            selector(place_ref, column, cells_y),
            (((1,), (1,)), ((), ())),
            preferred_element_type=jnp.float32,
        )
        covered = placed[2 * AVG_ROWS : 2 * AVG_ROWS + 8] > 0.5
        for plane in range(PLANES):
            values = (
                placed[plane * BLK : (plane + 1) * BLK]
                + placed[AVG_ROWS + plane * BLK : AVG_ROWS + (plane + 1) * BLK]
            )
            row = plane * cells_x + column * BLK
            for half in range(halves):
                cols = slice(half * LANES, (half + 1) * LANES)
                coarse = new_ref[row : row + BLK, cols]
                out_ref[row : row + BLK, cols] = jnp.where(
                    covered[:, cols], values[:, cols], coarse
                )


VMEM = pl.BlockSpec(memory_space=pltpu.VMEM)
HBM = pl.BlockSpec(memory_space=pltpu.HBM)
PARAMS = pltpu.CompilerParams(vmem_limit_bytes=40 * 1024 * 1024)


def f32(*shape):
    return jax.ShapeDtypeStruct(shape, jnp.float32)


def hbm32(*shape):
    return pltpu.HBM(shape, jnp.float32)


def pinned(*arrays):
    return [pltpu.with_memory_space_constraint(array, pltpu.HBM) for array in arrays]


def shifted(values, axis, step):
    count = lax.axis_size(axis)
    pairs = [(i, i + step) for i in range(count) if 0 <= i + step < count]
    return lax.ppermute(values, axis, pairs)


def exchange(chunks):
    return lax.all_to_all(chunks, "af", split_axis=0, concat_axis=0, tiled=True)


def per_device(
    coarse_state, coarse_kappa, coarse_rate, fine_state, fine_kappa, fine_rate, boxes, cover
):
    af_count = lax.axis_size("af")
    slots = fine_state.shape[0]
    cells_x, cells_y = coarse_state.shape[2:]
    group = af_count * slots
    lanes = group * BLK
    halves = cells_y // LANES
    rows = PLANES * cells_x
    plain = NZC * cells_x
    sizes = dict(cells_x=cells_x, cells_y=cells_y, group=group)

    span = cells_x + 2 * PAD
    new, send, place, xlo, xhi, ylo, yhi = pl.pallas_call(
        functools.partial(strips_kernel, slots=slots, **sizes),
        out_shape=[
            hbm32(rows, cells_y),
            hbm32(af_count, CHUNK_ROWS, LANES),
            jax.ShapeDtypeStruct((16, lanes), jnp.int32),
        ]
        + [f32(EDGE_ROWS, cells_y)] * 2
        + [f32(cells_x, LANES)] * 2,
        in_specs=[HBM] * 4,
        out_specs=[HBM] * 2 + [VMEM] * 5,
        scratch_shapes=[
            pltpu.VMEM((2, boxes.shape[0]), jnp.int32),
            pltpu.VMEM((rows, cells_y), jnp.float32),
            pltpu.VMEM((plain, cells_y), jnp.float32),
            pltpu.VMEM((plain, cells_y), jnp.float32),
            pltpu.VMEM((rows, cells_y), jnp.float32),
            pltpu.VMEM(((SPECIES + 1) * halves * NZC * span, LANES), jnp.float32),
            pltpu.VMEM((rows * halves, LANES), jnp.float32),
            pltpu.VMEM((af_count, CHUNK_ROWS, LANES), jnp.float32),
            pltpu.SemaphoreType.DMA((4,)),
            pltpu.SemaphoreType.DMA((af_count,)),
        ],
        compiler_params=PARAMS,
        name="strips",
    )(
        *pinned(
            boxes.T,
            coarse_state.reshape(rows, cells_y),
            coarse_kappa.reshape(plain, cells_y),
            coarse_rate.reshape(plain, cells_y),
        )
    )

    strips = exchange(send)

    xlo_sent, xhi_sent = pl.pallas_call(
        hand_on_kernel,
        out_shape=[f32(EDGE_ROWS, cells_y)] * 2,
        in_specs=[VMEM] * 2,
        out_specs=[VMEM] * 2,
        compiler_params=pltpu.CompilerParams(vmem_limit_bytes=1024 * 1024),
        name="hand_on",
    )(xlo, xhi)
    xl = shifted(xhi_sent, "af", 1)
    xr = shifted(xlo_sent, "af", -1)

    kept = [hbm32(slots * size, LANES) for size in (FIELD_ROWS, COEFF_ROWS, UPWARD_ROWS)]
    kept_scratch = [pltpu.VMEM((slots * size, LANES), jnp.float32)
        for size in (FIELD_ROWS, COEFF_ROWS, UPWARD_ROWS)]
    fields, coeffs, upward = pl.pallas_call(
        functools.partial(prepare_kernel, slots=slots),
        out_shape=kept,
        in_specs=[VMEM] + [HBM] * 3,
        out_specs=[HBM] * 3,
        scratch_shapes=kept_scratch
        + [
            pltpu.VMEM(fine_state.shape, jnp.float32),
            pltpu.VMEM(fine_kappa.shape, jnp.float32),
            pltpu.VMEM(fine_rate.shape, jnp.float32),
            pltpu.VMEM((slots * FIELD_ROWS, LANES), jnp.float32),
            pltpu.VMEM((slots * UPWARD_ROWS, LANES), jnp.float32),
            pltpu.SemaphoreType.DMA((3, slots)),
            pltpu.SemaphoreType.DMA((3, slots)),
        ],
        compiler_params=PARAMS,
        name="prepare",
    )(xlo_sent, *pinned(fine_state, fine_kappa, fine_rate))

    chunk = (AVG_ROWS // FACES, LANES)
    fine_out, averages = pl.pallas_call(
        functools.partial(finish_kernel, slots=slots),
        out_shape=[hbm32(*fine_state.shape), hbm32(af_count, *chunk)],
        in_specs=[VMEM] + [HBM] * 3 + [VMEM] * 2,
        out_specs=[HBM] * 2,
        scratch_shapes=kept_scratch
        + [
            pltpu.VMEM((2 * LANES, EDGE * EDGE), jnp.bfloat16),
            pltpu.VMEM((2 * SPECIES * FZ, STRIP_ROWS), jnp.bfloat16),
            pltpu.VMEM((2 * LANES, LANES), jnp.bfloat16),
            pltpu.VMEM(chunk, jnp.float32),
            pltpu.VMEM((slots * 2 * SPECIES * FZ, EDGE * EDGE), jnp.float32),
            pltpu.VMEM((slots * FIELD_ROWS, LANES), jnp.float32),
            pltpu.VMEM((RATIO - 1, SPECIES * TILES * FZ, LANES), jnp.float32),
            pltpu.VMEM(fine_state.shape, jnp.float32),
            pltpu.SemaphoreType.DMA((slots,)),
            pltpu.SemaphoreType.DMA((3, slots)),
            pltpu.SemaphoreType.DMA((af_count,)),
        ],
        compiler_params=PARAMS,
        name="finish",
    )(strips, *pinned(fields, coeffs, upward), xl, xr)

    arrived = exchange(averages)

    yl = shifted(yhi, "col", 1)
    yr = shifted(ylo, "col", -1)
    whole = pl.pallas_call(
        functools.partial(edges_kernel, cells_x=cells_x, cells_y=cells_y),
        out_shape=f32(rows, cells_y),
        in_specs=[HBM] + [VMEM] * 8,
        out_specs=VMEM,
        scratch_shapes=[pltpu.VMEM((rows, cells_y), jnp.float32), pltpu.SemaphoreType.DMA],
        compiler_params=PARAMS,
        name="edges",
    )(*pinned(new), xlo, xhi, ylo, yhi, xl, xr, yl, yr)

    placed = pl.pallas_call(
        functools.partial(place_kernel, slots=slots, **sizes),
        out_shape=f32(rows, cells_y),
        in_specs=[VMEM] * 3,
        out_specs=VMEM,
        compiler_params=PARAMS,
        name="place",
    )(place, arrived, whole)
    return (placed.reshape(coarse_state.shape), fine_out)


def solution(mesh):
    return jax.shard_map(
        per_device,
        mesh=mesh,
        in_specs=(
            P(None, None, "af", "col"),
            P(None, "af", "col"),
            P(None, "af", "col"),
            P(("col", "af"), None, None, None),
            P(("col", "af"), None, None),
            P(("col", "af"), None, None),
            P(),
            P(),
        ),
        out_specs=(P(None, None, "af", "col"), P(("col", "af"), None, None, None)),
        check_vma=False,
    )
```

```python
import functools

import jax
import jax.numpy as jnp
from jax import lax
from jax.experimental import pallas as pl
from jax.experimental.pallas import tpu as pltpu
from jax.sharding import PartitionSpec as P

NZC = 8
RATIO = 4
BLK = 8
SPECIES = 3
EDGE = BLK * RATIO
FZ = NZC * RATIO
LANES = 128
TILES = EDGE * EDGE // LANES
DEPTH = 8
ZTILES = FZ // DEPTH
STRIDE = 40
PAD = 8
FACES = 4
PLANES = SPECIES * NZC
STRIP_ROWS = 2 * PLANES
AVG_ROWS = PLANES * BLK
KINDS = 8
FIELD_ROWS = SPECIES * TILES * STRIDE + PAD
COEFF_ROWS = KINDS * TILES * FZ
UPWARD_ROWS = TILES * STRIDE + PAD
EDGE_ROWS = PLANES + NZC
BESIDE_ROWS = 2 * NZC
CHUNK_ROWS = STRIP_ROWS + BESIDE_ROWS

DT_COARSE = 1.0 / 28.0
DIFFUSE = (1.0, 0.7, 0.45)
SIGNS = (-1.0, -1.0, 1.0)
FINE_SCALE = RATIO * RATIO * DT_COARSE / RATIO
DT_FINE = DT_COARSE / RATIO


def lane_ids(shape):
    return lax.broadcasted_iota(jnp.int32, shape, len(shape) - 1)


def roll_lanes(values, shift):
    width = values.shape[-1]
    shift = shift % width
    return values if shift == 0 else pltpu.roll(values, shift, values.ndim - 1)


def split_pair(values):
    high = values.astype(jnp.bfloat16)
    low = (values - high.astype(jnp.float32)).astype(jnp.bfloat16)
    return high, low


def face(scale, one, other):
    summed = one + other
    inverse = pl.reciprocal(summed, approx=True)
    inverse = inverse * (2.0 - summed * inverse)
    return (2.0 * scale) * (one * other) * inverse


def start_all(copies):
    for copy in copies:
        copy.start()


def selector(place_ref, column, cells_y):
    wanted = jnp.where(place_ref[0:8, :] == column, place_ref[8:16, :], -1)
    row = lax.broadcasted_iota(jnp.int32, wanted.shape, 0)
    return jnp.concatenate(
        [jnp.where(row + 8 * at == wanted, 1.0, 0.0) for at in range(cells_y // 8)], axis=0
    ).astype(jnp.bfloat16)


def strips_kernel(
    boxes_hbm,
    state_hbm,
    kappa_hbm,
    rate_hbm,
    new_hbm,
    send_hbm,
    place_ref,
    xlo_ref,
    xhi_ref,
    ylo_ref,
    yhi_ref,
    boxes_ref,
    state_ref,
    kappa_ref,
    rate_ref,
    new_ref,
    padded,
    fresh,
    send_ref,
    sems,
    send_sems,
    *,
    cells_x,
    cells_y,
    group,
    slots,
):
    pairs = (
        (boxes_hbm, boxes_ref),
        (kappa_hbm, kappa_ref),
        (state_hbm, state_ref),
        (rate_hbm, rate_ref),
    )
    copies = [
        pltpu.make_async_copy(source, target, sems.at[index])
        for index, (source, target) in enumerate(pairs)
    ]
    start_all(copies)

    patches = boxes_ref.shape[1]
    lanes = group * BLK
    base_patch = lax.axis_index("col") * group
    member = lax.broadcasted_iota(jnp.int32, (patches, lanes), 0) - base_patch
    spread = jnp.where(member == lane_ids((patches, lanes)) // BLK, 1.0, 0.0).astype(jnp.bfloat16)
    first_col = lax.axis_index("af") * (cells_x // BLK)
    first_cell = lax.axis_index("col") * cells_y
    copies[0].wait()
    boxes = boxes_ref[...].astype(jnp.float32)
    stacked = jnp.concatenate(
        [jnp.broadcast_to(boxes[row : row + 1], (8, patches)) for row in range(2)], axis=0
    )
    found = jnp.dot(
        stacked.astype(jnp.bfloat16), spread, preferred_element_type=jnp.float32
    ).astype(jnp.int32)
    place_ref[0:8, :] = found[0:8] - first_col
    place_ref[8:16, :] = found[8:16] * BLK - first_cell + lane_ids((8, lanes)) % BLK

    halves = cells_y // LANES
    span = cells_x + 2 * PAD
    nothing = jnp.zeros((PAD, LANES), jnp.float32)

    def base(field, half, z):
        return ((field * halves + half) * NZC + z) * span

    for copy in copies[1:]:
        copy.wait()
    for field in range(SPECIES + 1):
        for half in range(halves):
            cols = pl.ds(half * LANES, LANES)
            for z in range(NZC):
                if field < SPECIES:
                    start = (field * NZC + z) * cells_x
                    plane = state_ref[start : start + cells_x, cols]
                else:
                    plane = kappa_ref[z * cells_x : (z + 1) * cells_x, cols]
                at = base(field, half, z)
                padded[at : at + PAD, :] = nothing
                padded[at + PAD : at + PAD + cells_x, :] = plane
                padded[at + PAD + cells_x : at + span, :] = nothing

    lane = lane_ids((cells_x, LANES))
    row_id = lax.broadcasted_iota(jnp.int32, (cells_x, LANES), 0)

    low = jnp.zeros((cells_x, LANES), jnp.float32)
    high = jnp.zeros((cells_x, LANES), jnp.float32)
    for plane in range(PLANES + NZC):
        field, z = divmod(plane, NZC)
        at = base(field, 0, z) + PAD
        first = padded[at : at + cells_x, :]
        at = base(field, halves - 1, z) + PAD
        last = padded[at : at + cells_x, :]
        low = jnp.where(lane == plane, roll_lanes(first, plane), low)
        high = jnp.where(lane == plane, roll_lanes(last, plane + 1), high)
    ylo_ref[...] = low
    yhi_ref[...] = high

    def load(field, half, z, shift):
        at = base(field, half, z) + PAD + shift
        return padded[at : at + cells_x, :]

    def neighbours(field, half, z):
        here = load(field, half, z, 0)
        after = roll_lanes(here, -1)
        if half + 1 < halves:
            after = jnp.where(
                lane == LANES - 1, roll_lanes(load(field, half + 1, z, 0), -1), after
            )
        before = roll_lanes(here, 1)
        if half > 0:
            before = jnp.where(lane == 0, roll_lanes(load(field, half - 1, z, 0), 1), before)
        found = [after, before, load(field, half, z, 1), load(field, half, z, -1)]
        if z + 1 < NZC:
            found.append(load(field, half, z + 1, 0))
        if z > 0:
            found.append(load(field, half, z - 1, 0))
        return found

    for z in range(NZC):
        for half in range(halves):
            cols = pl.ds(half * LANES, LANES)
            conduct = load(SPECIES, half, z, 0)
            coeffs = [face(DT_COARSE, conduct, other) for other in neighbours(SPECIES, half, z)]
            if half == halves - 1:
                coeffs[0] = jnp.where(lane == LANES - 1, 0.0, coeffs[0])
            if half == 0:
                coeffs[1] = jnp.where(lane == 0, 0.0, coeffs[1])
            coeffs[2] = jnp.where(row_id == cells_x - 1, 0.0, coeffs[2])
            coeffs[3] = jnp.where(row_id == 0, 0.0, coeffs[3])
            centers = [load(field, half, z, 0) for field in range(SPECIES)]
            forward = (DT_COARSE * rate_ref[z * cells_x : (z + 1) * cells_x, cols]) * (
                centers[0] * centers[1] - centers[2]
            )
            for field in range(SPECIES):
                center = centers[field]
                flux = None
                for coeff, other in zip(coeffs, neighbours(field, half, z)):
                    term = coeff * (other - center)
                    flux = term if flux is None else flux + term
                start = (field * NZC + z) * cells_x
                result = center + DIFFUSE[field] * flux + SIGNS[field] * forward
                new_ref[start : start + cells_x, cols] = result
                start = ((field * halves + half) * NZC + z) * cells_x
                fresh[start : start + cells_x, :] = result

    keep_new = pltpu.make_async_copy(new_ref, new_hbm, sems.at[0])
    keep_new.start()

    def old_row(field, half, row):
        return padded[pl.ds(base(field, half, 0) + PAD + row, NZC, stride=span), :]

    def edge_at(row):
        return jnp.concatenate(
            [
                jnp.concatenate([old_row(field, half, row) for field in range(SPECIES + 1)], axis=0)
                for half in range(halves)
            ],
            axis=1,
        )

    def rows_at(row):
        columns = []
        for half in range(halves):
            pieces = [old_row(field, half, row) for field in range(SPECIES)]
            for field in range(SPECIES):
                start = (field * halves + half) * NZC * cells_x
                pieces.append(fresh[pl.ds(start + row, NZC, stride=cells_x), :])
            columns.append(jnp.concatenate(pieces, axis=0))
        return jnp.concatenate(columns, axis=1)

    block_cols = cells_x // BLK
    spot = lane_ids((STRIP_ROWS, cells_y)) % BLK
    lower_y = []
    upper_y = []
    for column in range(block_cols):
        below = jnp.zeros((STRIP_ROWS, cells_y), jnp.float32)
        above = jnp.zeros((STRIP_ROWS, cells_y), jnp.float32)
        for x in range(BLK):
            turned = roll_lanes(rows_at(column * BLK + x), x + 1)
            below = jnp.where(spot == x, turned, below)
            above = jnp.where(spot == (x + 1) % BLK, turned, above)
        lower_y.append(below)
        upper_y.append(roll_lanes(above, -1 - BLK))

    first_row = edge_at(0)
    last_row = edge_at(cells_x - 1)
    xlo_ref[...] = first_row
    xhi_ref[...] = last_row
    place = lane_ids((NZC, cells_y)) % BLK
    ones = jnp.ones((NZC, cells_y), jnp.float32)

    def field_of(row, field):
        return row[field * NZC : (field + 1) * NZC]

    def corners(row, fields, first_at):
        found = jnp.zeros((NZC, cells_y), jnp.float32)
        for order, field in enumerate(fields):
            at = first_at + 2 * order
            values = field_of(row, field)
            found = jnp.where(place == at, roll_lanes(values, at + 1), found)
            found = jnp.where(place == at + 1, roll_lanes(values, at + 1 - BLK), found)
        return found

    every = range(SPECIES)

    def near(row):
        own = [(field, field_of(row, field)) for field in range(SPECIES + 1)]
        return own + [(5, corners(row, [SPECIES], 0))]

    def far(row):
        return [
            (4, field_of(row, SPECIES)),
            (5, corners(row, every, 2)),
            (6, corners(row, [SPECIES], 0)),
        ]

    extra_members = {
        -1: far(first_row),
        0: near(first_row),
        block_cols - 1: near(last_row) + [(7, ones)],
        block_cols: far(last_row),
    }

    faces = [None] * (3 * FACES)

    def add(index, part):
        faces[index] = part if faces[index] is None else faces[index] + part

    for column in range(-1, block_cols + 1):
        members = []
        if column >= 1:
            members.append((0, rows_at(column * BLK - 1)))
        if column < block_cols - 1:
            members.append((1, rows_at(column * BLK + BLK)))
        if 0 <= column < block_cols:
            members.append((2, lower_y[column]))
            members.append((3, upper_y[column]))
        for index, rows in extra_members.get(column, []):
            members.append((FACES + index, rows))
        operands = []
        for _, rows in members:
            operands.extend(split_pair(rows))
        moved = jnp.dot(
            jnp.concatenate(operands, axis=0),
            selector(place_ref, column, cells_y),
            preferred_element_type=jnp.float32,
        )
        at = 0
        for index, rows in members:
            size = rows.shape[0]
            add(index, moved[at : at + size] + moved[at + size : at + 2 * size])
            at += 2 * size

    width = slots * BLK
    outgoing = [
        pltpu.make_async_copy(send_ref.at[target], send_hbm.at[target], send_sems.at[target])
        for target in range(group // slots)
    ]
    for target in range(group // slots):
        first = target * width
        tile = first // LANES * LANES
        for start, size, kind in (
            (0, STRIP_ROWS, 0),
            (STRIP_ROWS, NZC, FACES),
            (STRIP_ROWS + NZC, NZC, 2 * FACES),
        ):
            part = lane_ids((size, LANES)) // width
            chunk = jnp.zeros((size, LANES), jnp.float32)
            for index in range(FACES):
                piece = faces[kind + index][:, tile : tile + LANES]
                chunk = jnp.where(
                    part == index, roll_lanes(piece, index * width - (first - tile)), chunk
                )
            send_ref[target, start : start + size, :] = chunk
        outgoing[target].start()
    for copy in outgoing:
        copy.wait()
    keep_new.wait()


def ghost_table(tile):
    lane = lane_ids((BLK, LANES))
    pos = lax.broadcasted_iota(jnp.int32, (BLK, LANES), 0)
    x = tile * (LANES // EDGE) + lane // EDGE
    y = lane % EDGE
    along_y = y // RATIO == pos
    along_x = x // RATIO == pos
    seen = (
        (x == 0) & along_y,
        (x == EDGE - 1) & along_y,
        (y == 0) & along_x,
        (y == EDGE - 1) & along_x,
    )
    nothing = jnp.zeros((LANES // FACES - BLK, LANES), jnp.float32)
    rows = []
    for where in seen:
        rows.extend([jnp.where(where, 1.0, 0.0), nothing])
    return jnp.concatenate(rows + rows, axis=0).astype(jnp.bfloat16)


def plane_table():
    shape = (2 * SPECIES * FZ, STRIP_ROWS)
    rows = lax.broadcasted_iota(jnp.int32, shape, 0)
    return jnp.where(rows // RATIO == lane_ids(shape), 1.0, 0.0).astype(jnp.bfloat16)


def mean_table():
    shape = (2 * LANES, LANES)
    rows = lax.broadcasted_iota(jnp.int32, shape, 0)
    same = rows % EDGE // RATIO == lane_ids(shape) % BLK
    return jnp.where(same, 1.0 / RATIO**3, 0.0).astype(jnp.bfloat16)


def complete_strips(gathered):
    width = LANES // FACES
    own = gathered[STRIP_ROWS : STRIP_ROWS + NZC]
    beside = gathered[STRIP_ROWS + NZC : STRIP_ROWS + 2 * NZC]
    lane = lane_ids((NZC, LANES))
    part = lane // width
    pos = lane % BLK
    flag = jnp.where(part == FACES - 1, beside, 0.0)
    flag = flag + roll_lanes(flag, width)
    upper = flag + roll_lanes(flag, 2 * width) > 0.5

    def coefficient(one, other):
        return face(DT_COARSE, jnp.maximum(one, 0.125), jnp.maximum(other, 0.125))

    block = coefficient(roll_lanes(own, width), beside)
    corner = coefficient(beside, roll_lanes(beside, -width))
    added = []
    for field in range(SPECIES):
        old = gathered[field * NZC : (field + 1) * NZC]
        there = jnp.where(upper, roll_lanes(old, -width), old)
        across = DIFFUSE[field] * block * (roll_lanes(own, -field * width) - there)
        below = jnp.where(upper, roll_lanes(old, -width - (BLK - 1)), roll_lanes(old, -width))
        above = jnp.where(
            upper, roll_lanes(old, -2 * width - (BLK - 2)), roll_lanes(old, 1 - 2 * width)
        )
        here = jnp.where(pos == 0, below, above)
        along = DIFFUSE[field] * corner * (roll_lanes(beside, -2 - 2 * field) - here)
        share = jnp.where((part == 0) & ~upper, across, 0.0)
        share = jnp.where((part == 1) & upper, roll_lanes(across, width), share)
        for index in range(2):
            for at, chosen in ((0, ~upper), (BLK - 1, upper)):
                moved = roll_lanes(along, (1 + index) * width + at - index)
                share = jnp.where((part == 2 + index) & (pos == at) & chosen, moved, share)
        added.append(share)
    new = gathered[PLANES:STRIP_ROWS] + jnp.concatenate(added, axis=0)
    return gathered[:PLANES], new


def aligned(start, size):
    return pl.ds(start if isinstance(start, int) else pl.multiple_of(start, 8), size)


def padded_at(block, ztile):
    return block * STRIDE + PAD + DEPTH * ztile


def advance(source, target, coeffs, upward, slot, from_rows, to_rows, ztile, ghosts):
    lane = lane_ids((DEPTH, LANES))

    def value(field, tile, shift):
        start = from_rows + padded_at(field * TILES + tile, ztile) + shift
        return source[aligned(start, DEPTH) if shift == 0 else pl.ds(start, DEPTH), :]

    def get(kind, tile):
        return coeffs[
            aligned(slot * COEFF_ROWS + (kind * TILES + tile) * FZ + DEPTH * ztile, DEPTH), :
        ]

    centers = [value(field, 0, 0) for field in range(SPECIES)]
    down = [roll_lanes(center, -EDGE) for center in centers]
    up = [roll_lanes(center, EDGE) for center in centers]
    up_before = list(up)
    for tile in range(TILES):
        if tile + 1 < TILES:
            centers_after = [value(field, tile + 1, 0) for field in range(SPECIES)]
            down_after = [roll_lanes(center, -EDGE) for center in centers_after]
        next_x, prev_x, next_y, rate = [get(kind, tile) for kind in range(4)]
        prev_y = roll_lanes(next_y, 1)
        base = slot * UPWARD_ROWS + padded_at(tile, ztile)
        next_z = upward[aligned(base, DEPTH), :]
        prev_z = upward[pl.ds(base - 1, DEPTH), :]
        forward = rate * (centers[0] * centers[1] - centers[2])
        for field in range(SPECIES):
            center = centers[field]
            ahead, behind = down[field], up[field]
            if tile + 1 < TILES:
                ahead = jnp.where(lane < LANES - EDGE, ahead, down_after[field])
            if tile > 0:
                behind = jnp.where(lane >= EDGE, behind, up_before[field])
            flux = (next_x * ahead + prev_x * behind) + (
                next_y * roll_lanes(center, -1) + prev_y * roll_lanes(center, 1)
            )
            flux = flux + (next_z * value(field, tile, 1) + prev_z * value(field, tile, -1))
            share = ghosts(field, tile)
            if share is not None:
                flux = flux + share
            if DIFFUSE[field] != 1.0:
                flux = DIFFUSE[field] * flux
            result = get(4 + field, tile) * center + flux
            result = result - forward if SIGNS[field] < 0 else result + forward
            target[aligned(to_rows + padded_at(field * TILES + tile, ztile), DEPTH), :] = result
        if tile + 1 < TILES:
            up_before = up
            centers, down = centers_after, down_after
            up = [roll_lanes(center, EDGE) for center in centers]


def clear_pads(ref, size):
    edge = jnp.zeros((PAD, LANES), jnp.float32)
    for start in range(0, ref.shape[0], size):
        for row in range(start, start + size, STRIDE):
            ref[row : row + PAD, :] = edge


def hand_on_kernel(low_ref, high_ref, low_out, high_out):
    low_out[...] = low_ref[...]
    high_out[...] = high_ref[...]


def prepare_kernel(
    after_ref,
    state_hbm,
    kappa_hbm,
    rate_hbm,
    fields_hbm,
    coeffs_hbm,
    upward_hbm,
    fields_ref,
    coeffs,
    upward,
    state_ref,
    kappa_ref,
    rate_ref,
    first,
    conduct,
    sems,
    out_sems,
    *,
    slots,
):
    def loads(slot):
        return [
            pltpu.make_async_copy(source.at[slot], target.at[slot], sems.at[order, slot])
            for order, (source, target) in enumerate(
                ((kappa_hbm, kappa_ref), (rate_hbm, rate_ref), (state_hbm, state_ref))
            )
        ]

    for slot in range(slots):
        start_all(loads(slot))

    def stores(slot, start, stop):
        return [
            pltpu.make_async_copy(
                source.at[aligned(slot * size, size)],
                target.at[aligned(slot * size, size)],
                out_sems.at[order, slot],
            )
            for order, (source, target, size) in enumerate(
                (
                    (fields_ref, fields_hbm, FIELD_ROWS),
                    (coeffs, coeffs_hbm, COEFF_ROWS),
                    (upward, upward_hbm, UPWARD_ROWS),
                )
            )
            if start <= order < stop
        ]

    for ref, size in (
        (conduct, UPWARD_ROWS),
        (upward, UPWARD_ROWS),
        (first, FIELD_ROWS),
        (fields_ref, FIELD_ROWS),
    ):
        clear_pads(ref, size)

    lane = lane_ids((DEPTH, LANES))
    column = lane % EDGE
    side_y = jnp.where((column == 0) | (column == EDGE - 1), 1.0, 0.0)

    def one_patch(slot):
        for copy in loads(slot):
            copy.wait()

        for tile in range(TILES):
            cols = pl.ds(tile * LANES, LANES)
            for field in range(SPECIES):
                spot = aligned(slot * FIELD_ROWS + padded_at(field * TILES + tile, 0), FZ)
                first[spot, :] = state_ref[slot, field, :, cols]
            spot = aligned(slot * UPWARD_ROWS + padded_at(tile, 0), FZ)
            conduct[spot, :] = kappa_ref[slot, :, cols]

        def keep(kind, tile, ztile, values):
            coeffs[
                aligned(slot * COEFF_ROWS + (kind * TILES + tile) * FZ + DEPTH * ztile, DEPTH), :
            ] = values

        for ztile in range(ZTILES):

            def here(tile, shift):
                start = slot * UPWARD_ROWS + padded_at(tile, ztile) + shift
                return conduct[aligned(start, DEPTH) if shift == 0 else pl.ds(start, DEPTH), :]

            center = here(0, 0)
            turned = roll_lanes(center, -EDGE)
            back_before = None
            for tile in range(TILES):
                other = turned
                if tile + 1 < TILES:
                    center_after = here(tile + 1, 0)
                    turned_after = roll_lanes(center_after, -EDGE)
                    other = jnp.where(lane < LANES - EDGE, turned, turned_after)
                next_x = face(FINE_SCALE, center, other)
                if tile == TILES - 1:
                    next_x = jnp.where(lane < LANES - EDGE, next_x, 0.0)
                back = roll_lanes(next_x, EDGE)
                prev_x = jnp.where(lane >= EDGE, back, 0.0 if tile == 0 else back_before)
                next_y = jnp.where(
                    column < EDGE - 1, face(FINE_SCALE, center, roll_lanes(center, -1)), 0.0
                )
                prev_y = roll_lanes(next_y, 1)
                next_z = face(FINE_SCALE, center, here(tile, 1))
                spot = slot * UPWARD_ROWS + padded_at(tile, ztile)
                upward[aligned(spot, DEPTH), :] = next_z
                prev_z = upward[pl.ds(spot - 1, DEPTH), :]
                sides = side_y
                if tile == 0:
                    sides = sides + jnp.where(lane < EDGE, 1.0, 0.0)
                if tile == TILES - 1:
                    sides = sides + jnp.where(lane >= LANES - EDGE, 1.0, 0.0)
                scale = FINE_SCALE * center
                total = (next_x + prev_x) + (next_y + prev_y) + (next_z + prev_z) + sides * scale
                keep(0, tile, ztile, next_x)
                keep(1, tile, ztile, prev_x)
                keep(2, tile, ztile, next_y)
                rate = rate_ref[slot, pl.ds(DEPTH * ztile, DEPTH), pl.ds(tile * LANES, LANES)]
                keep(3, tile, ztile, DT_FINE * rate)
                for field in range(SPECIES):
                    keep(4 + field, tile, ztile, 1.0 - DIFFUSE[field] * total)
                keep(7, tile, ztile, scale)
                back_before = back
                if tile + 1 < TILES:
                    center, turned = center_after, turned_after

        start_all(stores(slot, 1, 3))
        for ztile in range(ZTILES):
            advance(
                first,
                fields_ref,
                coeffs,
                upward,
                slot,
                slot * FIELD_ROWS,
                slot * FIELD_ROWS,
                ztile,
                lambda field, tile: None,
            )
        start_all(stores(slot, 0, 1))

    for slot in range(slots):
        one_patch(slot)
    for slot in range(slots):
        for copy in stores(slot, 0, 3):
            copy.wait()


def finish_kernel(
    strips_ref,
    fields_hbm,
    coeffs_hbm,
    upward_hbm,
    xl_ref,
    xr_ref,
    out_hbm,
    avg_hbm,
    fields_ref,
    coeffs,
    upward,
    ghost_ref,
    plane_ref,
    mean_ref,
    avg_ref,
    ghosts_ref,
    first,
    share,
    staged,
    sems,
    in_sems,
    avg_sems,
    *,
    slots,
):
    sources = strips_ref.shape[0]

    def loads(slot):
        return [
            pltpu.make_async_copy(
                source.at[aligned(slot * size, size)],
                target.at[aligned(slot * size, size)],
                in_sems.at[order, slot],
            )
            for order, (source, target, size) in enumerate(
                (
                    (fields_hbm, fields_ref, FIELD_ROWS),
                    (coeffs_hbm, coeffs, COEFF_ROWS),
                    (upward_hbm, upward, UPWARD_ROWS),
                )
            )
        ]

    start_all(loads(0))
    clear_pads(first, FIELD_ROWS)
    for tile in range(TILES):
        ghost_ref[:, tile * LANES : (tile + 1) * LANES] = ghost_table(tile)
    plane_ref[...] = plane_table()
    mean_ref[...] = mean_table()

    gathered = strips_ref[0]
    for source in range(1, sources):
        gathered = gathered + strips_ref[source]
    old, new = complete_strips(gathered)
    gathered = jnp.concatenate([old, (new - old) * (1.0 / RATIO)], axis=0)
    quarter = AVG_ROWS // FACES
    group_of = lane_ids((quarter, LANES)) // BLK

    def send_out(slot):
        return pltpu.make_async_copy(staged.at[slot], out_hbm.at[slot], sems.at[slot])

    ghost_rows = 2 * SPECIES * FZ

    def make_ghosts(slot):
        stretched = jnp.dot(
            plane_ref[...],
            jnp.concatenate(split_pair(roll_lanes(gathered, -slot * BLK)), axis=1),
            preferred_element_type=jnp.float32,
        ).astype(jnp.bfloat16)
        for pair in range(TILES // 2):
            cols = slice(2 * pair * LANES, 2 * (pair + 1) * LANES)
            ghosts_ref[slot * ghost_rows : (slot + 1) * ghost_rows, cols] = jnp.dot(
                stretched, ghost_ref[:, cols], preferred_element_type=jnp.float32
            )

    def one_patch(slot):
        for copy in loads(slot):
            copy.wait()
        if slot + 1 < slots:
            start_all(loads(slot + 1))
        base = slot * FIELD_ROWS
        scales = slot * COEFF_ROWS
        for tile in range(TILES):
            cols = pl.ds(tile * LANES, LANES)
            scale = coeffs[aligned(scales + (7 * TILES + tile) * FZ, FZ), :]
            for field in range(SPECIES):
                row = (field * TILES + tile) * FZ
                ghost = slot * ghost_rows + field * FZ
                old = scale * ghosts_ref[aligned(ghost, FZ), cols]
                drift = scale * ghosts_ref[aligned(ghost + SPECIES * FZ, FZ), cols]
                later = old
                for step in range(1, RATIO):
                    later = later + drift
                    share[step - 1, row : row + FZ, :] = later
                spot = aligned(base + padded_at(field * TILES + tile, 0), FZ)
                fields_ref[spot, :] = fields_ref[spot, :] + DIFFUSE[field] * old

        if slot + 1 < slots:
            make_ghosts(slot + 1)
        for step in range(1, RATIO):
            source, target = (fields_ref, first) if step % 2 else (first, fields_ref)
            for ztile in range(ZTILES):

                def ghosts(field, tile):
                    spot = pl.ds((field * TILES + tile) * FZ + DEPTH * ztile, DEPTH)
                    return share[step - 1, spot, :]

                advance(source, target, coeffs, upward, slot, base, base, ztile, ghosts)

        for tile in range(TILES):
            for field in range(SPECIES):
                spot = aligned(base + padded_at(field * TILES + tile, 0), FZ)
                staged[slot, field, :, pl.ds(tile * LANES, LANES)] = first[spot, :]
        send_out(slot).start()

        sums = []
        for field in range(SPECIES):
            for plane in range(NZC):
                start = slot * FIELD_ROWS + field * TILES * STRIDE + PAD + RATIO * plane
                part = [first[pl.ds(start + z, TILES, stride=STRIDE), :] for z in range(RATIO)]
                sums.append((part[0] + part[1]) + (part[2] + part[3]))
        means = jnp.dot(
            jnp.concatenate(split_pair(jnp.concatenate(sums, axis=0)), axis=1),
            mean_ref[...],
            preferred_element_type=jnp.float32,
        )
        chunk = jnp.zeros((quarter, LANES), jnp.float32) if slot == 0 else avg_ref[...]
        for part in range(FACES):
            row = part * quarter
            chunk = jnp.where(group_of == part * slots + slot, means[row : row + quarter], chunk)
        avg_ref[...] = chunk

    make_ghosts(0)
    for slot in range(slots):
        one_patch(slot)
    copies = [
        pltpu.make_async_copy(avg_ref, avg_hbm.at[target], avg_sems.at[target])
        for target in range(sources)
    ]
    start_all(copies)
    for copy in copies:
        copy.wait()
    for slot in range(slots):
        send_out(slot).wait()


def edges_kernel(
    new_hbm,
    xlo_ref,
    xhi_ref,
    ylo_ref,
    yhi_ref,
    xl_ref,
    xr_ref,
    yl_ref,
    yr_ref,
    out_ref,
    new_ref,
    sem,
    *,
    cells_x,
    cells_y,
):
    me = lax.axis_index("af")
    last = lax.axis_size("af") - 1
    fetch = pltpu.make_async_copy(new_hbm, new_ref, sem)
    fetch.start()

    def edge_share(own_ref, other_ref):
        own = own_ref[...]
        other = other_ref[...]
        coeff = face(DT_COARSE, jnp.maximum(own, 0.125), other)
        lane = lane_ids(own.shape)
        spread = jnp.zeros_like(own)
        for field in range(SPECIES):
            moved = roll_lanes(coeff, (field - SPECIES) * NZC)
            spread = jnp.where(lane // NZC == field, DIFFUSE[field] * moved, spread)
        return spread * (other - own)

    lower = edge_share(ylo_ref, yl_ref)
    upper = edge_share(yhi_ref, yr_ref)

    lane = lane_ids((BLK, LANES))
    row_id = lax.broadcasted_iota(jnp.int32, (BLK, LANES), 0)
    halves = cells_y // LANES

    def side_share(own_ref, other_ref, exists):
        shares = []
        for half in range(halves):
            own = own_ref[:, half * LANES : (half + 1) * LANES]
            other = other_ref[:, half * LANES : (half + 1) * LANES]
            coeff = face(DT_COARSE, own[PLANES:], other[PLANES:])
            coeff = jnp.where(exists, coeff, 0.0)
            shares.append(
                jnp.concatenate(
                    [
                        (DIFFUSE[field] * coeff)
                        * (
                            other[field * NZC : (field + 1) * NZC]
                            - own[field * NZC : (field + 1) * NZC]
                        )
                        for field in range(SPECIES)
                    ],
                    axis=0,
                )
            )
        return shares

    before = side_share(xlo_ref, xl_ref, me > 0)
    after = side_share(xhi_ref, xr_ref, me < last)
    fetch.wait()
    block_cols = cells_x // BLK
    for column in range(block_cols):
        for plane in range(PLANES):
            row = plane * cells_x + column * BLK
            edge_rows = slice(column * BLK, (column + 1) * BLK)
            for half in range(halves):
                cols = slice(half * LANES, (half + 1) * LANES)
                coarse = new_ref[row : row + BLK, cols]
                if column == 0:
                    share = before[half][plane : plane + 1]
                    coarse = coarse + jnp.where(row_id == 0, share, 0.0)
                if column == block_cols - 1:
                    share = after[half][plane : plane + 1]
                    coarse = coarse + jnp.where(row_id == BLK - 1, share, 0.0)
                if half == 0:
                    share = roll_lanes(lower[edge_rows], -plane)
                    coarse = coarse + jnp.where(lane == 0, share, 0.0)
                if half == halves - 1:
                    share = roll_lanes(upper[edge_rows], LANES - 1 - plane)
                    coarse = coarse + jnp.where(lane == LANES - 1, share, 0.0)
                out_ref[row : row + BLK, cols] = coarse


def place_kernel(
    place_ref, avg_ref, new_ref, out_ref, *, cells_x, cells_y, group, slots
):
    width = slots * BLK
    quarter = AVG_ROWS // FACES
    per_tile = LANES // width
    part = lane_ids((quarter, LANES)) // width
    columns = []
    for tile in range(group * BLK // LANES):
        rows = []
        for index in range(FACES):
            merged = jnp.zeros((quarter, LANES), jnp.float32)
            for place in range(per_tile):
                piece = roll_lanes(avg_ref[tile * per_tile + place], (place - index) * width)
                merged = jnp.where(part == place, piece, merged)
            rows.append(merged)
        columns.append(jnp.concatenate(rows, axis=0))
    high, low = split_pair(jnp.concatenate(columns, axis=1))
    ones = jnp.ones((16, high.shape[1]), jnp.bfloat16)
    stacked = jnp.concatenate([high, low, ones], axis=0)

    halves = cells_y // LANES
    for column in range(cells_x // BLK):
        placed = lax.dot_general(
            stacked,
            selector(place_ref, column, cells_y),
            (((1,), (1,)), ((), ())),
            preferred_element_type=jnp.float32,
        )
        covered = placed[2 * AVG_ROWS : 2 * AVG_ROWS + 8] > 0.5
        for plane in range(PLANES):
            values = (
                placed[plane * BLK : (plane + 1) * BLK]
                + placed[AVG_ROWS + plane * BLK : AVG_ROWS + (plane + 1) * BLK]
            )
            row = plane * cells_x + column * BLK
            for half in range(halves):
                cols = slice(half * LANES, (half + 1) * LANES)
                coarse = new_ref[row : row + BLK, cols]
                out_ref[row : row + BLK, cols] = jnp.where(
                    covered[:, cols], values[:, cols], coarse
                )


VMEM = pl.BlockSpec(memory_space=pltpu.VMEM)
HBM = pl.BlockSpec(memory_space=pltpu.HBM)
PARAMS = pltpu.CompilerParams(vmem_limit_bytes=40 * 1024 * 1024)


def f32(*shape):
    return jax.ShapeDtypeStruct(shape, jnp.float32)


def hbm32(*shape):
    return pltpu.HBM(shape, jnp.float32)


def pinned(*arrays):
    return [pltpu.with_memory_space_constraint(array, pltpu.HBM) for array in arrays]


def shifted(values, axis, step):
    count = lax.axis_size(axis)
    pairs = [(i, i + step) for i in range(count) if 0 <= i + step < count]
    return lax.ppermute(values, axis, pairs)


def exchange(chunks):
    return lax.all_to_all(chunks, "af", split_axis=0, concat_axis=0, tiled=True)


def per_device(
    coarse_state, coarse_kappa, coarse_rate, fine_state, fine_kappa, fine_rate, boxes, cover
):
    af_count = lax.axis_size("af")
    slots = fine_state.shape[0]
    cells_x, cells_y = coarse_state.shape[2:]
    group = af_count * slots
    lanes = group * BLK
    halves = cells_y // LANES
    rows = PLANES * cells_x
    plain = NZC * cells_x
    sizes = dict(cells_x=cells_x, cells_y=cells_y, group=group)

    span = cells_x + 2 * PAD
    new, send, place, xlo, xhi, ylo, yhi = pl.pallas_call(
        functools.partial(strips_kernel, slots=slots, **sizes),
        out_shape=[
            hbm32(rows, cells_y),
            hbm32(af_count, CHUNK_ROWS, LANES),
            jax.ShapeDtypeStruct((16, lanes), jnp.int32),
        ]
        + [f32(EDGE_ROWS, cells_y)] * 2
        + [f32(cells_x, LANES)] * 2,
        in_specs=[HBM] * 4,
        out_specs=[HBM] * 2 + [VMEM] * 5,
        scratch_shapes=[
            pltpu.VMEM((2, boxes.shape[0]), jnp.int32),
            pltpu.VMEM((rows, cells_y), jnp.float32),
            pltpu.VMEM((plain, cells_y), jnp.float32),
            pltpu.VMEM((plain, cells_y), jnp.float32),
            pltpu.VMEM((rows, cells_y), jnp.float32),
            pltpu.VMEM(((SPECIES + 1) * halves * NZC * span, LANES), jnp.float32),
            pltpu.VMEM((rows * halves, LANES), jnp.float32),
            pltpu.VMEM((af_count, CHUNK_ROWS, LANES), jnp.float32),
            pltpu.SemaphoreType.DMA((4,)),
            pltpu.SemaphoreType.DMA((af_count,)),
        ],
        compiler_params=PARAMS,
        name="strips",
    )(
        *pinned(
            boxes.T,
            coarse_state.reshape(rows, cells_y),
            coarse_kappa.reshape(plain, cells_y),
            coarse_rate.reshape(plain, cells_y),
        )
    )

    strips = exchange(send)

    xlo_sent, xhi_sent = pl.pallas_call(
        hand_on_kernel,
        out_shape=[f32(EDGE_ROWS, cells_y)] * 2,
        in_specs=[VMEM] * 2,
        out_specs=[VMEM] * 2,
        compiler_params=pltpu.CompilerParams(vmem_limit_bytes=1024 * 1024),
        name="hand_on",
    )(xlo, xhi)
    xl = shifted(xhi_sent, "af", 1)
    xr = shifted(xlo_sent, "af", -1)

    kept = [hbm32(slots * size, LANES) for size in (FIELD_ROWS, COEFF_ROWS, UPWARD_ROWS)]
    kept_scratch = [pltpu.VMEM((slots * size, LANES), jnp.float32)
        for size in (FIELD_ROWS, COEFF_ROWS, UPWARD_ROWS)]
    fields, coeffs, upward = pl.pallas_call(
        functools.partial(prepare_kernel, slots=slots),
        out_shape=kept,
        in_specs=[VMEM] + [HBM] * 3,
        out_specs=[HBM] * 3,
        scratch_shapes=kept_scratch
        + [
            pltpu.VMEM(fine_state.shape, jnp.float32),
            pltpu.VMEM(fine_kappa.shape, jnp.float32),
            pltpu.VMEM(fine_rate.shape, jnp.float32),
            pltpu.VMEM((slots * FIELD_ROWS, LANES), jnp.float32),
            pltpu.VMEM((slots * UPWARD_ROWS, LANES), jnp.float32),
            pltpu.SemaphoreType.DMA((3, slots)),
            pltpu.SemaphoreType.DMA((3, slots)),
        ],
        compiler_params=PARAMS,
        name="prepare",
    )(xlo_sent, *pinned(fine_state, fine_kappa, fine_rate))

    chunk = (AVG_ROWS // FACES, LANES)
    fine_out, averages = pl.pallas_call(
        functools.partial(finish_kernel, slots=slots),
        out_shape=[hbm32(*fine_state.shape), hbm32(af_count, *chunk)],
        in_specs=[VMEM] + [HBM] * 3 + [VMEM] * 2,
        out_specs=[HBM] * 2,
        scratch_shapes=kept_scratch
        + [
            pltpu.VMEM((2 * LANES, EDGE * EDGE), jnp.bfloat16),
            pltpu.VMEM((2 * SPECIES * FZ, STRIP_ROWS), jnp.bfloat16),
            pltpu.VMEM((2 * LANES, LANES), jnp.bfloat16),
            pltpu.VMEM(chunk, jnp.float32),
            pltpu.VMEM((slots * 2 * SPECIES * FZ, EDGE * EDGE), jnp.float32),
            pltpu.VMEM((slots * FIELD_ROWS, LANES), jnp.float32),
            pltpu.VMEM((RATIO - 1, SPECIES * TILES * FZ, LANES), jnp.float32),
            pltpu.VMEM(fine_state.shape, jnp.float32),
            pltpu.SemaphoreType.DMA((slots,)),
            pltpu.SemaphoreType.DMA((3, slots)),
            pltpu.SemaphoreType.DMA((af_count,)),
        ],
        compiler_params=PARAMS,
        name="finish",
    )(strips, *pinned(fields, coeffs, upward), xl, xr)

    arrived = exchange(averages)

    yl = shifted(yhi, "col", 1)
    yr = shifted(ylo, "col", -1)
    whole = pl.pallas_call(
        functools.partial(edges_kernel, cells_x=cells_x, cells_y=cells_y),
        out_shape=f32(rows, cells_y),
        in_specs=[HBM] + [VMEM] * 8,
        out_specs=VMEM,
        scratch_shapes=[pltpu.VMEM((rows, cells_y), jnp.float32), pltpu.SemaphoreType.DMA],
        compiler_params=PARAMS,
        name="edges",
    )(*pinned(new), xlo, xhi, ylo, yhi, xl, xr, yl, yr)

    placed = pl.pallas_call(
        functools.partial(place_kernel, slots=slots, **sizes),
        out_shape=f32(rows, cells_y),
        in_specs=[VMEM] * 3,
        out_specs=VMEM,
        compiler_params=PARAMS,
        name="place",
    )(place, arrived, whole)
    return (placed.reshape(coarse_state.shape), fine_out)


def solution(mesh):
    return jax.shard_map(
        per_device,
        mesh=mesh,
        in_specs=(
            P(None, None, "af", "col"),
            P(None, "af", "col"),
            P(None, "af", "col"),
            P(("col", "af"), None, None, None),
            P(("col", "af"), None, None),
            P(("col", "af"), None, None),
            P(),
            P(),
        ),
        out_specs=(P(None, None, "af", "col"), P(("col", "af"), None, None, None)),
        check_vma=False,
    )
```

```python
import functools

import jax
import jax.numpy as jnp
from jax import lax
from jax.experimental import pallas as pl
from jax.experimental.pallas import tpu as pltpu
from jax.sharding import PartitionSpec as P

NZC = 8
RATIO = 4
BLK = 8
SPECIES = 3
EDGE = BLK * RATIO
FZ = NZC * RATIO
LANES = 128
TILES = EDGE * EDGE // LANES
DEPTH = 8
ZTILES = FZ // DEPTH
STRIDE = 40
PAD = 8
FACES = 4
PLANES = SPECIES * NZC
STRIP_ROWS = 2 * PLANES
AVG_ROWS = PLANES * BLK
KINDS = 8
FIELD_ROWS = SPECIES * TILES * STRIDE + PAD
COEFF_ROWS = KINDS * TILES * FZ
UPWARD_ROWS = TILES * STRIDE + PAD
EDGE_ROWS = PLANES + NZC
BESIDE_ROWS = 2 * NZC
CHUNK_ROWS = STRIP_ROWS + BESIDE_ROWS

DT_COARSE = 1.0 / 28.0
DIFFUSE = (1.0, 0.7, 0.45)
SIGNS = (-1.0, -1.0, 1.0)
FINE_SCALE = RATIO * RATIO * DT_COARSE / RATIO
DT_FINE = DT_COARSE / RATIO


def lane_ids(shape):
    return lax.broadcasted_iota(jnp.int32, shape, len(shape) - 1)


def roll_lanes(values, shift):
    width = values.shape[-1]
    shift = shift % width
    return values if shift == 0 else pltpu.roll(values, shift, values.ndim - 1)


def split_pair(values):
    high = values.astype(jnp.bfloat16)
    low = (values - high.astype(jnp.float32)).astype(jnp.bfloat16)
    return high, low


def face(scale, one, other):
    summed = one + other
    inverse = pl.reciprocal(summed, approx=True)
    inverse = inverse * (2.0 - summed * inverse)
    return (2.0 * scale) * (one * other) * inverse


def start_all(copies):
    for copy in copies:
        copy.start()


def selector(place_ref, column, cells_y):
    wanted = jnp.where(place_ref[0:8, :] == column, place_ref[8:16, :], -1)
    row = lax.broadcasted_iota(jnp.int32, wanted.shape, 0)
    return jnp.concatenate(
        [jnp.where(row + 8 * at == wanted, 1.0, 0.0) for at in range(cells_y // 8)], axis=0
    ).astype(jnp.bfloat16)


def strips_kernel(
    boxes_hbm,
    state_hbm,
    kappa_hbm,
    rate_hbm,
    new_hbm,
    send_hbm,
    place_ref,
    xlo_ref,
    xhi_ref,
    ylo_ref,
    yhi_ref,
    boxes_ref,
    state_ref,
    kappa_ref,
    rate_ref,
    new_ref,
    padded,
    fresh,
    send_ref,
    sems,
    send_sems,
    *,
    cells_x,
    cells_y,
    group,
    slots,
):
    pairs = (
        (boxes_hbm, boxes_ref),
        (kappa_hbm, kappa_ref),
        (state_hbm, state_ref),
        (rate_hbm, rate_ref),
    )
    copies = [
        pltpu.make_async_copy(source, target, sems.at[index])
        for index, (source, target) in enumerate(pairs)
    ]
    start_all(copies)

    patches = boxes_ref.shape[1]
    lanes = group * BLK
    base_patch = lax.axis_index("col") * group
    member = lax.broadcasted_iota(jnp.int32, (patches, lanes), 0) - base_patch
    spread = jnp.where(member == lane_ids((patches, lanes)) // BLK, 1.0, 0.0).astype(jnp.bfloat16)
    first_col = lax.axis_index("af") * (cells_x // BLK)
    first_cell = lax.axis_index("col") * cells_y
    copies[0].wait()
    boxes = boxes_ref[...].astype(jnp.float32)
    stacked = jnp.concatenate(
        [jnp.broadcast_to(boxes[row : row + 1], (8, patches)) for row in range(2)], axis=0
    )
    found = jnp.dot(
        stacked.astype(jnp.bfloat16), spread, preferred_element_type=jnp.float32
    ).astype(jnp.int32)
    place_ref[0:8, :] = found[0:8] - first_col
    place_ref[8:16, :] = found[8:16] * BLK - first_cell + lane_ids((8, lanes)) % BLK

    halves = cells_y // LANES
    span = cells_x + 2 * PAD
    nothing = jnp.zeros((PAD, LANES), jnp.float32)

    def base(field, half, z):
        return ((field * halves + half) * NZC + z) * span

    for copy in copies[1:]:
        copy.wait()
    for field in range(SPECIES + 1):
        for half in range(halves):
            cols = pl.ds(half * LANES, LANES)
            for z in range(NZC):
                if field < SPECIES:
                    start = (field * NZC + z) * cells_x
                    plane = state_ref[start : start + cells_x, cols]
                else:
                    plane = kappa_ref[z * cells_x : (z + 1) * cells_x, cols]
                at = base(field, half, z)
                padded[at : at + PAD, :] = nothing
                padded[at + PAD : at + PAD + cells_x, :] = plane
                padded[at + PAD + cells_x : at + span, :] = nothing

    lane = lane_ids((cells_x, LANES))
    row_id = lax.broadcasted_iota(jnp.int32, (cells_x, LANES), 0)

    low = jnp.zeros((cells_x, LANES), jnp.float32)
    high = jnp.zeros((cells_x, LANES), jnp.float32)
    for plane in range(PLANES + NZC):
        field, z = divmod(plane, NZC)
        at = base(field, 0, z) + PAD
        first = padded[at : at + cells_x, :]
        at = base(field, halves - 1, z) + PAD
        last = padded[at : at + cells_x, :]
        low = jnp.where(lane == plane, roll_lanes(first, plane), low)
        high = jnp.where(lane == plane, roll_lanes(last, plane + 1), high)
    ylo_ref[...] = low
    yhi_ref[...] = high

    def load(field, half, z, shift):
        at = base(field, half, z) + PAD + shift
        return padded[at : at + cells_x, :]

    def neighbours(field, half, z):
        here = load(field, half, z, 0)
        after = roll_lanes(here, -1)
        if half + 1 < halves:
            after = jnp.where(
                lane == LANES - 1, roll_lanes(load(field, half + 1, z, 0), -1), after
            )
        before = roll_lanes(here, 1)
        if half > 0:
            before = jnp.where(lane == 0, roll_lanes(load(field, half - 1, z, 0), 1), before)
        found = [after, before, load(field, half, z, 1), load(field, half, z, -1)]
        if z + 1 < NZC:
            found.append(load(field, half, z + 1, 0))
        if z > 0:
            found.append(load(field, half, z - 1, 0))
        return found

    for z in range(NZC):
        for half in range(halves):
            cols = pl.ds(half * LANES, LANES)
            conduct = load(SPECIES, half, z, 0)
            coeffs = [face(DT_COARSE, conduct, other) for other in neighbours(SPECIES, half, z)]
            if half == halves - 1:
                coeffs[0] = jnp.where(lane == LANES - 1, 0.0, coeffs[0])
            if half == 0:
                coeffs[1] = jnp.where(lane == 0, 0.0, coeffs[1])
            coeffs[2] = jnp.where(row_id == cells_x - 1, 0.0, coeffs[2])
            coeffs[3] = jnp.where(row_id == 0, 0.0, coeffs[3])
            centers = [load(field, half, z, 0) for field in range(SPECIES)]
            forward = (DT_COARSE * rate_ref[z * cells_x : (z + 1) * cells_x, cols]) * (
                centers[0] * centers[1] - centers[2]
            )
            for field in range(SPECIES):
                center = centers[field]
                flux = None
                for coeff, other in zip(coeffs, neighbours(field, half, z)):
                    term = coeff * (other - center)
                    flux = term if flux is None else flux + term
                start = (field * NZC + z) * cells_x
                result = center + DIFFUSE[field] * flux + SIGNS[field] * forward
                new_ref[start : start + cells_x, cols] = result
                start = ((field * halves + half) * NZC + z) * cells_x
                fresh[start : start + cells_x, :] = result

    keep_new = pltpu.make_async_copy(new_ref, new_hbm, sems.at[0])
    keep_new.start()

    def old_row(field, half, row):
        return padded[pl.ds(base(field, half, 0) + PAD + row, NZC, stride=span), :]

    def edge_at(row):
        return jnp.concatenate(
            [
                jnp.concatenate([old_row(field, half, row) for field in range(SPECIES + 1)], axis=0)
                for half in range(halves)
            ],
            axis=1,
        )

    def rows_at(row):
        columns = []
        for half in range(halves):
            pieces = [old_row(field, half, row) for field in range(SPECIES)]
            for field in range(SPECIES):
                start = (field * halves + half) * NZC * cells_x
                pieces.append(fresh[pl.ds(start + row, NZC, stride=cells_x), :])
            columns.append(jnp.concatenate(pieces, axis=0))
        return jnp.concatenate(columns, axis=1)

    block_cols = cells_x // BLK
    spot = lane_ids((STRIP_ROWS, cells_y)) % BLK
    lower_y = []
    upper_y = []
    for column in range(block_cols):
        below = jnp.zeros((STRIP_ROWS, cells_y), jnp.float32)
        above = jnp.zeros((STRIP_ROWS, cells_y), jnp.float32)
        for x in range(BLK):
            turned = roll_lanes(rows_at(column * BLK + x), x + 1)
            below = jnp.where(spot == x, turned, below)
            above = jnp.where(spot == (x + 1) % BLK, turned, above)
        lower_y.append(below)
        upper_y.append(roll_lanes(above, -1 - BLK))

    first_row = edge_at(0)
    last_row = edge_at(cells_x - 1)
    xlo_ref[...] = first_row
    xhi_ref[...] = last_row
    place = lane_ids((NZC, cells_y)) % BLK
    ones = jnp.ones((NZC, cells_y), jnp.float32)

    def field_of(row, field):
        return row[field * NZC : (field + 1) * NZC]

    def corners(row, fields, first_at):
        found = jnp.zeros((NZC, cells_y), jnp.float32)
        for order, field in enumerate(fields):
            at = first_at + 2 * order
            values = field_of(row, field)
            found = jnp.where(place == at, roll_lanes(values, at + 1), found)
            found = jnp.where(place == at + 1, roll_lanes(values, at + 1 - BLK), found)
        return found

    every = range(SPECIES)

    def near(row):
        own = [(field, field_of(row, field)) for field in range(SPECIES + 1)]
        return own + [(5, corners(row, [SPECIES], 0))]

    def far(row):
        return [
            (4, field_of(row, SPECIES)),
            (5, corners(row, every, 2)),
            (6, corners(row, [SPECIES], 0)),
        ]

    extra_members = {
        -1: far(first_row),
        0: near(first_row),
        block_cols - 1: near(last_row) + [(7, ones)],
        block_cols: far(last_row),
    }

    faces = [None] * (3 * FACES)

    def add(index, part):
        faces[index] = part if faces[index] is None else faces[index] + part

    for column in range(-1, block_cols + 1):
        members = []
        if column >= 1:
            members.append((0, rows_at(column * BLK - 1)))
        if column < block_cols - 1:
            members.append((1, rows_at(column * BLK + BLK)))
        if 0 <= column < block_cols:
            members.append((2, lower_y[column]))
            members.append((3, upper_y[column]))
        for index, rows in extra_members.get(column, []):
            members.append((FACES + index, rows))
        operands = []
        for _, rows in members:
            operands.extend(split_pair(rows))
        moved = jnp.dot(
            jnp.concatenate(operands, axis=0),
            selector(place_ref, column, cells_y),
            preferred_element_type=jnp.float32,
        )
        at = 0
        for index, rows in members:
            size = rows.shape[0]
            add(index, moved[at : at + size] + moved[at + size : at + 2 * size])
            at += 2 * size

    width = slots * BLK
    outgoing = [
        pltpu.make_async_copy(send_ref.at[target], send_hbm.at[target], send_sems.at[target])
        for target in range(group // slots)
    ]
    for target in range(group // slots):
        first = target * width
        tile = first // LANES * LANES
        for start, size, kind in (
            (0, STRIP_ROWS, 0),
            (STRIP_ROWS, NZC, FACES),
            (STRIP_ROWS + NZC, NZC, 2 * FACES),
        ):
            part = lane_ids((size, LANES)) // width
            chunk = jnp.zeros((size, LANES), jnp.float32)
            for index in range(FACES):
                piece = faces[kind + index][:, tile : tile + LANES]
                chunk = jnp.where(
                    part == index, roll_lanes(piece, index * width - (first - tile)), chunk
                )
            send_ref[target, start : start + size, :] = chunk
        outgoing[target].start()
    for copy in outgoing:
        copy.wait()
    keep_new.wait()


def ghost_table(tile):
    lane = lane_ids((BLK, LANES))
    pos = lax.broadcasted_iota(jnp.int32, (BLK, LANES), 0)
    x = tile * (LANES // EDGE) + lane // EDGE
    y = lane % EDGE
    along_y = y // RATIO == pos
    along_x = x // RATIO == pos
    seen = (
        (x == 0) & along_y,
        (x == EDGE - 1) & along_y,
        (y == 0) & along_x,
        (y == EDGE - 1) & along_x,
    )
    nothing = jnp.zeros((LANES // FACES - BLK, LANES), jnp.float32)
    rows = []
    for where in seen:
        rows.extend([jnp.where(where, 1.0, 0.0), nothing])
    return jnp.concatenate(rows + rows, axis=0).astype(jnp.bfloat16)


def plane_table():
    shape = (2 * SPECIES * FZ, STRIP_ROWS)
    rows = lax.broadcasted_iota(jnp.int32, shape, 0)
    return jnp.where(rows // RATIO == lane_ids(shape), 1.0, 0.0).astype(jnp.bfloat16)


def mean_table():
    shape = (2 * LANES, LANES)
    rows = lax.broadcasted_iota(jnp.int32, shape, 0)
    same = rows % EDGE // RATIO == lane_ids(shape) % BLK
    return jnp.where(same, 1.0 / RATIO**3, 0.0).astype(jnp.bfloat16)


def complete_strips(gathered):
    width = LANES // FACES
    own = gathered[STRIP_ROWS : STRIP_ROWS + NZC]
    beside = gathered[STRIP_ROWS + NZC : STRIP_ROWS + 2 * NZC]
    lane = lane_ids((NZC, LANES))
    part = lane // width
    pos = lane % BLK
    flag = jnp.where(part == FACES - 1, beside, 0.0)
    flag = flag + roll_lanes(flag, width)
    upper = flag + roll_lanes(flag, 2 * width) > 0.5

    def coefficient(one, other):
        return face(DT_COARSE, jnp.maximum(one, 0.125), jnp.maximum(other, 0.125))

    block = coefficient(roll_lanes(own, width), beside)
    corner = coefficient(beside, roll_lanes(beside, -width))
    added = []
    for field in range(SPECIES):
        old = gathered[field * NZC : (field + 1) * NZC]
        there = jnp.where(upper, roll_lanes(old, -width), old)
        across = DIFFUSE[field] * block * (roll_lanes(own, -field * width) - there)
        below = jnp.where(upper, roll_lanes(old, -width - (BLK - 1)), roll_lanes(old, -width))
        above = jnp.where(
            upper, roll_lanes(old, -2 * width - (BLK - 2)), roll_lanes(old, 1 - 2 * width)
        )
        here = jnp.where(pos == 0, below, above)
        along = DIFFUSE[field] * corner * (roll_lanes(beside, -2 - 2 * field) - here)
        share = jnp.where((part == 0) & ~upper, across, 0.0)
        share = jnp.where((part == 1) & upper, roll_lanes(across, width), share)
        for index in range(2):
            for at, chosen in ((0, ~upper), (BLK - 1, upper)):
                moved = roll_lanes(along, (1 + index) * width + at - index)
                share = jnp.where((part == 2 + index) & (pos == at) & chosen, moved, share)
        added.append(share)
    new = gathered[PLANES:STRIP_ROWS] + jnp.concatenate(added, axis=0)
    return gathered[:PLANES], new


def aligned(start, size):
    return pl.ds(start if isinstance(start, int) else pl.multiple_of(start, 8), size)


def padded_at(block, ztile):
    return block * STRIDE + PAD + DEPTH * ztile


def advance(source, target, coeffs, upward, slot, from_rows, to_rows, ztile, ghosts):
    lane = lane_ids((DEPTH, LANES))

    def value(field, tile, shift):
        start = from_rows + padded_at(field * TILES + tile, ztile) + shift
        return source[aligned(start, DEPTH) if shift == 0 else pl.ds(start, DEPTH), :]

    def get(kind, tile):
        return coeffs[
            aligned(slot * COEFF_ROWS + (kind * TILES + tile) * FZ + DEPTH * ztile, DEPTH), :
        ]

    centers = [value(field, 0, 0) for field in range(SPECIES)]
    down = [roll_lanes(center, -EDGE) for center in centers]
    up = [roll_lanes(center, EDGE) for center in centers]
    up_before = list(up)
    for tile in range(TILES):
        if tile + 1 < TILES:
            centers_after = [value(field, tile + 1, 0) for field in range(SPECIES)]
            down_after = [roll_lanes(center, -EDGE) for center in centers_after]
        next_x, prev_x, next_y, rate = [get(kind, tile) for kind in range(4)]
        prev_y = roll_lanes(next_y, 1)
        base = slot * UPWARD_ROWS + padded_at(tile, ztile)
        next_z = upward[aligned(base, DEPTH), :]
        prev_z = upward[pl.ds(base - 1, DEPTH), :]
        forward = rate * (centers[0] * centers[1] - centers[2])
        for field in range(SPECIES):
            center = centers[field]
            ahead, behind = down[field], up[field]
            if tile + 1 < TILES:
                ahead = jnp.where(lane < LANES - EDGE, ahead, down_after[field])
            if tile > 0:
                behind = jnp.where(lane >= EDGE, behind, up_before[field])
            flux = (next_x * ahead + prev_x * behind) + (
                next_y * roll_lanes(center, -1) + prev_y * roll_lanes(center, 1)
            )
            flux = flux + (next_z * value(field, tile, 1) + prev_z * value(field, tile, -1))
            share = ghosts(field, tile)
            if share is not None:
                flux = flux + share
            if DIFFUSE[field] != 1.0:
                flux = DIFFUSE[field] * flux
            result = get(4 + field, tile) * center + flux
            result = result - forward if SIGNS[field] < 0 else result + forward
            target[aligned(to_rows + padded_at(field * TILES + tile, ztile), DEPTH), :] = result
        if tile + 1 < TILES:
            up_before = up
            centers, down = centers_after, down_after
            up = [roll_lanes(center, EDGE) for center in centers]


def clear_pads(ref, size):
    edge = jnp.zeros((PAD, LANES), jnp.float32)
    for start in range(0, ref.shape[0], size):
        for row in range(start, start + size, STRIDE):
            ref[row : row + PAD, :] = edge


def hand_on_kernel(low_ref, high_ref, low_out, high_out):
    low_out[...] = low_ref[...]
    high_out[...] = high_ref[...]


def prepare_kernel(
    after_ref,
    state_hbm,
    kappa_hbm,
    rate_hbm,
    fields_hbm,
    coeffs_hbm,
    upward_hbm,
    ghost_hbm,
    fields_ref,
    coeffs,
    upward,
    ghost_ref,
    state_ref,
    kappa_ref,
    rate_ref,
    first,
    conduct,
    sems,
    out_sems,
    ghost_sem,
    *,
    slots,
):
    def loads(slot):
        return [
            pltpu.make_async_copy(source.at[slot], target.at[slot], sems.at[order, slot])
            for order, (source, target) in enumerate(
                ((kappa_hbm, kappa_ref), (rate_hbm, rate_ref), (state_hbm, state_ref))
            )
        ]

    for slot in range(slots):
        start_all(loads(slot))

    def stores(slot, start, stop):
        return [
            pltpu.make_async_copy(
                source.at[aligned(slot * size, size)],
                target.at[aligned(slot * size, size)],
                out_sems.at[order, slot],
            )
            for order, (source, target, size) in enumerate(
                (
                    (fields_ref, fields_hbm, FIELD_ROWS),
                    (coeffs, coeffs_hbm, COEFF_ROWS),
                    (upward, upward_hbm, UPWARD_ROWS),
                )
            )
            if start <= order < stop
        ]

    for ref, size in (
        (conduct, UPWARD_ROWS),
        (upward, UPWARD_ROWS),
        (first, FIELD_ROWS),
        (fields_ref, FIELD_ROWS),
    ):
        clear_pads(ref, size)
    for tile in range(TILES):
        ghost_ref[:, tile * LANES : (tile + 1) * LANES] = ghost_table(tile)
    keep_ghost = pltpu.make_async_copy(ghost_ref, ghost_hbm, ghost_sem)
    keep_ghost.start()

    lane = lane_ids((DEPTH, LANES))
    column = lane % EDGE
    side_y = jnp.where((column == 0) | (column == EDGE - 1), 1.0, 0.0)

    def one_patch(slot):
        for copy in loads(slot):
            copy.wait()

        for tile in range(TILES):
            cols = pl.ds(tile * LANES, LANES)
            for field in range(SPECIES):
                spot = aligned(slot * FIELD_ROWS + padded_at(field * TILES + tile, 0), FZ)
                first[spot, :] = state_ref[slot, field, :, cols]
            spot = aligned(slot * UPWARD_ROWS + padded_at(tile, 0), FZ)
            conduct[spot, :] = kappa_ref[slot, :, cols]

        def keep(kind, tile, ztile, values):
            coeffs[
                aligned(slot * COEFF_ROWS + (kind * TILES + tile) * FZ + DEPTH * ztile, DEPTH), :
            ] = values

        for ztile in range(ZTILES):

            def here(tile, shift):
                start = slot * UPWARD_ROWS + padded_at(tile, ztile) + shift
                return conduct[aligned(start, DEPTH) if shift == 0 else pl.ds(start, DEPTH), :]

            tiles = range(TILES)
            centers = [here(tile, 0) for tile in tiles]
            turned = [roll_lanes(center, -EDGE) for center in centers]
            total = [FINE_SCALE * side_y * center for center in centers]
            next_x = []
            for tile in tiles:
                other = turned[tile]
                if tile + 1 < TILES:
                    other = jnp.where(lane < LANES - EDGE, other, turned[tile + 1])
                value = face(FINE_SCALE, centers[tile], other)
                if tile == TILES - 1:
                    value = jnp.where(lane < LANES - EDGE, value, 0.0)
                next_x.append(value)
                keep(0, tile, ztile, value)
            back = [roll_lanes(value, EDGE) for value in next_x]
            side = [roll_lanes(center, -1) for center in centers]
            for tile in tiles:
                prev_x = jnp.where(lane >= EDGE, back[tile], back[tile - 1] if tile else 0.0)
                keep(1, tile, ztile, prev_x)
                total[tile] = total[tile] + (next_x[tile] + prev_x)
            total[0] = total[0] + jnp.where(lane < EDGE, FINE_SCALE * centers[0], 0.0)
            total[-1] = total[-1] + jnp.where(lane >= LANES - EDGE, FINE_SCALE * centers[-1], 0.0)
            next_y = []
            for tile in tiles:
                value = face(FINE_SCALE, centers[tile], side[tile])
                next_y.append(jnp.where(column < EDGE - 1, value, 0.0))
                keep(2, tile, ztile, next_y[tile])
            prev_y = [roll_lanes(value, 1) for value in next_y]
            for tile in tiles:
                total[tile] = total[tile] + (next_y[tile] + prev_y[tile])
                next_z = face(FINE_SCALE, centers[tile], here(tile, 1))
                spot = slot * UPWARD_ROWS + padded_at(tile, ztile)
                upward[aligned(spot, DEPTH), :] = next_z
                total[tile] = total[tile] + next_z
                keep(7, tile, ztile, FINE_SCALE * centers[tile])
            for tile in tiles:
                spot = slot * UPWARD_ROWS + padded_at(tile, ztile)
                total[tile] = total[tile] + upward[pl.ds(spot - 1, DEPTH), :]
                rate = rate_ref[slot, pl.ds(DEPTH * ztile, DEPTH), pl.ds(tile * LANES, LANES)]
                keep(3, tile, ztile, DT_FINE * rate)
                for field in range(SPECIES):
                    keep(4 + field, tile, ztile, 1.0 - DIFFUSE[field] * total[tile])

        start_all(stores(slot, 1, 3))
        for ztile in range(ZTILES):
            advance(
                first,
                fields_ref,
                coeffs,
                upward,
                slot,
                slot * FIELD_ROWS,
                slot * FIELD_ROWS,
                ztile,
                lambda field, tile: None,
            )
        start_all(stores(slot, 0, 1))

    for slot in range(slots):
        one_patch(slot)
    for slot in range(slots):
        for copy in stores(slot, 0, 3):
            copy.wait()
    keep_ghost.wait()


def finish_kernel(
    strips_ref,
    fields_hbm,
    coeffs_hbm,
    upward_hbm,
    ghost_hbm,
    xl_ref,
    xr_ref,
    out_hbm,
    avg_hbm,
    fields_ref,
    coeffs,
    upward,
    ghost_ref,
    plane_ref,
    mean_ref,
    avg_ref,
    ghosts_ref,
    first,
    share,
    staged,
    sems,
    in_sems,
    avg_sems,
    ghost_sem,
    *,
    slots,
):
    sources = strips_ref.shape[0]

    def loads(slot):
        return [
            pltpu.make_async_copy(
                source.at[aligned(slot * size, size)],
                target.at[aligned(slot * size, size)],
                in_sems.at[order, slot],
            )
            for order, (source, target, size) in enumerate(
                (
                    (fields_hbm, fields_ref, FIELD_ROWS),
                    (coeffs_hbm, coeffs, COEFF_ROWS),
                    (upward_hbm, upward, UPWARD_ROWS),
                )
            )
        ]

    take_ghost = pltpu.make_async_copy(ghost_hbm, ghost_ref, ghost_sem)
    take_ghost.start()
    start_all(loads(0))
    clear_pads(first, FIELD_ROWS)
    plane_ref[...] = plane_table()
    mean_ref[...] = mean_table()

    gathered = strips_ref[0]
    for source in range(1, sources):
        gathered = gathered + strips_ref[source]
    old, new = complete_strips(gathered)
    gathered = jnp.concatenate([old, (new - old) * (1.0 / RATIO)], axis=0)
    quarter = AVG_ROWS // FACES
    group_of = lane_ids((quarter, LANES)) // BLK

    def send_out(slot):
        return pltpu.make_async_copy(staged.at[slot], out_hbm.at[slot], sems.at[slot])

    stretched = [
        jnp.dot(
            plane_ref[...],
            jnp.concatenate(split_pair(roll_lanes(gathered, -slot * BLK)), axis=1),
            preferred_element_type=jnp.float32,
        ).astype(jnp.bfloat16)
        for slot in range(slots)
    ]
    ghost_rows = 2 * SPECIES * FZ
    take_ghost.wait()
    for pair in range(TILES // 2):
        cols = slice(2 * pair * LANES, 2 * (pair + 1) * LANES)
        for slot in range(slots):
            ghosts_ref[slot * ghost_rows : (slot + 1) * ghost_rows, cols] = jnp.dot(
                stretched[slot], ghost_ref[:, cols], preferred_element_type=jnp.float32
            )

    def one_patch(slot):
        for copy in loads(slot):
            copy.wait()
        if slot + 1 < slots:
            start_all(loads(slot + 1))
        base = slot * FIELD_ROWS
        scales = slot * COEFF_ROWS
        for tile in range(TILES):
            cols = pl.ds(tile * LANES, LANES)
            scale = coeffs[aligned(scales + (7 * TILES + tile) * FZ, FZ), :]
            for field in range(SPECIES):
                row = (field * TILES + tile) * FZ
                ghost = slot * ghost_rows + field * FZ
                old = scale * ghosts_ref[aligned(ghost, FZ), cols]
                drift = scale * ghosts_ref[aligned(ghost + SPECIES * FZ, FZ), cols]
                later = old
                for step in range(1, RATIO):
                    later = later + drift
                    share[step - 1, row : row + FZ, :] = later
                spot = aligned(base + padded_at(field * TILES + tile, 0), FZ)
                fields_ref[spot, :] = fields_ref[spot, :] + DIFFUSE[field] * old

        for step in range(1, RATIO):
            source, target = (fields_ref, first) if step % 2 else (first, fields_ref)
            for ztile in range(ZTILES):

                def ghosts(field, tile):
                    spot = pl.ds((field * TILES + tile) * FZ + DEPTH * ztile, DEPTH)
                    return share[step - 1, spot, :]

                advance(source, target, coeffs, upward, slot, base, base, ztile, ghosts)

        for tile in range(TILES):
            for field in range(SPECIES):
                spot = aligned(base + padded_at(field * TILES + tile, 0), FZ)
                staged[slot, field, :, pl.ds(tile * LANES, LANES)] = first[spot, :]
        send_out(slot).start()

    for slot in range(slots):
        one_patch(slot)
    sums = []
    for slot in range(slots):
        for field in range(SPECIES):
            for plane in range(NZC):
                start = slot * FIELD_ROWS + field * TILES * STRIDE + PAD + RATIO * plane
                part = [first[pl.ds(start + z, TILES, stride=STRIDE), :] for z in range(RATIO)]
                sums.append((part[0] + part[1]) + (part[2] + part[3]))
    means = jnp.dot(
        jnp.concatenate(split_pair(jnp.concatenate(sums, axis=0)), axis=1),
        mean_ref[...],
        preferred_element_type=jnp.float32,
    )
    chunk = jnp.zeros((quarter, LANES), jnp.float32)
    for slot in range(slots):
        for part in range(FACES):
            row = slot * AVG_ROWS + part * quarter
            chunk = jnp.where(group_of == part * slots + slot, means[row : row + quarter], chunk)
    avg_ref[...] = chunk
    copies = [
        pltpu.make_async_copy(avg_ref, avg_hbm.at[target], avg_sems.at[target])
        for target in range(sources)
    ]
    start_all(copies)
    for copy in copies:
        copy.wait()
    for slot in range(slots):
        send_out(slot).wait()


def edges_kernel(
    new_hbm,
    xlo_ref,
    xhi_ref,
    ylo_ref,
    yhi_ref,
    xl_ref,
    xr_ref,
    yl_ref,
    yr_ref,
    out_ref,
    new_ref,
    sem,
    *,
    cells_x,
    cells_y,
):
    me = lax.axis_index("af")
    last = lax.axis_size("af") - 1
    fetch = pltpu.make_async_copy(new_hbm, new_ref, sem)
    fetch.start()

    def edge_share(own_ref, other_ref):
        own = own_ref[...]
        other = other_ref[...]
        coeff = face(DT_COARSE, jnp.maximum(own, 0.125), other)
        lane = lane_ids(own.shape)
        spread = jnp.zeros_like(own)
        for field in range(SPECIES):
            moved = roll_lanes(coeff, (field - SPECIES) * NZC)
            spread = jnp.where(lane // NZC == field, DIFFUSE[field] * moved, spread)
        return spread * (other - own)

    lower = edge_share(ylo_ref, yl_ref)
    upper = edge_share(yhi_ref, yr_ref)

    lane = lane_ids((BLK, LANES))
    row_id = lax.broadcasted_iota(jnp.int32, (BLK, LANES), 0)
    halves = cells_y // LANES

    def side_share(own_ref, other_ref, exists):
        shares = []
        for half in range(halves):
            own = own_ref[:, half * LANES : (half + 1) * LANES]
            other = other_ref[:, half * LANES : (half + 1) * LANES]
            coeff = face(DT_COARSE, own[PLANES:], other[PLANES:])
            coeff = jnp.where(exists, coeff, 0.0)
            shares.append(
                jnp.concatenate(
                    [
                        (DIFFUSE[field] * coeff)
                        * (
                            other[field * NZC : (field + 1) * NZC]
                            - own[field * NZC : (field + 1) * NZC]
                        )
                        for field in range(SPECIES)
                    ],
                    axis=0,
                )
            )
        return shares

    before = side_share(xlo_ref, xl_ref, me > 0)
    after = side_share(xhi_ref, xr_ref, me < last)
    fetch.wait()
    block_cols = cells_x // BLK
    for column in range(block_cols):
        for plane in range(PLANES):
            row = plane * cells_x + column * BLK
            edge_rows = slice(column * BLK, (column + 1) * BLK)
            for half in range(halves):
                cols = slice(half * LANES, (half + 1) * LANES)
                coarse = new_ref[row : row + BLK, cols]
                if column == 0:
                    share = before[half][plane : plane + 1]
                    coarse = coarse + jnp.where(row_id == 0, share, 0.0)
                if column == block_cols - 1:
                    share = after[half][plane : plane + 1]
                    coarse = coarse + jnp.where(row_id == BLK - 1, share, 0.0)
                if half == 0:
                    share = roll_lanes(lower[edge_rows], -plane)
                    coarse = coarse + jnp.where(lane == 0, share, 0.0)
                if half == halves - 1:
                    share = roll_lanes(upper[edge_rows], LANES - 1 - plane)
                    coarse = coarse + jnp.where(lane == LANES - 1, share, 0.0)
                out_ref[row : row + BLK, cols] = coarse


def place_kernel(
    place_ref, avg_ref, new_ref, out_ref, *, cells_x, cells_y, group, slots
):
    width = slots * BLK
    quarter = AVG_ROWS // FACES
    per_tile = LANES // width
    part = lane_ids((quarter, LANES)) // width
    columns = []
    for tile in range(group * BLK // LANES):
        rows = []
        for index in range(FACES):
            merged = jnp.zeros((quarter, LANES), jnp.float32)
            for place in range(per_tile):
                piece = roll_lanes(avg_ref[tile * per_tile + place], (place - index) * width)
                merged = jnp.where(part == place, piece, merged)
            rows.append(merged)
        columns.append(jnp.concatenate(rows, axis=0))
    high, low = split_pair(jnp.concatenate(columns, axis=1))
    ones = jnp.ones((16, high.shape[1]), jnp.bfloat16)
    stacked = jnp.concatenate([high, low, ones], axis=0)

    halves = cells_y // LANES
    for column in range(cells_x // BLK):
        placed = lax.dot_general(
            stacked,
            selector(place_ref, column, cells_y),
            (((1,), (1,)), ((), ())),
            preferred_element_type=jnp.float32,
        )
        covered = placed[2 * AVG_ROWS : 2 * AVG_ROWS + 8] > 0.5
        for plane in range(PLANES):
            values = (
                placed[plane * BLK : (plane + 1) * BLK]
                + placed[AVG_ROWS + plane * BLK : AVG_ROWS + (plane + 1) * BLK]
            )
            row = plane * cells_x + column * BLK
            for half in range(halves):
                cols = slice(half * LANES, (half + 1) * LANES)
                coarse = new_ref[row : row + BLK, cols]
                out_ref[row : row + BLK, cols] = jnp.where(
                    covered[:, cols], values[:, cols], coarse
                )


VMEM = pl.BlockSpec(memory_space=pltpu.VMEM)
HBM = pl.BlockSpec(memory_space=pltpu.HBM)
PARAMS = pltpu.CompilerParams(vmem_limit_bytes=40 * 1024 * 1024)


def f32(*shape):
    return jax.ShapeDtypeStruct(shape, jnp.float32)


def hbm32(*shape):
    return pltpu.HBM(shape, jnp.float32)


def pinned(*arrays):
    return [pltpu.with_memory_space_constraint(array, pltpu.HBM) for array in arrays]


def shifted(values, axis, step):
    count = lax.axis_size(axis)
    pairs = [(i, i + step) for i in range(count) if 0 <= i + step < count]
    return lax.ppermute(values, axis, pairs)


def exchange(chunks):
    return lax.all_to_all(chunks, "af", split_axis=0, concat_axis=0, tiled=True)


def per_device(
    coarse_state, coarse_kappa, coarse_rate, fine_state, fine_kappa, fine_rate, boxes, cover
):
    af_count = lax.axis_size("af")
    slots = fine_state.shape[0]
    cells_x, cells_y = coarse_state.shape[2:]
    group = af_count * slots
    lanes = group * BLK
    halves = cells_y // LANES
    rows = PLANES * cells_x
    plain = NZC * cells_x
    sizes = dict(cells_x=cells_x, cells_y=cells_y, group=group)

    span = cells_x + 2 * PAD
    new, send, place, xlo, xhi, ylo, yhi = pl.pallas_call(
        functools.partial(strips_kernel, slots=slots, **sizes),
        out_shape=[
            hbm32(rows, cells_y),
            hbm32(af_count, CHUNK_ROWS, LANES),
            jax.ShapeDtypeStruct((16, lanes), jnp.int32),
        ]
        + [f32(EDGE_ROWS, cells_y)] * 2
        + [f32(cells_x, LANES)] * 2,
        in_specs=[HBM] * 4,
        out_specs=[HBM] * 2 + [VMEM] * 5,
        scratch_shapes=[
            pltpu.VMEM((2, boxes.shape[0]), jnp.int32),
            pltpu.VMEM((rows, cells_y), jnp.float32),
            pltpu.VMEM((plain, cells_y), jnp.float32),
            pltpu.VMEM((plain, cells_y), jnp.float32),
            pltpu.VMEM((rows, cells_y), jnp.float32),
            pltpu.VMEM(((SPECIES + 1) * halves * NZC * span, LANES), jnp.float32),
            pltpu.VMEM((rows * halves, LANES), jnp.float32),
            pltpu.VMEM((af_count, CHUNK_ROWS, LANES), jnp.float32),
            pltpu.SemaphoreType.DMA((4,)),
            pltpu.SemaphoreType.DMA((af_count,)),
        ],
        compiler_params=PARAMS,
        name="strips",
    )(
        *pinned(
            boxes.T,
            coarse_state.reshape(rows, cells_y),
            coarse_kappa.reshape(plain, cells_y),
            coarse_rate.reshape(plain, cells_y),
        )
    )

    strips = exchange(send)

    xlo_sent, xhi_sent = pl.pallas_call(
        hand_on_kernel,
        out_shape=[f32(EDGE_ROWS, cells_y)] * 2,
        in_specs=[VMEM] * 2,
        out_specs=[VMEM] * 2,
        compiler_params=pltpu.CompilerParams(vmem_limit_bytes=1024 * 1024),
        name="hand_on",
    )(xlo, xhi)
    xl = shifted(xhi_sent, "af", 1)
    xr = shifted(xlo_sent, "af", -1)

    kept = [hbm32(slots * size, LANES) for size in (FIELD_ROWS, COEFF_ROWS, UPWARD_ROWS)]
    kept_scratch = [pltpu.VMEM((slots * size, LANES), jnp.float32)
        for size in (FIELD_ROWS, COEFF_ROWS, UPWARD_ROWS)]
    table = (2 * LANES, EDGE * EDGE)
    fields, coeffs, upward, ghost = pl.pallas_call(
        functools.partial(prepare_kernel, slots=slots),
        out_shape=kept + [pltpu.HBM(table, jnp.bfloat16)],
        in_specs=[VMEM] + [HBM] * 3,
        out_specs=[HBM] * 4,
        scratch_shapes=kept_scratch
        + [
            pltpu.VMEM(table, jnp.bfloat16),
            pltpu.VMEM(fine_state.shape, jnp.float32),
            pltpu.VMEM(fine_kappa.shape, jnp.float32),
            pltpu.VMEM(fine_rate.shape, jnp.float32),
            pltpu.VMEM((slots * FIELD_ROWS, LANES), jnp.float32),
            pltpu.VMEM((slots * UPWARD_ROWS, LANES), jnp.float32),
            pltpu.SemaphoreType.DMA((3, slots)),
            pltpu.SemaphoreType.DMA((3, slots)),
            pltpu.SemaphoreType.DMA,
        ],
        compiler_params=PARAMS,
        name="prepare",
    )(xlo_sent, *pinned(fine_state, fine_kappa, fine_rate))

    chunk = (AVG_ROWS // FACES, LANES)
    fine_out, averages = pl.pallas_call(
        functools.partial(finish_kernel, slots=slots),
        out_shape=[hbm32(*fine_state.shape), hbm32(af_count, *chunk)],
        in_specs=[VMEM] + [HBM] * 4 + [VMEM] * 2,
        out_specs=[HBM] * 2,
        scratch_shapes=kept_scratch
        + [
            pltpu.VMEM((2 * LANES, EDGE * EDGE), jnp.bfloat16),
            pltpu.VMEM((2 * SPECIES * FZ, STRIP_ROWS), jnp.bfloat16),
            pltpu.VMEM((2 * LANES, LANES), jnp.bfloat16),
            pltpu.VMEM(chunk, jnp.float32),
            pltpu.VMEM((slots * 2 * SPECIES * FZ, EDGE * EDGE), jnp.float32),
            pltpu.VMEM((slots * FIELD_ROWS, LANES), jnp.float32),
            pltpu.VMEM((RATIO - 1, SPECIES * TILES * FZ, LANES), jnp.float32),
            pltpu.VMEM(fine_state.shape, jnp.float32),
            pltpu.SemaphoreType.DMA((slots,)),
            pltpu.SemaphoreType.DMA((3, slots)),
            pltpu.SemaphoreType.DMA((af_count,)),
            pltpu.SemaphoreType.DMA,
        ],
        compiler_params=PARAMS,
        name="finish",
    )(strips, *pinned(fields, coeffs, upward, ghost), xl, xr)

    arrived = exchange(averages)

    yl = shifted(yhi, "col", 1)
    yr = shifted(ylo, "col", -1)
    whole = pl.pallas_call(
        functools.partial(edges_kernel, cells_x=cells_x, cells_y=cells_y),
        out_shape=f32(rows, cells_y),
        in_specs=[HBM] + [VMEM] * 8,
        out_specs=VMEM,
        scratch_shapes=[pltpu.VMEM((rows, cells_y), jnp.float32), pltpu.SemaphoreType.DMA],
        compiler_params=PARAMS,
        name="edges",
    )(*pinned(new), xlo, xhi, ylo, yhi, xl, xr, yl, yr)

    placed = pl.pallas_call(
        functools.partial(place_kernel, slots=slots, **sizes),
        out_shape=f32(rows, cells_y),
        in_specs=[VMEM] * 3,
        out_specs=VMEM,
        compiler_params=PARAMS,
        name="place",
    )(place, arrived, whole)
    return (placed.reshape(coarse_state.shape), fine_out)


def solution(mesh):
    return jax.shard_map(
        per_device,
        mesh=mesh,
        in_specs=(
            P(None, None, "af", "col"),
            P(None, "af", "col"),
            P(None, "af", "col"),
            P(("col", "af"), None, None, None),
            P(("col", "af"), None, None),
            P(("col", "af"), None, None),
            P(),
            P(),
        ),
        out_specs=(P(None, None, "af", "col"), P(("col", "af"), None, None, None)),
        check_vma=False,
    )
```
